32 devices in a mesh: dp: 8 (over z, y), expert: 4 (over x, core).
Axes of the slice: x: 2, y: 2, z: 4, core: 2. Of those that a mesh axis runs over, the one named last changes fastest.
Arguments:
- tokens: bfloat16 [4096, 1536], P(('dp', 'expert')), may hold values from -6 to 6
- segments: int32 [32, 128], P(('dp', 'expert')), may hold values from 0 to 3, never falling along the last dimension, each value on 1 to 64 neighbouring positions
- routes: int32 [4096, 8], P(('dp', 'expert')), may hold values from 0 to 39, all different within a row; in each aligned block of 128 rows (0 to 127, 128 to 255, ...) at most 40 rows name the same one
- w_query: bfloat16 [1536, 1536], P('dp'), may hold values from -0.15625 to 0.15625
- w_key: bfloat16 [1536, 512], P('dp'), may hold values from -0.15625 to 0.15625
- w_value: bfloat16 [1536, 512], P('dp'), may hold values from -0.15625 to 0.15625
- w_output: bfloat16 [1536, 1536], P('dp'), may hold values from -0.625 to 0.625
- w_router: bfloat16 [1536, 40], P('dp'), may hold values from -0.078125 to 0.078125
- gain_attn: bfloat16 [1536], P('dp'), may hold values from 0.099609375 to 1.8984375
- gain_moe: bfloat16 [1536], P('dp'), may hold values from 0.099609375 to 1.8984375
- w_gate_up: bfloat16 [40, 1536, 1024], P('expert'), may hold values from -0.15625 to 0.15625
- w_down: bfloat16 [40, 512, 1536], P('expert'), may hold values from -1 to 1
- cotangent: bfloat16 [4096, 1536], P(('dp', 'expert')), may hold values from -6 to 6
Outputs:
- output: bfloat16 [4096, 1536], P(('dp', 'expert'))
- grad_tokens: bfloat16 [4096, 1536], P(('dp', 'expert'))
- grad_query: float32 [1536, 1536], P('dp')
- grad_key: float32 [1536, 512], P('dp')
- grad_value: float32 [1536, 512], P('dp')
- grad_output: float32 [1536, 1536], P('dp')
- grad_router: float32 [1536, 40], P('dp')
- grad_gain_attn: float32 [1536], P('dp')
- grad_gain_moe: float32 [1536], P('dp')
- grad_gate_up: float32 [40, 1536, 1024], P('expert', 'dp')
- grad_down: float32 [40, 512, 1536], P('expert', 'dp')
The draws below stay inside these ranges and needn't reach their ends.
Inputs may be any that keep to these rules, and one draw needn't show every extreme that they name: `routes`: in each aligned block of 128 rows (the rows of one device) no expert is named by more than 40 rows, a bound that some block reaches; the 8 experts of a row differ. `segments`: along each row the numbers never fall; a segment spans at most half of 128 positions, some segment exactly that.
All inputs are finite; a program needn't handle non-finite values.
Results may differ from the reference program's by a relative error of at most 0.023.
Values may be sent and summed in bfloat16 or wider, within the bound.
A program may use at most 256 MiB of HBM per device.

```python
import math
import jax
import jax.numpy as jnp
import numpy as np
from jax import lax

D = 1536
H = 24
KV = 8
HD = 64
F = 512
EXPERTS = 40
TOPK = 8
TOK_DEV = 128
CAP = 40
SEQS = 32
TOKENS = 4096


def block_levels(rng, shape, shards, least, high):
    gain = 1.0
    for axis_at, blocks in shards:
        draws = jax.random.uniform(jax.random.fold_in(jax.random.fold_in(rng, 6), axis_at), (blocks,), jnp.float32, least / len(shards), high / len(shards))
        gain = gain * jnp.repeat(jnp.exp(draws), shape[axis_at] // blocks).reshape((-1,) + (1,) * (len(shape) - 1 - axis_at))
    return gain


def length_profile(number_of, total, bound, skew):
    portions = [(1 << 20) // math.isqrt(grade ** skew) + 1 for grade in range(2, number_of + 1)]
    surplus, given = total - bound - (number_of - 1), [1] * (number_of - 1)
    while surplus > 0:
        movable = [i for i in range(number_of - 1) if given[i] < bound]
        mass, remaining = sum([portions[i] for i in movable]), surplus
        for i in movable:
            extra = min(bound - given[i], max(1, remaining * portions[i] // mass), surplus)
            given[i] = given[i] + extra
            surplus = surplus - extra
    return np.array([bound] + given)


def ragged(rng, amount, total, reach, lean):
    if amount == 2:
        one = jax.random.randint(rng, (), max(1, total - reach), min(reach, total - 1) + 1)
        return jnp.stack([one, total - one])
    lengths = jnp.asarray(length_profile(amount, total, reach, lean), jnp.int32)
    pairs = (amount - 1) // 2
    source_of, sink = lengths[1:1 + 2 * pairs:2], lengths[2:2 + 2 * pairs:2]
    margin = jnp.minimum(source_of - 1, reach - sink)
    shifted = jax.random.randint(jax.random.fold_in(rng, 1), (pairs,), 0, 1 << 20) % (margin + 1)
    lengths = lengths.at[1:1 + 2 * pairs:2].set(source_of - shifted).at[2:2 + 2 * pairs:2].set(sink + shifted)
    return lengths[jax.random.permutation(jax.random.fold_in(rng, 2), amount)]


def shared_out(own_key, own, number, rows, count, top, bound, skew):
    order = jax.random.permutation(own_key, count)
    packed, common = shares(count, rows * top, bound, skew, True), shares(count, rows * top, bound, skew, False)
    places = jnp.arange(count)

    def named(sizes, turn):
        used = int((sizes > 0).sum())
        fixed = max(1, used // 4)
        moved = fixed + (places - fixed + turn * (used - fixed)) % max(1, count - fixed)
        return jnp.zeros((count,), jnp.int32).at[order[jnp.where(places < fixed, places, moved)]].set(jnp.asarray(sizes, jnp.int32))

    sizes = jnp.where(number % 4 == 0, named(packed, number // 4), named(common, number - number // 4 - 1))
    mixed = jax.random.permutation(jax.random.fold_in(own, 3), count)
    donor, taker = mixed[0:count // 2 * 2:2], mixed[1:count // 2 * 2:2]
    margin = jnp.minimum(sizes[donor] - 1, bound - sizes[taker]) // 2
    margin = jnp.where((donor == order[0]) | (taker == order[0]) | (sizes[taker] == 0), 0, jnp.maximum(margin, 0))
    moved = jax.random.randint(jax.random.fold_in(own, 4), (count // 2,), 0, 1 << 20) % (margin + 1)
    sizes = sizes.at[donor].add(-moved).at[taker].add(moved)
    items = jnp.searchsorted(jnp.cumsum(sizes), jnp.arange(rows * top), side="right").astype(jnp.int32)
    grid = items.reshape(top, rows).T
    grid = grid[jax.random.permutation(jax.random.fold_in(own, 1), rows)]
    turn = jax.random.randint(jax.random.fold_in(own, 2), (rows, 1), 0, top)
    return jnp.take_along_axis(grid, (jnp.arange(top)[None, :] + turn) % top, axis=1)


def shares(number_of, total, bound, skew, full):
    weights = [(1 << 20) // math.isqrt(grade ** skew) + 1 for grade in range(1, number_of + 1)]
    largest = bound if full else min(bound, max(-(-total // number_of), total * weights[0] // sum(weights)))
    least = 1 if total - largest >= number_of - 1 else 0
    holding, surplus = [largest] + [least] * (number_of - 1), total - largest - least * (number_of - 1)
    while surplus > 0:
        free = [i for i in range(1, number_of) if holding[i] < largest] or [i for i in range(1, number_of) if holding[i] < bound]
        pool, remaining = sum([weights[i] for i in free]), surplus
        for i in free:
            more = min(bound - holding[i], max(1, remaining * weights[i] // pool), surplus)
            holding[i] = holding[i] + more
            surplus = surplus - more
    return np.array(holding)


def centred(rng, extent, spread, limit, cuts=(), kind=jnp.bfloat16):
    values = jax.random.normal(rng, extent, jnp.float32) * spread
    if len(cuts) > 0:
        values = block_levels(rng, extent, cuts, -0.22, 0.18) * values
    return jnp.clip(values, min=-limit, max=limit).astype(kind)


def setup_inputs(seed: int = 0) -> dict:
    streams_of = jax.random.split(jax.random.key(seed), 14)
    tokens = centred(streams_of[0], (TOKENS, D), 1.0, 6.0, ((0, 32),))
    segments = jax.vmap(lambda own: jnp.searchsorted(jnp.cumsum(ragged(own, 4, TOK_DEV, TOK_DEV // 2, 1)), jnp.arange(TOK_DEV), side="right"))(jax.random.split(streams_of[1], SEQS)).reshape((SEQS, TOK_DEV)).astype(jnp.int32)
    routes_keys = jax.random.split(jax.random.fold_in(streams_of[2], 1), TOKENS // TOK_DEV)
    routes_turns = jax.random.permutation(jax.random.fold_in(streams_of[2], 3), TOKENS // TOK_DEV)
    routes = jax.vmap(lambda own, number: shared_out(jax.random.fold_in(streams_of[2], 2), own, number, TOK_DEV, EXPERTS, TOPK, CAP, 1))(routes_keys, routes_turns).reshape((TOKENS, TOPK))
    w_query = centred(streams_of[3], (D, H * HD), D ** -0.5, 0.15625, ((0, 8),))
    w_key = centred(streams_of[4], (D, KV * HD), D ** -0.5, 0.15625, ((0, 8),))
    w_value = centred(streams_of[5], (D, KV * HD), D ** -0.5, 0.15625, ((0, 8),))
    w_output = centred(streams_of[6], (H * HD, D), (H * HD // 16) ** -0.5, 0.625, ((0, 8),))
    w_router = centred(streams_of[7], (D, EXPERTS), (4 * D) ** -0.5, 0.078125, ((0, 8),))
    gain_attn = jnp.clip(1.0 + 0.18 * jax.random.normal(streams_of[8], (D,), jnp.float32), 0.099609375, 1.8984375).astype(jnp.bfloat16)
    gain_moe = jnp.clip(1.0 + 0.18 * jax.random.normal(streams_of[9], (D,), jnp.float32), 0.099609375, 1.8984375).astype(jnp.bfloat16)
    w_gate_up = centred(streams_of[10], (EXPERTS, D, 2 * F), D ** -0.5, 0.15625, ((0, 4),))
    w_down = centred(streams_of[11], (EXPERTS, F, D), (F // 16) ** -0.5, 1.0, ((0, 4),))
    cotangent = centred(streams_of[12], (TOKENS, D), 1.0, 6.0, ((0, 32),))
    return {"tokens": tokens, "segments": segments, "routes": routes, "w_query": w_query, "w_key": w_key, "w_value": w_value, "w_output": w_output, "w_router": w_router, "gain_attn": gain_attn, "gain_moe": gain_moe, "w_gate_up": w_gate_up, "w_down": w_down, "cotangent": cotangent}


@jax.custom_vjp
def low(v):
    return lax.optimization_barrier(v.astype(jnp.bfloat16)).astype(jnp.float32)

@jax.custom_vjp
def low_back(v):
    return v

def low_keep(v):
    return (low(v), None)

def low_pass(kept, grad):
    return (grad,)

def back_keep(v):
    return (v, None)

def back_low(kept, grad):
    return (low(grad),)
low.defvjp(low_keep, low_pass)
low_back.defvjp(back_keep, back_low)
epsilon = 1e-05
highest = lax.Precision.HIGHEST

def product(left_side, right_side):
    return jnp.dot(left_side, right_side, precision=highest, preferred_element_type=jnp.float32)

def tables(length, size):
    half_size = size // 2
    frequency = jnp.power(10000.0, -2.0 * jnp.arange(half_size, dtype=jnp.float32) / size)
    angles = jnp.arange(length, dtype=jnp.float32)[:, None] * frequency[None, :]
    return (jnp.cos(angles)[:, None, :], jnp.sin(angles)[:, None, :])

def rotate(source, cosine_table, sine_table):
    half_size = source.shape[-1] // 2
    first_half = source[..., :half_size]
    second_half = source[..., half_size:]
    return jnp.concatenate([first_half * cosine_table - second_half * sine_table, second_half * cosine_table + first_half * sine_table], axis=-1)

def attend(queries, key_rows, values, segment):
    length = queries.shape[0]
    grouped = queries.reshape(length, KV, H // KV, HD)
    scores = low_back(jnp.einsum('qkgd,skd->kgqs', grouped, key_rows, precision=highest) * 0.125)
    position = jnp.arange(length, dtype=jnp.int32)
    allowed = (segment[:, None] == segment[None, :]) & (position[:, None] >= position[None, :])
    scores = jnp.where(allowed, scores, -1e+30)
    maximum = lax.optimization_barrier(jnp.max(scores, axis=-1, keepdims=True))
    lifted = jnp.exp(scores - maximum)
    attn_weights = low(lifted / lax.optimization_barrier(jnp.sum(lifted, axis=-1, keepdims=True)))
    mixed = jnp.einsum('kgqs,skd->qkgd', attn_weights, values, precision=highest)
    return mixed.reshape(length, H * HD)

def expert_apply(pieces):
    rows, gate_up_weight, down_weight = pieces
    gate_up = low_back(product(rows, gate_up_weight))
    gate_part = gate_up[:, :F]
    up_part = gate_up[:, F:]
    activation = low(gate_part * jax.nn.sigmoid(gate_part) * up_part)
    return low(low_back(product(activation, down_weight)))

def forward(tokens, w_query, w_key, w_value, w_output, w_router, gain_attn, gain_moe, w_gate_up, w_down, segments, routes):
    sequences = TOKENS // TOK_DEV
    inv_attn = lax.rsqrt(lax.optimization_barrier(jnp.mean(tokens * tokens, axis=-1, keepdims=True)) + epsilon)
    normed = low(tokens * inv_attn * gain_attn)
    cosine_table, sine_table = tables(TOK_DEV, HD)
    queries = low(rotate(low_back(product(normed, w_query)).reshape(sequences, TOK_DEV, H, HD), cosine_table, sine_table))
    key_rows = low(rotate(low_back(product(normed, w_key)).reshape(sequences, TOK_DEV, KV, HD), cosine_table, sine_table))
    values = low(low_back(product(normed, w_value))).reshape(sequences, TOK_DEV, KV, HD)
    per_step = min(max(1, 4096 // TOK_DEV), sequences)
    step_count = sequences // per_step

    def attend_group(pieces):
        return jax.vmap(attend)(*pieces)
    mixed = lax.map(jax.checkpoint(attend_group), (queries.reshape(step_count, per_step, TOK_DEV, H, HD), key_rows.reshape(step_count, per_step, TOK_DEV, KV, HD), values.reshape(step_count, per_step, TOK_DEV, KV, HD), segments.reshape(step_count, per_step, TOK_DEV)))
    mixed = low(low_back(mixed.reshape(TOKENS, H * HD)))
    residual = tokens + low_back(product(mixed, w_output))
    inv_moe = lax.rsqrt(lax.optimization_barrier(jnp.mean(residual * residual, axis=-1, keepdims=True)) + epsilon)
    normed_moe = low(residual * inv_moe * gain_moe)
    logits = low_back(product(normed_moe, w_router))
    chosen_mask = routes[:, :, None] == jnp.arange(EXPERTS, dtype=jnp.int32)
    chosen = lax.optimization_barrier(jnp.sum(jnp.where(chosen_mask, logits[:, None, :], 0.0), axis=-1))
    largest = lax.optimization_barrier(jnp.max(chosen, axis=-1, keepdims=True))
    lifted = jnp.exp(chosen - largest)
    gate_weights = lifted / lax.optimization_barrier(jnp.sum(lifted, axis=-1, keepdims=True))
    blocks = TOKENS // TOK_DEV
    one_hot = chosen_mask.reshape(blocks, TOK_DEV * TOPK, EXPERTS).astype(jnp.int32)
    slot_index = lax.optimization_barrier(jnp.sum((jnp.cumsum(one_hot, axis=1) - one_hot) * one_hot, axis=-1))
    destination = routes.reshape(blocks, TOK_DEV * TOPK) * (blocks * CAP) + jnp.arange(blocks, dtype=jnp.int32)[:, None] * CAP + slot_index
    destination = destination.reshape(-1).astype(jnp.int32)
    rows = low_back(jnp.repeat(normed_moe, TOPK, axis=0))
    buffer = jnp.zeros((EXPERTS * blocks * CAP, D), jnp.float32).at[destination].set(rows)
    returned = lax.map(jax.checkpoint(expert_apply), (buffer.reshape(EXPERTS, blocks * CAP, D), w_gate_up, w_down))
    picked = returned.reshape(EXPERTS * blocks * CAP, D)[destination].reshape(TOKENS, TOPK, D)
    return residual + lax.optimization_barrier(jnp.sum(gate_weights[:, :, None] * picked, axis=1))

def reference(tokens, segments, routes, w_query, w_key, w_value, w_output, w_router, gain_attn, gain_moe, w_gate_up, w_down, cotangent):
    floats = tuple((item.astype(jnp.float32) for item in (tokens, w_query, w_key, w_value, w_output, w_router, gain_attn, gain_moe, w_gate_up, w_down)))

    def layer(*items):
        return forward(*items, segments, routes)
    result, pullback = jax.vjp(layer, *floats)
    grads = pullback(cotangent.astype(jnp.float32))
    return (result.astype(jnp.bfloat16), grads[0].astype(jnp.bfloat16), grads[1], grads[2], grads[3], grads[4], grads[5], grads[6], grads[7], grads[8], grads[9])
```

```python
import functools

import jax
import jax.numpy as jnp
from jax import lax
from jax.experimental import pallas as pl
from jax.experimental.pallas import tpu as pltpu
from jax.sharding import PartitionSpec as P

H = 24
KV = 8
HD = 64
F = 512
EXPERTS = 40
ZLINE = 4


epsilon = 1e-05
f32 = jnp.float32
bf16 = jnp.bfloat16


def tables(length, size):
    half_size = size // 2
    frequency = jnp.power(10000.0, -2.0 * jnp.arange(half_size, dtype=f32) / size)
    angles = jnp.arange(length, dtype=f32)[:, None] * frequency[None, :]
    return (jnp.cos(angles)[:, None, :], jnp.sin(angles)[:, None, :])


def rotate(source, cosine_table, sine_table):
    half_size = source.shape[-1] // 2
    first_half = source[..., :half_size]
    second_half = source[..., half_size:]
    return jnp.concatenate(
        [
            first_half * cosine_table - second_half * sine_table,
            second_half * cosine_table + first_half * sine_table,
        ],
        axis=-1,
    )


def dot(left_side, right_side):
    return jnp.dot(left_side, right_side, preferred_element_type=f32)


def transposed(left_side, right_side):
    return lax.dot_general(
        left_side, right_side, (((0,), (0,)), ((), ())), preferred_element_type=f32
    )


def against(left_side, right_side):
    return lax.dot_general(
        left_side, right_side, (((1,), (1,)), ((), ())), preferred_element_type=f32
    )


def swap(value, axis, mask):
    size = lax.axis_size(axis)
    return lax.ppermute(value, axis, [(i, i ^ mask) for i in range(size)])


def pick(value, at):
    return lax.dynamic_index_in_dim(value, at, 0, keepdims=False)


def bits(first, size):
    masks, step = [], 1
    while step < size:
        masks.append(first * step)
        step *= 2
    return masks


class Place:
    def __init__(self):
        self.dp_size = lax.axis_size("dp")
        self.ex_size = lax.axis_size("expert")
        self.dp = lax.axis_index("dp")
        self.ex = lax.axis_index("expert")
        self.rows_y = self.dp_size // ZLINE
        self.z = self.dp // self.rows_y
        self.y = self.dp % self.rows_y
        self.z_bits = bits(self.rows_y, ZLINE)
        self.y_bits = bits(1, self.rows_y)
        self.x_bits = bits(2, self.ex_size // 2)


def gather_weights(place, shard):
    n, columns = shard.shape
    piece = n // 6
    cut = shard.reshape(3, 2, piece, columns)
    core = place.ex % 2
    side = (place.ex // 2) % 2
    own = pick(cut.swapaxes(0, 1), core)
    sibling = pick(cut.swapaxes(0, 1), 1 - core)

    def ordered(parts):
        return jnp.stack([pick(parts, 2 * side), parts[1], pick(parts, 2 - 2 * side)])

    own, sibling = ordered(own), ordered(sibling)
    blocks = {0: own[:2]}
    for mask in place.z_bits + place.y_bits:
        blocks.update({m ^ mask: swap(v, "dp", mask) for m, v in list(blocks.items())})
    rows = []
    for m in range(place.dp_size):
        if m == 0:
            rows.append(jnp.stack([own, sibling], axis=1))
            continue
        other = swap(blocks[m][0], "expert", 2)
        trio = jnp.concatenate([blocks[m], other[None]], axis=0)
        rows.append(jnp.stack([trio, swap(trio, "expert", 1)], axis=1))
    full = jnp.stack(rows)
    total = place.dp_size * n
    k = jnp.arange(total, dtype=jnp.int32)
    block, part = k // n, (k % n) // (2 * piece)
    half, line = (k % (2 * piece)) // piece, k % piece
    part = jnp.where(part == 1, 1, jnp.where(part == 0, 2 * side, 2 - 2 * side))
    at = (block ^ place.dp) * n + part * 2 * piece + (half ^ core) * piece + line
    order = (at[:, None] == jnp.arange(total, dtype=jnp.int32)[None, :]).astype(bf16)
    return full.reshape(total, columns), order


def scatter_weights(place, part):
    total, columns = part.shape
    n = total // place.dp_size
    piece = n // 6
    core = place.ex % 2
    side = (place.ex // 2) % 2

    def add(left, right):
        return (left.astype(f32) + right.astype(f32)).astype(bf16)

    part = part.reshape(place.dp_size, 3, 2, piece, columns)
    kept = add(part[:, :, 0], swap(part[:, :, 1], "expert", 1))
    first = add(kept[:, 0], swap(kept[:, 2], "expert", 2))
    blocks = {m: jnp.stack([first[m], kept[m, 1]]) for m in range(place.dp_size)}
    for mask in (place.z_bits + place.y_bits)[::-1]:
        blocks = {
            m: add(v, swap(blocks[m ^ mask], "dp", mask))
            for m, v in blocks.items()
            if m & mask == 0
        }
    mine = blocks[0]
    middle = add(mine[1], swap(mine[1], "expert", 2))
    trio = jnp.stack([mine[0], middle, swap(mine[0], "expert", 2)])
    for mask in place.x_bits[1:]:
        trio = add(trio, swap(trio, "expert", mask))
    both = jnp.stack([trio, swap(trio, "expert", 1)], axis=1)
    both = jnp.where(side == 0, both, both[::-1])
    both = jnp.where(core == 0, both, both[:, ::-1])
    return both.reshape(n, columns).astype(f32)


def gather_tokens(place, block):
    blocks = {0: block}
    for mask in place.z_bits:
        blocks.update({m ^ mask: swap(v, "dp", mask) for m, v in list(blocks.items())})
    groups = []
    for r in range(ZLINE):
        row = [blocks[r * place.rows_y]]
        for mask in place.x_bits:
            row = row + [swap(v, "expert", mask) for v in row]
        row = jnp.concatenate(row, axis=0)
        groups.append(jnp.concatenate([row, swap(row, "expert", 1)], axis=0))
    return groups


def scatter_tokens(place, groups, length):
    def add(left, right):
        return left.astype(f32) + right.astype(f32)

    reduced = []
    for part in groups:
        half = part.shape[0] // 2
        kept = add(part[:half], swap(part[half:], "expert", 1)).astype(bf16)
        for mask in place.x_bits[::-1]:
            half = kept.shape[0] // 2
            kept = add(kept[:half], swap(kept[half:], "expert", mask)).astype(bf16)
        reduced.append(kept)
    two = [add(reduced[i], swap(reduced[i + 2], "dp", place.z_bits[1])) for i in range(2)]
    return add(two[0], swap(two[1].astype(bf16), "dp", place.z_bits[0]))


def other(index, mask):
    return index + mask - 2 * mask * ((index // mask) % 2)


class Links:
    def __init__(self, sends, recvs):
        self.sends, self.recvs, self.used, self.open = sends, recvs, 0, []

    def copy(self, source, target, partner):
        at = self.used
        self.used += 1
        made = pltpu.make_async_remote_copy(
            src_ref=source,
            dst_ref=target,
            send_sem=self.sends.at[at],
            recv_sem=self.recvs.at[at],
            device_id=partner,
            device_id_type=pl.DeviceIdType.MESH,
        )
        made.start()
        self.open.append(made)
        return made

    def close(self):
        for made in self.open:
            made.wait_send()


def partners(rows_y):
    dp, ex = lax.axis_index("dp"), lax.axis_index("expert")
    return {
        "z1": (other(dp, rows_y), ex),
        "z2": (other(dp, 2 * rows_y), ex),
        "y": (other(dp, 1), ex),
        "x": (dp, other(ex, 2)),
        "c": (dp, other(ex, 1)),
    }


def greet(devices):
    barrier = pltpu.get_barrier_semaphore()
    for device in devices:
        pl.semaphore_signal(
            barrier, inc=1, device_id=device, device_id_type=pl.DeviceIdType.MESH
        )
    pl.semaphore_wait(barrier, len(devices))


MOE_COPIES = 22


def moe_kernel(
    rows_y,
    normed_ref,
    dy_hbm,
    gate_up_hbm,
    down_hbm,
    router_ref,
    spread_ref,
    rows_out,
    grads_out,
    acts_out,
    total_ref,
    w_gate,
    w_up,
    w_down,
    rows,
    dy,
    grads,
    acts,
    gate_grads,
    parts,
    heard_c,
    heard_x,
    heard_z2,
    heard_z1,
    sends,
    recvs,
    load_sems,
    dy_sems,
    out_sems,
):
    owned, hidden = w_down.shape[:2]
    length, width = normed_ref.shape
    count = rows.shape[1]
    half = count // 2
    span = owned * hidden
    z = lax.axis_index("dp") // rows_y
    to = partners(rows_y)
    links = Links(sends, recvs)

    loads = []
    mine = pl.ds(pl.multiple_of(z * hidden, hidden), hidden)
    theirs = pl.ds(pl.multiple_of(F + z * hidden, hidden), hidden)
    for e in range(owned):
        at = pl.ds(e * hidden, hidden)
        for k, (cut, kept) in enumerate(((mine, w_gate), (theirs, w_up))):
            loads.append(
                pltpu.make_async_copy(
                    gate_up_hbm.at[e, :, cut], kept.at[:, at], load_sems.at[2 * e + k]
                )
            )
    loads.append(pltpu.make_async_copy(down_hbm.at[:, mine, :], w_down, load_sems.at[2 * owned]))
    for load in loads:
        load.start()

    def fetch(r):
        return pltpu.make_async_copy(dy_hbm.at[r], dy.at[r % 2], dy_sems.at[r % 2])

    fetch(0).start()
    fetch(1).start()
    rows[0, :length] = normed_ref[...]
    greet([to["z1"], to["z2"], to["x"], to["c"]])

    own = pl.ds(0, length)
    pair = pl.ds(length, length)
    near, far = pl.ds(0, half), pl.ds(half, half)

    def row_x(r):
        return links.copy(rows.at[r, own], rows.at[r, pair], to["x"])

    def row_c(r):
        return links.copy(rows.at[r, near], rows.at[r, far], to["c"])

    z1 = links.copy(rows.at[0, own], rows.at[1, own], to["z1"])
    x0 = row_x(0)
    z2 = links.copy(rows.at[0, own], rows.at[2, own], to["z2"])
    x0.wait_recv()
    c0 = row_c(0)
    z1.wait_recv()
    x1 = row_x(1)
    z3 = links.copy(rows.at[1, own], rows.at[3, own], to["z2"])
    c0.wait_recv()
    for load in loads:
        load.wait()

    stores = []

    def store(source, target):
        made = pltpu.make_async_copy(source, target, out_sems.at[len(stores)])
        made.start()
        stores.append(made)
        return made

    def forward(r):
        slot = r % 2
        fetch(r).wait()
        logits = jnp.dot(rows[r], router_ref[...], preferred_element_type=f32)
        mask = dy[slot, :, width:].astype(f32) > 0.5
        logits = jnp.where(mask, logits, -1e30)
        lifted = jnp.where(
            mask, jnp.exp(logits - jnp.max(logits, axis=-1, keepdims=True)), 0.0
        )
        gates = lifted / jnp.sum(lifted, axis=-1, keepdims=True)
        gates_high = gates.astype(bf16)
        gates_low = (gates - gates_high.astype(f32)).astype(bf16)
        gate_grads[...] = jnp.zeros_like(gate_grads)

        def step(p, _):
            at = pl.ds(pl.multiple_of(p * 2 * hidden, 2 * hidden), 2 * hidden)
            up_at = pl.ds(pl.multiple_of(span + p * 2 * hidden, 2 * hidden), 2 * hidden)
            spread = spread_ref[:, at]
            down = w_down[pl.ds(2 * p, 2)].reshape(2 * hidden, width)
            gate_part = jnp.dot(rows[r], w_gate[:, at], preferred_element_type=f32)
            up_part = jnp.dot(rows[r], w_up[:, at], preferred_element_type=f32)
            plain_grad = against(dy[slot, :, :width], down)
            spread_gates = jnp.dot(gates_high, spread, preferred_element_type=f32) + jnp.dot(
                gates_low, spread, preferred_element_type=f32
            )
            sigmoid_gate = 1.0 / (1.0 + jnp.exp(-gate_part))
            swished = gate_part * sigmoid_gate
            activation = swished * up_part
            gate_grads[...] += against((plain_grad * activation).astype(bf16), spread)
            acts[slot, :, at] = (spread_gates * activation).astype(bf16)
            grad_act = plain_grad * spread_gates
            grads[r, :, at] = (
                grad_act * up_part * (sigmoid_gate + swished * (1.0 - sigmoid_gate))
            ).astype(bf16)
            grads[r, :, up_at] = (grad_act * swished).astype(bf16)
            return 0

        lax.fori_loop(0, owned // 2, step, 0)
        parts[r, :, width:] = gate_grads[...].astype(bf16)
        if r + 2 < ZLINE:
            fetch(r + 2).start()
        store(rows.at[r], rows_out.at[r])
        store(grads.at[r], grads_out.at[r])
        return store(acts.at[slot], acts_out.at[r])

    def backward(r):
        def step(j, _):
            at = pl.ds(pl.multiple_of(j * 512, 512), 512)
            part = against(grads[r, :, :span], w_gate[at, :]) + against(
                grads[r, :, span:], w_up[at, :]
            )
            parts[r, :, at] = part.astype(bf16)
            return 0

        lax.fori_loop(0, width // 512, step, 0)

    kept = [forward(0)]
    x1.wait_recv()
    c1 = row_c(1)
    z2.wait_recv()
    x2 = row_x(2)
    c1.wait_recv()
    kept.append(forward(1))
    x2.wait_recv()
    c2 = row_c(2)
    z3.wait_recv()
    x3 = row_x(3)
    c2.wait_recv()
    kept[0].wait()
    kept.append(forward(2))
    x3.wait_recv()
    c3 = row_c(3)
    c3.wait_recv()
    kept[1].wait()
    kept.append(forward(3))

    def add(left, right):
        return (left[...].astype(f32) + right[...].astype(f32)).astype(bf16)

    def part_c(r):
        return links.copy(parts.at[r, far], heard_c.at[r], to["c"])

    def part_x(r, copy):
        copy.wait_recv()
        parts[r, near] = add(parts.at[r, near], heard_c.at[r])
        return links.copy(parts.at[r, pair], heard_x.at[r], to["x"])

    def part_z(r, copy):
        copy.wait_recv()
        parts[r, own] = add(parts.at[r, own], heard_x.at[r])

    backward(3)
    c3 = part_c(3)
    backward(2)
    c2 = part_c(2)
    x3 = part_x(3, c3)
    backward(1)
    c1 = part_c(1)
    x2 = part_x(2, c2)
    part_z(3, x3)
    z3 = links.copy(parts.at[3, own], heard_z2.at[1], to["z2"])
    backward(0)
    c0 = part_c(0)
    x1 = part_x(1, c1)
    part_z(2, x2)
    z2 = links.copy(parts.at[2, own], heard_z2.at[0], to["z2"])
    x0 = part_x(0, c0)
    part_z(1, x1)
    z3.wait_recv()
    parts[1, own] = add(parts.at[1, own], heard_z2.at[1])
    z1 = links.copy(parts.at[1, own], heard_z1, to["z1"])
    part_z(0, x0)
    z2.wait_recv()
    total = parts[0, own].astype(f32) + heard_z2[0].astype(f32)
    z1.wait_recv()
    total_ref[...] = total + heard_z1[...].astype(f32)
    links.close()
    for k, made in enumerate(stores):
        if k not in (2, 5):
            made.wait()


def moe(rows_y, normed, dy, w_gate_up, w_down, router, spread):
    owned, width, _ = w_gate_up.shape
    hidden = F // ZLINE
    length = normed.shape[0]
    count = dy.shape[1]
    wide = width + 128
    any_space = pl.BlockSpec(memory_space=pl.ANY)
    vmem = pl.BlockSpec(memory_space=pltpu.VMEM)
    span = owned * hidden
    return pl.pallas_call(
        functools.partial(moe_kernel, rows_y),
        name="moe",
        out_shape=(
            jax.ShapeDtypeStruct((ZLINE, count, width), bf16),
            jax.ShapeDtypeStruct((ZLINE, count, 2 * span), bf16),
            jax.ShapeDtypeStruct((ZLINE, count, span), bf16),
            jax.ShapeDtypeStruct((length, wide), f32),
        ),
        in_specs=[vmem, any_space, any_space, any_space, vmem, vmem],
        out_specs=(any_space, any_space, any_space, vmem),
        scratch_shapes=[
            pltpu.VMEM((width, span), bf16),
            pltpu.VMEM((width, span), bf16),
            pltpu.VMEM((owned, hidden, width), bf16),
            pltpu.VMEM((ZLINE, count, width), bf16),
            pltpu.VMEM((2, count, wide), bf16),
            pltpu.VMEM((ZLINE, count, 2 * span), bf16),
            pltpu.VMEM((2, count, span), bf16),
            pltpu.VMEM((count, 128), f32),
            pltpu.VMEM((ZLINE, count, wide), bf16),
            pltpu.VMEM((ZLINE, count // 2, wide), bf16),
            pltpu.VMEM((ZLINE, length, wide), bf16),
            pltpu.VMEM((2, length, wide), bf16),
            pltpu.VMEM((length, wide), bf16),
            pltpu.SemaphoreType.DMA((MOE_COPIES,)),
            pltpu.SemaphoreType.DMA((MOE_COPIES,)),
            pltpu.SemaphoreType.DMA((2 * owned + 1,)),
            pltpu.SemaphoreType.DMA((2,)),
            pltpu.SemaphoreType.DMA((12,)),
        ],
        compiler_params=pltpu.CompilerParams(
            collective_id=1, has_side_effects=True, vmem_limit_bytes=60 * 2**20
        ),
    )(normed, dy, w_gate_up, w_down, router, spread)


def local(
    tokens,
    segments,
    routes,
    w_query,
    w_key,
    w_value,
    w_output,
    w_router,
    gain_attn,
    gain_moe,
    w_gate_up,
    w_down,
    cotangent,
):
    place = Place()
    length, width = tokens.shape
    owned = w_gate_up.shape[0]
    rows = w_query.shape[0]
    hidden = F // ZLINE
    per_group = H // KV
    q_end, k_end, v_end = H * HD, (H + KV) * HD, (H + 2 * KV) * HD
    o_end = v_end + width

    small = jnp.concatenate(
        [w_router, gain_attn[:, None], gain_moe[:, None], jnp.zeros((rows, 128 - EXPERTS - 2), bf16)],
        axis=1,
    )
    shard = jnp.concatenate([w_query, w_key, w_value, w_output, small], axis=1)
    full, order = gather_weights(place, shard)
    full_qkv, full_output = full[:, :v_end], full[:, v_end:o_end]
    full_small = transposed(order, full[:, o_end:]).astype(bf16)
    full_router = full_small[:, :EXPERTS]
    attn_gain = full_small[:, EXPERTS].astype(f32)
    moe_gain = full_small[:, EXPERTS + 1].astype(f32)

    chosen_mask = jnp.any(
        routes[:, :, None] == jnp.arange(EXPERTS, dtype=jnp.int32), axis=1
    )
    dy_block = jnp.concatenate(
        [cotangent, chosen_mask.astype(bf16), jnp.zeros((length, 128 - EXPERTS), bf16)], axis=1
    )
    dy_groups = gather_tokens(place, dy_block)

    cosine_table, sine_table = tables(length, HD)
    inputs = tokens.astype(f32)
    inv_attn = lax.rsqrt(jnp.mean(inputs * inputs, axis=-1, keepdims=True) + epsilon)
    unit_attn = inputs * inv_attn
    normed = (unit_attn * attn_gain).astype(bf16)
    normed = against(normed, order).astype(bf16)
    qkv = dot(normed, full_qkv)
    queries = rotate(qkv[:, :q_end].reshape(length, H, HD), cosine_table, sine_table)
    queries = queries.astype(bf16).reshape(length, KV, per_group, HD)
    key_rows = rotate(
        qkv[:, q_end:k_end].reshape(length, KV, HD), cosine_table, sine_table
    ).astype(bf16)
    values = qkv[:, k_end:].astype(bf16).reshape(length, KV, HD)
    segment = segments[0]
    position = jnp.arange(length, dtype=jnp.int32)
    allowed = (segment[:, None] == segment[None, :]) & (position[:, None] >= position[None, :])
    scores = (
        jnp.einsum("qkgd,skd->kgqs", queries, key_rows, preferred_element_type=f32) * 0.125
    )
    scores = jnp.where(allowed, scores, -1e30)
    maximum = jnp.max(scores, axis=-1, keepdims=True)
    lifted_scores = jnp.exp(scores - maximum)
    full_weights = lifted_scores / jnp.sum(lifted_scores, axis=-1, keepdims=True)
    attn_weights = full_weights.astype(bf16)
    mixed = jnp.einsum("kgqs,skd->qkgd", attn_weights, values, preferred_element_type=f32)
    mixed = mixed.reshape(length, H * HD).astype(bf16)
    mixed = against(mixed, order).astype(bf16)
    residual = inputs + dot(mixed, full_output)
    inv_moe = lax.rsqrt(jnp.mean(residual * residual, axis=-1, keepdims=True) + epsilon)
    unit_moe = residual * inv_moe
    normed_moe = (unit_moe * moe_gain).astype(bf16)

    def gates_of(rows_in, mask):
        logits = jnp.where(mask, dot(rows_in, full_router), -1e30)
        lifted = jnp.where(mask, jnp.exp(logits - jnp.max(logits, axis=-1, keepdims=True)), 0.0)
        return lifted / jnp.sum(lifted, axis=-1, keepdims=True)

    gates = gates_of(normed_moe, chosen_mask)

    def columns(start):
        cut = lax.dynamic_slice_in_dim(w_gate_up, start + place.z * hidden, hidden, 2)
        return cut.swapaxes(0, 1).reshape(width, owned * hidden)

    span = owned * hidden
    slice_down = lax.dynamic_slice_in_dim(w_down, place.z * hidden, hidden, 1)
    slice_down = slice_down.reshape(span, width)
    if place.ex_size == 4 and place.rows_y == 2:
        wide_router = jnp.pad(full_router, ((0, 0), (0, 128 - EXPERTS)))
        lane = jnp.arange(128, dtype=jnp.int32)[:, None]
        column = jnp.arange(span, dtype=jnp.int32)[None, :]
        spread = (lane == place.ex * owned + column // hidden).astype(bf16)
        all_dy = jnp.stack(dy_groups)
        all_rows, all_grads, all_acts, total = moe(
            place.rows_y, normed_moe, all_dy, w_gate_up, w_down, wide_router, spread
        )
        all_dy = all_dy[:, :, :width].reshape(-1, width)
        all_rows = all_rows.reshape(-1, width)
        all_grads = all_grads.reshape(-1, 2 * span)
        row_grads, grad_gates = total[:, :width], total[:, width : width + EXPERTS]
        out_parts = [dot(all_acts[r], slice_down).astype(bf16) for r in range(ZLINE)]
        all_acts = all_acts.reshape(-1, span)
    else:
        slice_gate_up = jnp.concatenate([columns(0), columns(F)], axis=1)
        moe_groups = gather_tokens(place, normed_moe)
        acts, grads_gate_up, gate_parts = [], [], []
        for normed_rows, dy_rows in zip(moe_groups, dy_groups):
            count = normed_rows.shape[0]
            group_gates = gates_of(normed_rows, dy_rows[:, width : width + EXPERTS] > 0.5)
            group_gates = lax.dynamic_slice_in_dim(group_gates, place.ex * owned, owned, 1)
            spread_gates = jnp.broadcast_to(group_gates[:, :, None], (count, owned, hidden))
            spread_gates = spread_gates.reshape(count, span)
            gate_up = dot(normed_rows, slice_gate_up)
            gate_part, up_part = gate_up[:, :span], gate_up[:, span:]
            plain_grad = against(dy_rows[:, :width], slice_down)
            sigmoid_gate = jax.nn.sigmoid(gate_part)
            swished = gate_part * sigmoid_gate
            activation = swished * up_part
            grad_act = plain_grad * spread_gates
            gate_parts.append(jnp.sum((plain_grad * activation).reshape(count, owned, hidden), axis=-1))
            acts.append((spread_gates * activation).astype(bf16))
            grads_gate_up.append(
                jnp.concatenate(
                    [
                        grad_act * up_part * sigmoid_gate * (1.0 + gate_part * (1.0 - sigmoid_gate)),
                        grad_act * swished,
                    ],
                    axis=-1,
                ).astype(bf16)
            )
        row_parts = [against(g, slice_gate_up).astype(bf16) for g in grads_gate_up]
        row_grads = scatter_tokens(place, row_parts, length)
        out_parts = [dot(a, slice_down).astype(bf16) for a in acts]
        gate_parts = [g.T for g in gate_parts]
        two = [gate_parts[i] + swap(gate_parts[i + 2], "dp", place.z_bits[1]) for i in range(2)]
        mine = two[0] + swap(two[1], "dp", place.z_bits[0])
        mine = mine.reshape(owned, 2, place.ex_size // 2, length)
        heard = [
            swap(mine[:, m % 2, m // 2], "expert", m) if m else mine[:, 0, 0]
            for m in range(place.ex_size)
        ]
        heard = jnp.stack(heard)
        grad_gates = jnp.concatenate(
            [pick(heard, place.ex ^ j) for j in range(place.ex_size)], axis=0
        ).T
        all_rows = jnp.concatenate([v for v in moe_groups], axis=0)
        all_dy = jnp.concatenate([v[:, :width] for v in dy_groups], axis=0)
        all_grads = jnp.concatenate(grads_gate_up, axis=0)
        all_acts = jnp.concatenate(acts, axis=0)
    output = (residual + scatter_tokens(place, out_parts, length)).astype(bf16)
    grad_logits = (
        gates * (grad_gates - jnp.sum(gates * grad_gates, axis=-1, keepdims=True))
    ).astype(bf16)

    def reduce_y(part, axis):
        part = jnp.moveaxis(part, axis, 0)
        for mask in place.y_bits[::-1]:
            at = (place.y // mask) % 2
            half = part.reshape((2, part.shape[0] // 2) + part.shape[1:])
            away = swap(pick(half, 1 - at), "dp", mask)
            part = (pick(half, at).astype(f32) + away.astype(f32)).astype(bf16)
        return part[0]

    shard_down = transposed(all_acts, all_dy).astype(bf16)
    shard_down = shard_down.reshape(owned, place.rows_y, hidden // place.rows_y, width)
    shard_down = reduce_y(shard_down, 1).astype(f32)
    part_gate_up = transposed(all_rows, all_grads).astype(bf16)
    part_gate_up = part_gate_up.reshape(ZLINE, place.rows_y, rows, 2 * span)
    part_gate_up = reduce_y(part_gate_up, 1)
    heard = [pick(part_gate_up, place.z)] + [
        swap(pick(part_gate_up, place.z ^ m), "dp", m * place.rows_y) for m in range(1, ZLINE)
    ]
    heard = jnp.stack(heard)
    shard_gate_up = jnp.stack([pick(heard, place.z ^ j) for j in range(ZLINE)], axis=0)
    shard_gate_up = shard_gate_up.reshape(ZLINE, rows, 2, owned, hidden)
    shard_gate_up = shard_gate_up.transpose(3, 1, 2, 0, 4).reshape(owned, rows, 2 * F).astype(f32)

    grad_out = cotangent.astype(f32)
    part_router = transposed(normed_moe, grad_logits)
    grad_normed_moe = row_grads + against(grad_logits, full_router)
    part_gain_moe = jnp.sum(grad_normed_moe * unit_moe, axis=0)
    scaled_moe = grad_normed_moe * moe_gain
    grad_residual = grad_out + inv_moe * (
        scaled_moe - unit_moe * jnp.mean(scaled_moe * unit_moe, axis=-1, keepdims=True)
    )
    grad_branch = grad_residual.astype(bf16)
    part_output = transposed(mixed, grad_branch)
    grad_mixed = dot(against(grad_branch, full_output).astype(bf16), order).astype(bf16)
    grad_mixed = grad_mixed.reshape(length, KV, per_group, HD)
    grad_weights = jnp.einsum(
        "qkgd,skd->kgqs", grad_mixed, values, preferred_element_type=f32
    )
    grad_values = jnp.einsum(
        "kgqs,qkgd->skd", attn_weights, grad_mixed, preferred_element_type=f32
    )
    grad_values = grad_values.astype(bf16).reshape(length, KV * HD)
    grad_scores = (
        full_weights * (grad_weights - jnp.sum(full_weights * grad_weights, axis=-1, keepdims=True))
    ).astype(bf16)
    grad_queries = (
        jnp.einsum("kgqs,skd->qkgd", grad_scores, key_rows, preferred_element_type=f32) * 0.125
    )
    grad_queries = rotate(grad_queries.reshape(length, H, HD), cosine_table, -sine_table)
    grad_queries = grad_queries.astype(bf16).reshape(length, H * HD)
    grad_keys = (
        jnp.einsum("kgqs,qkgd->skd", grad_scores, queries, preferred_element_type=f32) * 0.125
    )
    grad_keys = rotate(grad_keys, cosine_table, -sine_table)
    grad_keys = grad_keys.astype(bf16).reshape(length, KV * HD)
    grad_qkv = jnp.concatenate([grad_queries, grad_keys, grad_values], axis=1)
    part_qkv = transposed(normed, grad_qkv)
    grad_normed = against(grad_qkv, full_qkv)
    grad_normed = lax.dot_general(
        grad_normed,
        order.astype(f32),
        (((1,), (0,)), ((), ())),
        precision=lax.Precision.HIGHEST,
        preferred_element_type=f32,
    )
    part_gain_attn = jnp.sum(grad_normed * unit_attn, axis=0)
    scaled_attn = grad_normed * attn_gain
    grad_tokens = (
        grad_residual
        + inv_attn
        * (scaled_attn - unit_attn * jnp.mean(scaled_attn * unit_attn, axis=-1, keepdims=True))
    ).astype(bf16)
    part_small = jnp.concatenate(
        [
            part_router.astype(bf16),
            part_gain_attn[:, None].astype(bf16),
            part_gain_moe[:, None].astype(bf16),
            jnp.zeros((width, 128 - EXPERTS - 2), bf16),
        ],
        axis=1,
    )
    part_small = dot(order, part_small).astype(bf16)
    summed = scatter_weights(
        place,
        jnp.concatenate([part_qkv.astype(bf16), part_output.astype(bf16), part_small], axis=1),
    )
    return (
        output,
        grad_tokens,
        summed[:, :q_end],
        summed[:, q_end:k_end],
        summed[:, k_end:v_end],
        summed[:, v_end:o_end],
        summed[:, o_end : o_end + EXPERTS],
        summed[:, o_end + EXPERTS],
        summed[:, o_end + EXPERTS + 1],
        shard_gate_up,
        shard_down,
    )


def solution(mesh):
    return jax.shard_map(
        local,
        mesh=mesh,
        in_specs=(
            P(("dp", "expert"), None),
            P(("dp", "expert"), None),
            P(("dp", "expert"), None),
            P("dp", None),
            P("dp", None),
            P("dp", None),
            P("dp", None),
            P("dp", None),
            P("dp"),
            P("dp"),
            P("expert", None, None),
            P("expert", None, None),
            P(("dp", "expert"), None),
        ),
        out_specs=(
            P(("dp", "expert"), None),
            P(("dp", "expert"), None),
            P("dp", None),
            P("dp", None),
            P("dp", None),
            P("dp", None),
            P("dp", None),
            P("dp"),
            P("dp"),
            P("expert", "dp", None),
            P("expert", "dp", None),
        ),
        check_vma=False,
    )
```

```python
import functools

import jax
import jax.numpy as jnp
from jax import lax
from jax.experimental import pallas as pl
from jax.experimental.pallas import tpu as pltpu
from jax.sharding import PartitionSpec as P

H = 24
KV = 8
HD = 64
F = 512
EXPERTS = 40
ZLINE = 4


epsilon = 1e-05
f32 = jnp.float32
bf16 = jnp.bfloat16


def tables(length, size):
    half_size = size // 2
    frequency = jnp.power(10000.0, -2.0 * jnp.arange(half_size, dtype=f32) / size)
    angles = jnp.arange(length, dtype=f32)[:, None] * frequency[None, :]
    return (jnp.cos(angles)[:, None, :], jnp.sin(angles)[:, None, :])


def rotate(source, cosine_table, sine_table):
    half_size = source.shape[-1] // 2
    first_half = source[..., :half_size]
    second_half = source[..., half_size:]
    return jnp.concatenate(
        [
            first_half * cosine_table - second_half * sine_table,
            second_half * cosine_table + first_half * sine_table,
        ],
        axis=-1,
    )


def dot(left_side, right_side):
    return jnp.dot(left_side, right_side, preferred_element_type=f32)


def transposed(left_side, right_side):
    return lax.dot_general(
        left_side, right_side, (((0,), (0,)), ((), ())), preferred_element_type=f32
    )


def against(left_side, right_side):
    return lax.dot_general(
        left_side, right_side, (((1,), (1,)), ((), ())), preferred_element_type=f32
    )


def swap(value, axis, mask):
    size = lax.axis_size(axis)
    return lax.ppermute(value, axis, [(i, i ^ mask) for i in range(size)])


def pick(value, at):
    return lax.dynamic_index_in_dim(value, at, 0, keepdims=False)


def bits(first, size):
    masks, step = [], 1
    while step < size:
        masks.append(first * step)
        step *= 2
    return masks


class Place:
    def __init__(self):
        self.dp_size = lax.axis_size("dp")
        self.ex_size = lax.axis_size("expert")
        self.dp = lax.axis_index("dp")
        self.ex = lax.axis_index("expert")
        self.rows_y = self.dp_size // ZLINE
        self.z = self.dp // self.rows_y
        self.y = self.dp % self.rows_y
        self.z_bits = bits(self.rows_y, ZLINE)
        self.y_bits = bits(1, self.rows_y)
        self.x_bits = bits(2, self.ex_size // 2)


def gather_weights(place, shard):
    n, columns = shard.shape
    piece = n // 6
    cut = shard.reshape(3, 2, piece, columns)
    core = place.ex % 2
    side = (place.ex // 2) % 2
    own = pick(cut.swapaxes(0, 1), core)
    sibling = pick(cut.swapaxes(0, 1), 1 - core)

    def ordered(parts):
        return jnp.stack([pick(parts, 2 * side), parts[1], pick(parts, 2 - 2 * side)])

    own, sibling = ordered(own), ordered(sibling)
    blocks = {0: own[:2]}
    for mask in place.z_bits + place.y_bits:
        blocks.update({m ^ mask: swap(v, "dp", mask) for m, v in list(blocks.items())})
    rows = []
    for m in range(place.dp_size):
        if m == 0:
            rows.append(jnp.stack([own, sibling], axis=1))
            continue
        other = swap(blocks[m][0], "expert", 2)
        trio = jnp.concatenate([blocks[m], other[None]], axis=0)
        rows.append(jnp.stack([trio, swap(trio, "expert", 1)], axis=1))
    full = jnp.stack(rows)
    total = place.dp_size * n
    k = jnp.arange(total, dtype=jnp.int32)
    block, part = k // n, (k % n) // (2 * piece)
    half, line = (k % (2 * piece)) // piece, k % piece
    part = jnp.where(part == 1, 1, jnp.where(part == 0, 2 * side, 2 - 2 * side))
    at = (block ^ place.dp) * n + part * 2 * piece + (half ^ core) * piece + line
    order = (at[:, None] == jnp.arange(total, dtype=jnp.int32)[None, :]).astype(bf16)
    return full.reshape(total, columns), order


def scatter_weights(place, part):
    total, columns = part.shape
    n = total // place.dp_size
    piece = n // 6
    core = place.ex % 2
    side = (place.ex // 2) % 2

    def add(left, right):
        return (left.astype(f32) + right.astype(f32)).astype(bf16)

    part = part.reshape(place.dp_size, 3, 2, piece, columns)
    kept = add(part[:, :, 0], swap(part[:, :, 1], "expert", 1))
    first = add(kept[:, 0], swap(kept[:, 2], "expert", 2))
    blocks = {m: jnp.stack([first[m], kept[m, 1]]) for m in range(place.dp_size)}
    for mask in (place.z_bits + place.y_bits)[::-1]:
        blocks = {
            m: add(v, swap(blocks[m ^ mask], "dp", mask))
            for m, v in blocks.items()
            if m & mask == 0
        }
    mine = blocks[0]
    middle = add(mine[1], swap(mine[1], "expert", 2))
    trio = jnp.stack([mine[0], middle, swap(mine[0], "expert", 2)])
    for mask in place.x_bits[1:]:
        trio = add(trio, swap(trio, "expert", mask))
    both = jnp.stack([trio, swap(trio, "expert", 1)], axis=1)
    both = jnp.where(side == 0, both, both[::-1])
    both = jnp.where(core == 0, both, both[:, ::-1])
    return both.reshape(n, columns).astype(f32)


def gather_tokens(place, block):
    blocks = {0: block}
    for mask in place.z_bits:
        blocks.update({m ^ mask: swap(v, "dp", mask) for m, v in list(blocks.items())})
    groups = []
    for r in range(ZLINE):
        row = [blocks[r * place.rows_y]]
        for mask in place.x_bits:
            row = row + [swap(v, "expert", mask) for v in row]
        row = jnp.concatenate(row, axis=0)
        groups.append(jnp.concatenate([row, swap(row, "expert", 1)], axis=0))
    return groups


def scatter_tokens(place, groups, length):
    def add(left, right):
        return left.astype(f32) + right.astype(f32)

    reduced = []
    for part in groups:
        half = part.shape[0] // 2
        kept = add(part[:half], swap(part[half:], "expert", 1)).astype(bf16)
        for mask in place.x_bits[::-1]:
            half = kept.shape[0] // 2
            kept = add(kept[:half], swap(kept[half:], "expert", mask)).astype(bf16)
        reduced.append(kept)
    two = [add(reduced[i], swap(reduced[i + 2], "dp", place.z_bits[1])) for i in range(2)]
    return add(two[0], swap(two[1].astype(bf16), "dp", place.z_bits[0]))


def other(index, mask):
    return index + mask - 2 * mask * ((index // mask) % 2)


class Links:
    def __init__(self, sends, recvs):
        self.sends, self.recvs, self.used, self.open = sends, recvs, 0, []

    def copy(self, source, target, partner):
        at = self.used
        self.used += 1
        made = pltpu.make_async_remote_copy(
            src_ref=source,
            dst_ref=target,
            send_sem=self.sends.at[at],
            recv_sem=self.recvs.at[at],
            device_id=partner,
            device_id_type=pl.DeviceIdType.MESH,
        )
        made.start()
        self.open.append(made)
        return made

    def close(self):
        for made in self.open:
            made.wait_send()


def partners(rows_y):
    dp, ex = lax.axis_index("dp"), lax.axis_index("expert")
    return {
        "z1": (other(dp, rows_y), ex),
        "z2": (other(dp, 2 * rows_y), ex),
        "y": (other(dp, 1), ex),
        "x": (dp, other(ex, 2)),
        "c": (dp, other(ex, 1)),
    }


def greet(devices):
    barrier = pltpu.get_barrier_semaphore()
    for device in devices:
        pl.semaphore_signal(
            barrier, inc=1, device_id=device, device_id_type=pl.DeviceIdType.MESH
        )
    pl.semaphore_wait(barrier, len(devices))


def gather_kernel(rows_y, exclusive, *refs):
    shards, dy = refs[:3], refs[3]
    fulls, dy_all = refs[4:7], refs[7]
    z_send, z_recv, y_send, y_recv, x_send, x_recv, c_send, c_recv = refs[8:16]
    dz_send, dz_recv, dx_send, dx_recv, dc_send, dc_recv, local_sems = refs[16:]
    n = shards[0].shape[0]
    half = n // 2
    piece = half - exclusive
    length = dy.shape[0]
    dp, ex = lax.axis_index("dp"), lax.axis_index("expert")
    z, y = dp // rows_y, dp % rows_y
    core, side = ex % 2, (ex // 2) % 2
    to = partners(rows_y)
    z_of = [z, other(z, 1), other(z, 2), other(other(z, 1), 2)]

    in_plane = pl.ds(pl.multiple_of(core * half + side * exclusive, 16), piece)
    alone = pl.ds(pl.multiple_of(core * half + side * piece, 16), exclusive)
    of_core = pl.ds(pl.multiple_of(core * half, 16), half)

    def remote(source, target, send_sem, recv_sem, device):
        return pltpu.make_async_remote_copy(
            src_ref=source,
            dst_ref=target,
            send_sem=send_sem,
            recv_sem=recv_sem,
            device_id=device,
            device_id_type=pl.DeviceIdType.MESH,
        )

    def copies(rows, m, ys, send, recv, at, device, own=False):
        made = []
        for k in range(3):
            block = fulls[k].at[z_of[m] * rows_y + ys, rows]
            source = shards[k].at[rows] if own else block
            made.append(remote(source, block, send.at[k, at], recv.at[k, at], device))
        return made

    def to_z(step):
        m, device = ((0, "z1"), (0, "z2"), (2, "z1"))[step]
        return copies(in_plane, m, y, z_send, z_recv, step, to[device], m == 0)

    def to_y(m):
        return copies(in_plane, m, y, y_send, y_recv, m, to["y"], m == 0)

    def to_x(m, k):
        ys = 1 - y if k else y
        return copies(alone, m, ys, x_send, x_recv, 2 * m + k, to["x"])

    def to_c(m, k):
        ys = 1 - y if k else y
        return copies(of_core, m, ys, c_send, c_recv, 2 * m + k, to["c"])

    near, pair = pl.ds(0, length), pl.ds(length, length)
    front, back = pl.ds(0, 2 * length), pl.ds(2 * length, 2 * length)

    def dy_z(step):
        m, target, device = ((0, 1, "z1"), (0, 2, "z2"), (2, 3, "z1"))[step]
        source = dy_all.at[m, near] if m else dy
        return remote(
            source, dy_all.at[target, near], dz_send.at[step], dz_recv.at[step], to[device]
        )

    def dy_x(m):
        source = dy_all.at[m, near] if m else dy
        return remote(source, dy_all.at[m, pair], dx_send.at[m], dx_recv.at[m], to["x"])

    def dy_c(m):
        return remote(
            dy_all.at[m, front], dy_all.at[m, back], dc_send.at[m], dc_recv.at[m], to["c"]
        )

    mine = [
        pltpu.make_async_copy(shards[k], fulls[k].at[dp], local_sems.at[k]) for k in range(3)
    ]
    mine.append(pltpu.make_async_copy(dy, dy_all.at[0, near], local_sems.at[3]))
    for made in mine:
        made.start()
    greet([to["z1"], to["z2"], to["y"], to["x"], to["c"]])

    def start(made):
        for copy in made:
            copy.start()

    def arrived(made):
        for copy in made:
            copy.wait_recv()

    start(to_z(1))
    start(to_z(0))
    start(to_y(0))
    dy_x(0).start()
    dy_z(1).start()
    dy_z(0).start()

    arrived(to_z(0))
    start(to_y(1))
    start(to_x(1, 0))
    arrived(to_z(1))
    start(to_z(2))
    start(to_y(2))
    start(to_x(2, 0))
    dy_z(0).wait_recv()
    dy_x(1).start()
    dy_z(1).wait_recv()
    dy_z(2).start()
    dy_x(2).start()
    arrived(to_y(0))
    start(to_x(0, 1))
    dy_x(0).wait_recv()
    mine[3].wait()
    dy_c(0).start()
    arrived(to_z(2))
    start(to_y(3))
    start(to_x(3, 0))
    arrived(to_y(1))
    start(to_x(1, 1))
    dy_x(1).wait_recv()
    dy_c(1).start()
    dy_z(2).wait_recv()
    dy_x(3).start()
    for m in (1, 2):
        arrived(to_x(m, 0))
        start(to_c(m, 0))
    arrived(to_x(0, 1))
    start(to_c(0, 1))
    arrived(to_y(2))
    start(to_x(2, 1))
    dy_x(2).wait_recv()
    dy_c(2).start()
    arrived(to_x(1, 1))
    start(to_c(1, 1))
    arrived(to_y(3))
    start(to_x(3, 1))
    for m, k in ((3, 0), (2, 1), (3, 1)):
        arrived(to_x(m, k))
        start(to_c(m, k))
    dy_x(3).wait_recv()
    dy_c(3).start()

    for made in mine[:3]:
        made.wait()
    for step in range(3):
        for made in to_z(step):
            made.wait_send()
        dy_z(step).wait_send()
    for m in range(ZLINE):
        for made in to_y(m):
            made.wait_send()
        dy_x(m).wait_send()
        dy_c(m).wait()
        for k in range(2):
            if m or k:
                for made in to_x(m, k):
                    made.wait_send()
                for made in to_c(m, k):
                    made.wait()


def gather(rows_y, shards, dy):
    exclusive = shards[0].shape[0] // 12
    dp_size = ZLINE * rows_y
    any_space = pl.BlockSpec(memory_space=pl.ANY)
    sems = pltpu.SemaphoreType.DMA
    return pl.pallas_call(
        functools.partial(gather_kernel, rows_y, exclusive),
        name="gather",
        out_shape=tuple(jax.ShapeDtypeStruct((dp_size,) + v.shape, bf16) for v in shards)
        + (jax.ShapeDtypeStruct((ZLINE, 4 * dy.shape[0], dy.shape[1]), bf16),),
        in_specs=[pl.BlockSpec(memory_space=pltpu.VMEM)] * 4,
        out_specs=(any_space,) * 4,
        scratch_shapes=[
            sems((3, 3)),
            sems((3, 3)),
            sems((3, ZLINE)),
            sems((3, ZLINE)),
            sems((3, dp_size)),
            sems((3, dp_size)),
            sems((3, dp_size)),
            sems((3, dp_size)),
            sems((3,)),
            sems((3,)),
            sems((ZLINE,)),
            sems((ZLINE,)),
            sems((ZLINE,)),
            sems((ZLINE,)),
            sems((4,)),
        ],
        compiler_params=pltpu.CompilerParams(
            collective_id=2, has_side_effects=True, vmem_limit_bytes=60 * 2**20
        ),
    )(*shards, dy)


MOE_COPIES = 22


def moe_kernel(
    rows_y,
    normed_ref,
    dy_hbm,
    gate_up_hbm,
    down_hbm,
    router_ref,
    spread_ref,
    rows_out,
    grads_out,
    acts_out,
    total_ref,
    w_gate,
    w_up,
    w_down,
    rows,
    dy,
    grads,
    acts,
    gate_grads,
    parts,
    heard_c,
    heard_x,
    heard_z2,
    heard_z1,
    sends,
    recvs,
    load_sems,
    dy_sems,
    out_sems,
):
    owned, hidden = w_down.shape[:2]
    length, width = normed_ref.shape
    count = rows.shape[1]
    half = count // 2
    span = owned * hidden
    z = lax.axis_index("dp") // rows_y
    to = partners(rows_y)
    links = Links(sends, recvs)

    loads = []
    mine = pl.ds(pl.multiple_of(z * hidden, hidden), hidden)
    theirs = pl.ds(pl.multiple_of(F + z * hidden, hidden), hidden)
    for e in range(owned):
        at = pl.ds(e * hidden, hidden)
        for k, (cut, kept) in enumerate(((mine, w_gate), (theirs, w_up))):
            loads.append(
                pltpu.make_async_copy(
                    gate_up_hbm.at[e, :, cut], kept.at[:, at], load_sems.at[2 * e + k]
                )
            )
    loads.append(pltpu.make_async_copy(down_hbm.at[:, mine, :], w_down, load_sems.at[2 * owned]))
    for load in loads:
        load.start()

    def fetch(r):
        return pltpu.make_async_copy(dy_hbm.at[r], dy.at[r % 2], dy_sems.at[r % 2])

    fetch(0).start()
    fetch(1).start()
    rows[0, :length] = normed_ref[...]
    greet([to["z1"], to["z2"], to["x"], to["c"]])

    own = pl.ds(0, length)
    pair = pl.ds(length, length)
    near, far = pl.ds(0, half), pl.ds(half, half)

    def row_x(r):
        return links.copy(rows.at[r, own], rows.at[r, pair], to["x"])

    def row_c(r):
        return links.copy(rows.at[r, near], rows.at[r, far], to["c"])

    z1 = links.copy(rows.at[0, own], rows.at[1, own], to["z1"])
    x0 = row_x(0)
    z2 = links.copy(rows.at[0, own], rows.at[2, own], to["z2"])
    x0.wait_recv()
    c0 = row_c(0)
    z1.wait_recv()
    x1 = row_x(1)
    z3 = links.copy(rows.at[1, own], rows.at[3, own], to["z2"])
    c0.wait_recv()
    for load in loads:
        load.wait()

    stores = []

    def store(source, target):
        made = pltpu.make_async_copy(source, target, out_sems.at[len(stores)])
        made.start()
        stores.append(made)
        return made

    def forward(r):
        slot = r % 2
        fetch(r).wait()
        logits = jnp.dot(rows[r], router_ref[...], preferred_element_type=f32)
        mask = dy[slot, :, width:].astype(f32) > 0.5
        logits = jnp.where(mask, logits, -1e30)
        lifted = jnp.where(
            mask, jnp.exp(logits - jnp.max(logits, axis=-1, keepdims=True)), 0.0
        )
        gates = lifted / jnp.sum(lifted, axis=-1, keepdims=True)
        gates_high = gates.astype(bf16)
        gates_low = (gates - gates_high.astype(f32)).astype(bf16)
        gate_grads[...] = jnp.zeros_like(gate_grads)

        def step(p, _):
            at = pl.ds(pl.multiple_of(p * 2 * hidden, 2 * hidden), 2 * hidden)
            up_at = pl.ds(pl.multiple_of(span + p * 2 * hidden, 2 * hidden), 2 * hidden)
            spread = spread_ref[:, at]
            down = w_down[pl.ds(2 * p, 2)].reshape(2 * hidden, width)
            gate_part = jnp.dot(rows[r], w_gate[:, at], preferred_element_type=f32)
            up_part = jnp.dot(rows[r], w_up[:, at], preferred_element_type=f32)
            plain_grad = against(dy[slot, :, :width], down)
            spread_gates = jnp.dot(gates_high, spread, preferred_element_type=f32) + jnp.dot(
                gates_low, spread, preferred_element_type=f32
            )
            sigmoid_gate = 1.0 / (1.0 + jnp.exp(-gate_part))
            swished = gate_part * sigmoid_gate
            activation = swished * up_part
            gate_grads[...] += against((plain_grad * activation).astype(bf16), spread)
            acts[slot, :, at] = (spread_gates * activation).astype(bf16)
            grad_act = plain_grad * spread_gates
            grads[r, :, at] = (
                grad_act * up_part * (sigmoid_gate + swished * (1.0 - sigmoid_gate))
            ).astype(bf16)
            grads[r, :, up_at] = (grad_act * swished).astype(bf16)
            return 0

        lax.fori_loop(0, owned // 2, step, 0)
        parts[r, :, width:] = gate_grads[...].astype(bf16)
        if r + 2 < ZLINE:
            fetch(r + 2).start()
        store(rows.at[r], rows_out.at[r])
        store(grads.at[r], grads_out.at[r])
        return store(acts.at[slot], acts_out.at[r])

    def backward(r):
        def step(j, _):
            at = pl.ds(pl.multiple_of(j * 512, 512), 512)
            part = against(grads[r, :, :span], w_gate[at, :]) + against(
                grads[r, :, span:], w_up[at, :]
            )
            parts[r, :, at] = part.astype(bf16)
            return 0

        lax.fori_loop(0, width // 512, step, 0)

    kept = [forward(0)]
    x1.wait_recv()
    c1 = row_c(1)
    z2.wait_recv()
    x2 = row_x(2)
    c1.wait_recv()
    kept.append(forward(1))
    x2.wait_recv()
    c2 = row_c(2)
    z3.wait_recv()
    x3 = row_x(3)
    c2.wait_recv()
    kept[0].wait()
    kept.append(forward(2))
    x3.wait_recv()
    c3 = row_c(3)
    c3.wait_recv()
    kept[1].wait()
    kept.append(forward(3))

    def add(left, right):
        return (left[...].astype(f32) + right[...].astype(f32)).astype(bf16)

    def part_c(r):
        return links.copy(parts.at[r, far], heard_c.at[r], to["c"])

    def part_x(r, copy):
        copy.wait_recv()
        parts[r, near] = add(parts.at[r, near], heard_c.at[r])
        return links.copy(parts.at[r, pair], heard_x.at[r], to["x"])

    def part_z(r, copy):
        copy.wait_recv()
        parts[r, own] = add(parts.at[r, own], heard_x.at[r])

    backward(3)
    c3 = part_c(3)
    backward(2)
    c2 = part_c(2)
    x3 = part_x(3, c3)
    backward(1)
    c1 = part_c(1)
    x2 = part_x(2, c2)
    part_z(3, x3)
    z3 = links.copy(parts.at[3, own], heard_z2.at[1], to["z2"])
    backward(0)
    c0 = part_c(0)
    x1 = part_x(1, c1)
    part_z(2, x2)
    z2 = links.copy(parts.at[2, own], heard_z2.at[0], to["z2"])
    x0 = part_x(0, c0)
    part_z(1, x1)
    z3.wait_recv()
    parts[1, own] = add(parts.at[1, own], heard_z2.at[1])
    z1 = links.copy(parts.at[1, own], heard_z1, to["z1"])
    part_z(0, x0)
    z2.wait_recv()
    total = parts[0, own].astype(f32) + heard_z2[0].astype(f32)
    z1.wait_recv()
    total_ref[...] = total + heard_z1[...].astype(f32)
    links.close()
    for k, made in enumerate(stores):
        if k not in (2, 5):
            made.wait()


def moe(rows_y, normed, dy, w_gate_up, w_down, router, spread):
    owned, width, _ = w_gate_up.shape
    hidden = F // ZLINE
    length = normed.shape[0]
    count = dy.shape[1]
    wide = width + 128
    any_space = pl.BlockSpec(memory_space=pl.ANY)
    vmem = pl.BlockSpec(memory_space=pltpu.VMEM)
    span = owned * hidden
    return pl.pallas_call(
        functools.partial(moe_kernel, rows_y),
        name="moe",
        out_shape=(
            jax.ShapeDtypeStruct((ZLINE, count, width), bf16),
            jax.ShapeDtypeStruct((ZLINE, count, 2 * span), bf16),
            jax.ShapeDtypeStruct((ZLINE, count, span), bf16),
            jax.ShapeDtypeStruct((length, wide), f32),
        ),
        in_specs=[vmem, any_space, any_space, any_space, vmem, vmem],
        out_specs=(any_space, any_space, any_space, vmem),
        scratch_shapes=[
            pltpu.VMEM((width, span), bf16),
            pltpu.VMEM((width, span), bf16),
            pltpu.VMEM((owned, hidden, width), bf16),
            pltpu.VMEM((ZLINE, count, width), bf16),
            pltpu.VMEM((2, count, wide), bf16),
            pltpu.VMEM((ZLINE, count, 2 * span), bf16),
            pltpu.VMEM((2, count, span), bf16),
            pltpu.VMEM((count, 128), f32),
            pltpu.VMEM((ZLINE, count, wide), bf16),
            pltpu.VMEM((ZLINE, count // 2, wide), bf16),
            pltpu.VMEM((ZLINE, length, wide), bf16),
            pltpu.VMEM((2, length, wide), bf16),
            pltpu.VMEM((length, wide), bf16),
            pltpu.SemaphoreType.DMA((MOE_COPIES,)),
            pltpu.SemaphoreType.DMA((MOE_COPIES,)),
            pltpu.SemaphoreType.DMA((2 * owned + 1,)),
            pltpu.SemaphoreType.DMA((2,)),
            pltpu.SemaphoreType.DMA((12,)),
        ],
        compiler_params=pltpu.CompilerParams(
            collective_id=1, has_side_effects=True, vmem_limit_bytes=60 * 2**20
        ),
    )(normed, dy, w_gate_up, w_down, router, spread)


def finish_kernel(
    rows_y,
    rows_hbm,
    grads_hbm,
    acts_hbm,
    dy_hbm,
    att_hbm,
    gate_up_out,
    down_out,
    att_out,
    wide,
    turned,
    grads,
    acts,
    part_gate_up,
    heard_gate_up,
    heard_z,
    part_down,
    heard_down,
    stage_gate_up,
    stage_down,
    own,
    heard_c,
    heard_x,
    heard_z1,
    heard_z2,
    heard_y,
    load_sems,
    grads_sems,
    acts_sems,
    store_sems,
    down_store_sems,
    y_send,
    y_recv,
    d_send,
    d_recv,
    z_send,
    z_recv,
    a_send,
    a_recv,
):
    owned, n = gate_up_out.shape[:2]
    hidden = F // ZLINE
    count, width = wide.shape[1:]
    tokens = ZLINE * count
    columns = att_out.shape[1]
    dp, ex = lax.axis_index("dp"), lax.axis_index("expert")
    z, y = dp // rows_y, dp % rows_y
    core, side = ex % 2, (ex // 2) % 2
    to = partners(rows_y)
    to["z3"] = (other(to["z1"][0], 2 * rows_y), ex)
    z_of = [z, other(z, 1), other(z, 2), other(other(z, 1), 2)]
    half, quarter = n // 2, n // 4
    of_core = pl.ds(pl.multiple_of(core * half, 16), half)
    of_sibling = pl.ds(pl.multiple_of((1 - core) * half, 16), half)
    of_side = pl.ds(pl.multiple_of(side * quarter, 16), quarter)
    of_far_side = pl.ds(pl.multiple_of((1 - side) * quarter, 16), quarter)

    def remote(source, target, send_sem, recv_sem, device):
        return pltpu.make_async_remote_copy(
            src_ref=source,
            dst_ref=target,
            send_sem=send_sem,
            recv_sem=recv_sem,
            device_id=device,
            device_id_type=pl.DeviceIdType.MESH,
        )

    def add(left, right):
        return (left.astype(f32) + right.astype(f32)).astype(bf16)

    def load_wide(source, r):
        return pltpu.make_async_copy(source.at[r, :, pl.ds(0, width)], wide.at[r], load_sems.at[r])

    load_own = pltpu.make_async_copy(att_hbm.at[:, of_core], own, load_sems.at[ZLINE])

    def load_acts(e):
        at = pl.ds(pl.multiple_of(e * hidden, hidden), hidden)
        return pltpu.make_async_copy(
            acts_hbm.at[:, :, at], acts.at[lax.rem(e, 2)], acts_sems.at[lax.rem(e, 2)]
        )

    def load_grads(e, k):
        at = pl.ds(pl.multiple_of((k * owned + e) * hidden, hidden), hidden)
        return pltpu.make_async_copy(
            grads_hbm.at[:, :, at],
            grads.at[lax.rem(e, 2), :, :, pl.ds(k * hidden, hidden)],
            grads_sems.at[lax.rem(e, 2), k],
        )

    load_acts(0).start()
    for r in range(ZLINE):
        load_wide(dy_hbm, r).start()
    load_acts(1).start()
    load_own.start()
    for e in range(2):
        for k in range(2):
            load_grads(e, k).start()
    greet([to["z1"], to["z2"], to["z3"], to["y"], to["x"], to["c"]])

    cuts = [pl.ds(0, 2048), pl.ds(2048, columns - 2048)]

    def att(k, step, source, target, device):
        return remote(source, target, a_send.at[k, step], a_recv.at[k, step], device)

    def att_c(k):
        return att(
            k, 0, att_hbm.at[:, of_sibling, cuts[k]], heard_c.at[:, :, cuts[k]], to["c"]
        )

    def att_x(k):
        return att(
            k, 1, own.at[:, of_far_side, cuts[k]], heard_x.at[:, :, cuts[k]], to["x"]
        )

    def line(m):
        return pl.ds(z_of[m] * rows_y, rows_y)

    def att_z1(k, m):
        return att(
            k, 2 + m, own.at[line(1 + 2 * m), of_side, cuts[k]], heard_z1.at[m, :, :, cuts[k]], to["z1"]
        )

    def att_z2(k):
        return att(k, 4, own.at[line(2), of_side, cuts[k]], heard_z2.at[:, :, cuts[k]], to["z2"])

    def att_y(k):
        return att(
            k, 5, own.at[other(dp, 1), of_side, cuts[k]], heard_y.at[:, cuts[k]], to["y"]
        )

    mine = pl.ds(pl.multiple_of(core * half + side * quarter, 16), quarter)

    def att_back_x(k):
        return att(k, 6, att_out.at[mine, cuts[k]], att_out.at[mine, cuts[k]], to["x"])

    def att_back_c(k):
        return att(k, 7, att_out.at[of_core, cuts[k]], att_out.at[of_core, cuts[k]], to["c"])

    def att_after_c(k):
        att_c(k).wait_recv()

        def step(b, _):
            own[b, :, cuts[k]] = add(own[b, :, cuts[k]], heard_c[b, :, cuts[k]])
            return 0

        lax.fori_loop(0, own.shape[0], step, 0)
        att_x(k).start()

    def att_after_x(k):
        att_x(k).wait_recv()

        def step(b, _):
            own[b, of_side, cuts[k]] = add(own[b, of_side, cuts[k]], heard_x[b, :, cuts[k]])
            return 0

        lax.fori_loop(0, own.shape[0], step, 0)
        for m in range(2):
            att_z1(k, m).start()

    def att_after_z1(k):
        for m in (1, 0):
            att_z1(k, m).wait_recv()
            own[line(2 * m), of_side, cuts[k]] = add(
                own[line(2 * m), of_side, cuts[k]], heard_z1[m, :, :, cuts[k]]
            )
            if m:
                att_z2(k).start()

    def att_after_z2(k):
        att_z2(k).wait_recv()
        own[line(0), of_side, cuts[k]] = add(
            own[line(0), of_side, cuts[k]], heard_z2[:, :, cuts[k]]
        )
        att_y(k).start()

    def att_after_y(k):
        att_y(k).wait_recv()
        att_out[mine, cuts[k]] = add(own[dp, of_side, cuts[k]], heard_y[:, cuts[k]])
        att_back_x(k).start()

    def att_after_back(k):
        att_back_x(k).wait_recv()
        att_back_c(k).start()

    for k in range(2):
        att_c(k).start()

    def send_down(e):
        return remote(
            part_down.at[e, 1 - y], heard_down.at[e], d_send.at[e], d_recv.at[e], to["y"]
        )

    for r in range(ZLINE):
        load_wide(dy_hbm, r).wait()

    early = 3

    def down(e, _):
        load_acts(e).wait()
        left = acts[lax.rem(e, 2)].reshape(tokens, hidden)

        def step(j, _):
            at = pl.ds(pl.multiple_of(j * 512, 512), 512)
            result = transposed(left, wide[:, :, at].reshape(tokens, 512)).astype(bf16)
            for k in range(rows_y):
                part_down[e, k, :, at] = result[k * (hidden // rows_y) : (k + 1) * (hidden // rows_y)]
            return 0

        lax.fori_loop(0, width // 512, step, 0)

        @pl.when(e + 2 < owned)
        def _():
            load_acts(e + 2).start()

        @pl.when(e < early)
        def _():
            send_down(e).start()

        return 0

    lax.fori_loop(0, owned, down, 0)
    for r in range(ZLINE):
        load_wide(rows_hbm, r).start()
    load_own.wait()
    att_after_c(0)
    for r in range(ZLINE):
        load_wide(rows_hbm, r).wait()

        def turn(j, _, r=r):
            at = pl.ds(pl.multiple_of(j * 256, 256), 256)
            turned[at, pl.ds(r * count, count)] = wide[r, :, at].T
            return 0

        lax.fori_loop(0, width // 256, turn, 0)

    def send_y(e):
        return remote(
            part_gate_up.at[e, 1 - y], heard_gate_up.at[e], y_send.at[e], y_recv.at[e], to["y"]
        )

    def send_z(e, m):
        return remote(
            part_gate_up.at[e, y, z_of[m]],
            heard_z.at[m - 1, e],
            z_send.at[m - 1, e],
            z_recv.at[m - 1, e],
            to[f"z{m}"],
        )

    def reduce(e):
        send_y(e).wait_recv()
        for b in range(ZLINE):
            part_gate_up[e, y, b] = add(part_gate_up[e, y, b], heard_gate_up[e, b])
        for m in range(1, ZLINE):
            send_z(e, m).start()

    def gate_up(e, _):
        for k in range(2):
            load_grads(e, k).wait()
        right = grads[lax.rem(e, 2)].reshape(tokens, 2 * hidden)

        def step(b, _):
            at = pl.ds(pl.multiple_of(b * rows_y * n, 128), rows_y * n)
            result = jnp.dot(turned[at, :], right, preferred_element_type=f32).astype(bf16)
            for k in range(rows_y):
                part_gate_up[e, k, b] = result[k * n : (k + 1) * n]
            return 0

        lax.fori_loop(0, ZLINE, step, 0)

        @pl.when(e + 2 < owned)
        def _():
            for k in range(2):
                load_grads(e + 2, k).start()

        send_y(e).start()

        @pl.when(e >= 2)
        def _():
            reduce(e - 2)

        return 0

    lax.fori_loop(0, 1, gate_up, 0)
    att_after_c(1)
    lax.fori_loop(1, 5, gate_up, 0)
    att_after_x(0)
    lax.fori_loop(5, 8, gate_up, 0)
    att_after_z1(0)
    lax.fori_loop(8, owned, gate_up, 0)
    att_after_x(1)
    for e in range(early, early + 2):
        send_down(e).start()
    reduce(owned - 2)
    reduce(owned - 1)
    for e in range(early + 2, owned):
        send_down(e).start()
    att_after_z2(0)

    def keep_gate_up(e):
        return pltpu.make_async_copy(
            stage_gate_up.at[lax.rem(e, 2)], gate_up_out.at[e], store_sems.at[lax.rem(e, 2)]
        )

    def finish_gate_up(e, _):
        slot = lax.rem(e, 2)

        @pl.when(e >= 2)
        def _():
            keep_gate_up(e - 2).wait()

        for m in range(ZLINE):
            if m:
                send_z(e, m).wait_recv()
                block = heard_z[m - 1, e]
            else:
                block = part_gate_up[e, y, z]
            for k in range(2):
                at = pl.ds(pl.multiple_of(k * F + z_of[m] * hidden, hidden), hidden)
                stage_gate_up[slot, :, at] = block[:, k * hidden : (k + 1) * hidden].astype(f32)
        keep_gate_up(e).start()
        return 0

    def keep_down(e):
        return pltpu.make_async_copy(
            stage_down.at[lax.rem(e, 2)], down_out.at[e], down_store_sems.at[lax.rem(e, 2)]
        )

    def finish_down(e, _):
        @pl.when(e >= 2)
        def _():
            keep_down(e - 2).wait()

        send_down(e).wait_recv()
        stage_down[lax.rem(e, 2)] = part_down[e, y].astype(f32) + heard_down[e].astype(f32)
        keep_down(e).start()
        return 0

    att_after_z1(1)
    lax.fori_loop(0, owned - 2, finish_gate_up, 0)
    att_after_y(0)
    att_after_z2(1)
    lax.fori_loop(0, owned - 3, finish_down, 0)
    att_after_back(0)
    lax.fori_loop(owned - 2, owned, finish_gate_up, 0)
    att_after_y(1)
    lax.fori_loop(owned - 3, owned, finish_down, 0)
    att_after_back(1)

    for e in (owned - 2, owned - 1):
        keep_gate_up(e).wait()
        keep_down(e).wait()

    def close(e, _):
        send_y(e).wait_send()
        send_down(e).wait_send()
        for m in range(1, ZLINE):
            send_z(e, m).wait_send()
        return 0

    lax.fori_loop(0, owned, close, 0)
    for k in range(2):
        att_back_c(k).wait()
        for made in (att_c(k), att_x(k), att_z1(k, 0), att_z1(k, 1), att_z2(k), att_y(k)):
            made.wait_send()
        att_back_x(k).wait_send()


def finish(rows_y, rows, grads, acts, dy, att):
    _, count, width = rows.shape
    span = acts.shape[2]
    hidden = F // ZLINE
    owned = span // hidden
    dp_size, n, columns = att.shape
    any_space = pl.BlockSpec(memory_space=pl.ANY)
    sems = pltpu.SemaphoreType.DMA
    return pl.pallas_call(
        functools.partial(finish_kernel, rows_y),
        name="finish",
        out_shape=(
            jax.ShapeDtypeStruct((owned, n, 2 * F), f32),
            jax.ShapeDtypeStruct((owned, hidden // rows_y, width), f32),
            jax.ShapeDtypeStruct((n, columns), bf16),
        ),
        in_specs=[any_space] * 5,
        out_specs=(any_space, any_space, pl.BlockSpec(memory_space=pltpu.VMEM)),
        scratch_shapes=[
            pltpu.VMEM((ZLINE, count, width), bf16),
            pltpu.VMEM((width, ZLINE * count), bf16),
            pltpu.VMEM((2, ZLINE, count, 2 * hidden), bf16),
            pltpu.VMEM((2, ZLINE, count, hidden), bf16),
            pltpu.VMEM((owned, rows_y, ZLINE, n, 2 * hidden), bf16),
            pltpu.VMEM((owned, ZLINE, n, 2 * hidden), bf16),
            pltpu.VMEM((ZLINE - 1, owned, n, 2 * hidden), bf16),
            pltpu.VMEM((owned, rows_y, hidden // rows_y, width), bf16),
            pltpu.VMEM((owned, hidden // rows_y, width), bf16),
            pltpu.VMEM((2, n, 2 * F), f32),
            pltpu.VMEM((2, hidden // rows_y, width), f32),
            pltpu.VMEM((dp_size, n // 2, columns), bf16),
            pltpu.VMEM((dp_size, n // 2, columns), bf16),
            pltpu.VMEM((dp_size, n // 4, columns), bf16),
            pltpu.VMEM((2, rows_y, n // 4, columns), bf16),
            pltpu.VMEM((rows_y, n // 4, columns), bf16),
            pltpu.VMEM((n // 4, columns), bf16),
            sems((ZLINE + 1,)),
            sems((2, 2)),
            sems((2,)),
            sems((2,)),
            sems((2,)),
            sems((owned,)),
            sems((owned,)),
            sems((owned,)),
            sems((owned,)),
            sems((ZLINE - 1, owned)),
            sems((ZLINE - 1, owned)),
            sems((2, 8)),
            sems((2, 8)),
        ],
        compiler_params=pltpu.CompilerParams(
            collective_id=3, has_side_effects=True, vmem_limit_bytes=63 * 2**20
        ),
    )(rows, grads, acts, dy, att)


def local(
    tokens,
    segments,
    routes,
    w_query,
    w_key,
    w_value,
    w_output,
    w_router,
    gain_attn,
    gain_moe,
    w_gate_up,
    w_down,
    cotangent,
):
    place = Place()
    length, width = tokens.shape
    owned = w_gate_up.shape[0]
    rows = w_query.shape[0]
    hidden = F // ZLINE
    per_group = H // KV
    q_end, k_end, v_end = H * HD, (H + KV) * HD, (H + 2 * KV) * HD
    o_end = v_end + width

    small = jnp.concatenate(
        [w_router, gain_attn[:, None], gain_moe[:, None], jnp.zeros((rows, 128 - EXPERTS - 2), bf16)],
        axis=1,
    )
    chosen_mask = jnp.any(
        routes[:, :, None] == jnp.arange(EXPERTS, dtype=jnp.int32), axis=1
    )
    dy_block = jnp.concatenate(
        [cotangent, chosen_mask.astype(bf16), jnp.zeros((length, 128 - EXPERTS), bf16)], axis=1
    )
    kernels = place.ex_size == 4 and place.rows_y == 2
    if kernels:
        qkv_shard = jnp.concatenate([w_query, w_key, w_value], axis=1)
        full_qkv, full_output, full_small, all_dy = gather(
            place.rows_y, (qkv_shard, w_output, small), dy_block
        )
        full_qkv = full_qkv.reshape(width, v_end)
        full_output = full_output.reshape(width, width)
        full_small = full_small.reshape(width, 128)

        def ordered(value):
            return value

        canonical = ordered
    else:
        shard = jnp.concatenate([w_query, w_key, w_value, w_output, small], axis=1)
        full, order = gather_weights(place, shard)
        full_qkv, full_output = full[:, :v_end], full[:, v_end:o_end]
        full_small = transposed(order, full[:, o_end:]).astype(bf16)
        dy_groups = gather_tokens(place, dy_block)

        def ordered(value):
            return against(value, order).astype(bf16)

        def canonical(value):
            return lax.dot_general(
                value,
                order.astype(value.dtype),
                (((1,), (0,)), ((), ())),
                precision=lax.Precision.HIGHEST,
                preferred_element_type=f32,
            ).astype(value.dtype)

    full_router = full_small[:, :EXPERTS]
    attn_gain = full_small[:, EXPERTS].astype(f32)
    moe_gain = full_small[:, EXPERTS + 1].astype(f32)

    cosine_table, sine_table = tables(length, HD)
    inputs = tokens.astype(f32)
    inv_attn = lax.rsqrt(jnp.mean(inputs * inputs, axis=-1, keepdims=True) + epsilon)
    unit_attn = inputs * inv_attn
    normed = (unit_attn * attn_gain).astype(bf16)
    normed = ordered(normed)
    qkv = dot(normed, full_qkv)
    queries = rotate(qkv[:, :q_end].reshape(length, H, HD), cosine_table, sine_table)
    queries = queries.astype(bf16).reshape(length, KV, per_group, HD)
    key_rows = rotate(
        qkv[:, q_end:k_end].reshape(length, KV, HD), cosine_table, sine_table
    ).astype(bf16)
    values = qkv[:, k_end:].astype(bf16).reshape(length, KV, HD)
    segment = segments[0]
    position = jnp.arange(length, dtype=jnp.int32)
    allowed = (segment[:, None] == segment[None, :]) & (position[:, None] >= position[None, :])
    scores = (
        jnp.einsum("qkgd,skd->kgqs", queries, key_rows, preferred_element_type=f32) * 0.125
    )
    scores = jnp.where(allowed, scores, -1e30)
    maximum = jnp.max(scores, axis=-1, keepdims=True)
    lifted_scores = jnp.exp(scores - maximum)
    full_weights = lifted_scores / jnp.sum(lifted_scores, axis=-1, keepdims=True)
    attn_weights = full_weights.astype(bf16)
    mixed = jnp.einsum("kgqs,skd->qkgd", attn_weights, values, preferred_element_type=f32)
    mixed = mixed.reshape(length, H * HD).astype(bf16)
    mixed = ordered(mixed)
    residual = inputs + dot(mixed, full_output)
    inv_moe = lax.rsqrt(jnp.mean(residual * residual, axis=-1, keepdims=True) + epsilon)
    unit_moe = residual * inv_moe
    normed_moe = (unit_moe * moe_gain).astype(bf16)

    def gates_of(rows_in, mask):
        logits = jnp.where(mask, dot(rows_in, full_router), -1e30)
        lifted = jnp.where(mask, jnp.exp(logits - jnp.max(logits, axis=-1, keepdims=True)), 0.0)
        return lifted / jnp.sum(lifted, axis=-1, keepdims=True)

    gates = gates_of(normed_moe, chosen_mask)

    def columns(start):
        cut = lax.dynamic_slice_in_dim(w_gate_up, start + place.z * hidden, hidden, 2)
        return cut.swapaxes(0, 1).reshape(width, owned * hidden)

    span = owned * hidden
    slice_down = lax.dynamic_slice_in_dim(w_down, place.z * hidden, hidden, 1)
    slice_down = slice_down.reshape(span, width)
    if kernels:
        wide_router = jnp.pad(full_router, ((0, 0), (0, 128 - EXPERTS)))
        lane = jnp.arange(128, dtype=jnp.int32)[:, None]
        column = jnp.arange(span, dtype=jnp.int32)[None, :]
        spread = (lane == place.ex * owned + column // hidden).astype(bf16)
        all_rows, all_grads, all_acts, total = moe(
            place.rows_y, normed_moe, all_dy, w_gate_up, w_down, wide_router, spread
        )
        row_grads, grad_gates = total[:, :width], total[:, width : width + EXPERTS]
        out_parts = [dot(all_acts[r], slice_down).astype(bf16) for r in range(ZLINE)]
    else:
        slice_gate_up = jnp.concatenate([columns(0), columns(F)], axis=1)
        moe_groups = gather_tokens(place, normed_moe)
        acts, grads_gate_up, gate_parts = [], [], []
        for normed_rows, dy_rows in zip(moe_groups, dy_groups):
            count = normed_rows.shape[0]
            group_gates = gates_of(normed_rows, dy_rows[:, width : width + EXPERTS] > 0.5)
            group_gates = lax.dynamic_slice_in_dim(group_gates, place.ex * owned, owned, 1)
            spread_gates = jnp.broadcast_to(group_gates[:, :, None], (count, owned, hidden))
            spread_gates = spread_gates.reshape(count, span)
            gate_up = dot(normed_rows, slice_gate_up)
            gate_part, up_part = gate_up[:, :span], gate_up[:, span:]
            plain_grad = against(dy_rows[:, :width], slice_down)
            sigmoid_gate = jax.nn.sigmoid(gate_part)
            swished = gate_part * sigmoid_gate
            activation = swished * up_part
            grad_act = plain_grad * spread_gates
            gate_parts.append(jnp.sum((plain_grad * activation).reshape(count, owned, hidden), axis=-1))
            acts.append((spread_gates * activation).astype(bf16))
            grads_gate_up.append(
                jnp.concatenate(
                    [
                        grad_act * up_part * sigmoid_gate * (1.0 + gate_part * (1.0 - sigmoid_gate)),
                        grad_act * swished,
                    ],
                    axis=-1,
                ).astype(bf16)
            )
        row_parts = [against(g, slice_gate_up).astype(bf16) for g in grads_gate_up]
        row_grads = scatter_tokens(place, row_parts, length)
        out_parts = [dot(a, slice_down).astype(bf16) for a in acts]
        gate_parts = [g.T for g in gate_parts]
        two = [gate_parts[i] + swap(gate_parts[i + 2], "dp", place.z_bits[1]) for i in range(2)]
        mine = two[0] + swap(two[1], "dp", place.z_bits[0])
        mine = mine.reshape(owned, 2, place.ex_size // 2, length)
        heard = [
            swap(mine[:, m % 2, m // 2], "expert", m) if m else mine[:, 0, 0]
            for m in range(place.ex_size)
        ]
        heard = jnp.stack(heard)
        grad_gates = jnp.concatenate(
            [pick(heard, place.ex ^ j) for j in range(place.ex_size)], axis=0
        ).T
        all_rows = jnp.concatenate([v for v in moe_groups], axis=0)
        all_dy = jnp.concatenate([v[:, :width] for v in dy_groups], axis=0)
        all_grads = jnp.concatenate(grads_gate_up, axis=0)
        all_acts = jnp.concatenate(acts, axis=0)
    output = (residual + scatter_tokens(place, out_parts, length)).astype(bf16)
    grad_logits = (
        gates * (grad_gates - jnp.sum(gates * grad_gates, axis=-1, keepdims=True))
    ).astype(bf16)

    grad_out = cotangent.astype(f32)
    part_router = transposed(normed_moe, grad_logits)
    grad_normed_moe = row_grads + against(grad_logits, full_router)
    part_gain_moe = jnp.sum(grad_normed_moe * unit_moe, axis=0)
    scaled_moe = grad_normed_moe * moe_gain
    grad_residual = grad_out + inv_moe * (
        scaled_moe - unit_moe * jnp.mean(scaled_moe * unit_moe, axis=-1, keepdims=True)
    )
    grad_branch = grad_residual.astype(bf16)
    part_output = transposed(mixed, grad_branch)
    grad_mixed = canonical(against(grad_branch, full_output).astype(bf16))
    grad_mixed = grad_mixed.reshape(length, KV, per_group, HD)
    grad_weights = jnp.einsum(
        "qkgd,skd->kgqs", grad_mixed, values, preferred_element_type=f32
    )
    grad_values = jnp.einsum(
        "kgqs,qkgd->skd", attn_weights, grad_mixed, preferred_element_type=f32
    )
    grad_values = grad_values.astype(bf16).reshape(length, KV * HD)
    grad_scores = (
        full_weights * (grad_weights - jnp.sum(full_weights * grad_weights, axis=-1, keepdims=True))
    ).astype(bf16)
    grad_queries = (
        jnp.einsum("kgqs,skd->qkgd", grad_scores, key_rows, preferred_element_type=f32) * 0.125
    )
    grad_queries = rotate(grad_queries.reshape(length, H, HD), cosine_table, -sine_table)
    grad_queries = grad_queries.astype(bf16).reshape(length, H * HD)
    grad_keys = (
        jnp.einsum("kgqs,qkgd->skd", grad_scores, queries, preferred_element_type=f32) * 0.125
    )
    grad_keys = rotate(grad_keys, cosine_table, -sine_table)
    grad_keys = grad_keys.astype(bf16).reshape(length, KV * HD)
    grad_qkv = jnp.concatenate([grad_queries, grad_keys, grad_values], axis=1)
    part_qkv = transposed(normed, grad_qkv)
    grad_normed = canonical(against(grad_qkv, full_qkv))
    part_gain_attn = jnp.sum(grad_normed * unit_attn, axis=0)
    scaled_attn = grad_normed * attn_gain
    grad_tokens = (
        grad_residual
        + inv_attn
        * (scaled_attn - unit_attn * jnp.mean(scaled_attn * unit_attn, axis=-1, keepdims=True))
    ).astype(bf16)
    part_small = jnp.concatenate(
        [
            part_router.astype(bf16),
            part_gain_attn[:, None].astype(bf16),
            part_gain_moe[:, None].astype(bf16),
            jnp.zeros((width, 128 - EXPERTS - 2), bf16),
        ],
        axis=1,
    )
    if kernels:
        parts = jnp.concatenate([part_qkv.astype(bf16), part_output.astype(bf16), part_small], axis=1)
        shard_gate_up, shard_down, summed = finish(
            place.rows_y,
            all_rows,
            all_grads,
            all_acts,
            all_dy,
            parts.reshape(place.dp_size, rows, -1),
        )
        summed = summed.astype(f32)
    else:
        part_small = dot(order, part_small).astype(bf16)
        summed = scatter_weights(
            place,
            jnp.concatenate([part_qkv.astype(bf16), part_output.astype(bf16), part_small], axis=1),
        )
        def reduce_y(part, axis):
            part = jnp.moveaxis(part, axis, 0)
            for mask in place.y_bits[::-1]:
                at = (place.y // mask) % 2
                half = part.reshape((2, part.shape[0] // 2) + part.shape[1:])
                away = swap(pick(half, 1 - at), "dp", mask)
                part = (pick(half, at).astype(f32) + away.astype(f32)).astype(bf16)
            return part[0]

        shard_down = transposed(all_acts, all_dy).astype(bf16)
        shard_down = shard_down.reshape(owned, place.rows_y, hidden // place.rows_y, width)
        shard_down = reduce_y(shard_down, 1).astype(f32)
        part_gate_up = transposed(all_rows, all_grads).astype(bf16)
        part_gate_up = part_gate_up.reshape(ZLINE, place.rows_y, rows, 2 * span)
        part_gate_up = reduce_y(part_gate_up, 1)
        heard = [pick(part_gate_up, place.z)] + [
            swap(pick(part_gate_up, place.z ^ m), "dp", m * place.rows_y) for m in range(1, ZLINE)
        ]
        heard = jnp.stack(heard)
        shard_gate_up = jnp.stack([pick(heard, place.z ^ j) for j in range(ZLINE)], axis=0)
        shard_gate_up = shard_gate_up.reshape(ZLINE, rows, 2, owned, hidden)
        shard_gate_up = shard_gate_up.transpose(3, 1, 2, 0, 4).reshape(owned, rows, 2 * F).astype(f32)
    return (
        output,
        grad_tokens,
        summed[:, :q_end],
        summed[:, q_end:k_end],
        summed[:, k_end:v_end],
        summed[:, v_end:o_end],
        summed[:, o_end : o_end + EXPERTS],
        summed[:, o_end + EXPERTS],
        summed[:, o_end + EXPERTS + 1],
        shard_gate_up,
        shard_down,
    )


def solution(mesh):
    return jax.shard_map(
        local,
        mesh=mesh,
        in_specs=(
            P(("dp", "expert"), None),
            P(("dp", "expert"), None),
            P(("dp", "expert"), None),
            P("dp", None),
            P("dp", None),
            P("dp", None),
            P("dp", None),
            P("dp", None),
            P("dp"),
            P("dp"),
            P("expert", None, None),
            P("expert", None, None),
            P(("dp", "expert"), None),
        ),
        out_specs=(
            P(("dp", "expert"), None),
            P(("dp", "expert"), None),
            P("dp", None),
            P("dp", None),
            P("dp", None),
            P("dp", None),
            P("dp", None),
            P("dp"),
            P("dp"),
            P("expert", "dp", None),
            P("expert", "dp", None),
        ),
        check_vma=False,
    )
```

```python
import functools

import jax
import jax.numpy as jnp
from jax import lax
from jax.experimental import pallas as pl
from jax.experimental.pallas import tpu as pltpu
from jax.sharding import PartitionSpec as P

H = 24
KV = 8
HD = 64
F = 512
EXPERTS = 40
ZLINE = 4


epsilon = 1e-05
f32 = jnp.float32
bf16 = jnp.bfloat16


def tables(length, size):
    half_size = size // 2
    frequency = jnp.power(10000.0, -2.0 * jnp.arange(half_size, dtype=f32) / size)
    angles = jnp.arange(length, dtype=f32)[:, None] * frequency[None, :]
    return (jnp.cos(angles)[:, None, :], jnp.sin(angles)[:, None, :])


def rotate(source, cosine_table, sine_table):
    half_size = source.shape[-1] // 2
    first_half = source[..., :half_size]
    second_half = source[..., half_size:]
    return jnp.concatenate(
        [
            first_half * cosine_table - second_half * sine_table,
            second_half * cosine_table + first_half * sine_table,
        ],
        axis=-1,
    )


def dot(left_side, right_side):
    return jnp.dot(left_side, right_side, preferred_element_type=f32)


def transposed(left_side, right_side):
    return lax.dot_general(
        left_side, right_side, (((0,), (0,)), ((), ())), preferred_element_type=f32
    )


def against(left_side, right_side):
    return lax.dot_general(
        left_side, right_side, (((1,), (1,)), ((), ())), preferred_element_type=f32
    )


def swap(value, axis, mask):
    size = lax.axis_size(axis)
    return lax.ppermute(value, axis, [(i, i ^ mask) for i in range(size)])


def pick(value, at):
    return lax.dynamic_index_in_dim(value, at, 0, keepdims=False)


def bits(first, size):
    masks, step = [], 1
    while step < size:
        masks.append(first * step)
        step *= 2
    return masks


class Place:
    def __init__(self):
        self.dp_size = lax.axis_size("dp")
        self.ex_size = lax.axis_size("expert")
        self.dp = lax.axis_index("dp")
        self.ex = lax.axis_index("expert")
        self.rows_y = self.dp_size // ZLINE
        self.z = self.dp // self.rows_y
        self.y = self.dp % self.rows_y
        self.z_bits = bits(self.rows_y, ZLINE)
        self.y_bits = bits(1, self.rows_y)
        self.x_bits = bits(2, self.ex_size // 2)


def gather_weights(place, shard):
    n, columns = shard.shape
    piece = n // 6
    cut = shard.reshape(3, 2, piece, columns)
    core = place.ex % 2
    side = (place.ex // 2) % 2
    own = pick(cut.swapaxes(0, 1), core)
    sibling = pick(cut.swapaxes(0, 1), 1 - core)

    def ordered(parts):
        return jnp.stack([pick(parts, 2 * side), parts[1], pick(parts, 2 - 2 * side)])

    own, sibling = ordered(own), ordered(sibling)
    blocks = {0: own[:2]}
    for mask in place.z_bits + place.y_bits:
        blocks.update({m ^ mask: swap(v, "dp", mask) for m, v in list(blocks.items())})
    rows = []
    for m in range(place.dp_size):
        if m == 0:
            rows.append(jnp.stack([own, sibling], axis=1))
            continue
        other = swap(blocks[m][0], "expert", 2)
        trio = jnp.concatenate([blocks[m], other[None]], axis=0)
        rows.append(jnp.stack([trio, swap(trio, "expert", 1)], axis=1))
    full = jnp.stack(rows)
    total = place.dp_size * n
    k = jnp.arange(total, dtype=jnp.int32)
    block, part = k // n, (k % n) // (2 * piece)
    half, line = (k % (2 * piece)) // piece, k % piece
    part = jnp.where(part == 1, 1, jnp.where(part == 0, 2 * side, 2 - 2 * side))
    at = (block ^ place.dp) * n + part * 2 * piece + (half ^ core) * piece + line
    order = (at[:, None] == jnp.arange(total, dtype=jnp.int32)[None, :]).astype(bf16)
    return full.reshape(total, columns), order


def scatter_weights(place, part):
    total, columns = part.shape
    n = total // place.dp_size
    piece = n // 6
    core = place.ex % 2
    side = (place.ex // 2) % 2

    def add(left, right):
        return (left.astype(f32) + right.astype(f32)).astype(bf16)

    part = part.reshape(place.dp_size, 3, 2, piece, columns)
    kept = add(part[:, :, 0], swap(part[:, :, 1], "expert", 1))
    first = add(kept[:, 0], swap(kept[:, 2], "expert", 2))
    blocks = {m: jnp.stack([first[m], kept[m, 1]]) for m in range(place.dp_size)}
    for mask in (place.z_bits + place.y_bits)[::-1]:
        blocks = {
            m: add(v, swap(blocks[m ^ mask], "dp", mask))
            for m, v in blocks.items()
            if m & mask == 0
        }
    mine = blocks[0]
    middle = add(mine[1], swap(mine[1], "expert", 2))
    trio = jnp.stack([mine[0], middle, swap(mine[0], "expert", 2)])
    for mask in place.x_bits[1:]:
        trio = add(trio, swap(trio, "expert", mask))
    both = jnp.stack([trio, swap(trio, "expert", 1)], axis=1)
    both = jnp.where(side == 0, both, both[::-1])
    both = jnp.where(core == 0, both, both[:, ::-1])
    return both.reshape(n, columns).astype(f32)


def gather_tokens(place, block):
    blocks = {0: block}
    for mask in place.z_bits:
        blocks.update({m ^ mask: swap(v, "dp", mask) for m, v in list(blocks.items())})
    groups = []
    for r in range(ZLINE):
        row = [blocks[r * place.rows_y]]
        for mask in place.x_bits:
            row = row + [swap(v, "expert", mask) for v in row]
        row = jnp.concatenate(row, axis=0)
        groups.append(jnp.concatenate([row, swap(row, "expert", 1)], axis=0))
    return groups


def scatter_tokens(place, groups, length):
    def add(left, right):
        return left.astype(f32) + right.astype(f32)

    reduced = []
    for part in groups:
        half = part.shape[0] // 2
        kept = add(part[:half], swap(part[half:], "expert", 1)).astype(bf16)
        for mask in place.x_bits[::-1]:
            half = kept.shape[0] // 2
            kept = add(kept[:half], swap(kept[half:], "expert", mask)).astype(bf16)
        reduced.append(kept)
    two = [add(reduced[i], swap(reduced[i + 2], "dp", place.z_bits[1])) for i in range(2)]
    return add(two[0], swap(two[1].astype(bf16), "dp", place.z_bits[0]))


def other(index, mask):
    return index + mask - 2 * mask * ((index // mask) % 2)


class Links:
    def __init__(self, sends, recvs):
        self.sends, self.recvs, self.used, self.open = sends, recvs, 0, []

    def copy(self, source, target, partner):
        at = self.used
        self.used += 1
        made = pltpu.make_async_remote_copy(
            src_ref=source,
            dst_ref=target,
            send_sem=self.sends.at[at],
            recv_sem=self.recvs.at[at],
            device_id=partner,
            device_id_type=pl.DeviceIdType.MESH,
        )
        made.start()
        self.open.append(made)
        return made

    def close(self):
        for made in self.open:
            made.wait_send()


def partners(rows_y):
    dp, ex = lax.axis_index("dp"), lax.axis_index("expert")
    return {
        "z1": (other(dp, rows_y), ex),
        "z2": (other(dp, 2 * rows_y), ex),
        "y": (other(dp, 1), ex),
        "x": (dp, other(ex, 2)),
        "c": (dp, other(ex, 1)),
    }


def greet(devices):
    barrier = pltpu.get_barrier_semaphore()
    for device in devices:
        pl.semaphore_signal(
            barrier, inc=1, device_id=device, device_id_type=pl.DeviceIdType.MESH
        )
    pl.semaphore_wait(barrier, len(devices))


def gather_kernel(rows_y, exclusive, *refs):
    shards, dy, down_hbm = refs[:3], refs[3], refs[4]
    fulls, dy_out, grads_out = refs[5:8], refs[8], refs[9]
    dy_all, w_down, grads = refs[10:13]
    z_send, z_recv, y_send, y_recv, x_send, x_recv, c_send, c_recv = refs[13:21]
    dz_send, dz_recv, dx_send, dx_recv, dc_send, dc_recv, local_sems, dy_sems, grads_sems = refs[21:]
    n = shards[0].shape[0]
    half = n // 2
    piece = half - exclusive
    length = dy.shape[0]
    dp, ex = lax.axis_index("dp"), lax.axis_index("expert")
    z, y = dp // rows_y, dp % rows_y
    core, side = ex % 2, (ex // 2) % 2
    to = partners(rows_y)
    z_of = [z, other(z, 1), other(z, 2), other(other(z, 1), 2)]

    in_plane = pl.ds(pl.multiple_of(core * half + side * exclusive, 16), piece)
    alone = pl.ds(pl.multiple_of(core * half + side * piece, 16), exclusive)
    of_core = pl.ds(pl.multiple_of(core * half, 16), half)

    def remote(source, target, send_sem, recv_sem, device):
        return pltpu.make_async_remote_copy(
            src_ref=source,
            dst_ref=target,
            send_sem=send_sem,
            recv_sem=recv_sem,
            device_id=device,
            device_id_type=pl.DeviceIdType.MESH,
        )

    def copies(rows, m, ys, send, recv, at, device, own=False):
        made = []
        for k in range(3):
            block = fulls[k].at[z_of[m] * rows_y + ys, rows]
            source = shards[k].at[rows] if own else block
            made.append(remote(source, block, send.at[k, at], recv.at[k, at], device))
        return made

    def to_z(step):
        m, device = ((0, "z1"), (0, "z2"), (2, "z1"))[step]
        return copies(in_plane, m, y, z_send, z_recv, step, to[device], m == 0)

    def to_y(m):
        return copies(in_plane, m, y, y_send, y_recv, m, to["y"], m == 0)

    def to_x(m, k):
        ys = 1 - y if k else y
        return copies(alone, m, ys, x_send, x_recv, 2 * m + k, to["x"])

    def to_c(m, k):
        ys = 1 - y if k else y
        return copies(of_core, m, ys, c_send, c_recv, 2 * m + k, to["c"])

    near, pair = pl.ds(0, length), pl.ds(length, length)
    front, back = pl.ds(0, 2 * length), pl.ds(2 * length, 2 * length)

    def dy_z(step):
        m, target, device = ((0, 1, "z1"), (0, 2, "z2"), (2, 3, "z1"))[step]
        source = dy_all.at[m, near] if m else dy
        return remote(
            source, dy_all.at[target, near], dz_send.at[step], dz_recv.at[step], to[device]
        )

    def dy_x(m):
        source = dy_all.at[m, near] if m else dy
        return remote(source, dy_all.at[m, pair], dx_send.at[m], dx_recv.at[m], to["x"])

    def dy_c(m):
        return remote(
            dy_all.at[m, front], dy_all.at[m, back], dc_send.at[m], dc_recv.at[m], to["c"]
        )

    owned, hidden, width = w_down.shape
    mine = [
        pltpu.make_async_copy(shards[k], fulls[k].at[dp], local_sems.at[k]) for k in range(3)
    ]
    at = pl.ds(pl.multiple_of(z * hidden, hidden), hidden)
    mine.append(pltpu.make_async_copy(down_hbm.at[:, at, :], w_down, local_sems.at[3]))
    for made in mine:
        made.start()
    dy_all[0, near] = dy[...]
    greet([to["z1"], to["z2"], to["y"], to["x"], to["c"]])

    def start(made):
        for copy in made:
            copy.start()

    def keep_dy(m):
        return pltpu.make_async_copy(dy_all.at[m], dy_out.at[m], dy_sems.at[m])

    def keep_grads(m):
        return pltpu.make_async_copy(grads.at[m % 2], grads_out.at[m], grads_sems.at[m % 2])

    def group(m):
        dy_c(m).wait_recv()
        keep_dy(m).start()
        if m >= 2:
            keep_grads(m - 2).wait()

        def step(p, _):
            at = pl.ds(pl.multiple_of(p * 2 * hidden, 2 * hidden), 2 * hidden)
            down = w_down[pl.ds(2 * p, 2)].reshape(2 * hidden, width)
            grads[m % 2, :, at] = against(dy_all[m, :, :width], down).astype(bf16)
            return 0

        lax.fori_loop(0, owned // 2, step, 0)
        keep_grads(m).start()

    def arrived(made):
        for copy in made:
            copy.wait_recv()

    start(to_z(1))
    start(to_z(0))
    start(to_y(0))
    dy_x(0).start()
    dy_z(1).start()
    dy_z(0).start()

    arrived(to_z(0))
    start(to_y(1))
    start(to_x(1, 0))
    arrived(to_z(1))
    start(to_z(2))
    start(to_y(2))
    start(to_x(2, 0))
    dy_z(0).wait_recv()
    dy_x(1).start()
    dy_z(1).wait_recv()
    dy_z(2).start()
    dy_x(2).start()
    arrived(to_y(0))
    start(to_x(0, 1))
    dy_x(0).wait_recv()
    dy_c(0).start()
    arrived(to_z(2))
    start(to_y(3))
    start(to_x(3, 0))
    arrived(to_y(1))
    start(to_x(1, 1))
    dy_x(1).wait_recv()
    dy_c(1).start()
    dy_z(2).wait_recv()
    dy_x(3).start()
    mine[3].wait()
    group(0)
    group(1)
    for m in (1, 2):
        arrived(to_x(m, 0))
        start(to_c(m, 0))
    arrived(to_x(0, 1))
    start(to_c(0, 1))
    arrived(to_y(2))
    start(to_x(2, 1))
    dy_x(2).wait_recv()
    dy_c(2).start()
    arrived(to_x(1, 1))
    start(to_c(1, 1))
    group(2)
    arrived(to_y(3))
    start(to_x(3, 1))
    dy_x(3).wait_recv()
    dy_c(3).start()
    for m, k in ((3, 0), (2, 1), (3, 1)):
        arrived(to_x(m, k))
        start(to_c(m, k))
    group(3)

    for made in mine[:3]:
        made.wait()
    for m in range(ZLINE):
        keep_dy(m).wait()
        if m >= 2:
            keep_grads(m).wait()
    for step in range(3):
        for made in to_z(step):
            made.wait_send()
        dy_z(step).wait_send()
    for m in range(ZLINE):
        for made in to_y(m):
            made.wait_send()
        dy_x(m).wait_send()
        dy_c(m).wait_send()
        for k in range(2):
            if m or k:
                for made in to_x(m, k):
                    made.wait_send()
                for made in to_c(m, k):
                    made.wait()


def gather(rows_y, shards, dy, w_down):
    exclusive = shards[0].shape[0] // 12
    dp_size = ZLINE * rows_y
    owned, _, width = w_down.shape
    hidden = F // ZLINE
    count = 4 * dy.shape[0]
    any_space = pl.BlockSpec(memory_space=pl.ANY)
    vmem = pl.BlockSpec(memory_space=pltpu.VMEM)
    sems = pltpu.SemaphoreType.DMA
    return pl.pallas_call(
        functools.partial(gather_kernel, rows_y, exclusive),
        name="gather",
        out_shape=tuple(jax.ShapeDtypeStruct((dp_size,) + v.shape, bf16) for v in shards)
        + (
            jax.ShapeDtypeStruct((ZLINE, count, dy.shape[1]), bf16),
            jax.ShapeDtypeStruct((ZLINE, count, owned * hidden), bf16),
        ),
        in_specs=[vmem] * 4 + [any_space],
        out_specs=(any_space,) * 5,
        scratch_shapes=[
            pltpu.VMEM((ZLINE, count, dy.shape[1]), bf16),
            pltpu.VMEM((owned, hidden, width), bf16),
            pltpu.VMEM((2, count, owned * hidden), bf16),
            sems((3, 3)),
            sems((3, 3)),
            sems((3, ZLINE)),
            sems((3, ZLINE)),
            sems((3, dp_size)),
            sems((3, dp_size)),
            sems((3, dp_size)),
            sems((3, dp_size)),
            sems((3,)),
            sems((3,)),
            sems((ZLINE,)),
            sems((ZLINE,)),
            sems((ZLINE,)),
            sems((ZLINE,)),
            sems((4,)),
            sems((ZLINE,)),
            sems((2,)),
        ],
        compiler_params=pltpu.CompilerParams(
            collective_id=2, has_side_effects=True, vmem_limit_bytes=60 * 2**20
        ),
    )(*shards, dy, w_down)


MOE_COPIES = 33


def moe_kernel(
    rows_y,
    normed_ref,
    dy_hbm,
    plain_hbm,
    gate_up_hbm,
    down_hbm,
    router_ref,
    spread_ref,
    rows_out,
    grads_out,
    down_out,
    total_ref,
    output_ref,
    w_gate,
    w_up,
    w_down,
    rows,
    masks,
    plain,
    grads,
    acts,
    gate_grads,
    stage_down,
    parts,
    heard_c,
    heard_x,
    heard_z1,
    heard_z2,
    out_parts,
    out_heard_c,
    out_heard_x,
    out_heard_z1,
    out_heard_z2,
    sends,
    recvs,
    load_sems,
    plain_sems,
    dy_sems,
    rows_sems,
    grads_sems,
    down_sems,
):
    owned, hidden = w_down.shape[:2]
    length, width = normed_ref.shape
    count = rows.shape[1]
    tokens = ZLINE * count
    half = count // 2
    span = owned * hidden
    z = lax.axis_index("dp") // rows_y
    to = partners(rows_y)
    links = Links(sends, recvs)

    loads = []
    mine = pl.ds(pl.multiple_of(z * hidden, hidden), hidden)
    theirs = pl.ds(pl.multiple_of(F + z * hidden, hidden), hidden)
    for e in range(owned):
        at = pl.ds(e * hidden, hidden)
        for k, (cut, kept) in enumerate(((mine, w_gate), (theirs, w_up))):
            loads.append(
                pltpu.make_async_copy(
                    gate_up_hbm.at[e, :, cut], kept.at[:, at], load_sems.at[2 * e + k]
                )
            )
    loads.append(
        pltpu.make_async_copy(dy_hbm.at[:, :, pl.ds(width, 128)], masks, load_sems.at[2 * owned])
    )
    load_down = pltpu.make_async_copy(
        down_hbm.at[:, mine, :], w_down, load_sems.at[2 * owned + 1]
    )
    for load in loads:
        load.start()

    def fetch(r):
        return pltpu.make_async_copy(plain_hbm.at[r], plain.at[r % 2], plain_sems.at[r % 2])

    fetch(0).start()
    fetch(1).start()
    load_down.start()
    rows[0, :length] = normed_ref[...]
    greet([to["z1"], to["z2"], to["x"], to["c"]])

    own = pl.ds(0, length)
    pair = pl.ds(length, length)
    near, far = pl.ds(0, half), pl.ds(half, half)

    def row_x(r):
        return links.copy(rows.at[r, own], rows.at[r, pair], to["x"])

    def row_c(r):
        return links.copy(rows.at[r, near], rows.at[r, far], to["c"])

    z1 = links.copy(rows.at[0, own], rows.at[1, own], to["z1"])
    z2 = links.copy(rows.at[0, own], rows.at[2, own], to["z2"])
    x0 = row_x(0)
    x0.wait_recv()
    c0 = row_c(0)
    z1.wait_recv()
    x1 = row_x(1)
    for load in loads:
        load.wait()
    c0.wait_recv()

    def keep_rows(r):
        return pltpu.make_async_copy(rows.at[r], rows_out.at[r], rows_sems.at[r])

    def keep_grads(r):
        return pltpu.make_async_copy(grads.at[min(r, 1)], grads_out.at[r], grads_sems.at[r])

    def forward(r):
        slot, held = r % 2, min(r, 1)
        keep_rows(r).start()
        fetch(r).wait()
        if r >= 2:
            keep_grads(r - 1).wait()
        logits = jnp.dot(rows[r], router_ref[...], preferred_element_type=f32)
        mask = masks[r].astype(f32) > 0.5
        logits = jnp.where(mask, logits, -1e30)
        lifted = jnp.where(
            mask, jnp.exp(logits - jnp.max(logits, axis=-1, keepdims=True)), 0.0
        )
        gates = lifted / jnp.sum(lifted, axis=-1, keepdims=True)
        gates_high = gates.astype(bf16)
        gates_low = (gates - gates_high.astype(f32)).astype(bf16)
        gate_grads[...] = jnp.zeros_like(gate_grads)

        def step(p, _):
            at = pl.ds(pl.multiple_of(p * 2 * hidden, 2 * hidden), 2 * hidden)
            up_at = pl.ds(pl.multiple_of(span + p * 2 * hidden, 2 * hidden), 2 * hidden)
            spread = spread_ref[:, at]
            gate_part = jnp.dot(rows[r], w_gate[:, at], preferred_element_type=f32)
            up_part = jnp.dot(rows[r], w_up[:, at], preferred_element_type=f32)
            plain_grad = plain[slot, :, at].astype(f32)
            spread_gates = jnp.dot(gates_high, spread, preferred_element_type=f32) + jnp.dot(
                gates_low, spread, preferred_element_type=f32
            )
            sigmoid_gate = 1.0 / (1.0 + jnp.exp(-gate_part))
            swished = gate_part * sigmoid_gate
            activation = swished * up_part
            gate_grads[...] += against((plain_grad * activation).astype(bf16), spread)
            acts[r, :, at] = (spread_gates * activation).astype(bf16)
            grad_act = plain_grad * spread_gates
            grads[held, :, at] = (
                grad_act * up_part * (sigmoid_gate + swished * (1.0 - sigmoid_gate))
            ).astype(bf16)
            grads[held, :, up_at] = (grad_act * swished).astype(bf16)
            return 0

        lax.fori_loop(0, owned // 2, step, 0)
        parts[r, :, width:] = gate_grads[...].astype(bf16)
        if r + 2 < ZLINE:
            fetch(r + 2).start()
        keep_grads(r).start()

    def backward(r):
        held = min(r, 1)

        def step(j, _):
            at = pl.ds(pl.multiple_of(j * 512, 512), 512)
            part = against(grads[held, :, :span], w_gate[at, :]) + against(
                grads[held, :, span:], w_up[at, :]
            )
            parts[r, :, at] = part.astype(bf16)
            return 0

        lax.fori_loop(0, width // 512, step, 0)

    def combine(r):
        def step(j, _):
            at = pl.ds(pl.multiple_of(j * 512, 512), 512)
            down = w_down[:, :, at].reshape(span, 512)
            out_parts[r, :, at] = jnp.dot(
                acts[r], down, preferred_element_type=f32
            ).astype(bf16)
            return 0

        lax.fori_loop(0, width // 512, step, 0)

    def add(left, right):
        return (left[...].astype(f32) + right[...].astype(f32)).astype(bf16)

    class Reduce:
        def __init__(self, parts, heard_c, heard_x, heard_z1, heard_z2, total):
            self.parts, self.c, self.x = parts, heard_c, heard_x
            self.z1, self.z2, self.total = heard_z1, heard_z2, total
            self.made = {}

        def start(self, r):
            self.made["c", r] = links.copy(self.parts.at[r, far], self.c.at[r], to["c"])

        def after_c(self, r):
            self.made["c", r].wait_recv()
            self.parts[r, near] = add(self.parts.at[r, near], self.c.at[r])
            self.made["x", r] = links.copy(self.parts.at[r, pair], self.x.at[r], to["x"])

        def after_x(self, r):
            self.made["x", r].wait_recv()
            self.parts[r, own] = add(self.parts.at[r, own], self.x.at[r])
            if r % 2:
                self.made["z1", r] = links.copy(
                    self.parts.at[r, own], self.z1.at[r // 2], to["z1"]
                )

        def after_z1(self, r):
            self.made["z1", r + 1].wait_recv()
            self.parts[r, own] = add(self.parts.at[r, own], self.z1.at[r // 2])
            if r:
                self.made["z2", r] = links.copy(self.parts.at[r, own], self.z2, to["z2"])

        def end(self):
            self.made["z2", 2].wait_recv()
            self.total[...] = self.parts[0, own].astype(f32) + self.z2[...].astype(f32)

    row_sum = Reduce(parts, heard_c, heard_x, heard_z1, heard_z2, total_ref)
    out_sum = Reduce(out_parts, out_heard_c, out_heard_x, out_heard_z1, out_heard_z2, output_ref)

    forward(0)
    x1.wait_recv()
    c1 = row_c(1)
    z2.wait_recv()
    z3 = links.copy(rows.at[2, own], rows.at[3, own], to["z1"])
    x2 = row_x(2)
    c1.wait_recv()
    forward(1)
    x2.wait_recv()
    c2 = row_c(2)
    z3.wait_recv()
    x3 = row_x(3)
    backward(1)
    row_sum.start(1)
    c2.wait_recv()
    forward(2)
    x3.wait_recv()
    c3 = row_c(3)
    row_sum.after_c(1)
    backward(2)
    row_sum.start(2)
    c3.wait_recv()
    forward(3)
    row_sum.after_x(1)
    row_sum.after_c(2)
    backward(3)
    row_sum.start(3)
    backward(0)
    row_sum.start(0)
    row_sum.after_c(3)
    row_sum.after_x(2)
    load_down.wait()
    combine(3)
    out_sum.start(3)
    row_sum.after_c(0)
    row_sum.after_x(3)
    combine(2)
    out_sum.start(2)
    out_sum.after_c(3)
    row_sum.after_z1(2)
    row_sum.after_x(0)
    row_sum.after_z1(0)
    combine(1)
    out_sum.start(1)
    out_sum.after_c(2)
    out_sum.after_x(3)
    combine(0)
    out_sum.start(0)
    out_sum.after_c(1)
    row_sum.end()
    out_sum.after_x(2)
    out_sum.after_z1(2)
    out_sum.after_c(0)

    for r in range(ZLINE):
        keep_rows(r).wait()
    gathered = (z1, z2, z3, x0, x1, x2, x3, c0, c1, c2, c3)
    for made in gathered:
        made.wait_send()
    links.open = [v for v in links.open if not any(v is made for made in gathered)]

    def fetch_dy(r):
        return pltpu.make_async_copy(
            dy_hbm.at[r, :, pl.ds(0, width)], rows.at[r], dy_sems.at[r]
        )

    for r in range(ZLINE):
        fetch_dy(r).start()
    for r in range(ZLINE):
        fetch_dy(r).wait()

    def keep_down(e):
        return pltpu.make_async_copy(
            stage_down.at[lax.rem(e, 2)], down_out.at[e], down_sems.at[lax.rem(e, 2)]
        )

    def down(e, _):
        @pl.when(e >= 2)
        def _():
            keep_down(e - 2).wait()

        at = pl.ds(pl.multiple_of(e * hidden, hidden), hidden)
        left = acts[:, :, at].reshape(tokens, hidden)

        def step(j, _):
            columns = pl.ds(pl.multiple_of(j * 512, 512), 512)
            stage_down[lax.rem(e, 2), :, columns] = transposed(
                left, rows[:, :, columns].reshape(tokens, 512)
            ).astype(bf16)
            return 0

        lax.fori_loop(0, width // 512, step, 0)
        keep_down(e).start()
        return 0

    lax.fori_loop(0, owned // 2, down, 0)
    out_sum.after_x(1)
    out_sum.after_x(0)
    lax.fori_loop(owned // 2, owned, down, 0)
    out_sum.after_z1(0)
    out_sum.end()
    links.close()
    for e in (owned - 2, owned - 1):
        keep_down(e).wait()
    for r in (0, ZLINE - 1):
        keep_grads(r).wait()


def moe(rows_y, normed, dy, plain, w_gate_up, w_down, router, spread):
    owned, width, _ = w_gate_up.shape
    hidden = F // ZLINE
    length = normed.shape[0]
    count = dy.shape[1]
    any_space = pl.BlockSpec(memory_space=pl.ANY)
    vmem = pl.BlockSpec(memory_space=pltpu.VMEM)
    sems = pltpu.SemaphoreType.DMA
    span = owned * hidden

    def reduced(wide):
        return [
            pltpu.VMEM((ZLINE, count, wide), bf16),
            pltpu.VMEM((ZLINE, count // 2, wide), bf16),
            pltpu.VMEM((ZLINE, length, wide), bf16),
            pltpu.VMEM((2, length, wide), bf16),
            pltpu.VMEM((length, wide), bf16),
        ]

    return pl.pallas_call(
        functools.partial(moe_kernel, rows_y),
        name="moe",
        out_shape=(
            jax.ShapeDtypeStruct((ZLINE, count, width), bf16),
            jax.ShapeDtypeStruct((ZLINE, count, 2 * span), bf16),
            jax.ShapeDtypeStruct((owned, hidden, width), bf16),
            jax.ShapeDtypeStruct((length, width + 128), f32),
            jax.ShapeDtypeStruct((length, width), f32),
        ),
        in_specs=[vmem, any_space, any_space, any_space, any_space, vmem, vmem],
        out_specs=(any_space, any_space, any_space, vmem, vmem),
        scratch_shapes=[
            pltpu.VMEM((width, span), bf16),
            pltpu.VMEM((width, span), bf16),
            pltpu.VMEM((owned, hidden, width), bf16),
            pltpu.VMEM((ZLINE, count, width), bf16),
            pltpu.VMEM((ZLINE, count, 128), bf16),
            pltpu.VMEM((2, count, span), bf16),
            pltpu.VMEM((2, count, 2 * span), bf16),
            pltpu.VMEM((ZLINE, count, span), bf16),
            pltpu.VMEM((count, 128), f32),
            pltpu.VMEM((2, hidden, width), bf16),
            *reduced(width + 128),
            *reduced(width),
            sems((MOE_COPIES,)),
            sems((MOE_COPIES,)),
            sems((2 * owned + 2,)),
            sems((2,)),
            sems((ZLINE,)),
            sems((ZLINE,)),
            sems((ZLINE,)),
            sems((2,)),
        ],
        compiler_params=pltpu.CompilerParams(
            collective_id=1, has_side_effects=True, vmem_limit_bytes=63 * 2**20
        ),
    )(normed, dy, plain, w_gate_up, w_down, router, spread)


def finish_kernel(
    rows_y,
    rows_hbm,
    grads_hbm,
    att_0,
    att_1,
    att_2,
    gate_up_out,
    out_0,
    out_1,
    out_2,
    wide,
    turned,
    grads,
    part_gate_up,
    heard_gate_up,
    heard_z,
    stage,
    *refs,
):
    owned, n = gate_up_out.shape[:2]
    hidden = F // ZLINE
    count, width = wide.shape[1:]
    tokens = ZLINE * count
    dp, ex = lax.axis_index("dp"), lax.axis_index("expert")
    z, y = dp // rows_y, dp % rows_y
    core, side = ex % 2, (ex // 2) % 2
    to = partners(rows_y)
    to["z3"] = (other(to["z1"][0], 2 * rows_y), ex)
    z_of = [z, other(z, 1), other(z, 2), other(other(z, 1), 2)]
    half, quarter = n // 2, n // 4
    of_core = pl.ds(pl.multiple_of(core * half, 16), half)
    of_sibling = pl.ds(pl.multiple_of((1 - core) * half, 16), half)
    of_side = pl.ds(pl.multiple_of(side * quarter, 16), quarter)
    of_far_side = pl.ds(pl.multiple_of((1 - side) * quarter, 16), quarter)
    mine = pl.ds(pl.multiple_of(core * half + side * quarter, 16), quarter)
    (
        load_sems,
        own_sems,
        grads_sems,
        store_sems,
        y_send,
        y_recv,
        z_send,
        z_recv,
        a_send,
        a_recv,
    ) = refs[18:]

    def remote(source, target, send_sem, recv_sem, device):
        return pltpu.make_async_remote_copy(
            src_ref=source,
            dst_ref=target,
            send_sem=send_sem,
            recv_sem=recv_sem,
            device_id=device,
            device_id_type=pl.DeviceIdType.MESH,
        )

    def add(left, right):
        return (left.astype(f32) + right.astype(f32)).astype(bf16)

    def load_wide(r):
        return pltpu.make_async_copy(rows_hbm.at[r], wide.at[r], load_sems.at[r])

    def load_grads(e, k):
        at = pl.ds(pl.multiple_of((k * owned + e) * hidden, hidden), hidden)
        return pltpu.make_async_copy(
            grads_hbm.at[:, :, at],
            grads.at[lax.rem(e, 2), :, :, pl.ds(k * hidden, hidden)],
            grads_sems.at[lax.rem(e, 2), k],
        )

    class Attention:
        def __init__(self, k, part, out, y_first):
            self.k, self.part, self.out, self.y_first = k, part, out, y_first
            self.own, self.c, self.x, self.z1, self.z2, self.y = refs[6 * k : 6 * k + 6]
            self.load = pltpu.make_async_copy(part.at[:, :, of_core], self.own, own_sems.at[k])

        def copy(self, step, source, target, device):
            return remote(
                source, target, a_send.at[self.k, step], a_recv.at[self.k, step], device
            )

        def to_c(self):
            return self.copy(0, self.part.at[:, :, of_sibling], self.c, to["c"])

        def to_x(self):
            return self.copy(1, self.own.at[:, :, of_far_side], self.x, to["x"])

        def line(self, m):
            if self.y_first:
                return self.own.at[z_of[m], pl.ds(y, 1), of_side]
            return self.own.at[z_of[m], :, of_side]

        def to_z1(self, m):
            return self.copy(2 + m, self.line(1 + 2 * m), self.z1.at[m], to["z1"])

        def to_z2(self):
            return self.copy(4, self.line(2), self.z2, to["z2"])

        def to_y(self):
            if self.y_first:
                source = self.own.at[:, 1 - y, of_side]
            else:
                source = self.own.at[z, 1 - y, of_side]
            return self.copy(5, source, self.y, to["y"])

        def back_x(self):
            return self.copy(6, self.out.at[mine], self.out.at[mine], to["x"])

        def back_c(self):
            return self.copy(7, self.out.at[of_core], self.out.at[of_core], to["c"])

        def after_c(self):
            self.load.wait()
            self.to_c().wait_recv()

            def step(b, _):
                for k in range(rows_y):
                    self.own[b, k] = add(self.own[b, k], self.c[b, k])
                return 0

            lax.fori_loop(0, ZLINE, step, 0)
            self.to_x().start()

        def after_x(self):
            self.to_x().wait_recv()

            def step(b, _):
                for k in range(rows_y):
                    self.own[b, k, of_side] = add(self.own[b, k, of_side], self.x[b, k])
                return 0

            lax.fori_loop(0, ZLINE, step, 0)
            if self.y_first:
                self.to_y().start()
            else:
                self.along_z()

        def along_z(self):
            for m in (1, 0):
                self.to_z1(m).start()

        def after_y(self):
            self.to_y().wait_recv()
            if self.y_first:
                for b in range(ZLINE):
                    self.own[b, y, of_side] = add(self.own[b, y, of_side], self.y[b])
                self.along_z()
            else:
                self.out[mine] = add(self.own[z, y, of_side], self.y[...])
                self.back_x().start()

        def after_z1(self):
            for m in (1, 0):
                self.to_z1(m).wait_recv()
                line = self.line(2 * m)
                line[...] = add(line[...], self.z1[m])
                if m:
                    self.to_z2().start()

        def after_z2(self):
            self.to_z2().wait_recv()
            line = self.line(0)
            if self.y_first:
                self.out[mine] = add(line[0], self.z2[0])
                self.back_x().start()
            else:
                line[...] = add(line[...], self.z2[...])
                self.to_y().start()

        def after_back(self):
            self.back_x().wait_recv()
            self.back_c().start()

        def close(self):
            self.back_c().wait()
            for made in (self.to_c(), self.to_x(), self.to_z1(0), self.to_z1(1)):
                made.wait_send()
            for made in (self.to_z2(), self.to_y(), self.back_x()):
                made.wait_send()

    output = Attention(0, att_0, out_0, False)
    small = Attention(1, att_1, out_1, False)
    qkv = Attention(2, att_2, out_2, True)
    for r in range(ZLINE):
        load_wide(r).start()
    for array in (output, small, qkv):
        array.load.start()
    for e in range(2):
        for k in range(2):
            load_grads(e, k).start()
    greet([to["z1"], to["z2"], to["z3"], to["y"], to["x"], to["c"]])
    for array in (output, small, qkv):
        array.to_c().start()

    for r in range(ZLINE):
        load_wide(r).wait()

        def turn(j, _, r=r):
            at = pl.ds(pl.multiple_of(j * 256, 256), 256)
            turned[at, pl.ds(r * count, count)] = wide[r, :, at].T
            return 0

        lax.fori_loop(0, width // 256, turn, 0)

    def send_y(e):
        return remote(
            part_gate_up.at[e, 1 - y], heard_gate_up.at[e], y_send.at[e], y_recv.at[e], to["y"]
        )

    def send_z(e, m):
        return remote(
            part_gate_up.at[e, y, z_of[m]],
            heard_z.at[m - 1, e],
            z_send.at[m - 1, e],
            z_recv.at[m - 1, e],
            to[f"z{m}"],
        )

    def reduce(e):
        send_y(e).wait_recv()
        for b in range(ZLINE):
            part_gate_up[e, y, b] = add(part_gate_up[e, y, b], heard_gate_up[e, b])
        for m in range(1, ZLINE):
            send_z(e, m).start()

    def gate_up(e, _):
        for k in range(2):
            load_grads(e, k).wait()
        right = grads[lax.rem(e, 2)].reshape(tokens, 2 * hidden)

        def step(b, _):
            at = pl.ds(pl.multiple_of(b * rows_y * n, 128), rows_y * n)
            result = jnp.dot(turned[at, :], right, preferred_element_type=f32).astype(bf16)
            for k in range(rows_y):
                part_gate_up[e, k, b] = result[k * n : (k + 1) * n]
            return 0

        lax.fori_loop(0, ZLINE, step, 0)

        @pl.when(e + 2 < owned)
        def _():
            for k in range(2):
                load_grads(e + 2, k).start()

        send_y(e).start()

        @pl.when(e >= 2)
        def _():
            reduce(e - 2)

        return 0

    lax.fori_loop(0, 1, gate_up, 0)
    output.after_c()
    small.after_c()
    lax.fori_loop(1, 2, gate_up, 0)
    qkv.after_c()
    lax.fori_loop(2, 5, gate_up, 0)
    output.after_x()
    small.after_x()
    lax.fori_loop(5, 7, gate_up, 0)
    output.after_z1()
    small.after_z1()
    lax.fori_loop(7, 9, gate_up, 0)
    qkv.after_x()
    lax.fori_loop(9, owned, gate_up, 0)
    output.after_z2()
    small.after_z2()
    reduce(owned - 2)
    reduce(owned - 1)

    def keep(e):
        return pltpu.make_async_copy(
            stage.at[lax.rem(e, 2)], gate_up_out.at[e], store_sems.at[lax.rem(e, 2)]
        )

    def collect(e, _):
        slot = lax.rem(e, 2)

        @pl.when(e >= 2)
        def _():
            keep(e - 2).wait()

        for m in range(ZLINE):
            if m:
                send_z(e, m).wait_recv()
                block = heard_z[m - 1, e]
            else:
                block = part_gate_up[e, y, z]
            for k in range(2):
                at = pl.ds(pl.multiple_of(k * F + z_of[m] * hidden, hidden), hidden)
                stage[slot, :, at] = block[:, k * hidden : (k + 1) * hidden]
        keep(e).start()
        return 0

    qkv.after_y()
    output.after_y()
    small.after_y()
    lax.fori_loop(0, owned - 2, collect, 0)
    qkv.after_z1()
    output.after_back()
    small.after_back()
    lax.fori_loop(owned - 2, owned, collect, 0)
    qkv.after_z2()
    qkv.after_back()

    for e in (owned - 2, owned - 1):
        keep(e).wait()

    def close(e, _):
        send_y(e).wait_send()
        for m in range(1, ZLINE):
            send_z(e, m).wait_send()
        return 0

    lax.fori_loop(0, owned, close, 0)
    for array in (output, small, qkv):
        array.close()


def finish(rows_y, rows, grads, parts):
    _, count, width = rows.shape
    hidden = F // ZLINE
    owned = grads.shape[2] // (2 * hidden)
    n = parts[0].shape[2]
    any_space = pl.BlockSpec(memory_space=pl.ANY)
    vmem = pl.BlockSpec(memory_space=pltpu.VMEM)
    sems = pltpu.SemaphoreType.DMA

    def reduced(columns, y_first):
        ends = 1 if y_first else rows_y
        heard_y = (ZLINE, n // 4, columns) if y_first else (n // 4, columns)
        return [
            pltpu.VMEM((ZLINE, rows_y, n // 2, columns), bf16),
            pltpu.VMEM((ZLINE, rows_y, n // 2, columns), bf16),
            pltpu.VMEM((ZLINE, rows_y, n // 4, columns), bf16),
            pltpu.VMEM((2, ends, n // 4, columns), bf16),
            pltpu.VMEM((ends, n // 4, columns), bf16),
            pltpu.VMEM(heard_y, bf16),
        ]

    return pl.pallas_call(
        functools.partial(finish_kernel, rows_y),
        name="finish",
        out_shape=(jax.ShapeDtypeStruct((owned, n, 2 * F), bf16),)
        + tuple(jax.ShapeDtypeStruct((n, v.shape[3]), bf16) for v in parts),
        in_specs=[any_space] * 5,
        out_specs=(any_space, vmem, vmem, vmem),
        scratch_shapes=[
            pltpu.VMEM((ZLINE, count, width), bf16),
            pltpu.VMEM((width, ZLINE * count), bf16),
            pltpu.VMEM((2, ZLINE, count, 2 * hidden), bf16),
            pltpu.VMEM((owned, rows_y, ZLINE, n, 2 * hidden), bf16),
            pltpu.VMEM((owned, ZLINE, n, 2 * hidden), bf16),
            pltpu.VMEM((ZLINE - 1, owned, n, 2 * hidden), bf16),
            pltpu.VMEM((2, n, 2 * F), bf16),
            *reduced(parts[0].shape[3], False),
            *reduced(parts[1].shape[3], False),
            *reduced(parts[2].shape[3], True),
            sems((ZLINE,)),
            sems((3,)),
            sems((2, 2)),
            sems((2,)),
            sems((owned,)),
            sems((owned,)),
            sems((ZLINE - 1, owned)),
            sems((ZLINE - 1, owned)),
            sems((3, 8)),
            sems((3, 8)),
        ],
        compiler_params=pltpu.CompilerParams(
            collective_id=3, has_side_effects=True, vmem_limit_bytes=63 * 2**20
        ),
    )(rows, grads, *parts)


def local(
    tokens,
    segments,
    routes,
    w_query,
    w_key,
    w_value,
    w_output,
    w_router,
    gain_attn,
    gain_moe,
    w_gate_up,
    w_down,
    cotangent,
):
    place = Place()
    length, width = tokens.shape
    owned = w_gate_up.shape[0]
    rows = w_query.shape[0]
    hidden = F // ZLINE
    per_group = H // KV
    q_end, k_end, v_end = H * HD, (H + KV) * HD, (H + 2 * KV) * HD
    o_end = v_end + width

    small = jnp.concatenate(
        [w_router, gain_attn[:, None], gain_moe[:, None], jnp.zeros((rows, 128 - EXPERTS - 2), bf16)],
        axis=1,
    )
    chosen_mask = jnp.any(
        routes[:, :, None] == jnp.arange(EXPERTS, dtype=jnp.int32), axis=1
    )
    dy_block = jnp.concatenate(
        [cotangent, chosen_mask.astype(bf16), jnp.zeros((length, 128 - EXPERTS), bf16)], axis=1
    )
    kernels = place.ex_size == 4 and place.rows_y == 2
    if kernels:
        qkv_shard = jnp.concatenate([w_query, w_key, w_value], axis=1)
        full_qkv, full_output, full_small, all_dy, plain_grads = gather(
            place.rows_y, (qkv_shard, w_output, small), dy_block, w_down
        )
        full_qkv = full_qkv.reshape(width, v_end)
        full_output = full_output.reshape(width, width)
        full_small = full_small.reshape(width, 128)

        def ordered(value):
            return value

        canonical = ordered
    else:
        shard = jnp.concatenate([w_query, w_key, w_value, w_output, small], axis=1)
        full, order = gather_weights(place, shard)
        full_qkv, full_output = full[:, :v_end], full[:, v_end:o_end]
        full_small = transposed(order, full[:, o_end:]).astype(bf16)
        dy_groups = gather_tokens(place, dy_block)

        def ordered(value):
            return against(value, order).astype(bf16)

        def canonical(value):
            return lax.dot_general(
                value,
                order.astype(value.dtype),
                (((1,), (0,)), ((), ())),
                precision=lax.Precision.HIGHEST,
                preferred_element_type=f32,
            ).astype(value.dtype)

    full_router = full_small[:, :EXPERTS]
    attn_gain = full_small[:, EXPERTS].astype(f32)
    moe_gain = full_small[:, EXPERTS + 1].astype(f32)

    cosine_table, sine_table = tables(length, HD)
    inputs = tokens.astype(f32)
    inv_attn = lax.rsqrt(jnp.mean(inputs * inputs, axis=-1, keepdims=True) + epsilon)
    unit_attn = inputs * inv_attn
    normed = (unit_attn * attn_gain).astype(bf16)
    normed = ordered(normed)
    qkv = dot(normed, full_qkv)
    queries = rotate(qkv[:, :q_end].reshape(length, H, HD), cosine_table, sine_table)
    queries = queries.astype(bf16).reshape(length, KV, per_group, HD)
    key_rows = rotate(
        qkv[:, q_end:k_end].reshape(length, KV, HD), cosine_table, sine_table
    ).astype(bf16)
    values = qkv[:, k_end:].astype(bf16).reshape(length, KV, HD)
    segment = segments[0]
    position = jnp.arange(length, dtype=jnp.int32)
    allowed = (segment[:, None] == segment[None, :]) & (position[:, None] >= position[None, :])
    scores = (
        jnp.einsum("qkgd,skd->kgqs", queries, key_rows, preferred_element_type=f32) * 0.125
    )
    scores = jnp.where(allowed, scores, -1e30)
    maximum = jnp.max(scores, axis=-1, keepdims=True)
    lifted_scores = jnp.exp(scores - maximum)
    full_weights = lifted_scores / jnp.sum(lifted_scores, axis=-1, keepdims=True)
    attn_weights = full_weights.astype(bf16)
    mixed = jnp.einsum("kgqs,skd->qkgd", attn_weights, values, preferred_element_type=f32)
    mixed = mixed.reshape(length, H * HD).astype(bf16)
    mixed = ordered(mixed)
    residual = inputs + dot(mixed, full_output)
    inv_moe = lax.rsqrt(jnp.mean(residual * residual, axis=-1, keepdims=True) + epsilon)
    unit_moe = residual * inv_moe
    normed_moe = (unit_moe * moe_gain).astype(bf16)

    def gates_of(rows_in, mask):
        logits = jnp.where(mask, dot(rows_in, full_router), -1e30)
        lifted = jnp.where(mask, jnp.exp(logits - jnp.max(logits, axis=-1, keepdims=True)), 0.0)
        return lifted / jnp.sum(lifted, axis=-1, keepdims=True)

    gates = gates_of(normed_moe, chosen_mask)

    def columns(start):
        cut = lax.dynamic_slice_in_dim(w_gate_up, start + place.z * hidden, hidden, 2)
        return cut.swapaxes(0, 1).reshape(width, owned * hidden)

    span = owned * hidden
    if kernels:
        wide_router = jnp.pad(full_router, ((0, 0), (0, 128 - EXPERTS)))
        lane = jnp.arange(128, dtype=jnp.int32)[:, None]
        column = jnp.arange(span, dtype=jnp.int32)[None, :]
        spread = (lane == place.ex * owned + column // hidden).astype(bf16)
        all_rows, all_grads, part_down, total, moe_output = moe(
            place.rows_y, normed_moe, all_dy, plain_grads, w_gate_up, w_down, wide_router, spread
        )
        row_grads, grad_gates = total[:, :width], total[:, width : width + EXPERTS]
    else:
        slice_down = lax.dynamic_slice_in_dim(w_down, place.z * hidden, hidden, 1)
        slice_down = slice_down.reshape(span, width)
        slice_gate_up = jnp.concatenate([columns(0), columns(F)], axis=1)
        moe_groups = gather_tokens(place, normed_moe)
        acts, grads_gate_up, gate_parts = [], [], []
        for normed_rows, dy_rows in zip(moe_groups, dy_groups):
            count = normed_rows.shape[0]
            group_gates = gates_of(normed_rows, dy_rows[:, width : width + EXPERTS] > 0.5)
            group_gates = lax.dynamic_slice_in_dim(group_gates, place.ex * owned, owned, 1)
            spread_gates = jnp.broadcast_to(group_gates[:, :, None], (count, owned, hidden))
            spread_gates = spread_gates.reshape(count, span)
            gate_up = dot(normed_rows, slice_gate_up)
            gate_part, up_part = gate_up[:, :span], gate_up[:, span:]
            plain_grad = against(dy_rows[:, :width], slice_down)
            sigmoid_gate = jax.nn.sigmoid(gate_part)
            swished = gate_part * sigmoid_gate
            activation = swished * up_part
            grad_act = plain_grad * spread_gates
            gate_parts.append(jnp.sum((plain_grad * activation).reshape(count, owned, hidden), axis=-1))
            acts.append((spread_gates * activation).astype(bf16))
            grads_gate_up.append(
                jnp.concatenate(
                    [
                        grad_act * up_part * sigmoid_gate * (1.0 + gate_part * (1.0 - sigmoid_gate)),
                        grad_act * swished,
                    ],
                    axis=-1,
                ).astype(bf16)
            )
        row_parts = [against(g, slice_gate_up).astype(bf16) for g in grads_gate_up]
        row_grads = scatter_tokens(place, row_parts, length)
        moe_output = scatter_tokens(place, [dot(a, slice_down).astype(bf16) for a in acts], length)
        gate_parts = [g.T for g in gate_parts]
        two = [gate_parts[i] + swap(gate_parts[i + 2], "dp", place.z_bits[1]) for i in range(2)]
        mine = two[0] + swap(two[1], "dp", place.z_bits[0])
        mine = mine.reshape(owned, 2, place.ex_size // 2, length)
        heard = [
            swap(mine[:, m % 2, m // 2], "expert", m) if m else mine[:, 0, 0]
            for m in range(place.ex_size)
        ]
        heard = jnp.stack(heard)
        grad_gates = jnp.concatenate(
            [pick(heard, place.ex ^ j) for j in range(place.ex_size)], axis=0
        ).T
        all_rows = jnp.concatenate([v for v in moe_groups], axis=0)
        all_dy = jnp.concatenate([v[:, :width] for v in dy_groups], axis=0)
        all_grads = jnp.concatenate(grads_gate_up, axis=0)
        all_acts = jnp.concatenate(acts, axis=0)
    output = (residual + moe_output).astype(bf16)
    grad_logits = (
        gates * (grad_gates - jnp.sum(gates * grad_gates, axis=-1, keepdims=True))
    ).astype(bf16)

    def reduce_y(part, axis):
        part = jnp.moveaxis(part, axis, 0)
        for mask in place.y_bits[::-1]:
            at = (place.y // mask) % 2
            half = part.reshape((2, part.shape[0] // 2) + part.shape[1:])
            away = swap(pick(half, 1 - at), "dp", mask)
            part = (pick(half, at).astype(f32) + away.astype(f32)).astype(bf16)
        return part[0]

    if kernels:
        part_down = part_down.reshape(owned, place.rows_y, hidden // place.rows_y, width)
        shard_down = reduce_y(part_down, 1).astype(f32)
    grad_out = cotangent.astype(f32)
    part_router = transposed(normed_moe, grad_logits)
    grad_normed_moe = row_grads + against(grad_logits, full_router)
    part_gain_moe = jnp.sum(grad_normed_moe * unit_moe, axis=0)
    scaled_moe = grad_normed_moe * moe_gain
    grad_residual = grad_out + inv_moe * (
        scaled_moe - unit_moe * jnp.mean(scaled_moe * unit_moe, axis=-1, keepdims=True)
    )
    grad_branch = grad_residual.astype(bf16)
    part_output = transposed(mixed, grad_branch)
    grad_mixed = canonical(against(grad_branch, full_output).astype(bf16))
    grad_mixed = grad_mixed.reshape(length, KV, per_group, HD)
    grad_weights = jnp.einsum(
        "qkgd,skd->kgqs", grad_mixed, values, preferred_element_type=f32
    )
    grad_values = jnp.einsum(
        "kgqs,qkgd->skd", attn_weights, grad_mixed, preferred_element_type=f32
    )
    grad_values = grad_values.astype(bf16).reshape(length, KV * HD)
    grad_scores = (
        full_weights * (grad_weights - jnp.sum(full_weights * grad_weights, axis=-1, keepdims=True))
    ).astype(bf16)
    grad_queries = (
        jnp.einsum("kgqs,skd->qkgd", grad_scores, key_rows, preferred_element_type=f32) * 0.125
    )
    grad_queries = rotate(grad_queries.reshape(length, H, HD), cosine_table, -sine_table)
    grad_queries = grad_queries.astype(bf16).reshape(length, H * HD)
    grad_keys = (
        jnp.einsum("kgqs,qkgd->skd", grad_scores, queries, preferred_element_type=f32) * 0.125
    )
    grad_keys = rotate(grad_keys, cosine_table, -sine_table)
    grad_keys = grad_keys.astype(bf16).reshape(length, KV * HD)
    grad_qkv = jnp.concatenate([grad_queries, grad_keys, grad_values], axis=1)
    part_qkv = transposed(normed, grad_qkv)
    grad_normed = canonical(against(grad_qkv, full_qkv))
    part_gain_attn = jnp.sum(grad_normed * unit_attn, axis=0)
    scaled_attn = grad_normed * attn_gain
    grad_tokens = (
        grad_residual
        + inv_attn
        * (scaled_attn - unit_attn * jnp.mean(scaled_attn * unit_attn, axis=-1, keepdims=True))
    ).astype(bf16)
    part_small = jnp.concatenate(
        [
            part_router.astype(bf16),
            part_gain_attn[:, None].astype(bf16),
            part_gain_moe[:, None].astype(bf16),
            jnp.zeros((width, 128 - EXPERTS - 2), bf16),
        ],
        axis=1,
    )
    if kernels:
        parts = tuple(
            v.astype(bf16).reshape(ZLINE, place.rows_y, rows, v.shape[1])
            for v in (part_output, part_small, part_qkv)
        )
        shard_gate_up, sum_output, sum_small, sum_qkv = finish(
            place.rows_y, all_rows, all_grads, parts
        )
        shard_gate_up = shard_gate_up.astype(f32)
        summed = (sum_qkv, sum_output, sum_small)
    else:
        part_small = dot(order, part_small).astype(bf16)
        summed = scatter_weights(
            place,
            jnp.concatenate([part_qkv.astype(bf16), part_output.astype(bf16), part_small], axis=1),
        )
        summed = summed[:, :v_end], summed[:, v_end:o_end], summed[:, o_end:]
        shard_down = transposed(all_acts, all_dy).astype(bf16)
        shard_down = shard_down.reshape(owned, place.rows_y, hidden // place.rows_y, width)
        shard_down = reduce_y(shard_down, 1).astype(f32)
        part_gate_up = transposed(all_rows, all_grads).astype(bf16)
        part_gate_up = part_gate_up.reshape(ZLINE, place.rows_y, rows, 2 * span)
        part_gate_up = reduce_y(part_gate_up, 1)
        heard = [pick(part_gate_up, place.z)] + [
            swap(pick(part_gate_up, place.z ^ m), "dp", m * place.rows_y) for m in range(1, ZLINE)
        ]
        heard = jnp.stack(heard)
        shard_gate_up = jnp.stack([pick(heard, place.z ^ j) for j in range(ZLINE)], axis=0)
        shard_gate_up = shard_gate_up.reshape(ZLINE, rows, 2, owned, hidden)
        shard_gate_up = shard_gate_up.transpose(3, 1, 2, 0, 4).reshape(owned, rows, 2 * F).astype(f32)
    sum_qkv, sum_output, sum_small = (v.astype(f32) for v in summed)
    return (
        output,
        grad_tokens,
        sum_qkv[:, :q_end],
        sum_qkv[:, q_end:k_end],
        sum_qkv[:, k_end:],
        sum_output,
        sum_small[:, :EXPERTS],
        sum_small[:, EXPERTS],
        sum_small[:, EXPERTS + 1],
        shard_gate_up,
        shard_down,
    )


def solution(mesh):
    return jax.shard_map(
        local,
        mesh=mesh,
        in_specs=(
            P(("dp", "expert"), None),
            P(("dp", "expert"), None),
            P(("dp", "expert"), None),
            P("dp", None),
            P("dp", None),
            P("dp", None),
            P("dp", None),
            P("dp", None),
            P("dp"),
            P("dp"),
            P("expert", None, None),
            P("expert", None, None),
            P(("dp", "expert"), None),
        ),
        out_specs=(
            P(("dp", "expert"), None),
            P(("dp", "expert"), None),
            P("dp", None),
            P("dp", None),
            P("dp", None),
            P("dp", None),
            P("dp", None),
            P("dp"),
            P("dp"),
            P("expert", "dp", None),
            P("expert", "dp", None),
        ),
        check_vma=False,
    )
```

```python
import functools

import jax
import jax.numpy as jnp
from jax import lax
from jax.experimental import pallas as pl
from jax.experimental.pallas import tpu as pltpu
from jax.sharding import PartitionSpec as P

H = 24
KV = 8
HD = 64
F = 512
EXPERTS = 40
ZLINE = 4


epsilon = 1e-05
f32 = jnp.float32
bf16 = jnp.bfloat16


def tables(length, size):
    half_size = size // 2
    frequency = jnp.power(10000.0, -2.0 * jnp.arange(half_size, dtype=f32) / size)
    angles = jnp.arange(length, dtype=f32)[:, None] * frequency[None, :]
    return (jnp.cos(angles)[:, None, :], jnp.sin(angles)[:, None, :])


def rotate(source, cosine_table, sine_table):
    half_size = source.shape[-1] // 2
    first_half = source[..., :half_size]
    second_half = source[..., half_size:]
    return jnp.concatenate(
        [
            first_half * cosine_table - second_half * sine_table,
            second_half * cosine_table + first_half * sine_table,
        ],
        axis=-1,
    )


def dot(left_side, right_side):
    return jnp.dot(left_side, right_side, preferred_element_type=f32)


def transposed(left_side, right_side):
    return lax.dot_general(
        left_side, right_side, (((0,), (0,)), ((), ())), preferred_element_type=f32
    )


def against(left_side, right_side):
    return lax.dot_general(
        left_side, right_side, (((1,), (1,)), ((), ())), preferred_element_type=f32
    )


def swap(value, axis, mask):
    size = lax.axis_size(axis)
    return lax.ppermute(value, axis, [(i, i ^ mask) for i in range(size)])


def pick(value, at):
    return lax.dynamic_index_in_dim(value, at, 0, keepdims=False)


def bits(first, size):
    masks, step = [], 1
    while step < size:
        masks.append(first * step)
        step *= 2
    return masks


class Place:
    def __init__(self):
        self.dp_size = lax.axis_size("dp")
        self.ex_size = lax.axis_size("expert")
        self.dp = lax.axis_index("dp")
        self.ex = lax.axis_index("expert")
        self.rows_y = self.dp_size // ZLINE
        self.z = self.dp // self.rows_y
        self.y = self.dp % self.rows_y
        self.z_bits = bits(self.rows_y, ZLINE)
        self.y_bits = bits(1, self.rows_y)
        self.x_bits = bits(2, self.ex_size // 2)


def gather_weights(place, shard):
    n, columns = shard.shape
    piece = n // 6
    cut = shard.reshape(3, 2, piece, columns)
    core = place.ex % 2
    side = (place.ex // 2) % 2
    own = pick(cut.swapaxes(0, 1), core)
    sibling = pick(cut.swapaxes(0, 1), 1 - core)

    def ordered(parts):
        return jnp.stack([pick(parts, 2 * side), parts[1], pick(parts, 2 - 2 * side)])

    own, sibling = ordered(own), ordered(sibling)
    blocks = {0: own[:2]}
    for mask in place.z_bits + place.y_bits:
        blocks.update({m ^ mask: swap(v, "dp", mask) for m, v in list(blocks.items())})
    rows = []
    for m in range(place.dp_size):
        if m == 0:
            rows.append(jnp.stack([own, sibling], axis=1))
            continue
        other = swap(blocks[m][0], "expert", 2)
        trio = jnp.concatenate([blocks[m], other[None]], axis=0)
        rows.append(jnp.stack([trio, swap(trio, "expert", 1)], axis=1))
    full = jnp.stack(rows)
    total = place.dp_size * n
    k = jnp.arange(total, dtype=jnp.int32)
    block, part = k // n, (k % n) // (2 * piece)
    half, line = (k % (2 * piece)) // piece, k % piece
    part = jnp.where(part == 1, 1, jnp.where(part == 0, 2 * side, 2 - 2 * side))
    at = (block ^ place.dp) * n + part * 2 * piece + (half ^ core) * piece + line
    order = (at[:, None] == jnp.arange(total, dtype=jnp.int32)[None, :]).astype(bf16)
    return full.reshape(total, columns), order


def scatter_weights(place, part):
    total, columns = part.shape
    n = total // place.dp_size
    piece = n // 6
    core = place.ex % 2
    side = (place.ex // 2) % 2

    def add(left, right):
        return (left.astype(f32) + right.astype(f32)).astype(bf16)

    part = part.reshape(place.dp_size, 3, 2, piece, columns)
    kept = add(part[:, :, 0], swap(part[:, :, 1], "expert", 1))
    first = add(kept[:, 0], swap(kept[:, 2], "expert", 2))
    blocks = {m: jnp.stack([first[m], kept[m, 1]]) for m in range(place.dp_size)}
    for mask in (place.z_bits + place.y_bits)[::-1]:
        blocks = {
            m: add(v, swap(blocks[m ^ mask], "dp", mask))
            for m, v in blocks.items()
            if m & mask == 0
        }
    mine = blocks[0]
    middle = add(mine[1], swap(mine[1], "expert", 2))
    trio = jnp.stack([mine[0], middle, swap(mine[0], "expert", 2)])
    for mask in place.x_bits[1:]:
        trio = add(trio, swap(trio, "expert", mask))
    both = jnp.stack([trio, swap(trio, "expert", 1)], axis=1)
    both = jnp.where(side == 0, both, both[::-1])
    both = jnp.where(core == 0, both, both[:, ::-1])
    return both.reshape(n, columns).astype(f32)


def gather_tokens(place, block):
    blocks = {0: block}
    for mask in place.z_bits:
        blocks.update({m ^ mask: swap(v, "dp", mask) for m, v in list(blocks.items())})
    groups = []
    for r in range(ZLINE):
        row = [blocks[r * place.rows_y]]
        for mask in place.x_bits:
            row = row + [swap(v, "expert", mask) for v in row]
        row = jnp.concatenate(row, axis=0)
        groups.append(jnp.concatenate([row, swap(row, "expert", 1)], axis=0))
    return groups


def scatter_tokens(place, groups, length):
    def add(left, right):
        return left.astype(f32) + right.astype(f32)

    reduced = []
    for part in groups:
        half = part.shape[0] // 2
        kept = add(part[:half], swap(part[half:], "expert", 1)).astype(bf16)
        for mask in place.x_bits[::-1]:
            half = kept.shape[0] // 2
            kept = add(kept[:half], swap(kept[half:], "expert", mask)).astype(bf16)
        reduced.append(kept)
    two = [add(reduced[i], swap(reduced[i + 2], "dp", place.z_bits[1])) for i in range(2)]
    return add(two[0], swap(two[1].astype(bf16), "dp", place.z_bits[0]))


def other(index, mask):
    return index + mask - 2 * mask * ((index // mask) % 2)


class Links:
    def __init__(self, sends, recvs):
        self.sends, self.recvs, self.used, self.open = sends, recvs, 0, []

    def copy(self, source, target, partner):
        at = self.used
        self.used += 1
        made = pltpu.make_async_remote_copy(
            src_ref=source,
            dst_ref=target,
            send_sem=self.sends.at[at],
            recv_sem=self.recvs.at[at],
            device_id=partner,
            device_id_type=pl.DeviceIdType.MESH,
        )
        made.start()
        self.open.append(made)
        return made

    def close(self):
        for made in self.open:
            made.wait_send()


def partners(rows_y):
    dp, ex = lax.axis_index("dp"), lax.axis_index("expert")
    return {
        "z1": (other(dp, rows_y), ex),
        "z2": (other(dp, 2 * rows_y), ex),
        "y": (other(dp, 1), ex),
        "x": (dp, other(ex, 2)),
        "c": (dp, other(ex, 1)),
    }


def greet(devices):
    barrier = pltpu.get_barrier_semaphore()
    for device in devices:
        pl.semaphore_signal(
            barrier, inc=1, device_id=device, device_id_type=pl.DeviceIdType.MESH
        )
    pl.semaphore_wait(barrier, len(devices))


def gather_kernel(rows_y, exclusive, *refs):
    shards, dy, down_hbm = refs[:3], refs[3], refs[4]
    fulls, dy_out, grads_out = refs[5:8], refs[8], refs[9]
    dy_all, w_down, grads = refs[10:13]
    z_send, z_recv, y_send, y_recv, x_send, x_recv, c_send, c_recv = refs[13:21]
    dz_send, dz_recv, dx_send, dx_recv, dc_send, dc_recv, local_sems, dy_sems, grads_sems = refs[21:]
    n = shards[0].shape[0]
    half = n // 2
    piece = half - exclusive
    length = dy.shape[0]
    dp, ex = lax.axis_index("dp"), lax.axis_index("expert")
    z, y = dp // rows_y, dp % rows_y
    core, side = ex % 2, (ex // 2) % 2
    to = partners(rows_y)
    z_of = [z, other(z, 1), other(z, 2), other(other(z, 1), 2)]

    in_plane = pl.ds(pl.multiple_of(core * half + side * exclusive, 16), piece)
    alone = pl.ds(pl.multiple_of(core * half + side * piece, 16), exclusive)
    of_core = pl.ds(pl.multiple_of(core * half, 16), half)

    def remote(source, target, send_sem, recv_sem, device):
        return pltpu.make_async_remote_copy(
            src_ref=source,
            dst_ref=target,
            send_sem=send_sem,
            recv_sem=recv_sem,
            device_id=device,
            device_id_type=pl.DeviceIdType.MESH,
        )

    def copies(rows, m, ys, send, recv, at, device, own=False):
        made = []
        for k in range(3):
            block = fulls[k].at[z_of[m] * rows_y + ys, rows]
            source = shards[k].at[rows] if own else block
            made.append(remote(source, block, send.at[k, at], recv.at[k, at], device))
        return made

    def to_z(step):
        m, device = ((0, "z1"), (0, "z2"), (2, "z1"))[step]
        return copies(in_plane, m, y, z_send, z_recv, step, to[device], m == 0)

    def to_y(m):
        return copies(in_plane, m, y, y_send, y_recv, m, to["y"], m == 0)

    def to_x(m, k):
        ys = 1 - y if k else y
        return copies(alone, m, ys, x_send, x_recv, 2 * m + k, to["x"])

    def to_c(m, k):
        ys = 1 - y if k else y
        return copies(of_core, m, ys, c_send, c_recv, 2 * m + k, to["c"])

    near, pair = pl.ds(0, length), pl.ds(length, length)
    front, back = pl.ds(0, 2 * length), pl.ds(2 * length, 2 * length)

    def dy_z(step):
        m, target, device = ((0, 1, "z1"), (0, 2, "z2"), (2, 3, "z1"))[step]
        source = dy_all.at[m, near] if m else dy
        return remote(
            source, dy_all.at[target, near], dz_send.at[step], dz_recv.at[step], to[device]
        )

    def dy_x(m):
        source = dy_all.at[m, near] if m else dy
        return remote(source, dy_all.at[m, pair], dx_send.at[m], dx_recv.at[m], to["x"])

    def dy_c(m):
        return remote(
            dy_all.at[m, front], dy_all.at[m, back], dc_send.at[m], dc_recv.at[m], to["c"]
        )

    owned, hidden, width = w_down.shape
    mine = [
        pltpu.make_async_copy(shards[k], fulls[k].at[dp], local_sems.at[k]) for k in range(3)
    ]
    at = pl.ds(pl.multiple_of(z * hidden, hidden), hidden)
    mine.append(pltpu.make_async_copy(down_hbm.at[:, at, :], w_down, local_sems.at[3]))
    for made in mine:
        made.start()
    dy_all[0, near] = dy[...]
    greet([to["z1"], to["z2"], to["y"], to["x"], to["c"]])

    def start(made):
        for copy in made:
            copy.start()

    def keep_dy(m):
        return pltpu.make_async_copy(dy_all.at[m], dy_out.at[m], dy_sems.at[m])

    def keep_grads(m):
        return pltpu.make_async_copy(grads.at[m % 2], grads_out.at[m], grads_sems.at[m % 2])

    def group(m):
        dy_c(m).wait_recv()
        keep_dy(m).start()
        if m >= 2:
            keep_grads(m - 2).wait()

        def step(p, _):
            at = pl.ds(pl.multiple_of(p * 2 * hidden, 2 * hidden), 2 * hidden)
            down = w_down[pl.ds(2 * p, 2)].reshape(2 * hidden, width)
            grads[m % 2, :, at] = against(dy_all[m, :, :width], down).astype(bf16)
            return 0

        lax.fori_loop(0, owned // 2, step, 0)
        keep_grads(m).start()

    def arrived(made):
        for copy in made:
            copy.wait_recv()

    start(to_z(1))
    start(to_z(0))
    start(to_y(0))
    dy_x(0).start()
    dy_z(1).start()
    dy_z(0).start()

    arrived(to_z(0))
    start(to_y(1))
    start(to_x(1, 0))
    arrived(to_z(1))
    start(to_z(2))
    start(to_y(2))
    start(to_x(2, 0))
    dy_z(0).wait_recv()
    dy_x(1).start()
    dy_z(1).wait_recv()
    dy_z(2).start()
    dy_x(2).start()
    arrived(to_y(0))
    start(to_x(0, 1))
    dy_x(0).wait_recv()
    dy_c(0).start()
    arrived(to_z(2))
    start(to_y(3))
    start(to_x(3, 0))
    arrived(to_y(1))
    start(to_x(1, 1))
    dy_x(1).wait_recv()
    dy_c(1).start()
    dy_z(2).wait_recv()
    dy_x(3).start()
    mine[3].wait()
    group(0)
    group(1)
    for m in (1, 2):
        arrived(to_x(m, 0))
        start(to_c(m, 0))
    arrived(to_x(0, 1))
    start(to_c(0, 1))
    arrived(to_y(2))
    start(to_x(2, 1))
    dy_x(2).wait_recv()
    dy_c(2).start()
    arrived(to_x(1, 1))
    start(to_c(1, 1))
    group(2)
    arrived(to_y(3))
    start(to_x(3, 1))
    dy_x(3).wait_recv()
    dy_c(3).start()
    for m, k in ((3, 0), (2, 1), (3, 1)):
        arrived(to_x(m, k))
        start(to_c(m, k))
    group(3)

    for made in mine[:3]:
        made.wait()
    for m in range(ZLINE):
        keep_dy(m).wait()
        if m >= 2:
            keep_grads(m).wait()
    for step in range(3):
        for made in to_z(step):
            made.wait_send()
        dy_z(step).wait_send()
    for m in range(ZLINE):
        for made in to_y(m):
            made.wait_send()
        dy_x(m).wait_send()
        dy_c(m).wait_send()
        for k in range(2):
            if m or k:
                for made in to_x(m, k):
                    made.wait_send()
                for made in to_c(m, k):
                    made.wait()


def gather(rows_y, shards, dy, w_down):
    exclusive = shards[0].shape[0] // 12
    dp_size = ZLINE * rows_y
    owned, _, width = w_down.shape
    hidden = F // ZLINE
    count = 4 * dy.shape[0]
    any_space = pl.BlockSpec(memory_space=pl.ANY)
    vmem = pl.BlockSpec(memory_space=pltpu.VMEM)
    sems = pltpu.SemaphoreType.DMA
    return pl.pallas_call(
        functools.partial(gather_kernel, rows_y, exclusive),
        name="gather",
        out_shape=tuple(jax.ShapeDtypeStruct((dp_size,) + v.shape, bf16) for v in shards)
        + (
            jax.ShapeDtypeStruct((ZLINE, count, dy.shape[1]), bf16),
            jax.ShapeDtypeStruct((ZLINE, count, owned * hidden), bf16),
        ),
        in_specs=[vmem] * 4 + [any_space],
        out_specs=(any_space,) * 5,
        scratch_shapes=[
            pltpu.VMEM((ZLINE, count, dy.shape[1]), bf16),
            pltpu.VMEM((owned, hidden, width), bf16),
            pltpu.VMEM((2, count, owned * hidden), bf16),
            sems((3, 3)),
            sems((3, 3)),
            sems((3, ZLINE)),
            sems((3, ZLINE)),
            sems((3, dp_size)),
            sems((3, dp_size)),
            sems((3, dp_size)),
            sems((3, dp_size)),
            sems((3,)),
            sems((3,)),
            sems((ZLINE,)),
            sems((ZLINE,)),
            sems((ZLINE,)),
            sems((ZLINE,)),
            sems((4,)),
            sems((ZLINE,)),
            sems((2,)),
        ],
        compiler_params=pltpu.CompilerParams(
            collective_id=2, has_side_effects=True, vmem_limit_bytes=60 * 2**20
        ),
    )(*shards, dy, w_down)


MOE_COPIES = 30


def moe_kernel(
    rows_y,
    normed_ref,
    dy_hbm,
    plain_hbm,
    gate_up_hbm,
    down_hbm,
    router_ref,
    spread_ref,
    rows_out,
    grads_out,
    down_out,
    combined_out,
    heard_out,
    total_ref,
    w_gate,
    w_up,
    w_down,
    rows,
    masks,
    plain,
    grads,
    acts,
    gate_grads,
    part_down,
    heard_down,
    stage_down,
    parts,
    heard_c,
    heard_x,
    heard_z,
    combined,
    heard_combined,
    sends,
    recvs,
    d_send,
    d_recv,
    load_sems,
    plain_sems,
    dy_sems,
    rows_sems,
    grads_sems,
    down_sems,
    combined_sems,
):
    owned, hidden = w_down.shape[:2]
    length, width = normed_ref.shape
    count = rows.shape[1]
    tokens = ZLINE * count
    half = count // 2
    span = owned * hidden
    dp = lax.axis_index("dp")
    z, y = dp // rows_y, dp % rows_y
    to = partners(rows_y)
    to["z3"] = (other(to["z1"][0], 2 * rows_y), lax.axis_index("expert"))
    links = Links(sends, recvs)

    loads = []
    mine = pl.ds(pl.multiple_of(z * hidden, hidden), hidden)
    theirs = pl.ds(pl.multiple_of(F + z * hidden, hidden), hidden)
    for e in range(owned):
        at = pl.ds(e * hidden, hidden)
        for k, (cut, kept) in enumerate(((mine, w_gate), (theirs, w_up))):
            loads.append(
                pltpu.make_async_copy(
                    gate_up_hbm.at[e, :, cut], kept.at[:, at], load_sems.at[2 * e + k]
                )
            )
    loads.append(
        pltpu.make_async_copy(dy_hbm.at[:, :, pl.ds(width, 128)], masks, load_sems.at[2 * owned])
    )
    load_down = pltpu.make_async_copy(
        down_hbm.at[:, mine, :], w_down, load_sems.at[2 * owned + 1]
    )
    for load in loads:
        load.start()

    def fetch(r):
        return pltpu.make_async_copy(plain_hbm.at[r], plain.at[r % 2], plain_sems.at[r % 2])

    fetch(0).start()
    fetch(1).start()
    load_down.start()
    rows[0, :length] = normed_ref[...]
    greet([to[name] for name in ("z1", "z2", "z3", "y", "x", "c")])

    own = pl.ds(0, length)
    pair = pl.ds(length, length)
    near, far = pl.ds(0, half), pl.ds(half, half)

    def row_x(r):
        return links.copy(rows.at[r, own], rows.at[r, pair], to["x"])

    def row_c(r):
        return links.copy(rows.at[r, near], rows.at[r, far], to["c"])

    z1 = links.copy(rows.at[0, own], rows.at[1, own], to["z1"])
    z2 = links.copy(rows.at[0, own], rows.at[2, own], to["z2"])
    x0 = row_x(0)
    for load in loads:
        load.wait()
    x0.wait_recv()
    c0 = row_c(0)
    c0.wait_recv()

    def keep_rows(r):
        return pltpu.make_async_copy(rows.at[r], rows_out.at[r], rows_sems.at[r])

    def keep_grads(r):
        return pltpu.make_async_copy(grads.at[min(r, 1)], grads_out.at[r], grads_sems.at[r])

    def forward(r):
        slot, held = r % 2, min(r, 1)
        keep_rows(r).start()
        fetch(r).wait()
        if r >= 2:
            keep_grads(r - 1).wait()
        logits = jnp.dot(rows[r], router_ref[...], preferred_element_type=f32)
        mask = masks[r].astype(f32) > 0.5
        logits = jnp.where(mask, logits, -1e30)
        lifted = jnp.where(
            mask, jnp.exp(logits - jnp.max(logits, axis=-1, keepdims=True)), 0.0
        )
        gates = lifted / jnp.sum(lifted, axis=-1, keepdims=True)
        gates_high = gates.astype(bf16)
        gates_low = (gates - gates_high.astype(f32)).astype(bf16)
        gate_grads[...] = jnp.zeros_like(gate_grads)

        def step(p, _):
            at = pl.ds(pl.multiple_of(p * 2 * hidden, 2 * hidden), 2 * hidden)
            up_at = pl.ds(pl.multiple_of(span + p * 2 * hidden, 2 * hidden), 2 * hidden)
            spread = spread_ref[:, at]
            gate_part = jnp.dot(rows[r], w_gate[:, at], preferred_element_type=f32)
            up_part = jnp.dot(rows[r], w_up[:, at], preferred_element_type=f32)
            plain_grad = plain[slot, :, at].astype(f32)
            spread_gates = jnp.dot(gates_high, spread, preferred_element_type=f32) + jnp.dot(
                gates_low, spread, preferred_element_type=f32
            )
            sigmoid_gate = 1.0 / (1.0 + jnp.exp(-gate_part))
            swished = gate_part * sigmoid_gate
            activation = swished * up_part
            gate_grads[...] += against((plain_grad * activation).astype(bf16), spread)
            acts[r, :, at] = (spread_gates * activation).astype(bf16)
            grad_act = plain_grad * spread_gates
            grads[held, :, at] = (
                grad_act * up_part * (sigmoid_gate + swished * (1.0 - sigmoid_gate))
            ).astype(bf16)
            grads[held, :, up_at] = (grad_act * swished).astype(bf16)
            return 0

        lax.fori_loop(0, owned // 2, step, 0, unroll=True)
        parts[r, :, width:] = gate_grads[...].astype(bf16)
        if r + 2 < ZLINE:
            fetch(r + 2).start()
        keep_grads(r).start()

    def backward(r):
        held = min(r, 1)

        def step(j, _):
            at = pl.ds(pl.multiple_of(j * 768, 768), 768)
            part = against(grads[held, :, :span], w_gate[at, :]) + against(
                grads[held, :, span:], w_up[at, :]
            )
            parts[r, :, at] = part.astype(bf16)
            return 0

        lax.fori_loop(0, width // 768, step, 0)

    def add(left, right):
        return (left[...].astype(f32) + right[...].astype(f32)).astype(bf16)

    made = {}

    def sum_c(r):
        made["c", r] = links.copy(parts.at[r, far], heard_c.at[r], to["c"])

    def sum_x(r):
        made["c", r].wait_recv()
        parts[r, near] = add(parts.at[r, near], heard_c.at[r])
        made["x", r] = links.copy(parts.at[r, pair], heard_x.at[r], to["x"])

    def sum_z(r):
        made["x", r].wait_recv()
        parts[r, own] = add(parts.at[r, own], heard_x.at[r])
        if r:
            made["z", r] = links.copy(parts.at[r, own], heard_z.at[r - 1], to[f"z{r}"])

    def keep_combined(r):
        return pltpu.make_async_copy(
            combined.at[r % 2, near], combined_out.at[r], combined_sems.at[r]
        )

    def combine(r):
        slot = r % 2
        if r >= 2:
            made["oc", r - 2].wait_send()
            keep_combined(r - 2).wait()
            out_x(r - 2)

        def step(j, _):
            at = pl.ds(pl.multiple_of(j * 512, 512), 512)
            down = w_down[:, :, at].reshape(span, 512)
            combined[slot, :, at] = jnp.dot(
                acts[r], down, preferred_element_type=f32
            ).astype(bf16)
            return 0

        lax.fori_loop(0, width // 512, step, 0)
        made["oc", r] = links.copy(combined.at[slot, far], heard_combined.at[r], to["c"])

    def out_c(r):
        made["oc", r].wait_recv()
        combined[r % 2, near] = add(combined.at[r % 2, near], heard_combined.at[r])
        keep_combined(r).start()

    def out_x(r):
        made["ox", r] = links.copy(combined_out.at[r, pair], heard_out.at[r], to["x"])

    def fetch_dy(r):
        return pltpu.make_async_copy(
            dy_hbm.at[r, :, pl.ds(0, width)], rows.at[r], dy_sems.at[r]
        )

    def send_down(e):
        return pltpu.make_async_remote_copy(
            src_ref=part_down.at[e, 1 - y],
            dst_ref=heard_down.at[e],
            send_sem=d_send.at[e],
            recv_sem=d_recv.at[e],
            device_id=to["y"],
            device_id_type=pl.DeviceIdType.MESH,
        )

    def down(p, _):
        at = pl.ds(pl.multiple_of(p * 2 * hidden, 2 * hidden), 2 * hidden)
        left = acts[:, :, at].reshape(tokens, 2 * hidden)

        def step(j, _):
            columns = pl.ds(pl.multiple_of(j * 768, 768), 768)
            result = transposed(left, rows[:, :, columns].reshape(tokens, 768)).astype(bf16)
            for k in range(2):
                for i in range(rows_y):
                    first = k * hidden + i * (hidden // rows_y)
                    part_down[2 * p + k, i, :, columns] = result[
                        first : first + hidden // rows_y
                    ]
            return 0

        lax.fori_loop(0, width // 768, step, 0)
        for k in range(2):
            send_down(2 * p + k).start()
        return 0

    def keep_down(e):
        return pltpu.make_async_copy(
            stage_down.at[lax.rem(e, 2)], down_out.at[e], down_sems.at[lax.rem(e, 2)]
        )

    def finish_down(e, _):
        @pl.when(e >= 2)
        def _():
            keep_down(e - 2).wait()

        send_down(e).wait_recv()
        stage_down[lax.rem(e, 2)] = add(part_down.at[e, y], heard_down.at[e])
        keep_down(e).start()
        return 0

    forward(0)
    z1.wait_recv()
    x1 = row_x(1)
    z2.wait_recv()
    z3 = links.copy(rows.at[2, own], rows.at[3, own], to["z1"])
    x2 = row_x(2)
    load_down.wait()
    combine(0)
    x1.wait_recv()
    c1 = row_c(1)
    c1.wait_recv()
    forward(1)
    z3.wait_recv()
    x3 = row_x(3)
    backward(1)
    sum_c(1)
    x2.wait_recv()
    c2 = row_c(2)
    out_c(0)
    sum_x(1)
    c2.wait_recv()
    forward(2)
    backward(2)
    sum_c(2)
    sum_z(1)
    x3.wait_recv()
    c3 = row_c(3)
    sum_x(2)
    c3.wait_recv()
    forward(3)
    backward(3)
    sum_c(3)
    backward(0)
    sum_x(3)
    sum_c(0)
    sum_z(2)
    for r in range(ZLINE):
        keep_rows(r).wait()
    gathered = (z1, z2, z3, x0, x1, x2, x3, c0, c1, c2, c3)
    for copy in gathered:
        copy.wait_send()
    for r in range(ZLINE):
        fetch_dy(r).start()
    sum_x(0)
    combine(1)
    for r in range(ZLINE):
        fetch_dy(r).wait()
    lax.fori_loop(0, 1, down, 0)
    sum_z(3)
    out_c(1)
    lax.fori_loop(1, 2, down, 0)
    combine(2)
    lax.fori_loop(2, 3, down, 0)
    sum_z(0)
    out_c(2)
    combine(3)
    lax.fori_loop(3, owned // 2, down, 0)
    out_c(3)
    total = parts[0, own].astype(f32)
    for r in (1, 2, 3):
        made["z", r].wait_recv()
        total = total + heard_z[r - 1].astype(f32)
    total_ref[...] = total
    for r in (2, 3):
        keep_combined(r).wait()
        out_x(r)
    lax.fori_loop(0, owned, finish_down, 0)
    for r in range(ZLINE):
        made["ox", r].wait_recv()
    done = gathered + (made["oc", 0], made["oc", 1])
    links.open = [v for v in links.open if not any(v is copy for copy in done)]
    links.close()
    for e in range(owned):
        send_down(e).wait_send()
    for e in (owned - 2, owned - 1):
        keep_down(e).wait()
    for r in (0, ZLINE - 1):
        keep_grads(r).wait()


def moe(rows_y, normed, dy, plain, w_gate_up, w_down, router, spread):
    owned, width, _ = w_gate_up.shape
    hidden = F // ZLINE
    length = normed.shape[0]
    count = dy.shape[1]
    any_space = pl.BlockSpec(memory_space=pl.ANY)
    vmem = pl.BlockSpec(memory_space=pltpu.VMEM)
    sems = pltpu.SemaphoreType.DMA
    span = owned * hidden
    wide = width + 128
    return pl.pallas_call(
        functools.partial(moe_kernel, rows_y),
        name="moe",
        out_shape=(
            jax.ShapeDtypeStruct((ZLINE, count, width), bf16),
            jax.ShapeDtypeStruct((ZLINE, count, 2 * span), bf16),
            jax.ShapeDtypeStruct((owned, hidden // rows_y, width), bf16),
            jax.ShapeDtypeStruct((ZLINE, count // 2, width), bf16),
            jax.ShapeDtypeStruct((ZLINE, length, width), bf16),
            jax.ShapeDtypeStruct((length, wide), f32),
        ),
        in_specs=[vmem, any_space, any_space, any_space, any_space, vmem, vmem],
        out_specs=(any_space,) * 5 + (vmem,),
        scratch_shapes=[
            pltpu.VMEM((width, span), bf16),
            pltpu.VMEM((width, span), bf16),
            pltpu.VMEM((owned, hidden, width), bf16),
            pltpu.VMEM((ZLINE, count, width), bf16),
            pltpu.VMEM((ZLINE, count, 128), bf16),
            pltpu.VMEM((2, count, span), bf16),
            pltpu.VMEM((2, count, 2 * span), bf16),
            pltpu.VMEM((ZLINE, count, span), bf16),
            pltpu.VMEM((count, 128), f32),
            pltpu.VMEM((owned, rows_y, hidden // rows_y, width), bf16),
            pltpu.VMEM((owned, hidden // rows_y, width), bf16),
            pltpu.VMEM((2, hidden // rows_y, width), bf16),
            pltpu.VMEM((ZLINE, count, wide), bf16),
            pltpu.VMEM((ZLINE, count // 2, wide), bf16),
            pltpu.VMEM((ZLINE, length, wide), bf16),
            pltpu.VMEM((ZLINE - 1, length, wide), bf16),
            pltpu.VMEM((2, count, width), bf16),
            pltpu.VMEM((ZLINE, count // 2, width), bf16),
            sems((MOE_COPIES,)),
            sems((MOE_COPIES,)),
            sems((owned,)),
            sems((owned,)),
            sems((2 * owned + 2,)),
            sems((2,)),
            sems((ZLINE,)),
            sems((ZLINE,)),
            sems((ZLINE,)),
            sems((2,)),
            sems((ZLINE,)),
        ],
        compiler_params=pltpu.CompilerParams(
            collective_id=1, has_side_effects=True, vmem_limit_bytes=63 * 2**20
        ),
    )(normed, dy, plain, w_gate_up, w_down, router, spread)


GROUP = 2


def finish_kernel(
    rows_y,
    rows_hbm,
    grads_hbm,
    combined_hbm,
    heard_hbm,
    w_output_hbm,
    w_qkv_hbm,
    residual,
    grad_residual,
    grad_branch,
    tokens_ref,
    gain,
    mixed,
    normed,
    queries,
    keys,
    values,
    allowed,
    cosine,
    sine,
    base_small,
    gate_up_out,
    output_out,
    grad_tokens_out,
    out_0,
    out_1,
    out_2,
    rows,
    turned,
    grads,
    part_gate_up,
    heard_gate_up,
    heard_z,
    stage,
    o_own,
    o_x,
    o_z1,
    o_z2,
    w_output,
    w_qkv,
    grad_qkv,
    grad_normed,
    left_output,
    left_qkv,
    right_output,
    right_qkv,
    part_small,
    *refs,
):
    owned, n = gate_up_out.shape[:2]
    hidden = F // ZLINE
    count, width = rows.shape
    length = grad_branch.shape[0]
    tokens = ZLINE * count
    dp, ex = lax.axis_index("dp"), lax.axis_index("expert")
    z, y = dp // rows_y, dp % rows_y
    core, side = ex % 2, (ex // 2) % 2
    to = partners(rows_y)
    to["z3"] = (other(to["z1"][0], 2 * rows_y), ex)
    to["xc"] = (dp, other(other(ex, 1), 2))
    z_of = [z, other(z, 1), other(z, 2), other(other(z, 1), 2)]
    half, quarter = n // 2, n // 4
    of_core = pl.ds(pl.multiple_of(core * half, 16), half)
    of_sibling = pl.ds(pl.multiple_of((1 - core) * half, 16), half)
    of_side = pl.ds(pl.multiple_of(side * quarter, 16), quarter)
    of_far_side = pl.ds(pl.multiple_of((1 - side) * quarter, 16), quarter)
    mine = pl.ds(pl.multiple_of(core * half + side * quarter, 16), quarter)
    (
        load_sem,
        own_sems,
        weight_sems,
        grads_sems,
        store_sems,
        y_send,
        y_recv,
        z_send,
        z_recv,
        a_send,
        a_recv,
        f_send,
        f_recv,
        o_send,
        o_recv,
    ) = refs[18:]

    def remote(source, target, send_sem, recv_sem, device):
        return pltpu.make_async_remote_copy(
            src_ref=source,
            dst_ref=target,
            send_sem=send_sem,
            recv_sem=recv_sem,
            device_id=device,
            device_id_type=pl.DeviceIdType.MESH,
        )

    def add(left, right):
        return (left.astype(f32) + right.astype(f32)).astype(bf16)

    def load_rows(r):
        return pltpu.make_async_copy(rows_hbm.at[r], rows, load_sem)

    def load_grads(e, k):
        at = pl.ds(pl.multiple_of((k * owned + e) * hidden, hidden), hidden)
        return pltpu.make_async_copy(
            grads_hbm.at[:, :, at],
            grads.at[lax.rem(e, 2), :, :, pl.ds(k * hidden, hidden)],
            grads_sems.at[lax.rem(e, 2), k],
        )

    load_combined = [
        pltpu.make_async_copy(combined_hbm.at[:, pl.ds(0, length)], o_own, own_sems.at[0]),
        pltpu.make_async_copy(heard_hbm, o_x, own_sems.at[1]),
    ]

    def o_copy(k):
        if k < 2:
            return remote(o_own.at[1 + 2 * k], o_z1.at[k], o_send.at[k], o_recv.at[k], to["z1"])
        return remote(o_own.at[2], o_z2, o_send.at[k], o_recv.at[k], to["z2"])

    def o_start():
        for load in load_combined:
            load.wait()
        for r in (3, 1, 2, 0):
            o_own[r] = add(o_own[r], o_x[r])
            if r % 2:
                o_copy(r // 2).start()

    def o_after_z1():
        for k in (1, 0):
            o_copy(k).wait_recv()
            o_own[2 * k] = add(o_own[2 * k], o_z1[k])
            if k:
                o_copy(2).start()

    def o_end():
        o_copy(2).wait_recv()
        total = o_own[0].astype(f32) + o_z2[...].astype(f32)
        output_out[...] = (residual[...] + total).astype(bf16)

    def left_copies(k, source, target):
        made = []
        for m, name in ((1, "c"), (2, "x"), (3, "xc")):
            c = 1 - core if m % 2 else core
            s = 1 - side if m // 2 else side
            made.append(
                remote(
                    source.at[:, c, s],
                    target.at[:, :, pl.ds(m * length, length)],
                    f_send.at[k, m],
                    f_recv.at[k, m],
                    to[name],
                )
            )
        return made

    def right_copy(k, source, target, m):
        if m == 3:
            source = target.at[pl.ds(2 * length, length)]
        return remote(
            source,
            target.at[pl.ds(m * length, length)],
            f_send.at[k, m],
            f_recv.at[k, m],
            to["x" if m == 2 else "c"],
        )

    class Sum:
        def __init__(self, k, out, rows):
            self.k, self.out, self.rows = k, out, rows
            self.own, self.c, self.x, self.y, self.z1, self.z2 = refs[6 * k : 6 * k + 6]

        def copy(self, step, source, target, device):
            return remote(
                source, target, a_send.at[self.k, step], a_recv.at[self.k, step], device
            )

        def to_y(self, b):
            return self.copy(8 + b, self.own.at[b, 1 - y, self.rows], self.y.at[b], to["y"])

        def to_z1(self, m):
            return self.copy(
                1 + m, self.own.at[z_of[1 + 2 * m], y, self.rows], self.z1.at[m], to["z1"]
            )

        def to_z2(self):
            return self.copy(3, self.own.at[z_of[2], y, self.rows], self.z2, to["z2"])

        def back_x(self):
            return self.copy(4, self.out.at[mine], self.out.at[mine], to["x"])

        def back_c(self):
            return self.copy(5, self.out.at[of_core], self.out.at[of_core], to["c"])

        def to_c(self):
            return self.copy(6, part_small.at[:, :, of_sibling], self.c, to["c"])

        def to_x(self):
            return self.copy(7, self.own.at[:, :, of_far_side], self.x, to["x"])

        def after_c(self):
            self.to_c().wait_recv()
            for b in range(ZLINE):
                for k in range(rows_y):
                    self.own[b, k] = add(part_small[b, k, of_core], self.c[b, k])
            self.to_x().start()

        def after_x(self):
            self.to_x().wait_recv()
            for b in range(ZLINE):
                for k in range(rows_y):
                    self.own[b, k, self.rows] = add(self.own[b, k, self.rows], self.x[b, k])
            self.along_y()

        def along_y(self):
            for b in range(ZLINE):
                self.to_y(b).start()

        def after_y(self):
            for b in range(ZLINE):
                self.to_y(b).wait_recv()
                self.own[b, y, self.rows] = add(self.own[b, y, self.rows], self.y[b])
            for m in (1, 0):
                self.to_z1(m).start()

        def after_z1(self):
            for m in (1, 0):
                self.to_z1(m).wait_recv()
                at = z_of[2 * m]
                self.own[at, y, self.rows] = add(self.own[at, y, self.rows], self.z1[m])
                if m:
                    self.to_z2().start()

        def after_z2(self):
            self.to_z2().wait_recv()
            self.out[mine] = add(self.own[z, y, self.rows], self.z2[...])
            self.back_x().start()

        def after_back(self):
            self.back_x().wait_recv()
            self.back_c().start()

        def close(self):
            self.back_c().wait()
            for made in (self.to_z1(0), self.to_z1(1), self.to_z2(), self.back_x()):
                made.wait_send()
            for b in range(ZLINE):
                self.to_y(b).wait_send()

    whole = pl.ds(0, quarter)
    output = Sum(0, out_0, whole)
    small = Sum(1, out_1, of_side)
    qkv = Sum(2, out_2, whole)

    def products(array, left, right):
        rows_all = left[...].reshape(ZLINE * rows_y * quarter, 4 * length)

        def step(j, _):
            at = pl.ds(pl.multiple_of(j * 512, 512), 512)
            result = jnp.dot(rows_all, right[:, at], preferred_element_type=f32).astype(bf16)
            array.own[:, :, :, at] = result.reshape(ZLINE, rows_y, quarter, 512)
            return 0

        lax.fori_loop(0, right.shape[1] // 512, step, 0)
        array.along_y()

    def load_output(i):
        step = w_output.shape[1]
        at = pl.ds(pl.multiple_of(i * step, step), step)
        return pltpu.make_async_copy(
            w_output_hbm.at[at], w_output.at[lax.rem(i, 2)], weight_sems.at[0, lax.rem(i, 2)]
        )

    def load_qkv(i):
        step = w_qkv.shape[1]
        at = pl.ds(pl.multiple_of(i * step, step), step)
        return pltpu.make_async_copy(
            w_qkv_hbm.at[at], w_qkv.at[lax.rem(i, 2)], weight_sems.at[1, lax.rem(i, 2)]
        )

    def unrotate(value):
        lanes = value.shape[1]
        lane = lax.broadcasted_iota(jnp.int32, value.shape, 1)
        swapped = jnp.where(
            lane % HD < HD // 2,
            pltpu.roll(value, lanes - HD // 2, 1),
            pltpu.roll(value, HD // 2, 1),
        )
        return (value * cosine[:, :lanes] + swapped * sine[:, :lanes]).astype(bf16)

    per_group = H // KV
    wide = GROUP * per_group * HD
    narrow = GROUP * HD

    def attend(i, _):
        load_output(i).wait()
        at = pl.ds(pl.multiple_of(i * wide, wide), wide)
        kv_at = pl.ds(pl.multiple_of(i * narrow, narrow), narrow)
        grad_mixed = against(grad_branch[...], w_output[lax.rem(i, 2)]).astype(bf16)
        query, key, value = queries[:, at], keys[:, kv_at], values[:, kv_at]
        is_allowed = allowed[...] > 0.5
        grad_queries, grad_keys, grad_values = [], [], []
        for k in range(GROUP):
            k_head, v_head = key[:, k * HD : (k + 1) * HD], value[:, k * HD : (k + 1) * HD]
            grad_k = grad_v = None
            for j in range(k * per_group, (k + 1) * per_group):
                q_head = query[:, j * HD : (j + 1) * HD]
                mixed_head = grad_mixed[:, j * HD : (j + 1) * HD]
                scores = jnp.where(is_allowed, against(q_head, k_head) * 0.125, -1e30)
                lifted = jnp.exp(scores - jnp.max(scores, axis=-1, keepdims=True))
                weights = lifted / jnp.sum(lifted, axis=-1, keepdims=True)
                grad_weights = against(mixed_head, v_head)
                inner = jnp.sum(weights * grad_weights, axis=-1, keepdims=True)
                grad_scores = (weights * (grad_weights - inner)).astype(bf16)
                part_v = transposed(weights.astype(bf16), mixed_head)
                part_k = transposed(grad_scores, q_head)
                grad_v = part_v if grad_v is None else grad_v + part_v
                grad_k = part_k if grad_k is None else grad_k + part_k
                grad_queries.append(
                    jnp.dot(grad_scores, k_head, preferred_element_type=f32) * 0.125
                )
            grad_keys.append(grad_k * 0.125)
            grad_values.append(grad_v)
        grad_qkv[:, at] = unrotate(jnp.concatenate(grad_queries, axis=1))
        k_at = pl.ds(pl.multiple_of(H * HD + i * narrow, narrow), narrow)
        v_at = pl.ds(pl.multiple_of((H + KV) * HD + i * narrow, narrow), narrow)
        grad_qkv[:, k_at] = unrotate(jnp.concatenate(grad_keys, axis=1))
        grad_qkv[:, v_at] = jnp.concatenate(grad_values, axis=1).astype(bf16)

        @pl.when(i + 2 < KV // GROUP)
        def _():
            load_output(i + 2).start()

        return 0

    def input_grads():
        tile = w_qkv.shape[1]

        def step(i, _):
            load_qkv(i).wait()
            at = pl.ds(pl.multiple_of(i * tile, tile), tile)
            grad_normed[:, at] = against(grad_qkv[...], w_qkv[lax.rem(i, 2)])

            @pl.when(i + 2 < width // tile)
            def _():
                load_qkv(i + 2).start()

            return 0

        lax.fori_loop(0, width // tile, step, 0)
        inputs = tokens_ref[...].astype(f32)
        inv = lax.rsqrt(jnp.mean(inputs * inputs, axis=-1, keepdims=True) + epsilon)
        unit = inputs * inv
        onto = grad_normed[...] * unit
        scaled = grad_normed[...] * gain[...]
        grad_tokens_out[...] = (
            grad_residual[...]
            + inv * (scaled - unit * jnp.mean(scaled * unit, axis=-1, keepdims=True))
        ).astype(bf16)
        lane = lax.broadcasted_iota(jnp.int32, (length, 128), 1)
        at_lane = (lane == EXPERTS).astype(bf16)
        high = onto.astype(bf16)
        low = (onto - high.astype(f32)).astype(bf16)
        column = transposed(high, at_lane) + transposed(low, at_lane)
        part_small[...] = (
            base_small[...].astype(f32) + column.reshape(part_small.shape)
        ).astype(bf16)
        small.to_c().start()

    load_rows(0).start()
    for load in load_combined:
        load.start()
    for e in range(2):
        for k in range(2):
            load_grads(e, k).start()
    for i in range(2):
        load_output(i).start()
        load_qkv(i).start()
    greet([to[name] for name in ("z1", "z2", "z3", "y", "x", "c", "xc")])
    own_tokens = pl.ds(0, length)
    lefts = left_copies(0, mixed, left_output) + left_copies(1, normed, left_qkv)
    rights = {m: right_copy(2, grad_branch, right_output, m) for m in (1, 2, 3)}
    qkv_rights = {m: right_copy(3, grad_qkv, right_qkv, m) for m in (1, 2, 3)}
    rights[2].start()
    rights[1].start()
    for made in lefts:
        made.start()
    left_output[:, :, own_tokens] = mixed[:, core, side]
    left_qkv[:, :, own_tokens] = normed[:, core, side]
    right_output[own_tokens] = grad_branch[...]
    o_start()

    for r in range(ZLINE):
        load_rows(r).wait()

        def turn(j, _, r=r):
            at = pl.ds(pl.multiple_of(j * 256, 256), 256)
            turned[at, pl.ds(r * count, count)] = rows[:, at].T
            return 0

        lax.fori_loop(0, width // 256, turn, 0)
        if r + 1 < ZLINE:
            load_rows(r + 1).start()

    def send_y(e):
        return remote(
            part_gate_up.at[e, 1 - y], heard_gate_up.at[e], y_send.at[e], y_recv.at[e], to["y"]
        )

    def send_z(e, m):
        return remote(
            part_gate_up.at[e, y, z_of[m]],
            heard_z.at[m - 1, e],
            z_send.at[m - 1, e],
            z_recv.at[m - 1, e],
            to[f"z{m}"],
        )

    def reduce(e):
        send_y(e).wait_recv()
        for b in range(ZLINE):
            part_gate_up[e, y, b] = add(part_gate_up[e, y, b], heard_gate_up[e, b])
        for m in range(1, ZLINE):
            send_z(e, m).start()

    def gate_up(e, _):
        for k in range(2):
            load_grads(e, k).wait()
        right = grads[lax.rem(e, 2)].reshape(tokens, 2 * hidden)

        def step(b, _):
            at = pl.ds(pl.multiple_of(b * rows_y * n, 128), rows_y * n)
            result = jnp.dot(turned[at, :], right, preferred_element_type=f32).astype(bf16)
            for k in range(rows_y):
                part_gate_up[e, k, b] = result[k * n : (k + 1) * n]
            return 0

        lax.fori_loop(0, ZLINE, step, 0)

        @pl.when(e + 2 < owned)
        def _():
            for k in range(2):
                load_grads(e + 2, k).start()

        return 0

    lax.fori_loop(0, 1, gate_up, 0)
    send_y(0).start()
    lax.fori_loop(1, 2, gate_up, 0)
    send_y(1).start()
    rights[2].wait_recv()
    rights[3].start()
    o_after_z1()
    for made in lefts:
        made.wait_recv()
    rights[1].wait_recv()
    rights[3].wait_recv()
    products(output, left_output, right_output)
    lax.fori_loop(0, KV // GROUP // 2, attend, 0)
    lax.fori_loop(2, 3, gate_up, 0)
    send_y(2).start()
    reduce(0)
    lax.fori_loop(KV // GROUP // 2, KV // GROUP, attend, 0)
    qkv_rights[2].start()
    qkv_rights[1].start()
    o_end()
    right_qkv[own_tokens] = grad_qkv[...]
    lax.fori_loop(3, 4, gate_up, 0)
    send_y(3).start()
    reduce(1)
    output.after_y()
    input_grads()
    lax.fori_loop(4, 5, gate_up, 0)
    send_y(4).start()
    qkv_rights[2].wait_recv()
    qkv_rights[3].start()
    reduce(2)
    qkv_rights[1].wait_recv()
    qkv_rights[3].wait_recv()
    products(qkv, left_qkv, right_qkv)
    small.after_c()
    reduce(3)
    output.after_z1()
    lax.fori_loop(5, 7, gate_up, 0)
    send_y(5).start()
    output.after_z2()
    lax.fori_loop(7, owned, gate_up, 0)
    small.after_x()
    reduce(4)
    send_y(6).start()
    qkv.after_y()
    send_y(7).start()
    output.after_back()
    reduce(5)
    send_y(8).start()
    small.after_y()
    reduce(6)
    send_y(9).start()
    qkv.after_z1()
    reduce(7)
    small.after_z1()
    qkv.after_z2()
    reduce(8)
    small.after_z2()
    qkv.after_back()
    small.after_back()
    reduce(9)

    def keep(e):
        return pltpu.make_async_copy(
            stage.at[lax.rem(e, 2)], gate_up_out.at[e], store_sems.at[lax.rem(e, 2)]
        )

    def collect(e, _):
        slot = lax.rem(e, 2)

        @pl.when(e >= 2)
        def _():
            keep(e - 2).wait()

        for m in range(ZLINE):
            if m:
                send_z(e, m).wait_recv()
                block = heard_z[m - 1, e]
            else:
                block = part_gate_up[e, y, z]
            for k in range(2):
                at = pl.ds(pl.multiple_of(k * F + z_of[m] * hidden, hidden), hidden)
                stage[slot, :, at] = block[:, k * hidden : (k + 1) * hidden]
        keep(e).start()
        return 0

    lax.fori_loop(0, owned, collect, 0)

    for e in (owned - 2, owned - 1):
        keep(e).wait()

    def close(e, _):
        send_y(e).wait_send()
        for m in range(1, ZLINE):
            send_z(e, m).wait_send()
        return 0

    lax.fori_loop(0, owned, close, 0)
    for array in (output, small, qkv):
        array.close()
    small.to_c().wait_send()
    small.to_x().wait_send()
    for k in range(3):
        o_copy(k).wait_send()
    for made in lefts + list(rights.values()) + list(qkv_rights.values()):
        made.wait_send()


def finish(rows_y, rows, grads, combined, heard, w_output, w_qkv, *small):
    _, count, width = rows.shape
    hidden = F // ZLINE
    owned = grads.shape[2] // (2 * hidden)
    length = small[0].shape[0]
    blocks = ZLINE * rows_y
    n = width // blocks
    columns = (w_output.shape[1], small[-1].shape[3], w_qkv.shape[1])
    any_space = pl.BlockSpec(memory_space=pl.ANY)
    vmem = pl.BlockSpec(memory_space=pltpu.VMEM)
    sems = pltpu.SemaphoreType.DMA

    def summed(wide, own_rows):
        heard = own_rows != n // 4
        return [
            pltpu.VMEM((ZLINE, rows_y, own_rows, wide), bf16),
            pltpu.VMEM((ZLINE, rows_y, n // 2, wide) if heard else (16, 128), bf16),
            pltpu.VMEM((ZLINE, rows_y, n // 4, wide) if heard else (16, 128), bf16),
            pltpu.VMEM((ZLINE, n // 4, wide), bf16),
            pltpu.VMEM((2, n // 4, wide), bf16),
            pltpu.VMEM((n // 4, wide), bf16),
        ]

    return pl.pallas_call(
        functools.partial(finish_kernel, rows_y),
        name="finish",
        out_shape=(
            jax.ShapeDtypeStruct((owned, n, 2 * F), bf16),
            jax.ShapeDtypeStruct((length, width), bf16),
            jax.ShapeDtypeStruct((length, width), bf16),
        )
        + tuple(jax.ShapeDtypeStruct((n, v), bf16) for v in columns),
        in_specs=[any_space] * 6 + [vmem] * len(small),
        out_specs=(any_space,) + (vmem,) * 5,
        scratch_shapes=[
            pltpu.VMEM((count, width), bf16),
            pltpu.VMEM((width, ZLINE * count), bf16),
            pltpu.VMEM((2, ZLINE, count, 2 * hidden), bf16),
            pltpu.VMEM((owned, rows_y, ZLINE, n, 2 * hidden), bf16),
            pltpu.VMEM((owned, ZLINE, n, 2 * hidden), bf16),
            pltpu.VMEM((ZLINE - 1, owned, n, 2 * hidden), bf16),
            pltpu.VMEM((2, n, 2 * F), bf16),
            pltpu.VMEM((ZLINE, length, width), bf16),
            pltpu.VMEM((ZLINE, length, width), bf16),
            pltpu.VMEM((2, length, width), bf16),
            pltpu.VMEM((length, width), bf16),
            pltpu.VMEM((2, GROUP * (H // KV) * HD, width), bf16),
            pltpu.VMEM((2, 256, columns[2]), bf16),
            pltpu.VMEM((length, columns[2]), bf16),
            pltpu.VMEM((length, width), f32),
            pltpu.VMEM((blocks, n // 4, 4 * length), bf16),
            pltpu.VMEM((blocks, n // 4, 4 * length), bf16),
            pltpu.VMEM((4 * length, columns[0]), bf16),
            pltpu.VMEM((4 * length, columns[2]), bf16),
            pltpu.VMEM(small[-1].shape, bf16),
            *summed(columns[0], n // 4),
            *summed(columns[1], n // 2),
            *summed(columns[2], n // 4),
            sems,
            sems((2,)),
            sems((2, 2)),
            sems((2, 2)),
            sems((2,)),
            sems((owned,)),
            sems((owned,)),
            sems((ZLINE - 1, owned)),
            sems((ZLINE - 1, owned)),
            sems((3, 8 + ZLINE)),
            sems((3, 8 + ZLINE)),
            sems((4, 4)),
            sems((4, 4)),
            sems((3,)),
            sems((3,)),
        ],
        compiler_params=pltpu.CompilerParams(
            collective_id=3, has_side_effects=True, vmem_limit_bytes=63 * 2**20
        ),
    )(rows, grads, combined, heard, w_output, w_qkv, *small)


def permuted(
    tokens,
    segments,
    routes,
    w_query,
    w_key,
    w_value,
    w_output,
    w_router,
    gain_attn,
    gain_moe,
    w_gate_up,
    w_down,
    cotangent,
):
    place = Place()
    length, width = tokens.shape
    owned = w_gate_up.shape[0]
    rows = w_query.shape[0]
    hidden = F // ZLINE
    per_group = H // KV
    q_end, k_end, v_end = H * HD, (H + KV) * HD, (H + 2 * KV) * HD
    o_end = v_end + width

    small = jnp.concatenate(
        [w_router, gain_attn[:, None], gain_moe[:, None], jnp.zeros((rows, 128 - EXPERTS - 2), bf16)],
        axis=1,
    )
    shard = jnp.concatenate([w_query, w_key, w_value, w_output, small], axis=1)
    full, order = gather_weights(place, shard)
    full_qkv, full_output = full[:, :v_end], full[:, v_end:o_end]
    full_small = transposed(order, full[:, o_end:]).astype(bf16)
    full_router = full_small[:, :EXPERTS]
    attn_gain = full_small[:, EXPERTS].astype(f32)
    moe_gain = full_small[:, EXPERTS + 1].astype(f32)

    chosen_mask = jnp.any(
        routes[:, :, None] == jnp.arange(EXPERTS, dtype=jnp.int32), axis=1
    )
    dy_block = jnp.concatenate(
        [cotangent, chosen_mask.astype(bf16), jnp.zeros((length, 128 - EXPERTS), bf16)], axis=1
    )
    dy_groups = gather_tokens(place, dy_block)

    cosine_table, sine_table = tables(length, HD)
    inputs = tokens.astype(f32)
    inv_attn = lax.rsqrt(jnp.mean(inputs * inputs, axis=-1, keepdims=True) + epsilon)
    unit_attn = inputs * inv_attn
    normed = (unit_attn * attn_gain).astype(bf16)
    normed = against(normed, order).astype(bf16)
    qkv = dot(normed, full_qkv)
    queries = rotate(qkv[:, :q_end].reshape(length, H, HD), cosine_table, sine_table)
    queries = queries.astype(bf16).reshape(length, KV, per_group, HD)
    key_rows = rotate(
        qkv[:, q_end:k_end].reshape(length, KV, HD), cosine_table, sine_table
    ).astype(bf16)
    values = qkv[:, k_end:].astype(bf16).reshape(length, KV, HD)
    segment = segments[0]
    position = jnp.arange(length, dtype=jnp.int32)
    allowed = (segment[:, None] == segment[None, :]) & (position[:, None] >= position[None, :])
    scores = (
        jnp.einsum("qkgd,skd->kgqs", queries, key_rows, preferred_element_type=f32) * 0.125
    )
    scores = jnp.where(allowed, scores, -1e30)
    maximum = jnp.max(scores, axis=-1, keepdims=True)
    lifted_scores = jnp.exp(scores - maximum)
    full_weights = lifted_scores / jnp.sum(lifted_scores, axis=-1, keepdims=True)
    attn_weights = full_weights.astype(bf16)
    mixed = jnp.einsum("kgqs,skd->qkgd", attn_weights, values, preferred_element_type=f32)
    mixed = mixed.reshape(length, H * HD).astype(bf16)
    mixed = against(mixed, order).astype(bf16)
    residual = inputs + dot(mixed, full_output)
    inv_moe = lax.rsqrt(jnp.mean(residual * residual, axis=-1, keepdims=True) + epsilon)
    unit_moe = residual * inv_moe
    normed_moe = (unit_moe * moe_gain).astype(bf16)

    def gates_of(rows_in, mask):
        logits = jnp.where(mask, dot(rows_in, full_router), -1e30)
        lifted = jnp.where(mask, jnp.exp(logits - jnp.max(logits, axis=-1, keepdims=True)), 0.0)
        return lifted / jnp.sum(lifted, axis=-1, keepdims=True)

    gates = gates_of(normed_moe, chosen_mask)

    def columns(start):
        cut = lax.dynamic_slice_in_dim(w_gate_up, start + place.z * hidden, hidden, 2)
        return cut.swapaxes(0, 1).reshape(width, owned * hidden)

    slice_gate_up = jnp.concatenate([columns(0), columns(F)], axis=1)
    slice_down = lax.dynamic_slice_in_dim(w_down, place.z * hidden, hidden, 1)
    slice_down = slice_down.reshape(owned * hidden, width)
    moe_groups = gather_tokens(place, normed_moe)
    span = owned * hidden
    acts, grads_gate_up, gate_parts = [], [], []
    for normed_rows, dy_rows in zip(moe_groups, dy_groups):
        count = normed_rows.shape[0]
        group_gates = gates_of(normed_rows, dy_rows[:, width : width + EXPERTS] > 0.5)
        group_gates = lax.dynamic_slice_in_dim(group_gates, place.ex * owned, owned, 1)
        spread_gates = jnp.broadcast_to(group_gates[:, :, None], (count, owned, hidden))
        spread_gates = spread_gates.reshape(count, span)
        gate_up = dot(normed_rows, slice_gate_up)
        gate_part, up_part = gate_up[:, :span], gate_up[:, span:]
        plain_grad = against(dy_rows[:, :width], slice_down)
        sigmoid_gate = jax.nn.sigmoid(gate_part)
        swished = gate_part * sigmoid_gate
        activation = swished * up_part
        grad_act = plain_grad * spread_gates
        gate_parts.append(jnp.sum((plain_grad * activation).reshape(count, owned, hidden), axis=-1))
        acts.append((spread_gates * activation).astype(bf16))
        grads_gate_up.append(
            jnp.concatenate(
                [
                    grad_act * up_part * sigmoid_gate * (1.0 + gate_part * (1.0 - sigmoid_gate)),
                    grad_act * swished,
                ],
                axis=-1,
            ).astype(bf16)
        )
    row_parts = [against(g, slice_gate_up).astype(bf16) for g in grads_gate_up]
    row_grads = scatter_tokens(place, row_parts, length)
    out_parts = [dot(a, slice_down).astype(bf16) for a in acts]
    output = (residual + scatter_tokens(place, out_parts, length)).astype(bf16)

    gate_parts = [g.T for g in gate_parts]
    two = [gate_parts[i] + swap(gate_parts[i + 2], "dp", place.z_bits[1]) for i in range(2)]
    mine = two[0] + swap(two[1], "dp", place.z_bits[0])
    mine = mine.reshape(owned, 2, place.ex_size // 2, length)
    heard = [
        swap(mine[:, m % 2, m // 2], "expert", m) if m else mine[:, 0, 0]
        for m in range(place.ex_size)
    ]
    heard = jnp.stack(heard)
    grad_gates = jnp.concatenate(
        [pick(heard, place.ex ^ j) for j in range(place.ex_size)], axis=0
    ).T
    grad_logits = (
        gates * (grad_gates - jnp.sum(gates * grad_gates, axis=-1, keepdims=True))
    ).astype(bf16)

    all_rows = jnp.concatenate([v for v in moe_groups], axis=0)
    all_dy = jnp.concatenate([v[:, :width] for v in dy_groups], axis=0)
    all_grads = jnp.concatenate(grads_gate_up, axis=0)
    all_acts = jnp.concatenate(acts, axis=0)

    def reduce_y(part, axis):
        part = jnp.moveaxis(part, axis, 0)
        for mask in place.y_bits[::-1]:
            at = (place.y // mask) % 2
            half = part.reshape((2, part.shape[0] // 2) + part.shape[1:])
            away = swap(pick(half, 1 - at), "dp", mask)
            part = (pick(half, at).astype(f32) + away.astype(f32)).astype(bf16)
        return part[0]

    shard_down = transposed(all_acts, all_dy).astype(bf16)
    shard_down = shard_down.reshape(owned, place.rows_y, hidden // place.rows_y, width)
    shard_down = reduce_y(shard_down, 1).astype(f32)
    part_gate_up = transposed(all_rows, all_grads).astype(bf16)
    part_gate_up = part_gate_up.reshape(ZLINE, place.rows_y, rows, 2 * span)
    part_gate_up = reduce_y(part_gate_up, 1)
    heard = [pick(part_gate_up, place.z)] + [
        swap(pick(part_gate_up, place.z ^ m), "dp", m * place.rows_y) for m in range(1, ZLINE)
    ]
    heard = jnp.stack(heard)
    shard_gate_up = jnp.stack([pick(heard, place.z ^ j) for j in range(ZLINE)], axis=0)
    shard_gate_up = shard_gate_up.reshape(ZLINE, rows, 2, owned, hidden)
    shard_gate_up = shard_gate_up.transpose(3, 1, 2, 0, 4).reshape(owned, rows, 2 * F).astype(f32)

    grad_out = cotangent.astype(f32)
    part_router = transposed(normed_moe, grad_logits)
    grad_normed_moe = row_grads + against(grad_logits, full_router)
    part_gain_moe = jnp.sum(grad_normed_moe * unit_moe, axis=0)
    scaled_moe = grad_normed_moe * moe_gain
    grad_residual = grad_out + inv_moe * (
        scaled_moe - unit_moe * jnp.mean(scaled_moe * unit_moe, axis=-1, keepdims=True)
    )
    grad_branch = grad_residual.astype(bf16)
    part_output = transposed(mixed, grad_branch)
    grad_mixed = dot(against(grad_branch, full_output).astype(bf16), order).astype(bf16)
    grad_mixed = grad_mixed.reshape(length, KV, per_group, HD)
    grad_weights = jnp.einsum(
        "qkgd,skd->kgqs", grad_mixed, values, preferred_element_type=f32
    )
    grad_values = jnp.einsum(
        "kgqs,qkgd->skd", attn_weights, grad_mixed, preferred_element_type=f32
    )
    grad_values = grad_values.astype(bf16).reshape(length, KV * HD)
    grad_scores = (
        full_weights * (grad_weights - jnp.sum(full_weights * grad_weights, axis=-1, keepdims=True))
    ).astype(bf16)
    grad_queries = (
        jnp.einsum("kgqs,skd->qkgd", grad_scores, key_rows, preferred_element_type=f32) * 0.125
    )
    grad_queries = rotate(grad_queries.reshape(length, H, HD), cosine_table, -sine_table)
    grad_queries = grad_queries.astype(bf16).reshape(length, H * HD)
    grad_keys = (
        jnp.einsum("kgqs,qkgd->skd", grad_scores, queries, preferred_element_type=f32) * 0.125
    )
    grad_keys = rotate(grad_keys, cosine_table, -sine_table)
    grad_keys = grad_keys.astype(bf16).reshape(length, KV * HD)
    grad_qkv = jnp.concatenate([grad_queries, grad_keys, grad_values], axis=1)
    part_qkv = transposed(normed, grad_qkv)
    grad_normed = against(grad_qkv, full_qkv)
    grad_normed = lax.dot_general(
        grad_normed,
        order.astype(f32),
        (((1,), (0,)), ((), ())),
        precision=lax.Precision.HIGHEST,
        preferred_element_type=f32,
    )
    part_gain_attn = jnp.sum(grad_normed * unit_attn, axis=0)
    scaled_attn = grad_normed * attn_gain
    grad_tokens = (
        grad_residual
        + inv_attn
        * (scaled_attn - unit_attn * jnp.mean(scaled_attn * unit_attn, axis=-1, keepdims=True))
    ).astype(bf16)
    part_small = jnp.concatenate(
        [
            part_router.astype(bf16),
            part_gain_attn[:, None].astype(bf16),
            part_gain_moe[:, None].astype(bf16),
            jnp.zeros((width, 128 - EXPERTS - 2), bf16),
        ],
        axis=1,
    )
    part_small = dot(order, part_small).astype(bf16)
    summed = scatter_weights(
        place,
        jnp.concatenate([part_qkv.astype(bf16), part_output.astype(bf16), part_small], axis=1),
    )
    return (
        output,
        grad_tokens,
        summed[:, :q_end],
        summed[:, q_end:k_end],
        summed[:, k_end:v_end],
        summed[:, v_end:o_end],
        summed[:, o_end : o_end + EXPERTS],
        summed[:, o_end + EXPERTS],
        summed[:, o_end + EXPERTS + 1],
        shard_gate_up,
        shard_down,
    )


def local(
    tokens,
    segments,
    routes,
    w_query,
    w_key,
    w_value,
    w_output,
    w_router,
    gain_attn,
    gain_moe,
    w_gate_up,
    w_down,
    cotangent,
):
    place = Place()
    if place.ex_size != 4 or place.rows_y != 2:
        return permuted(
            tokens,
            segments,
            routes,
            w_query,
            w_key,
            w_value,
            w_output,
            w_router,
            gain_attn,
            gain_moe,
            w_gate_up,
            w_down,
            cotangent,
        )
    length, width = tokens.shape
    owned = w_gate_up.shape[0]
    rows = w_query.shape[0]
    hidden = F // ZLINE
    span = owned * hidden
    per_group = H // KV
    q_end, k_end, v_end = H * HD, (H + KV) * HD, (H + 2 * KV) * HD

    small = jnp.concatenate(
        [w_router, gain_attn[:, None], gain_moe[:, None], jnp.zeros((rows, 128 - EXPERTS - 2), bf16)],
        axis=1,
    )
    chosen_mask = jnp.any(
        routes[:, :, None] == jnp.arange(EXPERTS, dtype=jnp.int32), axis=1
    )
    dy_block = jnp.concatenate(
        [cotangent, chosen_mask.astype(bf16), jnp.zeros((length, 128 - EXPERTS), bf16)], axis=1
    )
    qkv_shard = jnp.concatenate([w_query, w_key, w_value], axis=1)
    full_qkv, full_output, full_small, all_dy, plain_grads = gather(
        place.rows_y, (qkv_shard, w_output, small), dy_block, w_down
    )
    full_qkv = full_qkv.reshape(width, v_end)
    full_output = full_output.reshape(width, width)
    full_small = full_small.reshape(width, 128)
    attn_gain = full_small[:, EXPERTS].astype(f32)
    moe_gain = full_small[:, EXPERTS + 1].astype(f32)

    cosine_table, sine_table = tables(length, HD)
    inputs = tokens.astype(f32)
    inv_attn = lax.rsqrt(jnp.mean(inputs * inputs, axis=-1, keepdims=True) + epsilon)
    normed = (inputs * inv_attn * attn_gain).astype(bf16)
    qkv = dot(normed, full_qkv)
    queries = rotate(qkv[:, :q_end].reshape(length, H, HD), cosine_table, sine_table)
    queries = queries.astype(bf16).reshape(length, KV, per_group, HD)
    key_rows = rotate(
        qkv[:, q_end:k_end].reshape(length, KV, HD), cosine_table, sine_table
    ).astype(bf16)
    values = qkv[:, k_end:].astype(bf16).reshape(length, KV, HD)
    segment = segments[0]
    position = jnp.arange(length, dtype=jnp.int32)
    allowed = (segment[:, None] == segment[None, :]) & (position[:, None] >= position[None, :])
    scores = (
        jnp.einsum("qkgd,skd->kgqs", queries, key_rows, preferred_element_type=f32) * 0.125
    )
    scores = jnp.where(allowed, scores, -1e30)
    lifted = jnp.exp(scores - jnp.max(scores, axis=-1, keepdims=True))
    attn_weights = (lifted / jnp.sum(lifted, axis=-1, keepdims=True)).astype(bf16)
    mixed = jnp.einsum("kgqs,skd->qkgd", attn_weights, values, preferred_element_type=f32)
    mixed = mixed.reshape(length, H * HD).astype(bf16)
    residual = inputs + dot(mixed, full_output)
    inv_moe = lax.rsqrt(jnp.mean(residual * residual, axis=-1, keepdims=True) + epsilon)
    unit_moe = residual * inv_moe
    normed_moe = (unit_moe * moe_gain).astype(bf16)

    lane = jnp.arange(128, dtype=jnp.int32)
    wide_router = jnp.where(lane < EXPERTS, full_small, 0)
    column = jnp.arange(span, dtype=jnp.int32)
    spread = (lane[:, None] == place.ex * owned + column[None, :] // hidden).astype(bf16)
    all_rows, all_grads, shard_down, combined, heard, total = moe(
        place.rows_y, normed_moe, all_dy, plain_grads, w_gate_up, w_down, wide_router, spread
    )
    row_grads, grad_gates = total[:, :width], total[:, width:]

    mask = jnp.pad(chosen_mask, ((0, 0), (0, 128 - EXPERTS)))
    logits = jnp.where(mask, dot(normed_moe, wide_router), -1e30)
    lifted = jnp.where(mask, jnp.exp(logits - jnp.max(logits, axis=-1, keepdims=True)), 0.0)
    gates = lifted / jnp.sum(lifted, axis=-1, keepdims=True)
    grad_logits = (
        gates * (grad_gates - jnp.sum(gates * grad_gates, axis=-1, keepdims=True))
    ).astype(bf16)
    part_router = transposed(normed_moe, grad_logits)
    grad_normed_moe = row_grads + against(grad_logits, wide_router)
    part_gain_moe = jnp.sum(grad_normed_moe * unit_moe, axis=0)
    scaled_moe = grad_normed_moe * moe_gain
    grad_residual = cotangent.astype(f32) + inv_moe * (
        scaled_moe - unit_moe * jnp.mean(scaled_moe * unit_moe, axis=-1, keepdims=True)
    )
    part_small = jnp.where(
        lane == EXPERTS + 1, part_gain_moe[:, None], jnp.where(lane < EXPERTS, part_router, 0.0)
    ).astype(bf16)

    def cut(value):
        return value.T.reshape(place.dp_size, 2, 2, rows // 4, length)

    sign = jnp.where(jnp.arange(HD) < HD // 2, 1.0, -1.0)
    repeats = (1, GROUP * per_group)
    cosine = jnp.tile(jnp.tile(cosine_table[:, 0], (1, 2)), repeats)
    sine = jnp.tile(jnp.tile(sine_table[:, 0], (1, 2)) * sign, repeats)
    shard_gate_up, output, grad_tokens, sum_output, sum_small, sum_qkv = finish(
        place.rows_y,
        all_rows,
        all_grads,
        combined,
        heard,
        full_output,
        full_qkv,
        residual,
        grad_residual,
        grad_residual.astype(bf16),
        tokens,
        attn_gain[None, :],
        cut(mixed),
        cut(normed),
        queries.reshape(length, H * HD),
        key_rows.reshape(length, KV * HD),
        values.reshape(length, KV * HD),
        allowed.astype(f32),
        cosine,
        sine,
        part_small.reshape(ZLINE, place.rows_y, rows, 128),
    )
    return (
        output,
        grad_tokens,
        sum_qkv[:, :q_end].astype(f32),
        sum_qkv[:, q_end:k_end].astype(f32),
        sum_qkv[:, k_end:].astype(f32),
        sum_output.astype(f32),
        sum_small[:, :EXPERTS].astype(f32),
        sum_small[:, EXPERTS].astype(f32),
        sum_small[:, EXPERTS + 1].astype(f32),
        shard_gate_up.astype(f32),
        shard_down.astype(f32),
    )


def solution(mesh):
    return jax.shard_map(
        local,
        mesh=mesh,
        in_specs=(
            P(("dp", "expert"), None),
            P(("dp", "expert"), None),
            P(("dp", "expert"), None),
            P("dp", None),
            P("dp", None),
            P("dp", None),
            P("dp", None),
            P("dp", None),
            P("dp"),
            P("dp"),
            P("expert", None, None),
            P("expert", None, None),
            P(("dp", "expert"), None),
        ),
        out_specs=(
            P(("dp", "expert"), None),
            P(("dp", "expert"), None),
            P("dp", None),
            P("dp", None),
            P("dp", None),
            P("dp", None),
            P("dp", None),
            P("dp"),
            P("dp"),
            P("expert", "dp", None),
            P("expert", "dp", None),
        ),
        check_vma=False,
    )
```

```python
import functools

import jax
import jax.numpy as jnp
import numpy as np
from jax import lax
from jax.experimental import pallas as pl
from jax.experimental.pallas import tpu as pltpu
from jax.sharding import PartitionSpec as P

H = 24
KV = 8
HD = 64
F = 512
EXPERTS = 40
ZLINE = 4
GROUP = 2


epsilon = 1e-05
f32 = jnp.float32
bf16 = jnp.bfloat16


def tables(length, size):
    half_size = size // 2
    frequency = jnp.power(10000.0, -2.0 * jnp.arange(half_size, dtype=f32) / size)
    angles = jnp.arange(length, dtype=f32)[:, None] * frequency[None, :]
    return (jnp.cos(angles)[:, None, :], jnp.sin(angles)[:, None, :])


def rotate(source, cosine_table, sine_table):
    half_size = source.shape[-1] // 2
    first_half = source[..., :half_size]
    second_half = source[..., half_size:]
    return jnp.concatenate(
        [
            first_half * cosine_table - second_half * sine_table,
            second_half * cosine_table + first_half * sine_table,
        ],
        axis=-1,
    )


def dot(left_side, right_side):
    return jnp.dot(left_side, right_side, preferred_element_type=f32)


def transposed(left_side, right_side):
    return lax.dot_general(
        left_side, right_side, (((0,), (0,)), ((), ())), preferred_element_type=f32
    )


def against(left_side, right_side):
    return lax.dot_general(
        left_side, right_side, (((1,), (1,)), ((), ())), preferred_element_type=f32
    )


def swap(value, axis, mask):
    size = lax.axis_size(axis)
    return lax.ppermute(value, axis, [(i, i ^ mask) for i in range(size)])


def pick(value, at):
    return lax.dynamic_index_in_dim(value, at, 0, keepdims=False)


def bits(first, size):
    masks, step = [], 1
    while step < size:
        masks.append(first * step)
        step *= 2
    return masks


class Place:
    def __init__(self):
        self.dp_size = lax.axis_size("dp")
        self.ex_size = lax.axis_size("expert")
        self.dp = lax.axis_index("dp")
        self.ex = lax.axis_index("expert")
        self.rows_y = self.dp_size // ZLINE
        self.z = self.dp // self.rows_y
        self.y = self.dp % self.rows_y
        self.z_bits = bits(self.rows_y, ZLINE)
        self.y_bits = bits(1, self.rows_y)
        self.x_bits = bits(2, self.ex_size // 2)


def gather_weights(place, shard):
    n, columns = shard.shape
    piece = n // 6
    cut = shard.reshape(3, 2, piece, columns)
    core = place.ex % 2
    side = (place.ex // 2) % 2
    own = pick(cut.swapaxes(0, 1), core)
    sibling = pick(cut.swapaxes(0, 1), 1 - core)

    def ordered(parts):
        return jnp.stack([pick(parts, 2 * side), parts[1], pick(parts, 2 - 2 * side)])

    own, sibling = ordered(own), ordered(sibling)
    blocks = {0: own[:2]}
    for mask in place.z_bits + place.y_bits:
        blocks.update({m ^ mask: swap(v, "dp", mask) for m, v in list(blocks.items())})
    rows = []
    for m in range(place.dp_size):
        if m == 0:
            rows.append(jnp.stack([own, sibling], axis=1))
            continue
        other = swap(blocks[m][0], "expert", 2)
        trio = jnp.concatenate([blocks[m], other[None]], axis=0)
        rows.append(jnp.stack([trio, swap(trio, "expert", 1)], axis=1))
    full = jnp.stack(rows)
    total = place.dp_size * n
    k = jnp.arange(total, dtype=jnp.int32)
    block, part = k // n, (k % n) // (2 * piece)
    half, line = (k % (2 * piece)) // piece, k % piece
    part = jnp.where(part == 1, 1, jnp.where(part == 0, 2 * side, 2 - 2 * side))
    at = (block ^ place.dp) * n + part * 2 * piece + (half ^ core) * piece + line
    order = (at[:, None] == jnp.arange(total, dtype=jnp.int32)[None, :]).astype(bf16)
    return full.reshape(total, columns), order


def scatter_weights(place, part):
    total, columns = part.shape
    n = total // place.dp_size
    piece = n // 6
    core = place.ex % 2
    side = (place.ex // 2) % 2

    def add(left, right):
        return (left.astype(f32) + right.astype(f32)).astype(bf16)

    part = part.reshape(place.dp_size, 3, 2, piece, columns)
    kept = add(part[:, :, 0], swap(part[:, :, 1], "expert", 1))
    first = add(kept[:, 0], swap(kept[:, 2], "expert", 2))
    blocks = {m: jnp.stack([first[m], kept[m, 1]]) for m in range(place.dp_size)}
    for mask in (place.z_bits + place.y_bits)[::-1]:
        blocks = {
            m: add(v, swap(blocks[m ^ mask], "dp", mask))
            for m, v in blocks.items()
            if m & mask == 0
        }
    mine = blocks[0]
    middle = add(mine[1], swap(mine[1], "expert", 2))
    trio = jnp.stack([mine[0], middle, swap(mine[0], "expert", 2)])
    for mask in place.x_bits[1:]:
        trio = add(trio, swap(trio, "expert", mask))
    both = jnp.stack([trio, swap(trio, "expert", 1)], axis=1)
    both = jnp.where(side == 0, both, both[::-1])
    both = jnp.where(core == 0, both, both[:, ::-1])
    return both.reshape(n, columns).astype(f32)


def gather_tokens(place, block):
    blocks = {0: block}
    for mask in place.z_bits:
        blocks.update({m ^ mask: swap(v, "dp", mask) for m, v in list(blocks.items())})
    groups = []
    for r in range(ZLINE):
        row = [blocks[r * place.rows_y]]
        for mask in place.x_bits:
            row = row + [swap(v, "expert", mask) for v in row]
        row = jnp.concatenate(row, axis=0)
        groups.append(jnp.concatenate([row, swap(row, "expert", 1)], axis=0))
    return groups


def scatter_tokens(place, groups, length):
    def add(left, right):
        return left.astype(f32) + right.astype(f32)

    reduced = []
    for part in groups:
        half = part.shape[0] // 2
        kept = add(part[:half], swap(part[half:], "expert", 1)).astype(bf16)
        for mask in place.x_bits[::-1]:
            half = kept.shape[0] // 2
            kept = add(kept[:half], swap(kept[half:], "expert", mask)).astype(bf16)
        reduced.append(kept)
    two = [add(reduced[i], swap(reduced[i + 2], "dp", place.z_bits[1])) for i in range(2)]
    return add(two[0], swap(two[1].astype(bf16), "dp", place.z_bits[0]))


def other(index, mask):
    return index + mask - 2 * mask * ((index // mask) % 2)


class Links:
    def __init__(self, sends, recvs):
        self.sends, self.recvs, self.used, self.open = sends, recvs, 0, []

    def copy(self, source, target, partner):
        at = self.used
        self.used += 1
        made = pltpu.make_async_remote_copy(
            src_ref=source,
            dst_ref=target,
            send_sem=self.sends.at[at],
            recv_sem=self.recvs.at[at],
            device_id=partner,
            device_id_type=pl.DeviceIdType.MESH,
        )
        made.start()
        self.open.append(made)
        return made

    def close(self):
        for made in self.open:
            made.wait_send()


def partners(rows_y):
    dp, ex = lax.axis_index("dp"), lax.axis_index("expert")
    return {
        "z1": (other(dp, rows_y), ex),
        "z2": (other(dp, 2 * rows_y), ex),
        "y": (other(dp, 1), ex),
        "x": (dp, other(ex, 2)),
        "c": (dp, other(ex, 1)),
    }


def greet(devices):
    barrier = pltpu.get_barrier_semaphore()
    for device in devices:
        pl.semaphore_signal(
            barrier, inc=1, device_id=device, device_id_type=pl.DeviceIdType.MESH
        )
    pl.semaphore_wait(barrier, len(devices))


def gather_kernel(
    rows_y,
    exclusive,
    w_query,
    w_key,
    w_value,
    w_output,
    w_router,
    gain_attn,
    gain_moe,
    dy,
    tokens_ref,
    segments,
    routes,
    cosine,
    sine,
    down_hbm,
    qkv_out,
    output_out,
    dy_out,
    grads_out,
    small_out,
    queries_out,
    keys_out,
    values_out,
    residual_out,
    normed_moe_out,
    normed_turned,
    mixed_turned,
    gains_out,
    gates_out,
    allowed,
    full_qkv,
    full_output,
    dy_all,
    w_down,
    grads,
    projected,
    normed_out,
    mixed_out,
    *refs,
):
    z_send, z_recv, y_send, y_recv, x_send, x_recv, c_send, c_recv = refs[:8]
    dz_send, dz_recv, dx_send, dx_recv, dc_send, dc_recv, down_sem, dy_sems, grads_sems, keep_sems = refs[8:]
    fulls = (full_qkv, small_out, full_output)
    n = w_query.shape[0]
    half = n // 2
    piece = half - exclusive
    length = dy.shape[0]
    owned, hidden, width = w_down.shape
    dp, ex = lax.axis_index("dp"), lax.axis_index("expert")
    z, y = dp // rows_y, dp % rows_y
    core, side = ex % 2, (ex // 2) % 2
    to = partners(rows_y)
    z_of = [z, other(z, 1), other(z, 2), other(other(z, 1), 2)]

    in_plane = pl.ds(pl.multiple_of(core * half + side * exclusive, 16), piece)
    alone = pl.ds(pl.multiple_of(core * half + side * piece, 16), exclusive)
    of_core = pl.ds(pl.multiple_of(core * half, 16), half)

    def remote(source, target, send_sem, recv_sem, device):
        return pltpu.make_async_remote_copy(
            src_ref=source,
            dst_ref=target,
            send_sem=send_sem,
            recv_sem=recv_sem,
            device_id=device,
            device_id_type=pl.DeviceIdType.MESH,
        )

    first, second = (0, 1), (2,)

    def copies(arrays, rows, m, ys, send, recv, at, device):
        made = []
        for k in arrays:
            block = fulls[k].at[z_of[m] * rows_y + ys, rows]
            made.append(remote(block, block, send.at[k, at], recv.at[k, at], device))
        return made

    def to_z(arrays, step):
        m, device = ((0, "z1"), (0, "z2"), (2, "z1"))[step]
        return copies(arrays, in_plane, m, y, z_send, z_recv, step, to[device])

    def to_y(arrays, m):
        return copies(arrays, in_plane, m, y, y_send, y_recv, m, to["y"])

    def to_x(arrays, m, k):
        ys = 1 - y if k else y
        return copies(arrays, alone, m, ys, x_send, x_recv, 2 * m + k, to["x"])

    def to_c(arrays, m, k):
        ys = 1 - y if k else y
        return copies(arrays, of_core, m, ys, c_send, c_recv, 2 * m + k, to["c"])

    near, pair = pl.ds(0, length), pl.ds(length, length)
    front, back = pl.ds(0, 2 * length), pl.ds(2 * length, 2 * length)

    def dy_z(step):
        m, target, device = ((0, 1, "z1"), (0, 2, "z2"), (2, 3, "z1"))[step]
        return remote(
            dy_all.at[m, near], dy_all.at[target, near], dz_send.at[step], dz_recv.at[step], to[device]
        )

    def dy_x(m):
        return remote(
            dy_all.at[m, near], dy_all.at[m, pair], dx_send.at[m], dx_recv.at[m], to["x"]
        )

    def dy_c(m):
        return remote(
            dy_all.at[m, front], dy_all.at[m, back], dc_send.at[m], dc_recv.at[m], to["c"]
        )

    at = pl.ds(pl.multiple_of(z * hidden, hidden), hidden)
    load_down = pltpu.make_async_copy(down_hbm.at[:, at, :], w_down, down_sem)
    load_down.start()

    def iota(shape, axis):
        return lax.broadcasted_iota(jnp.int32, shape, axis)

    full_qkv[dp, :, : H * HD] = w_query[...]
    full_qkv[dp, :, H * HD : (H + KV) * HD] = w_key[...]
    full_qkv[dp, :, (H + KV) * HD :] = w_value[...]
    full_output[dp] = w_output[...]
    line = iota((8, n), 0)
    gain_rows = jnp.where(
        line == 0,
        gain_attn[...].astype(f32),
        jnp.where(line == 1, gain_moe[...].astype(f32), 0.0),
    ).astype(bf16)
    places = (iota((8, 128), 1) == iota((8, 128), 0) + EXPERTS) & (iota((8, 128), 0) < 2)
    columns = transposed(gain_rows, places.astype(f32).astype(bf16))
    router = jnp.concatenate(
        [w_router[...].astype(f32), jnp.zeros((n, 128 - EXPERTS), f32)], axis=1
    )
    small_out[dp] = (router + columns).astype(bf16)
    lane, row = iota((length, 128), 1), iota((length, 128), 0)
    chosen = routes[:, :1] == lane
    for k in range(1, routes.shape[1]):
        chosen = chosen | (routes[:, k : k + 1] == lane)
    chosen = chosen.astype(f32)
    dy_all[0, near, :width] = dy[...]
    dy_all[0, near, width:] = chosen.astype(bf16)
    greet([to[name] for name in ("z1", "z2", "y", "x", "c")])

    def start(made):
        for copy in made:
            copy.start()

    def arrived(made):
        for copy in made:
            copy.wait_recv()

    def keep_dy(m):
        return pltpu.make_async_copy(dy_all.at[m], dy_out.at[m], dy_sems.at[m])

    def keep_grads(m):
        return pltpu.make_async_copy(grads.at[m % 2], grads_out.at[m], grads_sems.at[m % 2])

    keep_qkv = pltpu.make_async_copy(full_qkv, qkv_out, keep_sems.at[0])
    keep_output = pltpu.make_async_copy(full_output, output_out, keep_sems.at[1])

    def group(m):
        dy_c(m).wait_recv()
        keep_dy(m).start()
        if m >= 2:
            keep_grads(m - 2).wait()

        def step(p, _):
            at = pl.ds(pl.multiple_of(p * 2 * hidden, 2 * hidden), 2 * hidden)
            down = w_down[pl.ds(2 * p, 2)].reshape(2 * hidden, width)
            grads[m % 2, :, at] = against(dy_all[m, :, :width], down).astype(bf16)
            return 0

        lax.fori_loop(0, owned // 2, step, 0)
        keep_grads(m).start()

    def turned(value, target):
        target[...] = value.T.reshape(target.shape)

    def rotated(value):
        lanes = value.shape[1]
        lane = lax.broadcasted_iota(jnp.int32, value.shape, 1)
        swapped = jnp.where(
            lane % HD < HD // 2,
            pltpu.roll(value, lanes - HD // 2, 1),
            pltpu.roll(value, HD // 2, 1),
        )
        return (value * cosine[:, :lanes] - swapped * sine[:, :lanes]).astype(bf16)

    per_group = H // KV
    wide = GROUP * per_group * HD
    narrow = GROUP * HD

    def project():
        inputs = tokens_ref[...].astype(f32)
        inv = lax.rsqrt(jnp.mean(inputs * inputs, axis=-1, keepdims=True) + epsilon)
        gains_out[...] = against(
            places.astype(f32).astype(bf16), small_out[...].reshape(width, 128)
        )
        normed_out[...] = (inputs * inv * gains_out[:1]).astype(bf16)
        segment = segments[...].astype(f32)
        same = against(
            (row == lane).astype(f32).astype(bf16), jnp.broadcast_to(segment, (8, length)).astype(bf16)
        )[:, :1]
        allowed[...] = ((same == segment) & (row >= lane)).astype(f32)

        def step(j, _):
            at = pl.ds(pl.multiple_of(j * 512, 512), 512)
            projected[:, at] = jnp.dot(
                normed_out[...], full_qkv[:, :, at].reshape(width, 512), preferred_element_type=f32
            )
            return 0

        lax.fori_loop(0, projected.shape[1] // 512, step, 0)

    def attend(i):
        at = pl.ds(i * wide, wide)
        kv_at = pl.ds(i * narrow, narrow)
        k_at = pl.ds(H * HD + i * narrow, narrow)
        v_at = pl.ds((H + KV) * HD + i * narrow, narrow)
        query = rotated(projected[:, at])
        key = rotated(projected[:, k_at])
        value = projected[:, v_at].astype(bf16)
        queries_out[:, at] = query
        keys_out[:, kv_at] = key
        values_out[:, kv_at] = value
        is_allowed = allowed[...] > 0.5
        heads = []
        for k in range(GROUP):
            k_head, v_head = key[:, k * HD : (k + 1) * HD], value[:, k * HD : (k + 1) * HD]
            for j in range(k * per_group, (k + 1) * per_group):
                q_head = query[:, j * HD : (j + 1) * HD]
                scores = jnp.where(is_allowed, against(q_head, k_head) * 0.125, -1e30)
                lifted = jnp.exp(scores - jnp.max(scores, axis=-1, keepdims=True))
                weights = (lifted / jnp.sum(lifted, axis=-1, keepdims=True)).astype(bf16)
                heads.append(jnp.dot(weights, v_head, preferred_element_type=f32))
        mixed_out[:, at] = jnp.concatenate(heads, axis=1).astype(bf16)

    def close_block():
        def step(j, _):
            at = pl.ds(pl.multiple_of(j * 512, 512), 512)
            residual_out[:, at] = tokens_ref[:, at].astype(f32) + jnp.dot(
                mixed_out[...], full_output[:, :, at].reshape(width, 512), preferred_element_type=f32
            )
            return 0

        lax.fori_loop(0, width // 512, step, 0)
        residual = residual_out[...]
        inv = lax.rsqrt(jnp.mean(residual * residual, axis=-1, keepdims=True) + epsilon)
        normed_moe_out[...] = (residual * inv * gains_out[1:2]).astype(bf16)
        logits = jnp.dot(
            normed_moe_out[...], small_out[...].reshape(width, 128), preferred_element_type=f32
        )
        logits = jnp.where(chosen > 0.5, logits, -1e30)
        lifted = jnp.exp(logits - jnp.max(logits, axis=-1, keepdims=True)) * chosen
        gates_out[...] = lifted / jnp.sum(lifted, axis=-1, keepdims=True)
        turned(mixed_out[...], mixed_turned)

    start(to_z(first, 1))
    start(to_z(first, 0))
    start(to_y(first, 0))
    dy_x(0).start()

    arrived(to_z(first, 0))
    start(to_y(first, 1))
    start(to_x(first, 1, 0))
    arrived(to_z(first, 1))
    start(to_z(first, 2))
    start(to_y(first, 2))
    start(to_x(first, 2, 0))
    start(to_z(second, 1))
    start(to_z(second, 0))
    start(to_y(second, 0))
    dy_x(0).wait_recv()
    dy_c(0).start()
    arrived(to_y(first, 0))
    start(to_x(first, 0, 1))
    load_down.wait()
    group(0)
    arrived(to_z(first, 2))
    start(to_y(first, 3))
    start(to_x(first, 3, 0))
    arrived(to_z(second, 0))
    start(to_y(second, 1))
    start(to_x(second, 1, 0))
    arrived(to_z(second, 1))
    start(to_z(second, 2))
    start(to_y(second, 2))
    start(to_x(second, 2, 0))
    dy_z(1).start()
    dy_z(0).start()
    arrived(to_y(first, 1))
    start(to_x(first, 1, 1))
    arrived(to_y(first, 2))
    start(to_x(first, 2, 1))
    for m, k in ((1, 0), (2, 0), (0, 1), (3, 0), (1, 1)):
        arrived(to_x(first, m, k))
        start(to_c(first, m, k))
    arrived(to_y(first, 3))
    start(to_x(first, 3, 1))
    arrived(to_x(first, 2, 1))
    start(to_c(first, 2, 1))
    arrived(to_z(second, 2))
    start(to_y(second, 3))
    start(to_x(second, 3, 0))
    arrived(to_y(second, 0))
    start(to_x(second, 0, 1))
    arrived(to_x(first, 3, 1))
    start(to_c(first, 3, 1))
    for m, k in ((1, 0), (2, 0), (0, 1), (3, 0), (1, 1), (2, 1), (3, 1)):
        arrived(to_c(first, m, k))
    keep_qkv.start()
    project()
    turned(normed_out[...], normed_turned)
    arrived(to_y(second, 1))
    start(to_x(second, 1, 1))
    arrived(to_y(second, 2))
    start(to_x(second, 2, 1))
    dy_z(0).wait_recv()
    dy_x(1).start()
    attend(0)
    dy_z(1).wait_recv()
    dy_z(2).start()
    dy_x(2).start()
    attend(1)
    for m, k in ((1, 0), (2, 0), (0, 1), (3, 0), (1, 1), (2, 1)):
        arrived(to_x(second, m, k))
        start(to_c(second, m, k))
    arrived(to_y(second, 3))
    start(to_x(second, 3, 1))
    attend(2)
    dy_x(1).wait_recv()
    dy_c(1).start()
    attend(3)
    arrived(to_x(second, 3, 1))
    start(to_c(second, 3, 1))
    group(1)
    dy_z(2).wait_recv()
    dy_x(3).start()
    for m, k in ((1, 0), (2, 0), (0, 1), (3, 0), (1, 1), (2, 1), (3, 1)):
        arrived(to_c(second, m, k))
    keep_output.start()
    close_block()
    dy_x(2).wait_recv()
    dy_c(2).start()
    group(2)
    dy_x(3).wait_recv()
    dy_c(3).start()
    group(3)

    keep_qkv.wait()
    keep_output.wait()
    for m in range(ZLINE):
        keep_dy(m).wait()
        if m >= 2:
            keep_grads(m).wait()
    every = first + second
    for step in range(3):
        for made in to_z(every, step):
            made.wait_send()
        dy_z(step).wait_send()
    for m in range(ZLINE):
        for made in to_y(every, m):
            made.wait_send()
        dy_x(m).wait_send()
        dy_c(m).wait_send()
        for k in range(2):
            if m or k:
                for made in to_x(every, m, k) + to_c(every, m, k):
                    made.wait_send()


def gather(rows_y, weights, dy, *rest):
    w_down = rest[-1]
    n, router_wide = weights[4].shape
    dp_size = ZLINE * rows_y
    owned, _, width = w_down.shape
    hidden = F // ZLINE
    length = dy.shape[0]
    count = 4 * length
    qkv_wide = weights[0].shape[1] + weights[1].shape[1] + weights[2].shape[1]
    any_space = pl.BlockSpec(memory_space=pl.ANY)
    vmem = pl.BlockSpec(memory_space=pltpu.VMEM)
    sems = pltpu.SemaphoreType.DMA

    def rows(wide, dtype=bf16):
        return jax.ShapeDtypeStruct((length, wide), dtype)

    turned = jax.ShapeDtypeStruct((dp_size, 2, 2, n // 4, length), bf16)
    return pl.pallas_call(
        functools.partial(gather_kernel, rows_y, n // 12),
        name="gather",
        out_shape=(
            jax.ShapeDtypeStruct((dp_size, n, qkv_wide), bf16),
            jax.ShapeDtypeStruct((dp_size, n, width), bf16),
            jax.ShapeDtypeStruct((ZLINE, count, width + 128), bf16),
            jax.ShapeDtypeStruct((ZLINE, count, owned * hidden), bf16),
            jax.ShapeDtypeStruct((dp_size, n, 128), bf16),
            rows(H * HD),
            rows(KV * HD),
            rows(KV * HD),
            rows(width, f32),
            rows(width),
            turned,
            turned,
            jax.ShapeDtypeStruct((8, width), f32),
            rows(128, f32),
            rows(length, f32),
        ),
        in_specs=[vmem] * (len(weights) + len(rest)) + [any_space],
        out_specs=(any_space,) * 4 + (vmem,) * 11,
        scratch_shapes=[
            pltpu.VMEM((dp_size, n, qkv_wide), bf16),
            pltpu.VMEM((dp_size, n, width), bf16),
            pltpu.VMEM((ZLINE, count, width + 128), bf16),
            pltpu.VMEM((owned, hidden, width), bf16),
            pltpu.VMEM((2, count, owned * hidden), bf16),
            pltpu.VMEM((length, qkv_wide), f32),
            pltpu.VMEM((length, width), bf16),
            pltpu.VMEM((length, H * HD), bf16),
            sems((3, 3)),
            sems((3, 3)),
            sems((3, ZLINE)),
            sems((3, ZLINE)),
            sems((3, dp_size)),
            sems((3, dp_size)),
            sems((3, dp_size)),
            sems((3, dp_size)),
            sems((3,)),
            sems((3,)),
            sems((ZLINE,)),
            sems((ZLINE,)),
            sems((ZLINE,)),
            sems((ZLINE,)),
            sems,
            sems((ZLINE,)),
            sems((2,)),
            sems((2,)),
        ],
        compiler_params=pltpu.CompilerParams(
            collective_id=2, has_side_effects=True, vmem_limit_bytes=60 * 2**20
        ),
    )(*weights, dy, *rest)


MOE_COPIES = 30


def moe_kernel(
    rows_y,
    normed_ref,
    dy_hbm,
    plain_hbm,
    gate_up_hbm,
    down_hbm,
    router_ref,
    rows_out,
    grads_out,
    down_out,
    combined_out,
    heard_out,
    total_ref,
    w_gate,
    w_up,
    w_down,
    rows,
    masks,
    plain,
    grads,
    acts,
    gate_grads,
    part_down,
    heard_down,
    stage_down,
    parts,
    heard_c,
    heard_x,
    heard_z,
    combined,
    heard_combined,
    spread_ref,
    sends,
    recvs,
    d_send,
    d_recv,
    load_sems,
    plain_sems,
    dy_sems,
    rows_sems,
    grads_sems,
    down_sems,
    combined_sems,
):
    owned, hidden = w_down.shape[:2]
    length, width = normed_ref.shape
    count = rows.shape[1]
    tokens = ZLINE * count
    half = count // 2
    span = owned * hidden
    dp = lax.axis_index("dp")
    z, y = dp // rows_y, dp % rows_y
    to = partners(rows_y)
    to["z3"] = (other(to["z1"][0], 2 * rows_y), lax.axis_index("expert"))
    links = Links(sends, recvs)

    loads = []
    mine = pl.ds(pl.multiple_of(z * hidden, hidden), hidden)
    theirs = pl.ds(pl.multiple_of(F + z * hidden, hidden), hidden)
    for e in range(owned):
        at = pl.ds(e * hidden, hidden)
        for k, (cut, kept) in enumerate(((mine, w_gate), (theirs, w_up))):
            loads.append(
                pltpu.make_async_copy(
                    gate_up_hbm.at[e, :, cut], kept.at[:, at], load_sems.at[2 * e + k]
                )
            )
    loads.append(
        pltpu.make_async_copy(dy_hbm.at[:, :, pl.ds(width, 128)], masks, load_sems.at[2 * owned])
    )
    load_down = pltpu.make_async_copy(
        down_hbm.at[:, mine, :], w_down, load_sems.at[2 * owned + 1]
    )
    for load in loads:
        load.start()

    def fetch(r):
        return pltpu.make_async_copy(plain_hbm.at[r], plain.at[r % 2], plain_sems.at[r % 2])

    fetch(0).start()
    fetch(1).start()
    load_down.start()
    rows[0, :length] = normed_ref[...]
    first = lax.axis_index("expert") * owned
    expert = first + lax.broadcasted_iota(jnp.int32, (128, span), 1) // hidden
    spread_ref[...] = (
        (lax.broadcasted_iota(jnp.int32, (128, span), 0) == expert).astype(f32).astype(bf16)
    )
    greet([to[name] for name in ("z1", "z2", "z3", "y", "x", "c")])

    own = pl.ds(0, length)
    pair = pl.ds(length, length)
    near, far = pl.ds(0, half), pl.ds(half, half)

    def row_x(r):
        return links.copy(rows.at[r, own], rows.at[r, pair], to["x"])

    def row_c(r):
        return links.copy(rows.at[r, near], rows.at[r, far], to["c"])

    z1 = links.copy(rows.at[0, own], rows.at[1, own], to["z1"])
    z2 = links.copy(rows.at[0, own], rows.at[2, own], to["z2"])
    x0 = row_x(0)
    for load in loads:
        load.wait()
    x0.wait_recv()
    c0 = row_c(0)
    c0.wait_recv()

    def keep_rows(r):
        return pltpu.make_async_copy(rows.at[r], rows_out.at[r], rows_sems.at[r])

    def keep_grads(r):
        return pltpu.make_async_copy(grads.at[min(r, 1)], grads_out.at[r], grads_sems.at[r])

    def forward(r):
        slot, held = r % 2, min(r, 1)
        keep_rows(r).start()
        fetch(r).wait()
        if r >= 2:
            keep_grads(r - 1).wait()
        logits = jnp.dot(rows[r], router_ref[...], preferred_element_type=f32)
        mask = masks[r].astype(f32) > 0.5
        logits = jnp.where(mask, logits, -1e30)
        lifted = jnp.where(
            mask, jnp.exp(logits - jnp.max(logits, axis=-1, keepdims=True)), 0.0
        )
        gates = lifted / jnp.sum(lifted, axis=-1, keepdims=True)
        gates_high = gates.astype(bf16)
        gates_low = (gates - gates_high.astype(f32)).astype(bf16)
        gate_grads[...] = jnp.zeros_like(gate_grads)

        def step(p, _):
            at = pl.ds(pl.multiple_of(p * 2 * hidden, 2 * hidden), 2 * hidden)
            up_at = pl.ds(pl.multiple_of(span + p * 2 * hidden, 2 * hidden), 2 * hidden)
            spread = spread_ref[:, at]
            gate_part = jnp.dot(rows[r], w_gate[:, at], preferred_element_type=f32)
            up_part = jnp.dot(rows[r], w_up[:, at], preferred_element_type=f32)
            plain_grad = plain[slot, :, at].astype(f32)
            spread_gates = jnp.dot(gates_high, spread, preferred_element_type=f32) + jnp.dot(
                gates_low, spread, preferred_element_type=f32
            )
            sigmoid_gate = 1.0 / (1.0 + jnp.exp(-gate_part))
            swished = gate_part * sigmoid_gate
            activation = swished * up_part
            gate_grads[...] += against((plain_grad * activation).astype(bf16), spread)
            acts[r, :, at] = (spread_gates * activation).astype(bf16)
            grad_act = plain_grad * spread_gates
            grads[held, :, at] = (
                grad_act * up_part * (sigmoid_gate + swished * (1.0 - sigmoid_gate))
            ).astype(bf16)
            grads[held, :, up_at] = (grad_act * swished).astype(bf16)
            return 0

        lax.fori_loop(0, owned // 2, step, 0, unroll=True)
        parts[r, :, width:] = gate_grads[...].astype(bf16)
        if r + 2 < ZLINE:
            fetch(r + 2).start()
        keep_grads(r).start()

    def backward(r):
        held = min(r, 1)

        def step(j, _):
            at = pl.ds(pl.multiple_of(j * 768, 768), 768)
            part = against(grads[held, :, :span], w_gate[at, :]) + against(
                grads[held, :, span:], w_up[at, :]
            )
            parts[r, :, at] = part.astype(bf16)
            return 0

        lax.fori_loop(0, width // 768, step, 0)

    def add(left, right):
        return (left[...].astype(f32) + right[...].astype(f32)).astype(bf16)

    made = {}

    def sum_c(r):
        made["c", r] = links.copy(parts.at[r, far], heard_c.at[r], to["c"])

    def sum_x(r):
        made["c", r].wait_recv()
        parts[r, near] = add(parts.at[r, near], heard_c.at[r])
        made["x", r] = links.copy(parts.at[r, pair], heard_x.at[r], to["x"])

    def sum_z(r):
        made["x", r].wait_recv()
        parts[r, own] = add(parts.at[r, own], heard_x.at[r])
        if r:
            made["z", r] = links.copy(parts.at[r, own], heard_z.at[r - 1], to[f"z{r}"])

    def keep_combined(r):
        return pltpu.make_async_copy(
            combined.at[r % 2, near], combined_out.at[r], combined_sems.at[r]
        )

    def combine(r):
        slot = r % 2
        if r >= 2:
            made["oc", r - 2].wait_send()
            keep_combined(r - 2).wait()
            out_x(r - 2)

        def step(j, _):
            at = pl.ds(pl.multiple_of(j * 512, 512), 512)
            down = w_down[:, :, at].reshape(span, 512)
            combined[slot, :, at] = jnp.dot(
                acts[r], down, preferred_element_type=f32
            ).astype(bf16)
            return 0

        lax.fori_loop(0, width // 512, step, 0)
        made["oc", r] = links.copy(combined.at[slot, far], heard_combined.at[r], to["c"])

    def out_c(r):
        made["oc", r].wait_recv()
        combined[r % 2, near] = add(combined.at[r % 2, near], heard_combined.at[r])
        keep_combined(r).start()

    def out_x(r):
        made["ox", r] = links.copy(combined_out.at[r, pair], heard_out.at[r], to["x"])

    def fetch_dy(r):
        return pltpu.make_async_copy(
            dy_hbm.at[r, :, pl.ds(0, width)], rows.at[r], dy_sems.at[r]
        )

    def send_down(e):
        return pltpu.make_async_remote_copy(
            src_ref=part_down.at[e, 1 - y],
            dst_ref=heard_down.at[e],
            send_sem=d_send.at[e],
            recv_sem=d_recv.at[e],
            device_id=to["y"],
            device_id_type=pl.DeviceIdType.MESH,
        )

    def down(p, _):
        at = pl.ds(pl.multiple_of(p * 2 * hidden, 2 * hidden), 2 * hidden)
        left = acts[:, :, at].reshape(tokens, 2 * hidden)

        def step(j, _):
            columns = pl.ds(pl.multiple_of(j * 768, 768), 768)
            result = transposed(left, rows[:, :, columns].reshape(tokens, 768)).astype(bf16)
            for k in range(2):
                for i in range(rows_y):
                    first = k * hidden + i * (hidden // rows_y)
                    part_down[2 * p + k, i, :, columns] = result[
                        first : first + hidden // rows_y
                    ]
            return 0

        lax.fori_loop(0, width // 768, step, 0)
        for k in range(2):
            send_down(2 * p + k).start()
        return 0

    def keep_down(e):
        return pltpu.make_async_copy(
            stage_down.at[lax.rem(e, 2)], down_out.at[e], down_sems.at[lax.rem(e, 2)]
        )

    def finish_down(e, _):
        @pl.when(e >= 2)
        def _():
            keep_down(e - 2).wait()

        send_down(e).wait_recv()
        stage_down[lax.rem(e, 2)] = add(part_down.at[e, y], heard_down.at[e])
        keep_down(e).start()
        return 0

    forward(0)
    z1.wait_recv()
    x1 = row_x(1)
    z2.wait_recv()
    z3 = links.copy(rows.at[2, own], rows.at[3, own], to["z1"])
    x2 = row_x(2)
    load_down.wait()
    combine(0)
    x1.wait_recv()
    c1 = row_c(1)
    c1.wait_recv()
    forward(1)
    z3.wait_recv()
    x3 = row_x(3)
    backward(1)
    sum_c(1)
    x2.wait_recv()
    c2 = row_c(2)
    out_c(0)
    sum_x(1)
    c2.wait_recv()
    forward(2)
    backward(2)
    sum_c(2)
    sum_z(1)
    x3.wait_recv()
    c3 = row_c(3)
    sum_x(2)
    c3.wait_recv()
    forward(3)
    backward(3)
    sum_c(3)
    backward(0)
    sum_x(3)
    sum_c(0)
    sum_z(2)
    for r in range(ZLINE):
        keep_rows(r).wait()
    gathered = (z1, z2, z3, x0, x1, x2, x3, c0, c1, c2, c3)
    for copy in gathered:
        copy.wait_send()
    for r in range(ZLINE):
        fetch_dy(r).start()
    sum_x(0)
    combine(1)
    for r in range(ZLINE):
        fetch_dy(r).wait()
    lax.fori_loop(0, 1, down, 0)
    sum_z(3)
    out_c(1)
    lax.fori_loop(1, 2, down, 0)
    combine(2)
    lax.fori_loop(2, 3, down, 0)
    sum_z(0)
    out_c(2)
    combine(3)
    lax.fori_loop(3, owned // 2, down, 0)
    out_c(3)
    total = parts[0, own].astype(f32)
    for r in (1, 2, 3):
        made["z", r].wait_recv()
        total = total + heard_z[r - 1].astype(f32)
    total_ref[...] = total
    for r in (2, 3):
        keep_combined(r).wait()
        out_x(r)
    lax.fori_loop(0, owned, finish_down, 0)
    for r in range(ZLINE):
        made["ox", r].wait_recv()
    done = gathered + (made["oc", 0], made["oc", 1])
    links.open = [v for v in links.open if not any(v is copy for copy in done)]
    links.close()
    for e in range(owned):
        send_down(e).wait_send()
    for e in (owned - 2, owned - 1):
        keep_down(e).wait()
    for r in (0, ZLINE - 1):
        keep_grads(r).wait()


def moe(rows_y, normed, dy, plain, w_gate_up, w_down, router):
    owned, width, _ = w_gate_up.shape
    hidden = F // ZLINE
    length = normed.shape[0]
    count = dy.shape[1]
    any_space = pl.BlockSpec(memory_space=pl.ANY)
    vmem = pl.BlockSpec(memory_space=pltpu.VMEM)
    sems = pltpu.SemaphoreType.DMA
    span = owned * hidden
    wide = width + 128
    return pl.pallas_call(
        functools.partial(moe_kernel, rows_y),
        name="moe",
        out_shape=(
            jax.ShapeDtypeStruct((ZLINE, count, width), bf16),
            jax.ShapeDtypeStruct((ZLINE, count, 2 * span), bf16),
            jax.ShapeDtypeStruct((owned, hidden // rows_y, width), bf16),
            jax.ShapeDtypeStruct((ZLINE, count // 2, width), bf16),
            jax.ShapeDtypeStruct((ZLINE, length, width), bf16),
            jax.ShapeDtypeStruct((length, wide), f32),
        ),
        in_specs=[vmem, any_space, any_space, any_space, any_space, vmem],
        out_specs=(any_space,) * 5 + (vmem,),
        scratch_shapes=[
            pltpu.VMEM((width, span), bf16),
            pltpu.VMEM((width, span), bf16),
            pltpu.VMEM((owned, hidden, width), bf16),
            pltpu.VMEM((ZLINE, count, width), bf16),
            pltpu.VMEM((ZLINE, count, 128), bf16),
            pltpu.VMEM((2, count, span), bf16),
            pltpu.VMEM((2, count, 2 * span), bf16),
            pltpu.VMEM((ZLINE, count, span), bf16),
            pltpu.VMEM((count, 128), f32),
            pltpu.VMEM((owned, rows_y, hidden // rows_y, width), bf16),
            pltpu.VMEM((owned, hidden // rows_y, width), bf16),
            pltpu.VMEM((2, hidden // rows_y, width), bf16),
            pltpu.VMEM((ZLINE, count, wide), bf16),
            pltpu.VMEM((ZLINE, count // 2, wide), bf16),
            pltpu.VMEM((ZLINE, length, wide), bf16),
            pltpu.VMEM((ZLINE - 1, length, wide), bf16),
            pltpu.VMEM((2, count, width), bf16),
            pltpu.VMEM((ZLINE, count // 2, width), bf16),
            pltpu.VMEM((128, span), bf16),
            sems((MOE_COPIES,)),
            sems((MOE_COPIES,)),
            sems((owned,)),
            sems((owned,)),
            sems((2 * owned + 2,)),
            sems((2,)),
            sems((ZLINE,)),
            sems((ZLINE,)),
            sems((ZLINE,)),
            sems((2,)),
            sems((ZLINE,)),
        ],
        compiler_params=pltpu.CompilerParams(
            collective_id=1, has_side_effects=True, vmem_limit_bytes=63 * 2**20
        ),
    )(normed, dy, plain, w_gate_up, w_down, router)


def finish_kernel(
    rows_y,
    rows_hbm,
    grads_hbm,
    combined_hbm,
    heard_hbm,
    w_output_hbm,
    w_qkv_hbm,
    row_grads,
    gates,
    cotangent,
    residual,
    normed_moe,
    gains,
    router,
    tokens_ref,
    mixed,
    normed,
    queries,
    keys,
    values,
    allowed,
    cosine,
    sine,
    gate_up_out,
    output_out,
    grad_tokens_out,
    out_0,
    out_1,
    out_2,
    rows,
    turned,
    grads,
    part_gate_up,
    heard_gate_up,
    heard_z,
    stage,
    o_own,
    o_x,
    o_z1,
    o_z2,
    w_output,
    w_qkv,
    grad_qkv,
    grad_normed,
    left_output,
    left_qkv,
    right_output,
    right_qkv,
    part_small,
    grad_residual,
    grad_branch,
    base_small,
    *refs,
):
    owned, n = gate_up_out.shape[:2]
    hidden = F // ZLINE
    count, width = rows.shape
    length = tokens_ref.shape[0]
    tokens = ZLINE * count
    dp, ex = lax.axis_index("dp"), lax.axis_index("expert")
    z, y = dp // rows_y, dp % rows_y
    core, side = ex % 2, (ex // 2) % 2
    to = partners(rows_y)
    to["z3"] = (other(to["z1"][0], 2 * rows_y), ex)
    to["xc"] = (dp, other(other(ex, 1), 2))
    z_of = [z, other(z, 1), other(z, 2), other(other(z, 1), 2)]
    half, quarter = n // 2, n // 4
    of_core = pl.ds(pl.multiple_of(core * half, 16), half)
    of_sibling = pl.ds(pl.multiple_of((1 - core) * half, 16), half)
    of_side = pl.ds(pl.multiple_of(side * quarter, 16), quarter)
    of_far_side = pl.ds(pl.multiple_of((1 - side) * quarter, 16), quarter)
    mine = pl.ds(pl.multiple_of(core * half + side * quarter, 16), quarter)
    (
        load_sem,
        own_sems,
        weight_sems,
        grads_sems,
        store_sems,
        y_send,
        y_recv,
        z_send,
        z_recv,
        a_send,
        a_recv,
        f_send,
        f_recv,
        o_send,
        o_recv,
    ) = refs[18:]

    def remote(source, target, send_sem, recv_sem, device):
        return pltpu.make_async_remote_copy(
            src_ref=source,
            dst_ref=target,
            send_sem=send_sem,
            recv_sem=recv_sem,
            device_id=device,
            device_id_type=pl.DeviceIdType.MESH,
        )

    def add(left, right):
        return (left.astype(f32) + right.astype(f32)).astype(bf16)

    def load_rows(r):
        return pltpu.make_async_copy(rows_hbm.at[r], rows, load_sem)

    def load_grads(e, k):
        at = pl.ds(pl.multiple_of((k * owned + e) * hidden, hidden), hidden)
        return pltpu.make_async_copy(
            grads_hbm.at[:, :, at],
            grads.at[lax.rem(e, 2), :, :, pl.ds(k * hidden, hidden)],
            grads_sems.at[lax.rem(e, 2), k],
        )

    load_combined = [
        pltpu.make_async_copy(combined_hbm.at[:, pl.ds(0, length)], o_own, own_sems.at[0]),
        pltpu.make_async_copy(heard_hbm, o_x, own_sems.at[1]),
    ]

    def o_copy(k):
        if k < 2:
            return remote(o_own.at[1 + 2 * k], o_z1.at[k], o_send.at[k], o_recv.at[k], to["z1"])
        return remote(o_own.at[2], o_z2, o_send.at[k], o_recv.at[k], to["z2"])

    def o_start():
        for load in load_combined:
            load.wait()
        for r in (3, 1, 2, 0):
            o_own[r] = add(o_own[r], o_x[r])
            if r % 2:
                o_copy(r // 2).start()

    def o_after_z1():
        for k in (1, 0):
            o_copy(k).wait_recv()
            o_own[2 * k] = add(o_own[2 * k], o_z1[k])
            if k:
                o_copy(2).start()

    def o_end():
        o_copy(2).wait_recv()
        total = o_own[0].astype(f32) + o_z2[...].astype(f32)
        output_out[...] = (residual[...] + total).astype(bf16)

    def left_copies(k, source, target):
        made = []
        for m, name in ((1, "c"), (2, "x"), (3, "xc")):
            c = 1 - core if m % 2 else core
            s = 1 - side if m // 2 else side
            made.append(
                remote(
                    source.at[:, c, s],
                    target.at[:, :, pl.ds(m * length, length)],
                    f_send.at[k, m],
                    f_recv.at[k, m],
                    to[name],
                )
            )
        return made

    def right_copy(k, source, target, m):
        if m == 3:
            source = target.at[pl.ds(2 * length, length)]
        return remote(
            source,
            target.at[pl.ds(m * length, length)],
            f_send.at[k, m],
            f_recv.at[k, m],
            to["x" if m == 2 else "c"],
        )

    class Sum:
        def __init__(self, k, out, rows):
            self.k, self.out, self.rows = k, out, rows
            self.own, self.c, self.x, self.y, self.z1, self.z2 = refs[6 * k : 6 * k + 6]

        def copy(self, step, source, target, device):
            return remote(
                source, target, a_send.at[self.k, step], a_recv.at[self.k, step], device
            )

        def to_y(self, b):
            return self.copy(8 + b, self.own.at[b, 1 - y, self.rows], self.y.at[b], to["y"])

        def to_z1(self, m):
            return self.copy(
                1 + m, self.own.at[z_of[1 + 2 * m], y, self.rows], self.z1.at[m], to["z1"]
            )

        def to_z2(self):
            return self.copy(3, self.own.at[z_of[2], y, self.rows], self.z2, to["z2"])

        def back_x(self):
            return self.copy(4, self.out.at[mine], self.out.at[mine], to["x"])

        def back_c(self):
            return self.copy(5, self.out.at[of_core], self.out.at[of_core], to["c"])

        def to_c(self):
            return self.copy(6, part_small.at[:, :, of_sibling], self.c, to["c"])

        def to_x(self):
            return self.copy(7, self.own.at[:, :, of_far_side], self.x, to["x"])

        def after_c(self):
            self.to_c().wait_recv()
            for b in range(ZLINE):
                for k in range(rows_y):
                    self.own[b, k] = add(part_small[b, k, of_core], self.c[b, k])
            self.to_x().start()

        def after_x(self):
            self.to_x().wait_recv()
            for b in range(ZLINE):
                for k in range(rows_y):
                    self.own[b, k, self.rows] = add(self.own[b, k, self.rows], self.x[b, k])
            self.along_y()

        def along_y(self):
            for b in range(ZLINE):
                self.to_y(b).start()

        def after_y(self):
            for b in range(ZLINE):
                self.to_y(b).wait_recv()
                self.own[b, y, self.rows] = add(self.own[b, y, self.rows], self.y[b])
            for m in (1, 0):
                self.to_z1(m).start()

        def after_z1(self):
            for m in (1, 0):
                self.to_z1(m).wait_recv()
                at = z_of[2 * m]
                self.own[at, y, self.rows] = add(self.own[at, y, self.rows], self.z1[m])
                if m:
                    self.to_z2().start()

        def after_z2(self):
            self.to_z2().wait_recv()
            self.out[mine] = add(self.own[z, y, self.rows], self.z2[...])
            self.back_x().start()

        def after_back(self):
            self.back_x().wait_recv()
            self.back_c().start()

        def close(self):
            self.back_c().wait()
            for made in (self.to_z1(0), self.to_z1(1), self.to_z2(), self.back_x()):
                made.wait_send()
            for b in range(ZLINE):
                self.to_y(b).wait_send()

    whole = pl.ds(0, quarter)
    output = Sum(0, out_0, whole)
    small = Sum(1, out_1, of_side)
    qkv = Sum(2, out_2, whole)

    def products(array, left, right):
        rows_all = left[...].reshape(ZLINE * rows_y * quarter, 4 * length)

        def step(j, _):
            at = pl.ds(pl.multiple_of(j * 512, 512), 512)
            result = jnp.dot(rows_all, right[:, at], preferred_element_type=f32).astype(bf16)
            array.own[:, :, :, at] = result.reshape(ZLINE, rows_y, quarter, 512)
            return 0

        lax.fori_loop(0, right.shape[1] // 512, step, 0)
        array.along_y()

    def load_output(i):
        step = w_output.shape[1]
        at = pl.ds(pl.multiple_of(i * step, step), step)
        return pltpu.make_async_copy(
            w_output_hbm.at[at], w_output.at[lax.rem(i, 2)], weight_sems.at[0, lax.rem(i, 2)]
        )

    def load_qkv(i):
        step = w_qkv.shape[1]
        at = pl.ds(pl.multiple_of(i * step, step), step)
        return pltpu.make_async_copy(
            w_qkv_hbm.at[at], w_qkv.at[lax.rem(i, 2)], weight_sems.at[1, lax.rem(i, 2)]
        )

    def unrotate(value):
        lanes = value.shape[1]
        lane = lax.broadcasted_iota(jnp.int32, value.shape, 1)
        swapped = jnp.where(
            lane % HD < HD // 2,
            pltpu.roll(value, lanes - HD // 2, 1),
            pltpu.roll(value, HD // 2, 1),
        )
        return (value * cosine[:, :lanes] + swapped * sine[:, :lanes]).astype(bf16)

    per_group = H // KV
    wide = GROUP * per_group * HD
    narrow = GROUP * HD

    def attend(i, _):
        load_output(i).wait()
        at = pl.ds(pl.multiple_of(i * wide, wide), wide)
        kv_at = pl.ds(pl.multiple_of(i * narrow, narrow), narrow)
        grad_mixed = against(grad_branch[...], w_output[lax.rem(i, 2)]).astype(bf16)
        query, key, value = queries[:, at], keys[:, kv_at], values[:, kv_at]
        is_allowed = allowed[...] > 0.5
        grad_queries, grad_keys, grad_values = [], [], []
        for k in range(GROUP):
            k_head, v_head = key[:, k * HD : (k + 1) * HD], value[:, k * HD : (k + 1) * HD]
            grad_k = grad_v = None
            for j in range(k * per_group, (k + 1) * per_group):
                q_head = query[:, j * HD : (j + 1) * HD]
                mixed_head = grad_mixed[:, j * HD : (j + 1) * HD]
                scores = jnp.where(is_allowed, against(q_head, k_head) * 0.125, -1e30)
                lifted = jnp.exp(scores - jnp.max(scores, axis=-1, keepdims=True))
                weights = lifted / jnp.sum(lifted, axis=-1, keepdims=True)
                grad_weights = against(mixed_head, v_head)
                inner = jnp.sum(weights * grad_weights, axis=-1, keepdims=True)
                grad_scores = (weights * (grad_weights - inner)).astype(bf16)
                part_v = transposed(weights.astype(bf16), mixed_head)
                part_k = transposed(grad_scores, q_head)
                grad_v = part_v if grad_v is None else grad_v + part_v
                grad_k = part_k if grad_k is None else grad_k + part_k
                grad_queries.append(
                    jnp.dot(grad_scores, k_head, preferred_element_type=f32) * 0.125
                )
            grad_keys.append(grad_k * 0.125)
            grad_values.append(grad_v)
        grad_qkv[:, at] = unrotate(jnp.concatenate(grad_queries, axis=1))
        k_at = pl.ds(pl.multiple_of(H * HD + i * narrow, narrow), narrow)
        v_at = pl.ds(pl.multiple_of((H + KV) * HD + i * narrow, narrow), narrow)
        grad_qkv[:, k_at] = unrotate(jnp.concatenate(grad_keys, axis=1))
        grad_qkv[:, v_at] = jnp.concatenate(grad_values, axis=1).astype(bf16)

        @pl.when(i + 2 < KV // GROUP)
        def _():
            load_output(i + 2).start()

        return 0

    def column(value, lane):
        at_lane = lax.broadcasted_iota(jnp.int32, (length, 128), 1) == lane
        at_lane = at_lane.astype(f32).astype(bf16)
        high = value.astype(bf16)
        low = (value - high.astype(f32)).astype(bf16)
        return transposed(high, at_lane) + transposed(low, at_lane)

    def norm_grads():
        grad_gates = row_grads[:, width:]
        inner = jnp.sum(gates[...] * grad_gates, axis=-1, keepdims=True)
        grad_logits = (gates[...] * (grad_gates - inner)).astype(bf16)
        grad_normed_moe = row_grads[:, :width] + against(grad_logits, router[...])
        inv = lax.rsqrt(jnp.mean(residual[...] * residual[...], axis=-1, keepdims=True) + epsilon)
        unit = residual[...] * inv
        scaled = grad_normed_moe * gains[1:2]
        total = cotangent[...].astype(f32) + inv * (
            scaled - unit * jnp.mean(scaled * unit, axis=-1, keepdims=True)
        )
        grad_residual[...] = total
        grad_branch[...] = total.astype(bf16)
        base_small[...] = transposed(normed_moe[...], grad_logits) + column(
            grad_normed_moe * unit, EXPERTS + 1
        )

    def input_grads():
        tile = w_qkv.shape[1]

        def step(i, _):
            load_qkv(i).wait()
            at = pl.ds(pl.multiple_of(i * tile, tile), tile)
            grad_normed[:, at] = against(grad_qkv[...], w_qkv[lax.rem(i, 2)])

            @pl.when(i + 2 < width // tile)
            def _():
                load_qkv(i + 2).start()

            return 0

        lax.fori_loop(0, width // tile, step, 0)
        inputs = tokens_ref[...].astype(f32)
        inv = lax.rsqrt(jnp.mean(inputs * inputs, axis=-1, keepdims=True) + epsilon)
        unit = inputs * inv
        onto = grad_normed[...] * unit
        scaled = grad_normed[...] * gains[:1]
        grad_tokens_out[...] = (
            grad_residual[...]
            + inv * (scaled - unit * jnp.mean(scaled * unit, axis=-1, keepdims=True))
        ).astype(bf16)
        part = base_small[...] + column(onto, EXPERTS)
        part_small[...] = part.astype(bf16).reshape(part_small.shape)
        small.to_c().start()

    load_rows(0).start()
    for load in load_combined:
        load.start()
    for e in range(2):
        for k in range(2):
            load_grads(e, k).start()
    for i in range(2):
        load_output(i).start()
        load_qkv(i).start()
    norm_grads()
    greet([to[name] for name in ("z1", "z2", "z3", "y", "x", "c", "xc")])
    own_tokens = pl.ds(0, length)
    lefts = left_copies(0, mixed, left_output) + left_copies(1, normed, left_qkv)
    rights = {m: right_copy(2, grad_branch, right_output, m) for m in (1, 2, 3)}
    qkv_rights = {m: right_copy(3, grad_qkv, right_qkv, m) for m in (1, 2, 3)}
    rights[2].start()
    rights[1].start()
    for made in lefts:
        made.start()
    left_output[:, :, own_tokens] = mixed[:, core, side]
    left_qkv[:, :, own_tokens] = normed[:, core, side]
    right_output[own_tokens] = grad_branch[...]
    o_start()

    for r in range(ZLINE):
        load_rows(r).wait()

        def turn(j, _, r=r):
            at = pl.ds(pl.multiple_of(j * 256, 256), 256)
            turned[at, pl.ds(r * count, count)] = rows[:, at].T
            return 0

        lax.fori_loop(0, width // 256, turn, 0)
        if r + 1 < ZLINE:
            load_rows(r + 1).start()

    def send_y(e):
        return remote(
            part_gate_up.at[e, 1 - y], heard_gate_up.at[e], y_send.at[e], y_recv.at[e], to["y"]
        )

    def send_z(e, m):
        return remote(
            part_gate_up.at[e, y, z_of[m]],
            heard_z.at[m - 1, e],
            z_send.at[m - 1, e],
            z_recv.at[m - 1, e],
            to[f"z{m}"],
        )

    def reduce(e):
        send_y(e).wait_recv()
        for b in range(ZLINE):
            part_gate_up[e, y, b] = add(part_gate_up[e, y, b], heard_gate_up[e, b])
        for m in range(1, ZLINE):
            send_z(e, m).start()

    def gate_up(e, _):
        for k in range(2):
            load_grads(e, k).wait()
        right = grads[lax.rem(e, 2)].reshape(tokens, 2 * hidden)

        def step(b, _):
            at = pl.ds(pl.multiple_of(b * rows_y * n, 128), rows_y * n)
            result = jnp.dot(turned[at, :], right, preferred_element_type=f32).astype(bf16)
            for k in range(rows_y):
                part_gate_up[e, k, b] = result[k * n : (k + 1) * n]
            return 0

        lax.fori_loop(0, ZLINE, step, 0)

        @pl.when(e + 2 < owned)
        def _():
            for k in range(2):
                load_grads(e + 2, k).start()

        return 0

    lax.fori_loop(0, 1, gate_up, 0)
    send_y(0).start()
    lax.fori_loop(1, 2, gate_up, 0)
    send_y(1).start()
    rights[2].wait_recv()
    rights[3].start()
    o_after_z1()
    for made in lefts:
        made.wait_recv()
    rights[1].wait_recv()
    rights[3].wait_recv()
    products(output, left_output, right_output)
    lax.fori_loop(0, KV // GROUP // 2, attend, 0)
    lax.fori_loop(2, 3, gate_up, 0)
    send_y(2).start()
    reduce(0)
    lax.fori_loop(KV // GROUP // 2, KV // GROUP, attend, 0)
    qkv_rights[2].start()
    qkv_rights[1].start()
    o_end()
    right_qkv[own_tokens] = grad_qkv[...]
    lax.fori_loop(3, 4, gate_up, 0)
    send_y(3).start()
    reduce(1)
    output.after_y()
    input_grads()
    lax.fori_loop(4, 5, gate_up, 0)
    send_y(4).start()
    qkv_rights[2].wait_recv()
    qkv_rights[3].start()
    reduce(2)
    qkv_rights[1].wait_recv()
    qkv_rights[3].wait_recv()
    products(qkv, left_qkv, right_qkv)
    small.after_c()
    reduce(3)
    output.after_z1()
    lax.fori_loop(5, 7, gate_up, 0)
    send_y(5).start()
    output.after_z2()
    lax.fori_loop(7, owned, gate_up, 0)
    small.after_x()
    reduce(4)
    send_y(6).start()
    qkv.after_y()
    send_y(7).start()
    output.after_back()
    reduce(5)
    send_y(8).start()
    small.after_y()
    reduce(6)
    send_y(9).start()
    qkv.after_z1()
    reduce(7)
    small.after_z1()
    qkv.after_z2()
    reduce(8)
    small.after_z2()
    qkv.after_back()
    small.after_back()
    reduce(9)

    def keep(e):
        return pltpu.make_async_copy(
            stage.at[lax.rem(e, 2)], gate_up_out.at[e], store_sems.at[lax.rem(e, 2)]
        )

    def collect(e, _):
        slot = lax.rem(e, 2)

        @pl.when(e >= 2)
        def _():
            keep(e - 2).wait()

        for m in range(ZLINE):
            if m:
                send_z(e, m).wait_recv()
                block = heard_z[m - 1, e]
            else:
                block = part_gate_up[e, y, z]
            for k in range(2):
                at = pl.ds(pl.multiple_of(k * F + z_of[m] * hidden, hidden), hidden)
                stage[slot, :, at] = block[:, k * hidden : (k + 1) * hidden]
        keep(e).start()
        return 0

    lax.fori_loop(0, owned, collect, 0)

    for e in (owned - 2, owned - 1):
        keep(e).wait()

    def close(e, _):
        send_y(e).wait_send()
        for m in range(1, ZLINE):
            send_z(e, m).wait_send()
        return 0

    lax.fori_loop(0, owned, close, 0)
    for array in (output, small, qkv):
        array.close()
    small.to_c().wait_send()
    small.to_x().wait_send()
    for k in range(3):
        o_copy(k).wait_send()
    for made in lefts + list(rights.values()) + list(qkv_rights.values()):
        made.wait_send()


def finish(rows_y, rows, grads, combined, heard, w_output, w_qkv, *small):
    _, count, width = rows.shape
    hidden = F // ZLINE
    owned = grads.shape[2] // (2 * hidden)
    length = small[0].shape[0]
    blocks = ZLINE * rows_y
    n = width // blocks
    columns = (w_output.shape[1], 128, w_qkv.shape[1])
    any_space = pl.BlockSpec(memory_space=pl.ANY)
    vmem = pl.BlockSpec(memory_space=pltpu.VMEM)
    sems = pltpu.SemaphoreType.DMA

    def summed(wide, own_rows):
        heard = own_rows != n // 4
        return [
            pltpu.VMEM((ZLINE, rows_y, own_rows, wide), bf16),
            pltpu.VMEM((ZLINE, rows_y, n // 2, wide) if heard else (16, 128), bf16),
            pltpu.VMEM((ZLINE, rows_y, n // 4, wide) if heard else (16, 128), bf16),
            pltpu.VMEM((ZLINE, n // 4, wide), bf16),
            pltpu.VMEM((2, n // 4, wide), bf16),
            pltpu.VMEM((n // 4, wide), bf16),
        ]

    return pl.pallas_call(
        functools.partial(finish_kernel, rows_y),
        name="finish",
        out_shape=(
            jax.ShapeDtypeStruct((owned, n, 2 * F), bf16),
            jax.ShapeDtypeStruct((length, width), bf16),
            jax.ShapeDtypeStruct((length, width), bf16),
        )
        + tuple(jax.ShapeDtypeStruct((n, v), bf16) for v in columns),
        in_specs=[any_space] * 6 + [vmem] * len(small),
        out_specs=(any_space,) + (vmem,) * 5,
        scratch_shapes=[
            pltpu.VMEM((count, width), bf16),
            pltpu.VMEM((width, ZLINE * count), bf16),
            pltpu.VMEM((2, ZLINE, count, 2 * hidden), bf16),
            pltpu.VMEM((owned, rows_y, ZLINE, n, 2 * hidden), bf16),
            pltpu.VMEM((owned, ZLINE, n, 2 * hidden), bf16),
            pltpu.VMEM((ZLINE - 1, owned, n, 2 * hidden), bf16),
            pltpu.VMEM((2, n, 2 * F), bf16),
            pltpu.VMEM((ZLINE, length, width), bf16),
            pltpu.VMEM((ZLINE, length, width), bf16),
            pltpu.VMEM((2, length, width), bf16),
            pltpu.VMEM((length, width), bf16),
            pltpu.VMEM((2, GROUP * (H // KV) * HD, width), bf16),
            pltpu.VMEM((2, 256, columns[2]), bf16),
            pltpu.VMEM((length, columns[2]), bf16),
            pltpu.VMEM((length, width), f32),
            pltpu.VMEM((blocks, n // 4, 4 * length), bf16),
            pltpu.VMEM((blocks, n // 4, 4 * length), bf16),
            pltpu.VMEM((4 * length, columns[0]), bf16),
            pltpu.VMEM((4 * length, columns[2]), bf16),
            pltpu.VMEM((ZLINE, rows_y, n, 128), bf16),
            pltpu.VMEM((length, width), f32),
            pltpu.VMEM((length, width), bf16),
            pltpu.VMEM((width, 128), f32),
            *summed(columns[0], n // 4),
            *summed(columns[1], n // 2),
            *summed(columns[2], n // 4),
            sems,
            sems((2,)),
            sems((2, 2)),
            sems((2, 2)),
            sems((2,)),
            sems((owned,)),
            sems((owned,)),
            sems((ZLINE - 1, owned)),
            sems((ZLINE - 1, owned)),
            sems((3, 8 + ZLINE)),
            sems((3, 8 + ZLINE)),
            sems((4, 4)),
            sems((4, 4)),
            sems((3,)),
            sems((3,)),
        ],
        compiler_params=pltpu.CompilerParams(
            collective_id=3, has_side_effects=True, vmem_limit_bytes=63 * 2**20
        ),
    )(rows, grads, combined, heard, w_output, w_qkv, *small)


def permuted(
    tokens,
    segments,
    routes,
    w_query,
    w_key,
    w_value,
    w_output,
    w_router,
    gain_attn,
    gain_moe,
    w_gate_up,
    w_down,
    cotangent,
):
    place = Place()
    length, width = tokens.shape
    owned = w_gate_up.shape[0]
    rows = w_query.shape[0]
    hidden = F // ZLINE
    per_group = H // KV
    q_end, k_end, v_end = H * HD, (H + KV) * HD, (H + 2 * KV) * HD
    o_end = v_end + width

    small = jnp.concatenate(
        [w_router, gain_attn[:, None], gain_moe[:, None], jnp.zeros((rows, 128 - EXPERTS - 2), bf16)],
        axis=1,
    )
    shard = jnp.concatenate([w_query, w_key, w_value, w_output, small], axis=1)
    full, order = gather_weights(place, shard)
    full_qkv, full_output = full[:, :v_end], full[:, v_end:o_end]
    full_small = transposed(order, full[:, o_end:]).astype(bf16)
    full_router = full_small[:, :EXPERTS]
    attn_gain = full_small[:, EXPERTS].astype(f32)
    moe_gain = full_small[:, EXPERTS + 1].astype(f32)

    chosen_mask = jnp.any(
        routes[:, :, None] == jnp.arange(EXPERTS, dtype=jnp.int32), axis=1
    )
    dy_block = jnp.concatenate(
        [cotangent, chosen_mask.astype(bf16), jnp.zeros((length, 128 - EXPERTS), bf16)], axis=1
    )
    dy_groups = gather_tokens(place, dy_block)

    cosine_table, sine_table = tables(length, HD)
    inputs = tokens.astype(f32)
    inv_attn = lax.rsqrt(jnp.mean(inputs * inputs, axis=-1, keepdims=True) + epsilon)
    unit_attn = inputs * inv_attn
    normed = (unit_attn * attn_gain).astype(bf16)
    normed = against(normed, order).astype(bf16)
    qkv = dot(normed, full_qkv)
    queries = rotate(qkv[:, :q_end].reshape(length, H, HD), cosine_table, sine_table)
    queries = queries.astype(bf16).reshape(length, KV, per_group, HD)
    key_rows = rotate(
        qkv[:, q_end:k_end].reshape(length, KV, HD), cosine_table, sine_table
    ).astype(bf16)
    values = qkv[:, k_end:].astype(bf16).reshape(length, KV, HD)
    segment = segments[0]
    position = jnp.arange(length, dtype=jnp.int32)
    allowed = (segment[:, None] == segment[None, :]) & (position[:, None] >= position[None, :])
    scores = (
        jnp.einsum("qkgd,skd->kgqs", queries, key_rows, preferred_element_type=f32) * 0.125
    )
    scores = jnp.where(allowed, scores, -1e30)
    maximum = jnp.max(scores, axis=-1, keepdims=True)
    lifted_scores = jnp.exp(scores - maximum)
    full_weights = lifted_scores / jnp.sum(lifted_scores, axis=-1, keepdims=True)
    attn_weights = full_weights.astype(bf16)
    mixed = jnp.einsum("kgqs,skd->qkgd", attn_weights, values, preferred_element_type=f32)
    mixed = mixed.reshape(length, H * HD).astype(bf16)
    mixed = against(mixed, order).astype(bf16)
    residual = inputs + dot(mixed, full_output)
    inv_moe = lax.rsqrt(jnp.mean(residual * residual, axis=-1, keepdims=True) + epsilon)
    unit_moe = residual * inv_moe
    normed_moe = (unit_moe * moe_gain).astype(bf16)

    def gates_of(rows_in, mask):
        logits = jnp.where(mask, dot(rows_in, full_router), -1e30)
        lifted = jnp.where(mask, jnp.exp(logits - jnp.max(logits, axis=-1, keepdims=True)), 0.0)
        return lifted / jnp.sum(lifted, axis=-1, keepdims=True)

    gates = gates_of(normed_moe, chosen_mask)

    def columns(start):
        cut = lax.dynamic_slice_in_dim(w_gate_up, start + place.z * hidden, hidden, 2)
        return cut.swapaxes(0, 1).reshape(width, owned * hidden)

    slice_gate_up = jnp.concatenate([columns(0), columns(F)], axis=1)
    slice_down = lax.dynamic_slice_in_dim(w_down, place.z * hidden, hidden, 1)
    slice_down = slice_down.reshape(owned * hidden, width)
    moe_groups = gather_tokens(place, normed_moe)
    span = owned * hidden
    acts, grads_gate_up, gate_parts = [], [], []
    for normed_rows, dy_rows in zip(moe_groups, dy_groups):
        count = normed_rows.shape[0]
        group_gates = gates_of(normed_rows, dy_rows[:, width : width + EXPERTS] > 0.5)
        group_gates = lax.dynamic_slice_in_dim(group_gates, place.ex * owned, owned, 1)
        spread_gates = jnp.broadcast_to(group_gates[:, :, None], (count, owned, hidden))
        spread_gates = spread_gates.reshape(count, span)
        gate_up = dot(normed_rows, slice_gate_up)
        gate_part, up_part = gate_up[:, :span], gate_up[:, span:]
        plain_grad = against(dy_rows[:, :width], slice_down)
        sigmoid_gate = jax.nn.sigmoid(gate_part)
        swished = gate_part * sigmoid_gate
        activation = swished * up_part
        grad_act = plain_grad * spread_gates
        gate_parts.append(jnp.sum((plain_grad * activation).reshape(count, owned, hidden), axis=-1))
        acts.append((spread_gates * activation).astype(bf16))
        grads_gate_up.append(
            jnp.concatenate(
                [
                    grad_act * up_part * sigmoid_gate * (1.0 + gate_part * (1.0 - sigmoid_gate)),
                    grad_act * swished,
                ],
                axis=-1,
            ).astype(bf16)
        )
    row_parts = [against(g, slice_gate_up).astype(bf16) for g in grads_gate_up]
    row_grads = scatter_tokens(place, row_parts, length)
    out_parts = [dot(a, slice_down).astype(bf16) for a in acts]
    output = (residual + scatter_tokens(place, out_parts, length)).astype(bf16)

    gate_parts = [g.T for g in gate_parts]
    two = [gate_parts[i] + swap(gate_parts[i + 2], "dp", place.z_bits[1]) for i in range(2)]
    mine = two[0] + swap(two[1], "dp", place.z_bits[0])
    mine = mine.reshape(owned, 2, place.ex_size // 2, length)
    heard = [
        swap(mine[:, m % 2, m // 2], "expert", m) if m else mine[:, 0, 0]
        for m in range(place.ex_size)
    ]
    heard = jnp.stack(heard)
    grad_gates = jnp.concatenate(
        [pick(heard, place.ex ^ j) for j in range(place.ex_size)], axis=0
    ).T
    grad_logits = (
        gates * (grad_gates - jnp.sum(gates * grad_gates, axis=-1, keepdims=True))
    ).astype(bf16)

    all_rows = jnp.concatenate([v for v in moe_groups], axis=0)
    all_dy = jnp.concatenate([v[:, :width] for v in dy_groups], axis=0)
    all_grads = jnp.concatenate(grads_gate_up, axis=0)
    all_acts = jnp.concatenate(acts, axis=0)

    def reduce_y(part, axis):
        part = jnp.moveaxis(part, axis, 0)
        for mask in place.y_bits[::-1]:
            at = (place.y // mask) % 2
            half = part.reshape((2, part.shape[0] // 2) + part.shape[1:])
            away = swap(pick(half, 1 - at), "dp", mask)
            part = (pick(half, at).astype(f32) + away.astype(f32)).astype(bf16)
        return part[0]

    shard_down = transposed(all_acts, all_dy).astype(bf16)
    shard_down = shard_down.reshape(owned, place.rows_y, hidden // place.rows_y, width)
    shard_down = reduce_y(shard_down, 1).astype(f32)
    part_gate_up = transposed(all_rows, all_grads).astype(bf16)
    part_gate_up = part_gate_up.reshape(ZLINE, place.rows_y, rows, 2 * span)
    part_gate_up = reduce_y(part_gate_up, 1)
    heard = [pick(part_gate_up, place.z)] + [
        swap(pick(part_gate_up, place.z ^ m), "dp", m * place.rows_y) for m in range(1, ZLINE)
    ]
    heard = jnp.stack(heard)
    shard_gate_up = jnp.stack([pick(heard, place.z ^ j) for j in range(ZLINE)], axis=0)
    shard_gate_up = shard_gate_up.reshape(ZLINE, rows, 2, owned, hidden)
    shard_gate_up = shard_gate_up.transpose(3, 1, 2, 0, 4).reshape(owned, rows, 2 * F).astype(f32)

    grad_out = cotangent.astype(f32)
    part_router = transposed(normed_moe, grad_logits)
    grad_normed_moe = row_grads + against(grad_logits, full_router)
    part_gain_moe = jnp.sum(grad_normed_moe * unit_moe, axis=0)
    scaled_moe = grad_normed_moe * moe_gain
    grad_residual = grad_out + inv_moe * (
        scaled_moe - unit_moe * jnp.mean(scaled_moe * unit_moe, axis=-1, keepdims=True)
    )
    grad_branch = grad_residual.astype(bf16)
    part_output = transposed(mixed, grad_branch)
    grad_mixed = dot(against(grad_branch, full_output).astype(bf16), order).astype(bf16)
    grad_mixed = grad_mixed.reshape(length, KV, per_group, HD)
    grad_weights = jnp.einsum(
        "qkgd,skd->kgqs", grad_mixed, values, preferred_element_type=f32
    )
    grad_values = jnp.einsum(
        "kgqs,qkgd->skd", attn_weights, grad_mixed, preferred_element_type=f32
    )
    grad_values = grad_values.astype(bf16).reshape(length, KV * HD)
    grad_scores = (
        full_weights * (grad_weights - jnp.sum(full_weights * grad_weights, axis=-1, keepdims=True))
    ).astype(bf16)
    grad_queries = (
        jnp.einsum("kgqs,skd->qkgd", grad_scores, key_rows, preferred_element_type=f32) * 0.125
    )
    grad_queries = rotate(grad_queries.reshape(length, H, HD), cosine_table, -sine_table)
    grad_queries = grad_queries.astype(bf16).reshape(length, H * HD)
    grad_keys = (
        jnp.einsum("kgqs,qkgd->skd", grad_scores, queries, preferred_element_type=f32) * 0.125
    )
    grad_keys = rotate(grad_keys, cosine_table, -sine_table)
    grad_keys = grad_keys.astype(bf16).reshape(length, KV * HD)
    grad_qkv = jnp.concatenate([grad_queries, grad_keys, grad_values], axis=1)
    part_qkv = transposed(normed, grad_qkv)
    grad_normed = against(grad_qkv, full_qkv)
    grad_normed = lax.dot_general(
        grad_normed,
        order.astype(f32),
        (((1,), (0,)), ((), ())),
        precision=lax.Precision.HIGHEST,
        preferred_element_type=f32,
    )
    part_gain_attn = jnp.sum(grad_normed * unit_attn, axis=0)
    scaled_attn = grad_normed * attn_gain
    grad_tokens = (
        grad_residual
        + inv_attn
        * (scaled_attn - unit_attn * jnp.mean(scaled_attn * unit_attn, axis=-1, keepdims=True))
    ).astype(bf16)
    part_small = jnp.concatenate(
        [
            part_router.astype(bf16),
            part_gain_attn[:, None].astype(bf16),
            part_gain_moe[:, None].astype(bf16),
            jnp.zeros((width, 128 - EXPERTS - 2), bf16),
        ],
        axis=1,
    )
    part_small = dot(order, part_small).astype(bf16)
    summed = scatter_weights(
        place,
        jnp.concatenate([part_qkv.astype(bf16), part_output.astype(bf16), part_small], axis=1),
    )
    return (
        output,
        grad_tokens,
        summed[:, :q_end],
        summed[:, q_end:k_end],
        summed[:, k_end:v_end],
        summed[:, v_end:o_end],
        summed[:, o_end : o_end + EXPERTS],
        summed[:, o_end + EXPERTS],
        summed[:, o_end + EXPERTS + 1],
        shard_gate_up,
        shard_down,
    )


def local(
    tokens,
    segments,
    routes,
    w_query,
    w_key,
    w_value,
    w_output,
    w_router,
    gain_attn,
    gain_moe,
    w_gate_up,
    w_down,
    cotangent,
):
    place = Place()
    if place.ex_size != 4 or place.rows_y != 2:
        return permuted(
            tokens,
            segments,
            routes,
            w_query,
            w_key,
            w_value,
            w_output,
            w_router,
            gain_attn,
            gain_moe,
            w_gate_up,
            w_down,
            cotangent,
        )
    length, width = tokens.shape
    per_group = H // KV
    q_end, k_end, v_end = H * HD, (H + KV) * HD, (H + 2 * KV) * HD

    angles = np.arange(length)[:, None] * 10000.0 ** (-2.0 * np.arange(HD // 2) / HD)[None, :]
    repeats = (1, GROUP * per_group)
    cosine = jnp.asarray(np.tile(np.tile(np.cos(angles), (1, 2)), repeats), f32)
    sine = np.concatenate([np.sin(angles), -np.sin(angles)], axis=1)
    sine = jnp.asarray(np.tile(sine, repeats), f32)
    (
        full_qkv,
        full_output,
        all_dy,
        plain_grads,
        full_small,
        queries,
        key_rows,
        values,
        residual,
        normed_moe,
        normed,
        mixed,
        gains,
        gates,
        allowed,
    ) = gather(
        place.rows_y,
        (w_query, w_key, w_value, w_output, w_router, gain_attn[None, :], gain_moe[None, :]),
        cotangent,
        tokens,
        segments,
        routes,
        cosine,
        sine,
        w_down,
    )
    full_small = full_small.reshape(width, 128)
    all_rows, all_grads, shard_down, combined, heard, row_grads = moe(
        place.rows_y, normed_moe, all_dy, plain_grads, w_gate_up, w_down, full_small
    )
    shard_gate_up, output, grad_tokens, sum_output, sum_small, sum_qkv = finish(
        place.rows_y,
        all_rows,
        all_grads,
        combined,
        heard,
        full_output.reshape(width, width),
        full_qkv.reshape(width, v_end),
        row_grads,
        gates,
        cotangent,
        residual,
        normed_moe,
        gains,
        full_small,
        tokens,
        mixed,
        normed,
        queries,
        key_rows,
        values,
        allowed,
        cosine,
        sine,
    )
    return (
        output,
        grad_tokens,
        sum_qkv[:, :q_end].astype(f32),
        sum_qkv[:, q_end:k_end].astype(f32),
        sum_qkv[:, k_end:].astype(f32),
        sum_output.astype(f32),
        sum_small[:, :EXPERTS].astype(f32),
        sum_small[:, EXPERTS].astype(f32),
        sum_small[:, EXPERTS + 1].astype(f32),
        shard_gate_up.astype(f32),
        shard_down.astype(f32),
    )


def solution(mesh):
    return jax.shard_map(
        local,
        mesh=mesh,
        in_specs=(
            P(("dp", "expert"), None),
            P(("dp", "expert"), None),
            P(("dp", "expert"), None),
            P("dp", None),
            P("dp", None),
            P("dp", None),
            P("dp", None),
            P("dp", None),
            P("dp"),
            P("dp"),
            P("expert", None, None),
            P("expert", None, None),
            P(("dp", "expert"), None),
        ),
        out_specs=(
            P(("dp", "expert"), None),
            P(("dp", "expert"), None),
            P("dp", None),
            P("dp", None),
            P("dp", None),
            P("dp", None),
            P("dp", None),
            P("dp"),
            P("dp"),
            P("expert", "dp", None),
            P("expert", "dp", None),
        ),
        check_vma=False,
    )
```

```python
import functools

import jax
import jax.numpy as jnp
import numpy as np
from jax import lax
from jax.experimental import pallas as pl
from jax.experimental.pallas import tpu as pltpu
from jax.sharding import PartitionSpec as P

H = 24
KV = 8
HD = 64
F = 512
EXPERTS = 40
ZLINE = 4
GROUP = 2


epsilon = 1e-05
f32 = jnp.float32
bf16 = jnp.bfloat16


def tables(length, size):
    half_size = size // 2
    frequency = jnp.power(10000.0, -2.0 * jnp.arange(half_size, dtype=f32) / size)
    angles = jnp.arange(length, dtype=f32)[:, None] * frequency[None, :]
    return (jnp.cos(angles)[:, None, :], jnp.sin(angles)[:, None, :])


def rotate(source, cosine_table, sine_table):
    half_size = source.shape[-1] // 2
    first_half = source[..., :half_size]
    second_half = source[..., half_size:]
    return jnp.concatenate(
        [
            first_half * cosine_table - second_half * sine_table,
            second_half * cosine_table + first_half * sine_table,
        ],
        axis=-1,
    )


def dot(left_side, right_side):
    return jnp.dot(left_side, right_side, preferred_element_type=f32)


def transposed(left_side, right_side):
    return lax.dot_general(
        left_side, right_side, (((0,), (0,)), ((), ())), preferred_element_type=f32
    )


def against(left_side, right_side):
    return lax.dot_general(
        left_side, right_side, (((1,), (1,)), ((), ())), preferred_element_type=f32
    )


def swap(value, axis, mask):
    size = lax.axis_size(axis)
    return lax.ppermute(value, axis, [(i, i ^ mask) for i in range(size)])


def pick(value, at):
    return lax.dynamic_index_in_dim(value, at, 0, keepdims=False)


def bits(first, size):
    masks, step = [], 1
    while step < size:
        masks.append(first * step)
        step *= 2
    return masks


class Place:
    def __init__(self):
        self.dp_size = lax.axis_size("dp")
        self.ex_size = lax.axis_size("expert")
        self.dp = lax.axis_index("dp")
        self.ex = lax.axis_index("expert")
        self.rows_y = self.dp_size // ZLINE
        self.z = self.dp // self.rows_y
        self.y = self.dp % self.rows_y
        self.z_bits = bits(self.rows_y, ZLINE)
        self.y_bits = bits(1, self.rows_y)
        self.x_bits = bits(2, self.ex_size // 2)


def gather_weights(place, shard):
    n, columns = shard.shape
    piece = n // 6
    cut = shard.reshape(3, 2, piece, columns)
    core = place.ex % 2
    side = (place.ex // 2) % 2
    own = pick(cut.swapaxes(0, 1), core)
    sibling = pick(cut.swapaxes(0, 1), 1 - core)

    def ordered(parts):
        return jnp.stack([pick(parts, 2 * side), parts[1], pick(parts, 2 - 2 * side)])

    own, sibling = ordered(own), ordered(sibling)
    blocks = {0: own[:2]}
    for mask in place.z_bits + place.y_bits:
        blocks.update({m ^ mask: swap(v, "dp", mask) for m, v in list(blocks.items())})
    rows = []
    for m in range(place.dp_size):
        if m == 0:
            rows.append(jnp.stack([own, sibling], axis=1))
            continue
        other = swap(blocks[m][0], "expert", 2)
        trio = jnp.concatenate([blocks[m], other[None]], axis=0)
        rows.append(jnp.stack([trio, swap(trio, "expert", 1)], axis=1))
    full = jnp.stack(rows)
    total = place.dp_size * n
    k = jnp.arange(total, dtype=jnp.int32)
    block, part = k // n, (k % n) // (2 * piece)
    half, line = (k % (2 * piece)) // piece, k % piece
    part = jnp.where(part == 1, 1, jnp.where(part == 0, 2 * side, 2 - 2 * side))
    at = (block ^ place.dp) * n + part * 2 * piece + (half ^ core) * piece + line
    order = (at[:, None] == jnp.arange(total, dtype=jnp.int32)[None, :]).astype(bf16)
    return full.reshape(total, columns), order


def scatter_weights(place, part):
    total, columns = part.shape
    n = total // place.dp_size
    piece = n // 6
    core = place.ex % 2
    side = (place.ex // 2) % 2

    def add(left, right):
        return (left.astype(f32) + right.astype(f32)).astype(bf16)

    part = part.reshape(place.dp_size, 3, 2, piece, columns)
    kept = add(part[:, :, 0], swap(part[:, :, 1], "expert", 1))
    first = add(kept[:, 0], swap(kept[:, 2], "expert", 2))
    blocks = {m: jnp.stack([first[m], kept[m, 1]]) for m in range(place.dp_size)}
    for mask in (place.z_bits + place.y_bits)[::-1]:
        blocks = {
            m: add(v, swap(blocks[m ^ mask], "dp", mask))
            for m, v in blocks.items()
            if m & mask == 0
        }
    mine = blocks[0]
    middle = add(mine[1], swap(mine[1], "expert", 2))
    trio = jnp.stack([mine[0], middle, swap(mine[0], "expert", 2)])
    for mask in place.x_bits[1:]:
        trio = add(trio, swap(trio, "expert", mask))
    both = jnp.stack([trio, swap(trio, "expert", 1)], axis=1)
    both = jnp.where(side == 0, both, both[::-1])
    both = jnp.where(core == 0, both, both[:, ::-1])
    return both.reshape(n, columns).astype(f32)


def gather_tokens(place, block):
    blocks = {0: block}
    for mask in place.z_bits:
        blocks.update({m ^ mask: swap(v, "dp", mask) for m, v in list(blocks.items())})
    groups = []
    for r in range(ZLINE):
        row = [blocks[r * place.rows_y]]
        for mask in place.x_bits:
            row = row + [swap(v, "expert", mask) for v in row]
        row = jnp.concatenate(row, axis=0)
        groups.append(jnp.concatenate([row, swap(row, "expert", 1)], axis=0))
    return groups


def scatter_tokens(place, groups, length):
    def add(left, right):
        return left.astype(f32) + right.astype(f32)

    reduced = []
    for part in groups:
        half = part.shape[0] // 2
        kept = add(part[:half], swap(part[half:], "expert", 1)).astype(bf16)
        for mask in place.x_bits[::-1]:
            half = kept.shape[0] // 2
            kept = add(kept[:half], swap(kept[half:], "expert", mask)).astype(bf16)
        reduced.append(kept)
    two = [add(reduced[i], swap(reduced[i + 2], "dp", place.z_bits[1])) for i in range(2)]
    return add(two[0], swap(two[1].astype(bf16), "dp", place.z_bits[0]))


def other(index, mask):
    return index + mask - 2 * mask * ((index // mask) % 2)


class Links:
    def __init__(self, sends, recvs):
        self.sends, self.recvs, self.used, self.open = sends, recvs, 0, []

    def copy(self, source, target, partner):
        at = self.used
        self.used += 1
        made = pltpu.make_async_remote_copy(
            src_ref=source,
            dst_ref=target,
            send_sem=self.sends.at[at],
            recv_sem=self.recvs.at[at],
            device_id=partner,
            device_id_type=pl.DeviceIdType.MESH,
        )
        made.start()
        self.open.append(made)
        return made

    def close(self):
        for made in self.open:
            made.wait_send()


def partners(rows_y):
    dp, ex = lax.axis_index("dp"), lax.axis_index("expert")
    return {
        "z1": (other(dp, rows_y), ex),
        "z2": (other(dp, 2 * rows_y), ex),
        "y": (other(dp, 1), ex),
        "x": (dp, other(ex, 2)),
        "c": (dp, other(ex, 1)),
    }


def greet(devices):
    barrier = pltpu.get_barrier_semaphore()
    for device in devices:
        pl.semaphore_signal(
            barrier, inc=1, device_id=device, device_id_type=pl.DeviceIdType.MESH
        )
    pl.semaphore_wait(barrier, len(devices))


def gather_kernel(
    rows_y,
    exclusive,
    w_query,
    w_key,
    w_value,
    w_output,
    w_router,
    gain_attn,
    gain_moe,
    dy,
    tokens_ref,
    segments,
    routes,
    cosine,
    sine,
    down_hbm,
    qkv_out,
    output_out,
    dy_out,
    grads_out,
    small_out,
    queries_out,
    keys_out,
    values_out,
    residual_out,
    normed_moe_out,
    normed_turned,
    mixed_turned,
    gains_out,
    gates_out,
    allowed,
    full_qkv,
    full_output,
    dy_all,
    w_down,
    grads,
    projected,
    normed_out,
    mixed_out,
    *refs,
):
    z_send, z_recv, y_send, y_recv, x_send, x_recv, c_send, c_recv = refs[:8]
    dz_send, dz_recv, dx_send, dx_recv, dc_send, dc_recv, down_sem, dy_sems, grads_sems, keep_sems = refs[8:]
    fulls = (full_qkv, small_out, full_output)
    n = w_query.shape[0]
    half = n // 2
    piece = half - exclusive
    length = dy.shape[0]
    owned, hidden, width = w_down.shape
    dp, ex = lax.axis_index("dp"), lax.axis_index("expert")
    z, y = dp // rows_y, dp % rows_y
    core, side = ex % 2, (ex // 2) % 2
    to = partners(rows_y)
    z_of = [z, other(z, 1), other(z, 2), other(other(z, 1), 2)]

    in_plane = pl.ds(pl.multiple_of(core * half + side * exclusive, 16), piece)
    alone = pl.ds(pl.multiple_of(core * half + side * piece, 16), exclusive)
    of_core = pl.ds(pl.multiple_of(core * half, 16), half)

    def remote(source, target, send_sem, recv_sem, device):
        return pltpu.make_async_remote_copy(
            src_ref=source,
            dst_ref=target,
            send_sem=send_sem,
            recv_sem=recv_sem,
            device_id=device,
            device_id_type=pl.DeviceIdType.MESH,
        )

    first, second = (0, 1), (2,)

    def copies(arrays, rows, m, ys, send, recv, at, device):
        made = []
        for k in arrays:
            block = fulls[k].at[z_of[m] * rows_y + ys, rows]
            made.append(remote(block, block, send.at[k, at], recv.at[k, at], device))
        return made

    def to_z(arrays, step):
        m, device = ((0, "z1"), (0, "z2"), (2, "z1"))[step]
        return copies(arrays, in_plane, m, y, z_send, z_recv, step, to[device])

    def to_y(arrays, m):
        return copies(arrays, in_plane, m, y, y_send, y_recv, m, to["y"])

    def to_x(arrays, m, k):
        ys = 1 - y if k else y
        return copies(arrays, alone, m, ys, x_send, x_recv, 2 * m + k, to["x"])

    def to_c(arrays, m, k):
        ys = 1 - y if k else y
        return copies(arrays, of_core, m, ys, c_send, c_recv, 2 * m + k, to["c"])

    near, pair = pl.ds(0, length), pl.ds(length, length)
    front, back = pl.ds(0, 2 * length), pl.ds(2 * length, 2 * length)

    def dy_z(step):
        m, target, device = ((0, 1, "z1"), (0, 2, "z2"), (2, 3, "z1"))[step]
        return remote(
            dy_all.at[m, near], dy_all.at[target, near], dz_send.at[step], dz_recv.at[step], to[device]
        )

    def dy_x(m):
        return remote(
            dy_all.at[m, near], dy_all.at[m, pair], dx_send.at[m], dx_recv.at[m], to["x"]
        )

    def dy_c(m):
        return remote(
            dy_all.at[m, front], dy_all.at[m, back], dc_send.at[m], dc_recv.at[m], to["c"]
        )

    at = pl.ds(pl.multiple_of(z * hidden, hidden), hidden)
    load_down = pltpu.make_async_copy(down_hbm.at[:, at, :], w_down, down_sem)
    load_down.start()

    def iota(shape, axis):
        return lax.broadcasted_iota(jnp.int32, shape, axis)

    full_qkv[dp, :, : H * HD] = w_query[...]
    full_qkv[dp, :, H * HD : (H + KV) * HD] = w_key[...]
    full_qkv[dp, :, (H + KV) * HD :] = w_value[...]
    full_output[dp] = w_output[...]
    line = iota((8, n), 0)
    gain_rows = jnp.where(
        line == 0,
        gain_attn[...].astype(f32),
        jnp.where(line == 1, gain_moe[...].astype(f32), 0.0),
    ).astype(bf16)
    places = (iota((8, 128), 1) == iota((8, 128), 0) + EXPERTS) & (iota((8, 128), 0) < 2)
    columns = transposed(gain_rows, places.astype(f32).astype(bf16))
    shape = (w_router.shape[0], 128)
    router = transposed(w_router[...], (iota(shape, 0) == iota(shape, 1)).astype(f32).astype(bf16))
    small_out[dp] = (router + columns).astype(bf16)
    lane, row = iota((length, 128), 1), iota((length, 128), 0)
    chosen = routes[:1] == iota((128, length), 0)
    for k in range(1, routes.shape[0]):
        chosen = chosen | (routes[k : k + 1] == iota((128, length), 0))
    same = (iota((128, 128), 0) == iota((128, 128), 1)).astype(f32).astype(bf16)
    chosen = transposed(chosen.astype(f32).astype(bf16), same)
    dy_all[0, near, :width] = dy[...]
    dy_all[0, near, width:] = chosen.astype(bf16)
    greet([to[name] for name in ("z1", "z2", "y", "x", "c")])

    def start(made):
        for copy in made:
            copy.start()

    def arrived(made):
        for copy in made:
            copy.wait_recv()

    def keep_dy(m):
        return pltpu.make_async_copy(dy_all.at[m], dy_out.at[m], dy_sems.at[m])

    def keep_grads(m):
        return pltpu.make_async_copy(grads.at[m % 2], grads_out.at[m], grads_sems.at[m % 2])

    keep_qkv = pltpu.make_async_copy(full_qkv, qkv_out, keep_sems.at[0])
    keep_output = pltpu.make_async_copy(full_output, output_out, keep_sems.at[1])

    def group(m):
        dy_c(m).wait_recv()
        keep_dy(m).start()
        if m >= 2:
            keep_grads(m - 2).wait()

        def step(p, _):
            at = pl.ds(pl.multiple_of(p * 2 * hidden, 2 * hidden), 2 * hidden)
            down = w_down[pl.ds(2 * p, 2)].reshape(2 * hidden, width)
            grads[m % 2, :, at] = against(dy_all[m, :, :width], down).astype(bf16)
            return 0

        lax.fori_loop(0, owned // 2, step, 0)
        keep_grads(m).start()

    def turned(value, target):
        target[...] = value.T.reshape(target.shape)

    def rotated(value):
        lanes = value.shape[1]
        lane = lax.broadcasted_iota(jnp.int32, value.shape, 1)
        swapped = jnp.where(
            lane % HD < HD // 2,
            pltpu.roll(value, lanes - HD // 2, 1),
            pltpu.roll(value, HD // 2, 1),
        )
        return (value * cosine[:, :lanes] - swapped * sine[:, :lanes]).astype(bf16)

    per_group = H // KV
    wide = GROUP * per_group * HD
    narrow = GROUP * HD

    def project():
        inputs = tokens_ref[...].astype(f32)
        inv = lax.rsqrt(jnp.mean(inputs * inputs, axis=-1, keepdims=True) + epsilon)
        gains_out[...] = against(
            places.astype(f32).astype(bf16), small_out[...].reshape(width, 128)
        )
        normed_out[...] = (inputs * inv * gains_out[:1]).astype(bf16)
        segment = segments[...].astype(f32)
        same = against(
            (row == lane).astype(f32).astype(bf16), jnp.broadcast_to(segment, (8, length)).astype(bf16)
        )[:, :1]
        allowed[...] = ((same == segment) & (row >= lane)).astype(f32)

        def step(j, _):
            at = pl.ds(pl.multiple_of(j * 512, 512), 512)
            projected[:, at] = jnp.dot(
                normed_out[...], full_qkv[:, :, at].reshape(width, 512), preferred_element_type=f32
            )
            return 0

        lax.fori_loop(0, projected.shape[1] // 512, step, 0)

    def attend(i):
        at = pl.ds(i * wide, wide)
        kv_at = pl.ds(i * narrow, narrow)
        k_at = pl.ds(H * HD + i * narrow, narrow)
        v_at = pl.ds((H + KV) * HD + i * narrow, narrow)
        query = rotated(projected[:, at])
        key = rotated(projected[:, k_at])
        value = projected[:, v_at].astype(bf16)
        queries_out[:, at] = query
        keys_out[:, kv_at] = key
        values_out[:, kv_at] = value
        is_allowed = allowed[...] > 0.5
        heads = []
        for k in range(GROUP):
            k_head, v_head = key[:, k * HD : (k + 1) * HD], value[:, k * HD : (k + 1) * HD]
            for j in range(k * per_group, (k + 1) * per_group):
                q_head = query[:, j * HD : (j + 1) * HD]
                scores = jnp.where(is_allowed, against(q_head, k_head) * 0.125, -1e30)
                lifted = jnp.exp(scores - jnp.max(scores, axis=-1, keepdims=True))
                weights = (lifted / jnp.sum(lifted, axis=-1, keepdims=True)).astype(bf16)
                heads.append(jnp.dot(weights, v_head, preferred_element_type=f32))
        mixed_out[:, at] = jnp.concatenate(heads, axis=1).astype(bf16)

    def close_block():
        def step(j, _):
            at = pl.ds(pl.multiple_of(j * 512, 512), 512)
            residual_out[:, at] = tokens_ref[:, at].astype(f32) + jnp.dot(
                mixed_out[...], full_output[:, :, at].reshape(width, 512), preferred_element_type=f32
            )
            return 0

        lax.fori_loop(0, width // 512, step, 0)
        residual = residual_out[...]
        inv = lax.rsqrt(jnp.mean(residual * residual, axis=-1, keepdims=True) + epsilon)
        normed_moe_out[...] = (residual * inv * gains_out[1:2]).astype(bf16)
        logits = jnp.dot(
            normed_moe_out[...], small_out[...].reshape(width, 128), preferred_element_type=f32
        )
        logits = jnp.where(chosen > 0.5, logits, -1e30)
        lifted = jnp.exp(logits - jnp.max(logits, axis=-1, keepdims=True)) * chosen
        gates_out[...] = lifted / jnp.sum(lifted, axis=-1, keepdims=True)
        turned(mixed_out[...], mixed_turned)

    start(to_z(first, 1))
    start(to_z(first, 0))
    start(to_y(first, 0))
    dy_x(0).start()

    arrived(to_z(first, 0))
    start(to_y(first, 1))
    start(to_x(first, 1, 0))
    arrived(to_z(first, 1))
    start(to_z(first, 2))
    start(to_y(first, 2))
    start(to_x(first, 2, 0))
    start(to_z(second, 1))
    start(to_z(second, 0))
    start(to_y(second, 0))
    dy_x(0).wait_recv()
    dy_c(0).start()
    arrived(to_y(first, 0))
    start(to_x(first, 0, 1))
    load_down.wait()
    group(0)
    arrived(to_z(first, 2))
    start(to_y(first, 3))
    start(to_x(first, 3, 0))
    arrived(to_z(second, 0))
    start(to_y(second, 1))
    start(to_x(second, 1, 0))
    arrived(to_z(second, 1))
    start(to_z(second, 2))
    start(to_y(second, 2))
    start(to_x(second, 2, 0))
    dy_z(1).start()
    dy_z(0).start()
    arrived(to_y(first, 1))
    start(to_x(first, 1, 1))
    arrived(to_y(first, 2))
    start(to_x(first, 2, 1))
    for m, k in ((1, 0), (2, 0), (0, 1), (3, 0), (1, 1)):
        arrived(to_x(first, m, k))
        start(to_c(first, m, k))
    arrived(to_y(first, 3))
    start(to_x(first, 3, 1))
    arrived(to_x(first, 2, 1))
    start(to_c(first, 2, 1))
    arrived(to_z(second, 2))
    start(to_y(second, 3))
    start(to_x(second, 3, 0))
    arrived(to_y(second, 0))
    start(to_x(second, 0, 1))
    arrived(to_x(first, 3, 1))
    start(to_c(first, 3, 1))
    for m, k in ((1, 0), (2, 0), (0, 1), (3, 0), (1, 1), (2, 1), (3, 1)):
        arrived(to_c(first, m, k))
    keep_qkv.start()
    project()
    turned(normed_out[...], normed_turned)
    arrived(to_y(second, 1))
    start(to_x(second, 1, 1))
    arrived(to_y(second, 2))
    start(to_x(second, 2, 1))
    dy_z(0).wait_recv()
    dy_x(1).start()
    attend(0)
    dy_z(1).wait_recv()
    dy_z(2).start()
    dy_x(2).start()
    attend(1)
    for m, k in ((1, 0), (2, 0), (0, 1), (3, 0), (1, 1), (2, 1)):
        arrived(to_x(second, m, k))
        start(to_c(second, m, k))
    arrived(to_y(second, 3))
    start(to_x(second, 3, 1))
    attend(2)
    dy_x(1).wait_recv()
    dy_c(1).start()
    attend(3)
    arrived(to_x(second, 3, 1))
    start(to_c(second, 3, 1))
    group(1)
    dy_z(2).wait_recv()
    dy_x(3).start()
    for m, k in ((1, 0), (2, 0), (0, 1), (3, 0), (1, 1), (2, 1), (3, 1)):
        arrived(to_c(second, m, k))
    keep_output.start()
    close_block()
    dy_x(2).wait_recv()
    dy_c(2).start()
    group(2)
    dy_x(3).wait_recv()
    dy_c(3).start()
    group(3)

    keep_qkv.wait()
    keep_output.wait()
    for m in range(ZLINE):
        keep_dy(m).wait()
        if m >= 2:
            keep_grads(m).wait()
    every = first + second
    for step in range(3):
        for made in to_z(every, step):
            made.wait_send()
        dy_z(step).wait_send()
    for m in range(ZLINE):
        for made in to_y(every, m):
            made.wait_send()
        dy_x(m).wait_send()
        dy_c(m).wait_send()
        for k in range(2):
            if m or k:
                for made in to_x(every, m, k) + to_c(every, m, k):
                    made.wait_send()


def gather(rows_y, weights, dy, *rest):
    w_down = rest[-1]
    n = weights[0].shape[0]
    dp_size = ZLINE * rows_y
    owned, _, width = w_down.shape
    hidden = F // ZLINE
    length = dy.shape[0]
    count = 4 * length
    qkv_wide = weights[0].shape[1] + weights[1].shape[1] + weights[2].shape[1]
    any_space = pl.BlockSpec(memory_space=pl.ANY)
    vmem = pl.BlockSpec(memory_space=pltpu.VMEM)
    sems = pltpu.SemaphoreType.DMA

    def rows(wide, dtype=bf16):
        return jax.ShapeDtypeStruct((length, wide), dtype)

    turned = jax.ShapeDtypeStruct((dp_size, 2, 2, n // 4, length), bf16)
    return pl.pallas_call(
        functools.partial(gather_kernel, rows_y, n // 6),
        name="gather",
        out_shape=(
            jax.ShapeDtypeStruct((dp_size, n, qkv_wide), bf16),
            jax.ShapeDtypeStruct((dp_size, n, width), bf16),
            jax.ShapeDtypeStruct((ZLINE, count, width + 128), bf16),
            jax.ShapeDtypeStruct((ZLINE, count, owned * hidden), bf16),
            jax.ShapeDtypeStruct((dp_size, n, 128), bf16),
            rows(H * HD),
            rows(KV * HD),
            rows(KV * HD),
            rows(width, f32),
            rows(width),
            turned,
            turned,
            jax.ShapeDtypeStruct((8, width), f32),
            rows(128, f32),
            rows(length, f32),
        ),
        in_specs=[vmem] * (len(weights) + len(rest)) + [any_space],
        out_specs=(any_space,) * 4 + (vmem,) * 11,
        scratch_shapes=[
            pltpu.VMEM((dp_size, n, qkv_wide), bf16),
            pltpu.VMEM((dp_size, n, width), bf16),
            pltpu.VMEM((ZLINE, count, width + 128), bf16),
            pltpu.VMEM((owned, hidden, width), bf16),
            pltpu.VMEM((2, count, owned * hidden), bf16),
            pltpu.VMEM((length, qkv_wide), f32),
            pltpu.VMEM((length, width), bf16),
            pltpu.VMEM((length, H * HD), bf16),
            sems((3, 3)),
            sems((3, 3)),
            sems((3, ZLINE)),
            sems((3, ZLINE)),
            sems((3, dp_size)),
            sems((3, dp_size)),
            sems((3, dp_size)),
            sems((3, dp_size)),
            sems((3,)),
            sems((3,)),
            sems((ZLINE,)),
            sems((ZLINE,)),
            sems((ZLINE,)),
            sems((ZLINE,)),
            sems,
            sems((ZLINE,)),
            sems((2,)),
            sems((2,)),
        ],
        compiler_params=pltpu.CompilerParams(
            collective_id=2, has_side_effects=True, vmem_limit_bytes=60 * 2**20
        ),
    )(*weights, dy, *rest)


MOE_COPIES = 30


def moe_kernel(
    rows_y,
    normed_ref,
    dy_hbm,
    plain_hbm,
    gate_up_hbm,
    down_hbm,
    router_ref,
    rows_out,
    grads_out,
    down_out,
    combined_out,
    heard_out,
    total_ref,
    w_gate,
    w_up,
    w_down,
    rows,
    masks,
    plain,
    grads,
    acts,
    gate_grads,
    part_down,
    heard_down,
    stage_down,
    parts,
    heard_c,
    heard_x,
    heard_z1,
    heard_z,
    combined,
    heard_combined,
    spread_ref,
    sends,
    recvs,
    d_send,
    d_recv,
    load_sems,
    plain_sems,
    dy_sems,
    rows_sems,
    grads_sems,
    down_sems,
    combined_sems,
):
    owned, hidden = w_down.shape[:2]
    length, width = normed_ref.shape
    count = rows.shape[1]
    tokens = ZLINE * count
    half = count // 2
    span = owned * hidden
    dp = lax.axis_index("dp")
    z, y = dp // rows_y, dp % rows_y
    to = partners(rows_y)
    to["z3"] = (other(to["z1"][0], 2 * rows_y), lax.axis_index("expert"))
    links = Links(sends, recvs)

    loads = []
    mine = pl.ds(pl.multiple_of(z * hidden, hidden), hidden)
    theirs = pl.ds(pl.multiple_of(F + z * hidden, hidden), hidden)
    for e in range(owned):
        at = pl.ds(e * hidden, hidden)
        for k, (cut, kept) in enumerate(((mine, w_gate), (theirs, w_up))):
            loads.append(
                pltpu.make_async_copy(
                    gate_up_hbm.at[e, :, cut], kept.at[:, at], load_sems.at[2 * e + k]
                )
            )
    loads.append(
        pltpu.make_async_copy(dy_hbm.at[:, :, pl.ds(width, 128)], masks, load_sems.at[2 * owned])
    )
    load_down = pltpu.make_async_copy(
        down_hbm.at[:, mine, :], w_down, load_sems.at[2 * owned + 1]
    )
    for load in loads:
        load.start()

    def fetch(r):
        return pltpu.make_async_copy(plain_hbm.at[r], plain.at[r % 2], plain_sems.at[r % 2])

    fetch(0).start()
    fetch(1).start()
    load_down.start()
    rows[0, :length] = normed_ref[...]
    first = lax.axis_index("expert") * owned
    expert = first + lax.broadcasted_iota(jnp.int32, (128, span), 1) // hidden
    spread_ref[...] = (
        (lax.broadcasted_iota(jnp.int32, (128, span), 0) == expert).astype(f32).astype(bf16)
    )
    greet([to[name] for name in ("z1", "z2", "z3", "y", "x", "c")])

    own = pl.ds(0, length)
    pair = pl.ds(length, length)
    near, far = pl.ds(0, half), pl.ds(half, half)

    def row_x(r):
        return links.copy(rows.at[r, own], rows.at[r, pair], to["x"])

    def row_c(r):
        return links.copy(rows.at[r, near], rows.at[r, far], to["c"])

    z1 = links.copy(rows.at[0, own], rows.at[1, own], to["z1"])
    z2 = links.copy(rows.at[0, own], rows.at[2, own], to["z2"])
    x0 = row_x(0)
    for load in loads:
        load.wait()
    x0.wait_recv()
    z1_pair = links.copy(rows.at[0, pair], rows.at[1, pair], to["z1"])
    c0 = row_c(0)
    c0.wait_recv()

    def keep_rows(r):
        return pltpu.make_async_copy(rows.at[r], rows_out.at[r], rows_sems.at[r])

    def keep_grads(r):
        return pltpu.make_async_copy(grads.at[min(r, 1)], grads_out.at[r], grads_sems.at[r])

    def forward(r):
        slot, held = r % 2, min(r, 1)
        keep_rows(r).start()
        fetch(r).wait()
        if r >= 2:
            keep_grads(r - 1).wait()
        logits = jnp.dot(rows[r], router_ref[...], preferred_element_type=f32)
        mask = masks[r].astype(f32) > 0.5
        logits = jnp.where(mask, logits, -1e30)
        lifted = jnp.where(
            mask, jnp.exp(logits - jnp.max(logits, axis=-1, keepdims=True)), 0.0
        )
        gates = lifted / jnp.sum(lifted, axis=-1, keepdims=True)
        gates_high = gates.astype(bf16)
        gates_low = (gates - gates_high.astype(f32)).astype(bf16)
        gate_grads[...] = jnp.zeros_like(gate_grads)

        def step(p, _):
            at = pl.ds(pl.multiple_of(p * 2 * hidden, 2 * hidden), 2 * hidden)
            up_at = pl.ds(pl.multiple_of(span + p * 2 * hidden, 2 * hidden), 2 * hidden)
            spread = spread_ref[:, at]
            gate_part = jnp.dot(rows[r], w_gate[:, at], preferred_element_type=f32)
            up_part = jnp.dot(rows[r], w_up[:, at], preferred_element_type=f32)
            plain_grad = plain[slot, :, at].astype(f32)
            spread_gates = jnp.dot(gates_high, spread, preferred_element_type=f32) + jnp.dot(
                gates_low, spread, preferred_element_type=f32
            )
            sigmoid_gate = 1.0 / (1.0 + jnp.exp(-gate_part))
            swished = gate_part * sigmoid_gate
            activation = swished * up_part
            gate_grads[...] += against((plain_grad * activation).astype(bf16), spread)
            acts[r, :, at] = (spread_gates * activation).astype(bf16)
            grad_act = plain_grad * spread_gates
            grads[held, :, at] = (
                grad_act * up_part * (sigmoid_gate + swished * (1.0 - sigmoid_gate))
            ).astype(bf16)
            grads[held, :, up_at] = (grad_act * swished).astype(bf16)
            return 0

        lax.fori_loop(0, owned // 2, step, 0, unroll=True)
        parts[r, :, width:] = gate_grads[...].astype(bf16)
        if r + 2 < ZLINE:
            fetch(r + 2).start()
        keep_grads(r).start()

    def backward(r):
        held = min(r, 1)

        def step(j, _):
            at = pl.ds(pl.multiple_of(j * 768, 768), 768)
            part = against(grads[held, :, :span], w_gate[at, :]) + against(
                grads[held, :, span:], w_up[at, :]
            )
            parts[r, :, at] = part.astype(bf16)
            return 0

        lax.fori_loop(0, width // 768, step, 0)

    def add(left, right):
        return (left[...].astype(f32) + right[...].astype(f32)).astype(bf16)

    made = {}

    def sum_c(r):
        made["c", r] = links.copy(parts.at[r, far], heard_c.at[r], to["c"])

    def sum_x(r):
        made["c", r].wait_recv()
        parts[r, near] = add(parts.at[r, near], heard_c.at[r])
        if r == 1:
            made["z", 1] = links.copy(parts.at[1, near], heard_z1, to["z1"])
            return
        if r == 0:
            made["z", 1].wait_recv()
            parts[0, near] = add(parts.at[0, near], heard_z1)
        made["x", r] = links.copy(parts.at[r, pair], heard_x.at[r], to["x"])

    def sum_z(r):
        made["x", r].wait_recv()
        parts[r, own] = add(parts.at[r, own], heard_x.at[r])
        if r:
            made["z", r] = links.copy(parts.at[r, own], heard_z.at[r - 2], to[f"z{r}"])

    def keep_combined(r):
        return pltpu.make_async_copy(
            combined.at[r % 2, near], combined_out.at[r], combined_sems.at[r]
        )

    def combine(r):
        slot = r % 2
        if r >= 2:
            made["oc", r - 2].wait_send()

        def step(j, _):
            at = pl.ds(pl.multiple_of(j * 512, 512), 512)
            down = w_down[:, :, at].reshape(span, 512)
            combined[slot, :, at] = jnp.dot(
                acts[r], down, preferred_element_type=f32
            ).astype(bf16)
            return 0

        lax.fori_loop(0, width // 512, step, 0)
        made["oc", r] = links.copy(combined.at[slot, far], heard_combined.at[r], to["c"])

    def out_c(r):
        made["oc", r].wait_recv()
        combined[r % 2, near] = add(combined.at[r % 2, near], heard_combined.at[r])
        keep_combined(r).start()

    def out_x(r):
        made["ox", r] = links.copy(combined_out.at[r, pair], heard_out.at[r], to["x"])

    def fetch_dy(r):
        return pltpu.make_async_copy(
            dy_hbm.at[r, :, pl.ds(0, width)], rows.at[r], dy_sems.at[r]
        )

    def send_down(e):
        return pltpu.make_async_remote_copy(
            src_ref=part_down.at[e, 1 - y],
            dst_ref=heard_down.at[e],
            send_sem=d_send.at[e],
            recv_sem=d_recv.at[e],
            device_id=to["y"],
            device_id_type=pl.DeviceIdType.MESH,
        )

    def down(p, _):
        at = pl.ds(pl.multiple_of(p * 2 * hidden, 2 * hidden), 2 * hidden)
        left = acts[:, :, at].reshape(tokens, 2 * hidden)

        def step(j, _):
            columns = pl.ds(pl.multiple_of(j * 768, 768), 768)
            result = transposed(left, rows[:, :, columns].reshape(tokens, 768)).astype(bf16)
            for k in range(2):
                for i in range(rows_y):
                    first = k * hidden + i * (hidden // rows_y)
                    part_down[2 * p + k, i, :, columns] = result[
                        first : first + hidden // rows_y
                    ]
            return 0

        lax.fori_loop(0, width // 768, step, 0)
        for k in range(2):
            send_down(2 * p + k).start()
        return 0

    def keep_down(e):
        return pltpu.make_async_copy(
            stage_down.at[lax.rem(e, 2)], down_out.at[e], down_sems.at[lax.rem(e, 2)]
        )

    def finish_down(e, _):
        @pl.when(e >= 2)
        def _():
            keep_down(e - 2).wait()

        send_down(e).wait_recv()
        stage_down[lax.rem(e, 2)] = add(part_down.at[e, y], heard_down.at[e])
        keep_down(e).start()
        return 0

    forward(0)
    z2.wait_recv()
    z3 = links.copy(rows.at[2, own], rows.at[3, own], to["z1"])
    x2 = row_x(2)
    load_down.wait()
    combine(0)
    z1.wait_recv()
    z1_pair.wait_recv()
    c1 = row_c(1)
    c1.wait_recv()
    forward(1)
    z3.wait_recv()
    x3 = row_x(3)
    backward(1)
    sum_c(1)
    x2.wait_recv()
    c2 = row_c(2)
    out_c(0)
    sum_x(1)
    c2.wait_recv()
    forward(2)
    backward(2)
    sum_c(2)
    x3.wait_recv()
    c3 = row_c(3)
    sum_x(2)
    c3.wait_recv()
    forward(3)
    backward(3)
    sum_c(3)
    keep_combined(0).wait()
    out_x(0)
    for r in range(ZLINE):
        keep_rows(r).wait()
    gathered = (z1, z2, z3, z1_pair, x0, x2, x3, c0, c1, c2, c3)
    for copy in gathered:
        copy.wait_send()
    for r in range(ZLINE):
        fetch_dy(r).start()
    sum_x(3)
    sum_z(2)
    for r in range(ZLINE):
        fetch_dy(r).wait()
    lax.fori_loop(0, 2, down, 0)
    backward(0)
    sum_c(0)
    combine(1)
    sum_z(3)
    sum_x(0)
    lax.fori_loop(2, 3, down, 0)
    out_c(1)
    combine(2)
    keep_combined(1).wait()
    out_x(1)
    sum_z(0)
    lax.fori_loop(3, 4, down, 0)
    out_c(2)
    combine(3)
    keep_combined(2).wait()
    out_x(2)
    lax.fori_loop(4, owned // 2, down, 0)
    out_c(3)
    total = parts[0, own].astype(f32)
    for r in (2, 3):
        made["z", r].wait_recv()
        total = total + heard_z[r - 2].astype(f32)
    total_ref[...] = total
    keep_combined(3).wait()
    out_x(3)
    lax.fori_loop(0, owned, finish_down, 0)
    for r in range(ZLINE):
        made["ox", r].wait_recv()
    done = gathered + (made["oc", 0], made["oc", 1])
    links.open = [v for v in links.open if not any(v is copy for copy in done)]
    links.close()
    for e in range(owned):
        send_down(e).wait_send()
    for e in (owned - 2, owned - 1):
        keep_down(e).wait()
    for r in (0, ZLINE - 1):
        keep_grads(r).wait()


def moe(rows_y, normed, dy, plain, w_gate_up, w_down, router):
    owned, width, _ = w_gate_up.shape
    hidden = F // ZLINE
    length = normed.shape[0]
    count = dy.shape[1]
    any_space = pl.BlockSpec(memory_space=pl.ANY)
    vmem = pl.BlockSpec(memory_space=pltpu.VMEM)
    sems = pltpu.SemaphoreType.DMA
    span = owned * hidden
    wide = width + 128
    return pl.pallas_call(
        functools.partial(moe_kernel, rows_y),
        name="moe",
        out_shape=(
            jax.ShapeDtypeStruct((ZLINE, count, width), bf16),
            jax.ShapeDtypeStruct((ZLINE, count, 2 * span), bf16),
            jax.ShapeDtypeStruct((owned, hidden // rows_y, width), bf16),
            jax.ShapeDtypeStruct((ZLINE, count // 2, width), bf16),
            jax.ShapeDtypeStruct((ZLINE, length, width), bf16),
            jax.ShapeDtypeStruct((length, wide), f32),
        ),
        in_specs=[vmem, any_space, any_space, any_space, any_space, vmem],
        out_specs=(any_space,) * 5 + (vmem,),
        scratch_shapes=[
            pltpu.VMEM((width, span), bf16),
            pltpu.VMEM((width, span), bf16),
            pltpu.VMEM((owned, hidden, width), bf16),
            pltpu.VMEM((ZLINE, count, width), bf16),
            pltpu.VMEM((ZLINE, count, 128), bf16),
            pltpu.VMEM((2, count, span), bf16),
            pltpu.VMEM((2, count, 2 * span), bf16),
            pltpu.VMEM((ZLINE, count, span), bf16),
            pltpu.VMEM((count, 128), f32),
            pltpu.VMEM((owned, rows_y, hidden // rows_y, width), bf16),
            pltpu.VMEM((owned, hidden // rows_y, width), bf16),
            pltpu.VMEM((2, hidden // rows_y, width), bf16),
            pltpu.VMEM((ZLINE, count, wide), bf16),
            pltpu.VMEM((ZLINE, count // 2, wide), bf16),
            pltpu.VMEM((ZLINE, length, wide), bf16),
            pltpu.VMEM((count // 2, wide), bf16),
            pltpu.VMEM((ZLINE - 2, length, wide), bf16),
            pltpu.VMEM((2, count, width), bf16),
            pltpu.VMEM((ZLINE, count // 2, width), bf16),
            pltpu.VMEM((128, span), bf16),
            sems((MOE_COPIES,)),
            sems((MOE_COPIES,)),
            sems((owned,)),
            sems((owned,)),
            sems((2 * owned + 2,)),
            sems((2,)),
            sems((ZLINE,)),
            sems((ZLINE,)),
            sems((ZLINE,)),
            sems((2,)),
            sems((ZLINE,)),
        ],
        compiler_params=pltpu.CompilerParams(
            collective_id=1, has_side_effects=True, vmem_limit_bytes=63 * 2**20
        ),
    )(normed, dy, plain, w_gate_up, w_down, router)


def finish_kernel(
    rows_y,
    rows_hbm,
    grads_hbm,
    combined_hbm,
    heard_hbm,
    w_output_hbm,
    w_qkv_hbm,
    row_grads,
    gates,
    cotangent,
    residual,
    normed_moe,
    gains,
    router,
    tokens_ref,
    mixed,
    normed,
    queries,
    keys,
    values,
    allowed,
    cosine,
    sine,
    gate_up_out,
    output_out,
    grad_tokens_out,
    out_0,
    out_1,
    out_2,
    rows,
    turned,
    grads,
    part_gate_up,
    heard_gate_up,
    heard_z,
    stage,
    o_own,
    o_x,
    o_z1,
    o_z2,
    w_output,
    w_qkv,
    grad_qkv,
    grad_normed,
    left_output,
    left_qkv,
    right_output,
    right_qkv,
    part_small,
    grad_residual,
    grad_branch,
    base_small,
    *refs,
):
    owned, n = gate_up_out.shape[:2]
    hidden = F // ZLINE
    count, width = rows.shape
    length = tokens_ref.shape[0]
    tokens = ZLINE * count
    dp, ex = lax.axis_index("dp"), lax.axis_index("expert")
    z, y = dp // rows_y, dp % rows_y
    core, side = ex % 2, (ex // 2) % 2
    to = partners(rows_y)
    to["z3"] = (other(to["z1"][0], 2 * rows_y), ex)
    to["xc"] = (dp, other(other(ex, 1), 2))
    z_of = [z, other(z, 1), other(z, 2), other(other(z, 1), 2)]
    half, quarter = n // 2, n // 4
    of_core = pl.ds(pl.multiple_of(core * half, 16), half)
    of_sibling = pl.ds(pl.multiple_of((1 - core) * half, 16), half)
    of_side = pl.ds(pl.multiple_of(side * quarter, 16), quarter)
    of_far_side = pl.ds(pl.multiple_of((1 - side) * quarter, 16), quarter)
    mine = pl.ds(pl.multiple_of(core * half + side * quarter, 16), quarter)
    (
        load_sem,
        own_sems,
        weight_sems,
        grads_sems,
        store_sems,
        y_send,
        y_recv,
        z_send,
        z_recv,
        a_send,
        a_recv,
        f_send,
        f_recv,
        o_send,
        o_recv,
    ) = refs[18:]

    def remote(source, target, send_sem, recv_sem, device):
        return pltpu.make_async_remote_copy(
            src_ref=source,
            dst_ref=target,
            send_sem=send_sem,
            recv_sem=recv_sem,
            device_id=device,
            device_id_type=pl.DeviceIdType.MESH,
        )

    def add(left, right):
        return (left.astype(f32) + right.astype(f32)).astype(bf16)

    def load_rows(r):
        return pltpu.make_async_copy(rows_hbm.at[r], rows, load_sem)

    def load_grads(e, k):
        at = pl.ds(pl.multiple_of((k * owned + e) * hidden, hidden), hidden)
        return pltpu.make_async_copy(
            grads_hbm.at[:, :, at],
            grads.at[lax.rem(e, 2), :, :, pl.ds(k * hidden, hidden)],
            grads_sems.at[lax.rem(e, 2), k],
        )

    load_combined = [
        pltpu.make_async_copy(combined_hbm.at[:, pl.ds(0, length)], o_own, own_sems.at[0]),
        pltpu.make_async_copy(heard_hbm, o_x, own_sems.at[1]),
    ]

    def o_copy(k):
        if k < 2:
            return remote(o_own.at[1 + 2 * k], o_z1.at[k], o_send.at[k], o_recv.at[k], to["z1"])
        return remote(o_own.at[2], o_z2, o_send.at[k], o_recv.at[k], to["z2"])

    def o_start():
        for load in load_combined:
            load.wait()
        for r in (3, 1, 2, 0):
            o_own[r] = add(o_own[r], o_x[r])
            if r % 2:
                o_copy(r // 2).start()

    def o_after_z1():
        for k in (1, 0):
            o_copy(k).wait_recv()
            o_own[2 * k] = add(o_own[2 * k], o_z1[k])
            if k:
                o_copy(2).start()

    def o_end():
        o_copy(2).wait_recv()
        total = o_own[0].astype(f32) + o_z2[...].astype(f32)
        output_out[...] = (residual[...] + total).astype(bf16)

    def left_copies(k, source, target):
        made = []
        for m, name in ((1, "c"), (2, "x"), (3, "xc")):
            c = 1 - core if m % 2 else core
            s = 1 - side if m // 2 else side
            made.append(
                remote(
                    source.at[:, c, s],
                    target.at[:, :, pl.ds(m * length, length)],
                    f_send.at[k, m],
                    f_recv.at[k, m],
                    to[name],
                )
            )
        return made

    def right_copy(k, source, target, m):
        if m == 3:
            source = target.at[pl.ds(2 * length, length)]
        return remote(
            source,
            target.at[pl.ds(m * length, length)],
            f_send.at[k, m],
            f_recv.at[k, m],
            to["x" if m == 2 else "c"],
        )

    class Sum:
        def __init__(self, k, out, rows, z_first=False):
            self.k, self.out, self.rows, self.z_first = k, out, rows, z_first
            self.own, self.c, self.x, self.y, self.z1, self.z2 = refs[6 * k : 6 * k + 6]

        def copy(self, step, source, target, device):
            return remote(
                source, target, a_send.at[self.k, step], a_recv.at[self.k, step], device
            )

        def line(self, m):
            if self.z_first:
                return self.own.at[z_of[m], :, self.rows]
            return self.own.at[z_of[m], y, self.rows]

        def last_y(self):
            return self.copy(8, self.own.at[z, 1 - y, self.rows], self.y.at[0], to["y"])

        def to_y(self, b):
            return self.copy(8 + b, self.own.at[b, 1 - y, self.rows], self.y.at[b], to["y"])

        def to_z1(self, m):
            return self.copy(1 + m, self.line(1 + 2 * m), self.z1.at[m], to["z1"])

        def to_z2(self):
            return self.copy(3, self.line(2), self.z2, to["z2"])

        def back_x(self):
            return self.copy(4, self.out.at[mine], self.out.at[mine], to["x"])

        def back_c(self):
            return self.copy(5, self.out.at[of_core], self.out.at[of_core], to["c"])

        def to_c(self):
            return self.copy(6, part_small.at[:, :, of_sibling], self.c, to["c"])

        def to_x(self):
            return self.copy(7, self.own.at[:, :, of_far_side], self.x, to["x"])

        def after_c(self):
            self.to_c().wait_recv()
            for b in range(ZLINE):
                for k in range(rows_y):
                    self.own[b, k] = add(part_small[b, k, of_core], self.c[b, k])
            self.to_x().start()

        def after_x(self):
            self.to_x().wait_recv()
            for b in range(ZLINE):
                for k in range(rows_y):
                    self.own[b, k, self.rows] = add(self.own[b, k, self.rows], self.x[b, k])
            self.along_y()

        def begin(self):
            if self.z_first:
                self.along_z()
            else:
                self.along_y()

        def along_y(self):
            for b in range(ZLINE):
                self.to_y(b).start()

        def along_z(self):
            for m in (1, 0):
                self.to_z1(m).start()

        def after_y(self):
            if self.z_first:
                self.last_y().wait_recv()
                self.out[mine] = add(self.own[z, y, self.rows], self.y[0])
                self.back_x().start()
                return
            for b in range(ZLINE):
                self.to_y(b).wait_recv()
                self.own[b, y, self.rows] = add(self.own[b, y, self.rows], self.y[b])
            self.along_z()

        def after_z1(self):
            for m in (1, 0):
                self.to_z1(m).wait_recv()
                line = self.line(2 * m)
                line[...] = add(line[...], self.z1[m])
                if m:
                    self.to_z2().start()

        def after_z2(self):
            self.to_z2().wait_recv()
            if self.z_first:
                line = self.line(0)
                line[...] = add(line[...], self.z2[...])
                self.last_y().start()
                return
            self.out[mine] = add(self.own[z, y, self.rows], self.z2[...])
            self.back_x().start()

        def after_back(self):
            self.back_x().wait_recv()
            self.back_c().start()

        def close(self):
            self.back_c().wait()
            for made in (self.to_z1(0), self.to_z1(1), self.to_z2(), self.back_x()):
                made.wait_send()
            if self.z_first:
                self.last_y().wait_send()
                return
            for b in range(ZLINE):
                self.to_y(b).wait_send()

    whole = pl.ds(0, quarter)
    output = Sum(0, out_0, whole, True)
    small = Sum(1, out_1, of_side)
    qkv = Sum(2, out_2, whole)

    def products(array, left, right):
        rows_all = left[...].reshape(ZLINE * rows_y * quarter, 4 * length)

        def step(j, _):
            at = pl.ds(pl.multiple_of(j * 512, 512), 512)
            result = jnp.dot(rows_all, right[:, at], preferred_element_type=f32).astype(bf16)
            array.own[:, :, :, at] = result.reshape(ZLINE, rows_y, quarter, 512)
            return 0

        lax.fori_loop(0, right.shape[1] // 512, step, 0)
        array.begin()

    def load_output(i):
        step = w_output.shape[1]
        at = pl.ds(pl.multiple_of(i * step, step), step)
        return pltpu.make_async_copy(
            w_output_hbm.at[at], w_output.at[lax.rem(i, 2)], weight_sems.at[0, lax.rem(i, 2)]
        )

    def load_qkv(i):
        step = w_qkv.shape[1]
        at = pl.ds(pl.multiple_of(i * step, step), step)
        return pltpu.make_async_copy(
            w_qkv_hbm.at[at], w_qkv.at[lax.rem(i, 2)], weight_sems.at[1, lax.rem(i, 2)]
        )

    def unrotate(value):
        lanes = value.shape[1]
        lane = lax.broadcasted_iota(jnp.int32, value.shape, 1)
        swapped = jnp.where(
            lane % HD < HD // 2,
            pltpu.roll(value, lanes - HD // 2, 1),
            pltpu.roll(value, HD // 2, 1),
        )
        return (value * cosine[:, :lanes] + swapped * sine[:, :lanes]).astype(bf16)

    per_group = H // KV
    wide = GROUP * per_group * HD
    narrow = GROUP * HD

    def attend(i, _):
        load_output(i).wait()
        at = pl.ds(pl.multiple_of(i * wide, wide), wide)
        kv_at = pl.ds(pl.multiple_of(i * narrow, narrow), narrow)
        grad_mixed = against(grad_branch[...], w_output[lax.rem(i, 2)]).astype(bf16)
        query, key, value = queries[:, at], keys[:, kv_at], values[:, kv_at]
        is_allowed = allowed[...] > 0.5
        grad_queries, grad_keys, grad_values = [], [], []
        for k in range(GROUP):
            k_head, v_head = key[:, k * HD : (k + 1) * HD], value[:, k * HD : (k + 1) * HD]
            grad_k = grad_v = None
            for j in range(k * per_group, (k + 1) * per_group):
                q_head = query[:, j * HD : (j + 1) * HD]
                mixed_head = grad_mixed[:, j * HD : (j + 1) * HD]
                scores = jnp.where(is_allowed, against(q_head, k_head) * 0.125, -1e30)
                lifted = jnp.exp(scores - jnp.max(scores, axis=-1, keepdims=True))
                weights = lifted / jnp.sum(lifted, axis=-1, keepdims=True)
                grad_weights = against(mixed_head, v_head)
                inner = jnp.sum(weights * grad_weights, axis=-1, keepdims=True)
                grad_scores = (weights * (grad_weights - inner)).astype(bf16)
                part_v = transposed(weights.astype(bf16), mixed_head)
                part_k = transposed(grad_scores, q_head)
                grad_v = part_v if grad_v is None else grad_v + part_v
                grad_k = part_k if grad_k is None else grad_k + part_k
                grad_queries.append(
                    jnp.dot(grad_scores, k_head, preferred_element_type=f32) * 0.125
                )
            grad_keys.append(grad_k * 0.125)
            grad_values.append(grad_v)
        grad_qkv[:, at] = unrotate(jnp.concatenate(grad_queries, axis=1))
        k_at = pl.ds(pl.multiple_of(H * HD + i * narrow, narrow), narrow)
        v_at = pl.ds(pl.multiple_of((H + KV) * HD + i * narrow, narrow), narrow)
        grad_qkv[:, k_at] = unrotate(jnp.concatenate(grad_keys, axis=1))
        grad_qkv[:, v_at] = jnp.concatenate(grad_values, axis=1).astype(bf16)

        @pl.when(i + 2 < KV // GROUP)
        def _():
            load_output(i + 2).start()

        return 0

    def column(value, lane):
        at_lane = lax.broadcasted_iota(jnp.int32, (length, 128), 1) == lane
        at_lane = at_lane.astype(f32).astype(bf16)
        high = value.astype(bf16)
        low = (value - high.astype(f32)).astype(bf16)
        return transposed(high, at_lane) + transposed(low, at_lane)

    def norm_grads():
        grad_gates = row_grads[:, width:]
        inner = jnp.sum(gates[...] * grad_gates, axis=-1, keepdims=True)
        grad_logits = (gates[...] * (grad_gates - inner)).astype(bf16)
        grad_normed_moe = row_grads[:, :width] + against(grad_logits, router[...])
        inv = lax.rsqrt(jnp.mean(residual[...] * residual[...], axis=-1, keepdims=True) + epsilon)
        unit = residual[...] * inv
        scaled = grad_normed_moe * gains[1:2]
        total = cotangent[...].astype(f32) + inv * (
            scaled - unit * jnp.mean(scaled * unit, axis=-1, keepdims=True)
        )
        grad_residual[...] = total
        grad_branch[...] = total.astype(bf16)
        base_small[...] = transposed(normed_moe[...], grad_logits) + column(
            grad_normed_moe * unit, EXPERTS + 1
        )

    def input_grads():
        tile = w_qkv.shape[1]

        def step(i, _):
            load_qkv(i).wait()
            at = pl.ds(pl.multiple_of(i * tile, tile), tile)
            grad_normed[:, at] = against(grad_qkv[...], w_qkv[lax.rem(i, 2)])

            @pl.when(i + 2 < width // tile)
            def _():
                load_qkv(i + 2).start()

            return 0

        lax.fori_loop(0, width // tile, step, 0)
        inputs = tokens_ref[...].astype(f32)
        inv = lax.rsqrt(jnp.mean(inputs * inputs, axis=-1, keepdims=True) + epsilon)
        unit = inputs * inv
        onto = grad_normed[...] * unit
        scaled = grad_normed[...] * gains[:1]
        grad_tokens_out[...] = (
            grad_residual[...]
            + inv * (scaled - unit * jnp.mean(scaled * unit, axis=-1, keepdims=True))
        ).astype(bf16)
        part = base_small[...] + column(onto, EXPERTS)
        part_small[...] = part.astype(bf16).reshape(part_small.shape)
        small.to_c().start()

    load_rows(0).start()
    for load in load_combined:
        load.start()
    for e in range(2):
        for k in range(2):
            load_grads(e, k).start()
    for i in range(2):
        load_output(i).start()
        load_qkv(i).start()
    norm_grads()
    greet([to[name] for name in ("z1", "z2", "z3", "y", "x", "c", "xc")])
    own_tokens = pl.ds(0, length)
    lefts = left_copies(0, mixed, left_output) + left_copies(1, normed, left_qkv)
    rights = {m: right_copy(2, grad_branch, right_output, m) for m in (1, 2, 3)}
    qkv_rights = {m: right_copy(3, grad_qkv, right_qkv, m) for m in (1, 2, 3)}
    rights[2].start()
    rights[1].start()
    for made in lefts:
        made.start()
    left_output[:, :, own_tokens] = mixed[:, core, side]
    left_qkv[:, :, own_tokens] = normed[:, core, side]
    right_output[own_tokens] = grad_branch[...]
    o_start()

    for r in range(ZLINE):
        load_rows(r).wait()

        def turn(j, _, r=r):
            at = pl.ds(pl.multiple_of(j * 256, 256), 256)
            turned[at, pl.ds(r * count, count)] = rows[:, at].T
            return 0

        lax.fori_loop(0, width // 256, turn, 0)
        if r + 1 < ZLINE:
            load_rows(r + 1).start()

    def send_y(e):
        return remote(
            part_gate_up.at[e, 1 - y], heard_gate_up.at[e], y_send.at[e], y_recv.at[e], to["y"]
        )

    def send_z(e, m):
        return remote(
            part_gate_up.at[e, y, z_of[m]],
            heard_z.at[m - 1, e],
            z_send.at[m - 1, e],
            z_recv.at[m - 1, e],
            to[f"z{m}"],
        )

    def reduce(e):
        send_y(e).wait_recv()
        for b in range(ZLINE):
            part_gate_up[e, y, b] = add(part_gate_up[e, y, b], heard_gate_up[e, b])
        for m in range(1, ZLINE):
            send_z(e, m).start()

    def gate_up(e, _):
        for k in range(2):
            load_grads(e, k).wait()
        right = grads[lax.rem(e, 2)].reshape(tokens, 2 * hidden)

        def step(b, _):
            at = pl.ds(pl.multiple_of(b * rows_y * n, 128), rows_y * n)
            result = jnp.dot(turned[at, :], right, preferred_element_type=f32).astype(bf16)
            for k in range(rows_y):
                part_gate_up[e, k, b] = result[k * n : (k + 1) * n]
            return 0

        lax.fori_loop(0, ZLINE, step, 0)

        @pl.when(e + 2 < owned)
        def _():
            for k in range(2):
                load_grads(e + 2, k).start()

        return 0

    rights[2].wait_recv()
    rights[3].start()
    lax.fori_loop(0, 1, gate_up, 0)
    send_y(0).start()
    lax.fori_loop(0, KV // GROUP // 2, attend, 0)
    lax.fori_loop(1, 2, gate_up, 0)
    send_y(1).start()
    lax.fori_loop(KV // GROUP // 2, KV // GROUP, attend, 0)
    qkv_rights[2].start()
    qkv_rights[1].start()
    right_qkv[own_tokens] = grad_qkv[...]
    o_after_z1()
    for made in lefts:
        made.wait_recv()
    rights[1].wait_recv()
    rights[3].wait_recv()
    products(output, left_output, right_output)
    reduce(0)
    lax.fori_loop(2, 3, gate_up, 0)
    send_y(2).start()
    o_end()
    qkv_rights[2].wait_recv()
    qkv_rights[3].start()
    reduce(1)
    lax.fori_loop(3, 4, gate_up, 0)
    send_y(3).start()
    qkv_rights[1].wait_recv()
    qkv_rights[3].wait_recv()
    products(qkv, left_qkv, right_qkv)
    input_grads()
    reduce(2)
    lax.fori_loop(4, 5, gate_up, 0)
    send_y(4).start()
    small.after_c()
    output.after_z1()
    reduce(3)
    lax.fori_loop(5, 6, gate_up, 0)
    send_y(5).start()
    lax.fori_loop(6, 7, gate_up, 0)
    small.after_x()
    output.after_z2()
    reduce(4)
    send_y(6).start()
    lax.fori_loop(7, 8, gate_up, 0)
    qkv.after_y()
    reduce(5)
    send_y(7).start()
    lax.fori_loop(8, 9, gate_up, 0)
    lax.fori_loop(9, 10, gate_up, 0)
    output.after_y()
    qkv.after_z1()
    reduce(6)
    send_y(8).start()
    small.after_y()
    reduce(7)
    send_y(9).start()
    qkv.after_z2()
    output.after_back()
    small.after_z1()
    reduce(8)
    small.after_z2()
    qkv.after_back()
    small.after_back()
    reduce(9)

    def keep(e):
        return pltpu.make_async_copy(
            stage.at[lax.rem(e, 2)], gate_up_out.at[e], store_sems.at[lax.rem(e, 2)]
        )

    def collect(e, _):
        slot = lax.rem(e, 2)

        @pl.when(e >= 2)
        def _():
            keep(e - 2).wait()

        for m in range(ZLINE):
            if m:
                send_z(e, m).wait_recv()
                block = heard_z[m - 1, e]
            else:
                block = part_gate_up[e, y, z]
            for k in range(2):
                at = pl.ds(pl.multiple_of(k * F + z_of[m] * hidden, hidden), hidden)
                stage[slot, :, at] = block[:, k * hidden : (k + 1) * hidden]
        keep(e).start()
        return 0

    lax.fori_loop(0, owned, collect, 0)

    for e in (owned - 2, owned - 1):
        keep(e).wait()

    def close(e, _):
        send_y(e).wait_send()
        for m in range(1, ZLINE):
            send_z(e, m).wait_send()
        return 0

    lax.fori_loop(0, owned, close, 0)
    for array in (output, small, qkv):
        array.close()
    small.to_c().wait_send()
    small.to_x().wait_send()
    for k in range(3):
        o_copy(k).wait_send()
    for made in lefts + list(rights.values()) + list(qkv_rights.values()):
        made.wait_send()


def finish(rows_y, rows, grads, combined, heard, w_output, w_qkv, *small):
    _, count, width = rows.shape
    hidden = F // ZLINE
    owned = grads.shape[2] // (2 * hidden)
    length = small[0].shape[0]
    blocks = ZLINE * rows_y
    n = width // blocks
    columns = (w_output.shape[1], 128, w_qkv.shape[1])
    any_space = pl.BlockSpec(memory_space=pl.ANY)
    vmem = pl.BlockSpec(memory_space=pltpu.VMEM)
    sems = pltpu.SemaphoreType.DMA

    def summed(wide, own_rows, z_first=False):
        heard = own_rows != n // 4
        ends = (rows_y, n // 4, wide) if z_first else (n // 4, wide)
        return [
            pltpu.VMEM((ZLINE, rows_y, own_rows, wide), bf16),
            pltpu.VMEM((ZLINE, rows_y, n // 2, wide) if heard else (16, 128), bf16),
            pltpu.VMEM((ZLINE, rows_y, n // 4, wide) if heard else (16, 128), bf16),
            pltpu.VMEM((1 if z_first else ZLINE, n // 4, wide), bf16),
            pltpu.VMEM((2,) + ends, bf16),
            pltpu.VMEM(ends, bf16),
        ]

    return pl.pallas_call(
        functools.partial(finish_kernel, rows_y),
        name="finish",
        out_shape=(
            jax.ShapeDtypeStruct((owned, n, 2 * F), bf16),
            jax.ShapeDtypeStruct((length, width), bf16),
            jax.ShapeDtypeStruct((length, width), bf16),
        )
        + tuple(jax.ShapeDtypeStruct((n, v), bf16) for v in columns),
        in_specs=[any_space] * 6 + [vmem] * len(small),
        out_specs=(any_space,) + (vmem,) * 5,
        scratch_shapes=[
            pltpu.VMEM((count, width), bf16),
            pltpu.VMEM((width, ZLINE * count), bf16),
            pltpu.VMEM((2, ZLINE, count, 2 * hidden), bf16),
            pltpu.VMEM((owned, rows_y, ZLINE, n, 2 * hidden), bf16),
            pltpu.VMEM((owned, ZLINE, n, 2 * hidden), bf16),
            pltpu.VMEM((ZLINE - 1, owned, n, 2 * hidden), bf16),
            pltpu.VMEM((2, n, 2 * F), bf16),
            pltpu.VMEM((ZLINE, length, width), bf16),
            pltpu.VMEM((ZLINE, length, width), bf16),
            pltpu.VMEM((2, length, width), bf16),
            pltpu.VMEM((length, width), bf16),
            pltpu.VMEM((2, GROUP * (H // KV) * HD, width), bf16),
            pltpu.VMEM((2, 256, columns[2]), bf16),
            pltpu.VMEM((length, columns[2]), bf16),
            pltpu.VMEM((length, width), f32),
            pltpu.VMEM((blocks, n // 4, 4 * length), bf16),
            pltpu.VMEM((blocks, n // 4, 4 * length), bf16),
            pltpu.VMEM((4 * length, columns[0]), bf16),
            pltpu.VMEM((4 * length, columns[2]), bf16),
            pltpu.VMEM((ZLINE, rows_y, n, 128), bf16),
            pltpu.VMEM((length, width), f32),
            pltpu.VMEM((length, width), bf16),
            pltpu.VMEM((width, 128), f32),
            *summed(columns[0], n // 4, True),
            *summed(columns[1], n // 2),
            *summed(columns[2], n // 4),
            sems,
            sems((2,)),
            sems((2, 2)),
            sems((2, 2)),
            sems((2,)),
            sems((owned,)),
            sems((owned,)),
            sems((ZLINE - 1, owned)),
            sems((ZLINE - 1, owned)),
            sems((3, 8 + ZLINE)),
            sems((3, 8 + ZLINE)),
            sems((4, 4)),
            sems((4, 4)),
            sems((3,)),
            sems((3,)),
        ],
        compiler_params=pltpu.CompilerParams(
            collective_id=3, has_side_effects=True, vmem_limit_bytes=63 * 2**20
        ),
    )(rows, grads, combined, heard, w_output, w_qkv, *small)


def widen_kernel(
    gate_up,
    down,
    qkv,
    output,
    small,
    tokens,
    grad_tokens,
    gate_up_out,
    down_out,
    query_out,
    key_out,
    value_out,
    output_out,
    router_out,
    gains_out,
    tokens_out,
    grad_tokens_out,
):
    gate_up_out[...] = gate_up[...].astype(f32)
    down_out[...] = down[...].astype(f32)

    @pl.when(pl.program_id(0) == 0)
    def _():
        query_out[...] = qkv[:, : H * HD].astype(f32)
        key_out[...] = qkv[:, H * HD : (H + KV) * HD].astype(f32)
        value_out[...] = qkv[:, (H + KV) * HD :].astype(f32)
        output_out[...] = output[...].astype(f32)
        router_out[...] = small[:, :EXPERTS].astype(f32)
        lane, row = (lax.broadcasted_iota(jnp.int32, (8, 128), k) for k in (1, 0))
        gains_out[...] = against((lane == row + EXPERTS).astype(f32).astype(bf16), small[...])
        tokens_out[...] = tokens[...]
        grad_tokens_out[...] = grad_tokens[...]


def widen(*sums):
    gate_up, down, qkv, output, small, tokens, grad_tokens = sums
    n = qkv.shape[0]

    def whole(shape):
        return pl.BlockSpec(shape, lambda e: (0,) * len(shape))

    def one(shape):
        return pl.BlockSpec((1,) + shape[1:], lambda e: (e, 0, 0))

    shapes = [(n, H * HD), (n, KV * HD), (n, KV * HD), output.shape, (n, EXPERTS), (8, n)]
    return pl.pallas_call(
        widen_kernel,
        name="widen",
        grid=(gate_up.shape[0],),
        out_shape=[jax.ShapeDtypeStruct(v, f32) for v in [gate_up.shape, down.shape] + shapes]
        + [jax.ShapeDtypeStruct(tokens.shape, bf16)] * 2,
        in_specs=[one(gate_up.shape), one(down.shape)] + [whole(v.shape) for v in sums[2:]],
        out_specs=[one(gate_up.shape), one(down.shape)]
        + [whole(v) for v in shapes + [tokens.shape] * 2],
        compiler_params=pltpu.CompilerParams(vmem_limit_bytes=63 * 2**20),
    )(*sums)


def permuted(
    tokens,
    segments,
    routes,
    w_query,
    w_key,
    w_value,
    w_output,
    w_router,
    gain_attn,
    gain_moe,
    w_gate_up,
    w_down,
    cotangent,
):
    place = Place()
    length, width = tokens.shape
    owned = w_gate_up.shape[0]
    rows = w_query.shape[0]
    hidden = F // ZLINE
    per_group = H // KV
    q_end, k_end, v_end = H * HD, (H + KV) * HD, (H + 2 * KV) * HD
    o_end = v_end + width

    small = jnp.concatenate(
        [w_router, gain_attn[:, None], gain_moe[:, None], jnp.zeros((rows, 128 - EXPERTS - 2), bf16)],
        axis=1,
    )
    shard = jnp.concatenate([w_query, w_key, w_value, w_output, small], axis=1)
    full, order = gather_weights(place, shard)
    full_qkv, full_output = full[:, :v_end], full[:, v_end:o_end]
    full_small = transposed(order, full[:, o_end:]).astype(bf16)
    full_router = full_small[:, :EXPERTS]
    attn_gain = full_small[:, EXPERTS].astype(f32)
    moe_gain = full_small[:, EXPERTS + 1].astype(f32)

    chosen_mask = jnp.any(
        routes[:, :, None] == jnp.arange(EXPERTS, dtype=jnp.int32), axis=1
    )
    dy_block = jnp.concatenate(
        [cotangent, chosen_mask.astype(bf16), jnp.zeros((length, 128 - EXPERTS), bf16)], axis=1
    )
    dy_groups = gather_tokens(place, dy_block)

    cosine_table, sine_table = tables(length, HD)
    inputs = tokens.astype(f32)
    inv_attn = lax.rsqrt(jnp.mean(inputs * inputs, axis=-1, keepdims=True) + epsilon)
    unit_attn = inputs * inv_attn
    normed = (unit_attn * attn_gain).astype(bf16)
    normed = against(normed, order).astype(bf16)
    qkv = dot(normed, full_qkv)
    queries = rotate(qkv[:, :q_end].reshape(length, H, HD), cosine_table, sine_table)
    queries = queries.astype(bf16).reshape(length, KV, per_group, HD)
    key_rows = rotate(
        qkv[:, q_end:k_end].reshape(length, KV, HD), cosine_table, sine_table
    ).astype(bf16)
    values = qkv[:, k_end:].astype(bf16).reshape(length, KV, HD)
    segment = segments[0]
    position = jnp.arange(length, dtype=jnp.int32)
    allowed = (segment[:, None] == segment[None, :]) & (position[:, None] >= position[None, :])
    scores = (
        jnp.einsum("qkgd,skd->kgqs", queries, key_rows, preferred_element_type=f32) * 0.125
    )
    scores = jnp.where(allowed, scores, -1e30)
    maximum = jnp.max(scores, axis=-1, keepdims=True)
    lifted_scores = jnp.exp(scores - maximum)
    full_weights = lifted_scores / jnp.sum(lifted_scores, axis=-1, keepdims=True)
    attn_weights = full_weights.astype(bf16)
    mixed = jnp.einsum("kgqs,skd->qkgd", attn_weights, values, preferred_element_type=f32)
    mixed = mixed.reshape(length, H * HD).astype(bf16)
    mixed = against(mixed, order).astype(bf16)
    residual = inputs + dot(mixed, full_output)
    inv_moe = lax.rsqrt(jnp.mean(residual * residual, axis=-1, keepdims=True) + epsilon)
    unit_moe = residual * inv_moe
    normed_moe = (unit_moe * moe_gain).astype(bf16)

    def gates_of(rows_in, mask):
        logits = jnp.where(mask, dot(rows_in, full_router), -1e30)
        lifted = jnp.where(mask, jnp.exp(logits - jnp.max(logits, axis=-1, keepdims=True)), 0.0)
        return lifted / jnp.sum(lifted, axis=-1, keepdims=True)

    gates = gates_of(normed_moe, chosen_mask)

    def columns(start):
        cut = lax.dynamic_slice_in_dim(w_gate_up, start + place.z * hidden, hidden, 2)
        return cut.swapaxes(0, 1).reshape(width, owned * hidden)

    slice_gate_up = jnp.concatenate([columns(0), columns(F)], axis=1)
    slice_down = lax.dynamic_slice_in_dim(w_down, place.z * hidden, hidden, 1)
    slice_down = slice_down.reshape(owned * hidden, width)
    moe_groups = gather_tokens(place, normed_moe)
    span = owned * hidden
    acts, grads_gate_up, gate_parts = [], [], []
    for normed_rows, dy_rows in zip(moe_groups, dy_groups):
        count = normed_rows.shape[0]
        group_gates = gates_of(normed_rows, dy_rows[:, width : width + EXPERTS] > 0.5)
        group_gates = lax.dynamic_slice_in_dim(group_gates, place.ex * owned, owned, 1)
        spread_gates = jnp.broadcast_to(group_gates[:, :, None], (count, owned, hidden))
        spread_gates = spread_gates.reshape(count, span)
        gate_up = dot(normed_rows, slice_gate_up)
        gate_part, up_part = gate_up[:, :span], gate_up[:, span:]
        plain_grad = against(dy_rows[:, :width], slice_down)
        sigmoid_gate = jax.nn.sigmoid(gate_part)
        swished = gate_part * sigmoid_gate
        activation = swished * up_part
        grad_act = plain_grad * spread_gates
        gate_parts.append(jnp.sum((plain_grad * activation).reshape(count, owned, hidden), axis=-1))
        acts.append((spread_gates * activation).astype(bf16))
        grads_gate_up.append(
            jnp.concatenate(
                [
                    grad_act * up_part * sigmoid_gate * (1.0 + gate_part * (1.0 - sigmoid_gate)),
                    grad_act * swished,
                ],
                axis=-1,
            ).astype(bf16)
        )
    row_parts = [against(g, slice_gate_up).astype(bf16) for g in grads_gate_up]
    row_grads = scatter_tokens(place, row_parts, length)
    out_parts = [dot(a, slice_down).astype(bf16) for a in acts]
    output = (residual + scatter_tokens(place, out_parts, length)).astype(bf16)

    gate_parts = [g.T for g in gate_parts]
    two = [gate_parts[i] + swap(gate_parts[i + 2], "dp", place.z_bits[1]) for i in range(2)]
    mine = two[0] + swap(two[1], "dp", place.z_bits[0])
    mine = mine.reshape(owned, 2, place.ex_size // 2, length)
    heard = [
        swap(mine[:, m % 2, m // 2], "expert", m) if m else mine[:, 0, 0]
        for m in range(place.ex_size)
    ]
    heard = jnp.stack(heard)
    grad_gates = jnp.concatenate(
        [pick(heard, place.ex ^ j) for j in range(place.ex_size)], axis=0
    ).T
    grad_logits = (
        gates * (grad_gates - jnp.sum(gates * grad_gates, axis=-1, keepdims=True))
    ).astype(bf16)

    all_rows = jnp.concatenate([v for v in moe_groups], axis=0)
    all_dy = jnp.concatenate([v[:, :width] for v in dy_groups], axis=0)
    all_grads = jnp.concatenate(grads_gate_up, axis=0)
    all_acts = jnp.concatenate(acts, axis=0)

    def reduce_y(part, axis):
        part = jnp.moveaxis(part, axis, 0)
        for mask in place.y_bits[::-1]:
            at = (place.y // mask) % 2
            half = part.reshape((2, part.shape[0] // 2) + part.shape[1:])
            away = swap(pick(half, 1 - at), "dp", mask)
            part = (pick(half, at).astype(f32) + away.astype(f32)).astype(bf16)
        return part[0]

    shard_down = transposed(all_acts, all_dy).astype(bf16)
    shard_down = shard_down.reshape(owned, place.rows_y, hidden // place.rows_y, width)
    shard_down = reduce_y(shard_down, 1).astype(f32)
    part_gate_up = transposed(all_rows, all_grads).astype(bf16)
    part_gate_up = part_gate_up.reshape(ZLINE, place.rows_y, rows, 2 * span)
    part_gate_up = reduce_y(part_gate_up, 1)
    heard = [pick(part_gate_up, place.z)] + [
        swap(pick(part_gate_up, place.z ^ m), "dp", m * place.rows_y) for m in range(1, ZLINE)
    ]
    heard = jnp.stack(heard)
    shard_gate_up = jnp.stack([pick(heard, place.z ^ j) for j in range(ZLINE)], axis=0)
    shard_gate_up = shard_gate_up.reshape(ZLINE, rows, 2, owned, hidden)
    shard_gate_up = shard_gate_up.transpose(3, 1, 2, 0, 4).reshape(owned, rows, 2 * F).astype(f32)

    grad_out = cotangent.astype(f32)
    part_router = transposed(normed_moe, grad_logits)
    grad_normed_moe = row_grads + against(grad_logits, full_router)
    part_gain_moe = jnp.sum(grad_normed_moe * unit_moe, axis=0)
    scaled_moe = grad_normed_moe * moe_gain
    grad_residual = grad_out + inv_moe * (
        scaled_moe - unit_moe * jnp.mean(scaled_moe * unit_moe, axis=-1, keepdims=True)
    )
    grad_branch = grad_residual.astype(bf16)
    part_output = transposed(mixed, grad_branch)
    grad_mixed = dot(against(grad_branch, full_output).astype(bf16), order).astype(bf16)
    grad_mixed = grad_mixed.reshape(length, KV, per_group, HD)
    grad_weights = jnp.einsum(
        "qkgd,skd->kgqs", grad_mixed, values, preferred_element_type=f32
    )
    grad_values = jnp.einsum(
        "kgqs,qkgd->skd", attn_weights, grad_mixed, preferred_element_type=f32
    )
    grad_values = grad_values.astype(bf16).reshape(length, KV * HD)
    grad_scores = (
        full_weights * (grad_weights - jnp.sum(full_weights * grad_weights, axis=-1, keepdims=True))
    ).astype(bf16)
    grad_queries = (
        jnp.einsum("kgqs,skd->qkgd", grad_scores, key_rows, preferred_element_type=f32) * 0.125
    )
    grad_queries = rotate(grad_queries.reshape(length, H, HD), cosine_table, -sine_table)
    grad_queries = grad_queries.astype(bf16).reshape(length, H * HD)
    grad_keys = (
        jnp.einsum("kgqs,qkgd->skd", grad_scores, queries, preferred_element_type=f32) * 0.125
    )
    grad_keys = rotate(grad_keys, cosine_table, -sine_table)
    grad_keys = grad_keys.astype(bf16).reshape(length, KV * HD)
    grad_qkv = jnp.concatenate([grad_queries, grad_keys, grad_values], axis=1)
    part_qkv = transposed(normed, grad_qkv)
    grad_normed = against(grad_qkv, full_qkv)
    grad_normed = lax.dot_general(
        grad_normed,
        order.astype(f32),
        (((1,), (0,)), ((), ())),
        precision=lax.Precision.HIGHEST,
        preferred_element_type=f32,
    )
    part_gain_attn = jnp.sum(grad_normed * unit_attn, axis=0)
    scaled_attn = grad_normed * attn_gain
    grad_tokens = (
        grad_residual
        + inv_attn
        * (scaled_attn - unit_attn * jnp.mean(scaled_attn * unit_attn, axis=-1, keepdims=True))
    ).astype(bf16)
    part_small = jnp.concatenate(
        [
            part_router.astype(bf16),
            part_gain_attn[:, None].astype(bf16),
            part_gain_moe[:, None].astype(bf16),
            jnp.zeros((width, 128 - EXPERTS - 2), bf16),
        ],
        axis=1,
    )
    part_small = dot(order, part_small).astype(bf16)
    summed = scatter_weights(
        place,
        jnp.concatenate([part_qkv.astype(bf16), part_output.astype(bf16), part_small], axis=1),
    )
    return (
        output,
        grad_tokens,
        summed[:, :q_end],
        summed[:, q_end:k_end],
        summed[:, k_end:v_end],
        summed[:, v_end:o_end],
        summed[:, o_end : o_end + EXPERTS],
        summed[:, o_end + EXPERTS],
        summed[:, o_end + EXPERTS + 1],
        shard_gate_up,
        shard_down,
    )


def local(
    tokens,
    segments,
    routes,
    w_query,
    w_key,
    w_value,
    w_output,
    w_router,
    gain_attn,
    gain_moe,
    w_gate_up,
    w_down,
    cotangent,
):
    place = Place()
    if place.ex_size != 4 or place.rows_y != 2:
        return permuted(
            tokens,
            segments,
            routes,
            w_query,
            w_key,
            w_value,
            w_output,
            w_router,
            gain_attn,
            gain_moe,
            w_gate_up,
            w_down,
            cotangent,
        )
    length, width = tokens.shape
    per_group = H // KV
    v_end = (H + 2 * KV) * HD

    angles = np.arange(length)[:, None] * 10000.0 ** (-2.0 * np.arange(HD // 2) / HD)[None, :]
    repeats = (1, GROUP * per_group)
    cosine = jnp.asarray(np.tile(np.tile(np.cos(angles), (1, 2)), repeats), f32)
    sine = np.concatenate([np.sin(angles), -np.sin(angles)], axis=1)
    sine = jnp.asarray(np.tile(sine, repeats), f32)
    (
        full_qkv,
        full_output,
        all_dy,
        plain_grads,
        full_small,
        queries,
        key_rows,
        values,
        residual,
        normed_moe,
        normed,
        mixed,
        gains,
        gates,
        allowed,
    ) = gather(
        place.rows_y,
        (w_query, w_key, w_value, w_output, w_router.T, gain_attn[None, :], gain_moe[None, :]),
        cotangent,
        tokens,
        segments,
        routes.T,
        cosine,
        sine,
        w_down,
    )
    full_small = full_small.reshape(width, 128)
    all_rows, all_grads, shard_down, combined, heard, row_grads = moe(
        place.rows_y, normed_moe, all_dy, plain_grads, w_gate_up, w_down, full_small
    )
    shard_gate_up, output, grad_tokens, sum_output, sum_small, sum_qkv = finish(
        place.rows_y,
        all_rows,
        all_grads,
        combined,
        heard,
        full_output.reshape(width, width),
        full_qkv.reshape(width, v_end),
        row_grads,
        gates,
        cotangent,
        residual,
        normed_moe,
        gains,
        full_small,
        tokens,
        mixed,
        normed,
        queries,
        key_rows,
        values,
        allowed,
        cosine,
        sine,
    )
    (
        shard_gate_up,
        shard_down,
        shard_query,
        shard_key,
        shard_value,
        shard_output,
        shard_router,
        shard_gains,
        output,
        grad_tokens,
    ) = widen(shard_gate_up, shard_down, sum_qkv, sum_output, sum_small, output, grad_tokens)
    return (
        output,
        grad_tokens,
        shard_query,
        shard_key,
        shard_value,
        shard_output,
        shard_router,
        shard_gains[0],
        shard_gains[1],
        shard_gate_up,
        shard_down,
    )


def solution(mesh):
    return jax.shard_map(
        local,
        mesh=mesh,
        in_specs=(
            P(("dp", "expert"), None),
            P(("dp", "expert"), None),
            P(("dp", "expert"), None),
            P("dp", None),
            P("dp", None),
            P("dp", None),
            P("dp", None),
            P("dp", None),
            P("dp"),
            P("dp"),
            P("expert", None, None),
            P("expert", None, None),
            P(("dp", "expert"), None),
        ),
        out_specs=(
            P(("dp", "expert"), None),
            P(("dp", "expert"), None),
            P("dp", None),
            P("dp", None),
            P("dp", None),
            P("dp", None),
            P("dp", None),
            P("dp"),
            P("dp"),
            P("expert", "dp", None),
            P("expert", "dp", None),
        ),
        check_vma=False,
    )
```

```python
import functools

import jax
import jax.numpy as jnp
import numpy as np
from jax import lax
from jax.experimental import pallas as pl
from jax.experimental.pallas import tpu as pltpu
from jax.sharding import PartitionSpec as P

H = 24
KV = 8
HD = 64
F = 512
EXPERTS = 40
ZLINE = 4
GROUP = 2


epsilon = 1e-05
f32 = jnp.float32
bf16 = jnp.bfloat16


def tables(length, size):
    half_size = size // 2
    frequency = jnp.power(10000.0, -2.0 * jnp.arange(half_size, dtype=f32) / size)
    angles = jnp.arange(length, dtype=f32)[:, None] * frequency[None, :]
    return (jnp.cos(angles)[:, None, :], jnp.sin(angles)[:, None, :])


def rotate(source, cosine_table, sine_table):
    half_size = source.shape[-1] // 2
    first_half = source[..., :half_size]
    second_half = source[..., half_size:]
    return jnp.concatenate(
        [
            first_half * cosine_table - second_half * sine_table,
            second_half * cosine_table + first_half * sine_table,
        ],
        axis=-1,
    )


def dot(left_side, right_side):
    return jnp.dot(left_side, right_side, preferred_element_type=f32)


def transposed(left_side, right_side):
    return lax.dot_general(
        left_side, right_side, (((0,), (0,)), ((), ())), preferred_element_type=f32
    )


def against(left_side, right_side):
    return lax.dot_general(
        left_side, right_side, (((1,), (1,)), ((), ())), preferred_element_type=f32
    )


def swap(value, axis, mask):
    size = lax.axis_size(axis)
    return lax.ppermute(value, axis, [(i, i ^ mask) for i in range(size)])


def pick(value, at):
    return lax.dynamic_index_in_dim(value, at, 0, keepdims=False)


def bits(first, size):
    masks, step = [], 1
    while step < size:
        masks.append(first * step)
        step *= 2
    return masks


class Place:
    def __init__(self):
        self.dp_size = lax.axis_size("dp")
        self.ex_size = lax.axis_size("expert")
        self.dp = lax.axis_index("dp")
        self.ex = lax.axis_index("expert")
        self.rows_y = self.dp_size // ZLINE
        self.z = self.dp // self.rows_y
        self.y = self.dp % self.rows_y
        self.z_bits = bits(self.rows_y, ZLINE)
        self.y_bits = bits(1, self.rows_y)
        self.x_bits = bits(2, self.ex_size // 2)


def gather_weights(place, shard):
    n, columns = shard.shape
    piece = n // 6
    cut = shard.reshape(3, 2, piece, columns)
    core = place.ex % 2
    side = (place.ex // 2) % 2
    own = pick(cut.swapaxes(0, 1), core)
    sibling = pick(cut.swapaxes(0, 1), 1 - core)

    def ordered(parts):
        return jnp.stack([pick(parts, 2 * side), parts[1], pick(parts, 2 - 2 * side)])

    own, sibling = ordered(own), ordered(sibling)
    blocks = {0: own[:2]}
    for mask in place.z_bits + place.y_bits:
        blocks.update({m ^ mask: swap(v, "dp", mask) for m, v in list(blocks.items())})
    rows = []
    for m in range(place.dp_size):
        if m == 0:
            rows.append(jnp.stack([own, sibling], axis=1))
            continue
        other = swap(blocks[m][0], "expert", 2)
        trio = jnp.concatenate([blocks[m], other[None]], axis=0)
        rows.append(jnp.stack([trio, swap(trio, "expert", 1)], axis=1))
    full = jnp.stack(rows)
    total = place.dp_size * n
    k = jnp.arange(total, dtype=jnp.int32)
    block, part = k // n, (k % n) // (2 * piece)
    half, line = (k % (2 * piece)) // piece, k % piece
    part = jnp.where(part == 1, 1, jnp.where(part == 0, 2 * side, 2 - 2 * side))
    at = (block ^ place.dp) * n + part * 2 * piece + (half ^ core) * piece + line
    order = (at[:, None] == jnp.arange(total, dtype=jnp.int32)[None, :]).astype(bf16)
    return full.reshape(total, columns), order


def scatter_weights(place, part):
    total, columns = part.shape
    n = total // place.dp_size
    piece = n // 6
    core = place.ex % 2
    side = (place.ex // 2) % 2

    def add(left, right):
        return (left.astype(f32) + right.astype(f32)).astype(bf16)

    part = part.reshape(place.dp_size, 3, 2, piece, columns)
    kept = add(part[:, :, 0], swap(part[:, :, 1], "expert", 1))
    first = add(kept[:, 0], swap(kept[:, 2], "expert", 2))
    blocks = {m: jnp.stack([first[m], kept[m, 1]]) for m in range(place.dp_size)}
    for mask in (place.z_bits + place.y_bits)[::-1]:
        blocks = {
            m: add(v, swap(blocks[m ^ mask], "dp", mask))
            for m, v in blocks.items()
            if m & mask == 0
        }
    mine = blocks[0]
    middle = add(mine[1], swap(mine[1], "expert", 2))
    trio = jnp.stack([mine[0], middle, swap(mine[0], "expert", 2)])
    for mask in place.x_bits[1:]:
        trio = add(trio, swap(trio, "expert", mask))
    both = jnp.stack([trio, swap(trio, "expert", 1)], axis=1)
    both = jnp.where(side == 0, both, both[::-1])
    both = jnp.where(core == 0, both, both[:, ::-1])
    return both.reshape(n, columns).astype(f32)


def gather_tokens(place, block):
    blocks = {0: block}
    for mask in place.z_bits:
        blocks.update({m ^ mask: swap(v, "dp", mask) for m, v in list(blocks.items())})
    groups = []
    for r in range(ZLINE):
        row = [blocks[r * place.rows_y]]
        for mask in place.x_bits:
            row = row + [swap(v, "expert", mask) for v in row]
        row = jnp.concatenate(row, axis=0)
        groups.append(jnp.concatenate([row, swap(row, "expert", 1)], axis=0))
    return groups


def scatter_tokens(place, groups, length):
    def add(left, right):
        return left.astype(f32) + right.astype(f32)

    reduced = []
    for part in groups:
        half = part.shape[0] // 2
        kept = add(part[:half], swap(part[half:], "expert", 1)).astype(bf16)
        for mask in place.x_bits[::-1]:
            half = kept.shape[0] // 2
            kept = add(kept[:half], swap(kept[half:], "expert", mask)).astype(bf16)
        reduced.append(kept)
    two = [add(reduced[i], swap(reduced[i + 2], "dp", place.z_bits[1])) for i in range(2)]
    return add(two[0], swap(two[1].astype(bf16), "dp", place.z_bits[0]))


def other(index, mask):
    return index + mask - 2 * mask * ((index // mask) % 2)


class Links:
    def __init__(self, sends, recvs):
        self.sends, self.recvs, self.used, self.open = sends, recvs, 0, []

    def copy(self, source, target, partner):
        at = self.used
        self.used += 1
        made = pltpu.make_async_remote_copy(
            src_ref=source,
            dst_ref=target,
            send_sem=self.sends.at[at],
            recv_sem=self.recvs.at[at],
            device_id=partner,
            device_id_type=pl.DeviceIdType.MESH,
        )
        made.start()
        self.open.append(made)
        return made

    def close(self):
        for made in self.open:
            made.wait_send()


def partners(rows_y):
    dp, ex = lax.axis_index("dp"), lax.axis_index("expert")
    return {
        "z1": (other(dp, rows_y), ex),
        "z2": (other(dp, 2 * rows_y), ex),
        "y": (other(dp, 1), ex),
        "x": (dp, other(ex, 2)),
        "c": (dp, other(ex, 1)),
    }


def greet(devices):
    barrier = pltpu.get_barrier_semaphore()
    for device in devices:
        pl.semaphore_signal(
            barrier, inc=1, device_id=device, device_id_type=pl.DeviceIdType.MESH
        )
    pl.semaphore_wait(barrier, len(devices))


def gather_kernel(
    rows_y,
    exclusive,
    w_query,
    w_key,
    w_value,
    w_output,
    w_router,
    gain_attn,
    gain_moe,
    dy,
    tokens_ref,
    segments,
    routes,
    cosine,
    sine,
    down_hbm,
    qkv_out,
    output_out,
    dy_out,
    grads_out,
    small_out,
    queries_out,
    keys_out,
    values_out,
    residual_out,
    normed_moe_out,
    normed_turned,
    mixed_turned,
    gains_out,
    gates_out,
    allowed,
    full_qkv,
    full_output,
    dy_all,
    w_down,
    grads,
    projected,
    normed_out,
    mixed_out,
    *refs,
):
    z_send, z_recv, y_send, y_recv, x_send, x_recv, c_send, c_recv = refs[:8]
    dz_send, dz_recv, dx_send, dx_recv, dc_send, dc_recv, down_sem, dy_sems, grads_sems, keep_sems = refs[8:]
    fulls = (full_qkv, small_out, full_output)
    n = w_query.shape[0]
    half = n // 2
    piece = half - exclusive
    length = dy.shape[0]
    owned, hidden, width = w_down.shape
    dp, ex = lax.axis_index("dp"), lax.axis_index("expert")
    z, y = dp // rows_y, dp % rows_y
    core, side = ex % 2, (ex // 2) % 2
    to = partners(rows_y)
    z_of = [z, other(z, 1), other(z, 2), other(other(z, 1), 2)]

    in_plane = pl.ds(pl.multiple_of(core * half + side * exclusive, 16), piece)
    alone = pl.ds(pl.multiple_of(core * half + side * piece, 16), exclusive)
    of_core = pl.ds(pl.multiple_of(core * half, 16), half)

    def remote(source, target, send_sem, recv_sem, device):
        return pltpu.make_async_remote_copy(
            src_ref=source,
            dst_ref=target,
            send_sem=send_sem,
            recv_sem=recv_sem,
            device_id=device,
            device_id_type=pl.DeviceIdType.MESH,
        )

    first, second = (0, 1), (2,)

    def copies(arrays, rows, m, ys, send, recv, at, device):
        made = []
        for k in arrays:
            block = fulls[k].at[z_of[m] * rows_y + ys, rows]
            made.append(remote(block, block, send.at[k, at], recv.at[k, at], device))
        return made

    def to_z(arrays, step):
        m, device = ((0, "z1"), (0, "z2"), (2, "z1"))[step]
        return copies(arrays, in_plane, m, y, z_send, z_recv, step, to[device])

    def to_y(arrays, m):
        return copies(arrays, in_plane, m, y, y_send, y_recv, m, to["y"])

    def to_x(arrays, m, k):
        ys = 1 - y if k else y
        return copies(arrays, alone, m, ys, x_send, x_recv, 2 * m + k, to["x"])

    def to_c(arrays, m, k):
        ys = 1 - y if k else y
        return copies(arrays, of_core, m, ys, c_send, c_recv, 2 * m + k, to["c"])

    near, pair = pl.ds(0, length), pl.ds(length, length)
    front, back = pl.ds(0, 2 * length), pl.ds(2 * length, 2 * length)

    def dy_z(step):
        m, target, device = ((0, 1, "z1"), (0, 2, "z2"), (2, 3, "z1"))[step]
        return remote(
            dy_all.at[m, near], dy_all.at[target, near], dz_send.at[step], dz_recv.at[step], to[device]
        )

    def dy_x(m):
        return remote(
            dy_all.at[m, near], dy_all.at[m, pair], dx_send.at[m], dx_recv.at[m], to["x"]
        )

    def dy_c(m):
        return remote(
            dy_all.at[m, front], dy_all.at[m, back], dc_send.at[m], dc_recv.at[m], to["c"]
        )

    at = pl.ds(pl.multiple_of(z * hidden, hidden), hidden)
    load_down = pltpu.make_async_copy(down_hbm.at[:, at, :], w_down, down_sem)
    load_down.start()

    def iota(shape, axis):
        return lax.broadcasted_iota(jnp.int32, shape, axis)

    full_qkv[dp, :, : H * HD] = w_query[...]
    full_qkv[dp, :, H * HD : (H + KV) * HD] = w_key[...]
    full_qkv[dp, :, (H + KV) * HD :] = w_value[...]
    full_output[dp] = w_output[...]
    line = iota((8, n), 0)
    gain_rows = jnp.where(
        line == 0,
        gain_attn[...].astype(f32).reshape(1, n),
        jnp.where(line == 1, gain_moe[...].astype(f32).reshape(1, n), 0.0),
    ).astype(bf16)
    places = (iota((8, 128), 1) == iota((8, 128), 0) + EXPERTS) & (iota((8, 128), 0) < 2)
    columns = transposed(gain_rows, places.astype(f32).astype(bf16))
    shape = (w_router.shape[0], 128)
    router = transposed(w_router[...], (iota(shape, 0) == iota(shape, 1)).astype(f32).astype(bf16))
    small_out[dp] = (router + columns).astype(bf16)
    lane, row = iota((length, 128), 1), iota((length, 128), 0)
    chosen = routes[:1] == iota((128, length), 0)
    for k in range(1, routes.shape[0]):
        chosen = chosen | (routes[k : k + 1] == iota((128, length), 0))
    same = (iota((128, 128), 0) == iota((128, 128), 1)).astype(f32).astype(bf16)
    chosen = transposed(chosen.astype(f32).astype(bf16), same)
    dy_all[0, near, :width] = dy[...]
    dy_all[0, near, width:] = chosen.astype(bf16)
    greet([to[name] for name in ("z1", "z2", "y", "x", "c")])

    def start(made):
        for copy in made:
            copy.start()

    def arrived(made):
        for copy in made:
            copy.wait_recv()

    def keep_dy(m):
        return pltpu.make_async_copy(dy_all.at[m], dy_out.at[m], dy_sems.at[m])

    def keep_grads(m):
        return pltpu.make_async_copy(grads.at[m % 2], grads_out.at[m], grads_sems.at[m % 2])

    keep_qkv = pltpu.make_async_copy(full_qkv, qkv_out, keep_sems.at[0])
    keep_output = pltpu.make_async_copy(full_output, output_out, keep_sems.at[1])

    def group(m):
        dy_c(m).wait_recv()
        keep_dy(m).start()
        if m >= 2:
            keep_grads(m - 2).wait()

        def step(p, _):
            at = pl.ds(pl.multiple_of(p * 2 * hidden, 2 * hidden), 2 * hidden)
            down = w_down[pl.ds(2 * p, 2)].reshape(2 * hidden, width)
            grads[m % 2, :, at] = against(dy_all[m, :, :width], down).astype(bf16)
            return 0

        lax.fori_loop(0, owned // 2, step, 0)
        keep_grads(m).start()

    def turned(value, target):
        target[...] = value.T.reshape(target.shape)

    def rotated(value):
        lanes = value.shape[1]
        lane = lax.broadcasted_iota(jnp.int32, value.shape, 1)
        swapped = jnp.where(
            lane % HD < HD // 2,
            pltpu.roll(value, lanes - HD // 2, 1),
            pltpu.roll(value, HD // 2, 1),
        )
        return (value * cosine[:, :lanes] - swapped * sine[:, :lanes]).astype(bf16)

    per_group = H // KV
    wide = GROUP * per_group * HD
    narrow = GROUP * HD

    def project():
        inputs = tokens_ref[...].astype(f32)
        inv = lax.rsqrt(jnp.mean(inputs * inputs, axis=-1, keepdims=True) + epsilon)
        gains_out[...] = against(
            places.astype(f32).astype(bf16), small_out[...].reshape(width, 128)
        )
        normed_out[...] = (inputs * inv * gains_out[:1]).astype(bf16)
        segment = segments[...].astype(f32)
        same = against(
            (row == lane).astype(f32).astype(bf16), jnp.broadcast_to(segment, (8, length)).astype(bf16)
        )[:, :1]
        allowed[...] = ((same == segment) & (row >= lane)).astype(f32)

        def step(j, _):
            at = pl.ds(pl.multiple_of(j * 512, 512), 512)
            projected[:, at] = jnp.dot(
                normed_out[...], full_qkv[:, :, at].reshape(width, 512), preferred_element_type=f32
            )
            return 0

        lax.fori_loop(0, projected.shape[1] // 512, step, 0)

    def attend(i):
        at = pl.ds(i * wide, wide)
        kv_at = pl.ds(i * narrow, narrow)
        k_at = pl.ds(H * HD + i * narrow, narrow)
        v_at = pl.ds((H + KV) * HD + i * narrow, narrow)
        query = rotated(projected[:, at])
        key = rotated(projected[:, k_at])
        value = projected[:, v_at].astype(bf16)
        queries_out[:, at] = query
        keys_out[:, kv_at] = key
        values_out[:, kv_at] = value
        is_allowed = allowed[...] > 0.5
        heads = []
        for k in range(GROUP):
            k_head, v_head = key[:, k * HD : (k + 1) * HD], value[:, k * HD : (k + 1) * HD]
            for j in range(k * per_group, (k + 1) * per_group):
                q_head = query[:, j * HD : (j + 1) * HD]
                scores = jnp.where(is_allowed, against(q_head, k_head) * 0.125, -1e30)
                lifted = jnp.exp(scores - jnp.max(scores, axis=-1, keepdims=True))
                weights = (lifted / jnp.sum(lifted, axis=-1, keepdims=True)).astype(bf16)
                heads.append(jnp.dot(weights, v_head, preferred_element_type=f32))
        mixed_out[:, at] = jnp.concatenate(heads, axis=1).astype(bf16)

    def close_block():
        def step(j, _):
            at = pl.ds(pl.multiple_of(j * 512, 512), 512)
            residual_out[:, at] = tokens_ref[:, at].astype(f32) + jnp.dot(
                mixed_out[...], full_output[:, :, at].reshape(width, 512), preferred_element_type=f32
            )
            return 0

        lax.fori_loop(0, width // 512, step, 0)
        residual = residual_out[...]
        inv = lax.rsqrt(jnp.mean(residual * residual, axis=-1, keepdims=True) + epsilon)
        normed_moe_out[...] = (residual * inv * gains_out[1:2]).astype(bf16)
        logits = jnp.dot(
            normed_moe_out[...], small_out[...].reshape(width, 128), preferred_element_type=f32
        )
        logits = jnp.where(chosen > 0.5, logits, -1e30)
        lifted = jnp.exp(logits - jnp.max(logits, axis=-1, keepdims=True)) * chosen
        gates_out[...] = lifted / jnp.sum(lifted, axis=-1, keepdims=True)
        turned(mixed_out[...], mixed_turned)

    start(to_z(first, 1))
    start(to_z(first, 0))
    start(to_y(first, 0))
    dy_x(0).start()

    arrived(to_z(first, 0))
    start(to_y(first, 1))
    start(to_x(first, 1, 0))
    arrived(to_z(first, 1))
    start(to_z(first, 2))
    start(to_y(first, 2))
    start(to_x(first, 2, 0))
    start(to_z(second, 1))
    start(to_z(second, 0))
    start(to_y(second, 0))
    dy_x(0).wait_recv()
    dy_c(0).start()
    arrived(to_y(first, 0))
    start(to_x(first, 0, 1))
    load_down.wait()
    group(0)
    arrived(to_z(first, 2))
    start(to_y(first, 3))
    start(to_x(first, 3, 0))
    arrived(to_z(second, 0))
    start(to_y(second, 1))
    start(to_x(second, 1, 0))
    arrived(to_z(second, 1))
    start(to_z(second, 2))
    start(to_y(second, 2))
    start(to_x(second, 2, 0))
    dy_z(1).start()
    dy_z(0).start()
    arrived(to_y(first, 1))
    start(to_x(first, 1, 1))
    arrived(to_y(first, 2))
    start(to_x(first, 2, 1))
    for m, k in ((1, 0), (2, 0), (0, 1), (3, 0), (1, 1)):
        arrived(to_x(first, m, k))
        start(to_c(first, m, k))
    arrived(to_y(first, 3))
    start(to_x(first, 3, 1))
    arrived(to_x(first, 2, 1))
    start(to_c(first, 2, 1))
    arrived(to_z(second, 2))
    start(to_y(second, 3))
    start(to_x(second, 3, 0))
    arrived(to_y(second, 0))
    start(to_x(second, 0, 1))
    arrived(to_x(first, 3, 1))
    start(to_c(first, 3, 1))
    for m, k in ((1, 0), (2, 0), (0, 1), (3, 0), (1, 1), (2, 1), (3, 1)):
        arrived(to_c(first, m, k))
    keep_qkv.start()
    project()
    turned(normed_out[...], normed_turned)
    arrived(to_y(second, 1))
    start(to_x(second, 1, 1))
    arrived(to_y(second, 2))
    start(to_x(second, 2, 1))
    dy_z(0).wait_recv()
    dy_x(1).start()
    attend(0)
    dy_z(1).wait_recv()
    dy_z(2).start()
    dy_x(2).start()
    attend(1)
    for m, k in ((1, 0), (2, 0), (0, 1), (3, 0), (1, 1), (2, 1)):
        arrived(to_x(second, m, k))
        start(to_c(second, m, k))
    arrived(to_y(second, 3))
    start(to_x(second, 3, 1))
    attend(2)
    dy_x(1).wait_recv()
    dy_c(1).start()
    attend(3)
    arrived(to_x(second, 3, 1))
    start(to_c(second, 3, 1))
    group(1)
    dy_z(2).wait_recv()
    dy_x(3).start()
    for m, k in ((1, 0), (2, 0), (0, 1), (3, 0), (1, 1), (2, 1), (3, 1)):
        arrived(to_c(second, m, k))
    keep_output.start()
    close_block()
    dy_x(2).wait_recv()
    dy_c(2).start()
    group(2)
    dy_x(3).wait_recv()
    dy_c(3).start()
    group(3)

    keep_qkv.wait()
    keep_output.wait()
    for m in range(ZLINE):
        keep_dy(m).wait()
        if m >= 2:
            keep_grads(m).wait()
    every = first + second
    for step in range(3):
        for made in to_z(every, step):
            made.wait_send()
        dy_z(step).wait_send()
    for m in range(ZLINE):
        for made in to_y(every, m):
            made.wait_send()
        dy_x(m).wait_send()
        dy_c(m).wait_send()
        for k in range(2):
            if m or k:
                for made in to_x(every, m, k) + to_c(every, m, k):
                    made.wait_send()


def gather(rows_y, weights, dy, *rest):
    w_down = rest[-1]
    n = weights[0].shape[0]
    dp_size = ZLINE * rows_y
    owned, _, width = w_down.shape
    hidden = F // ZLINE
    length = dy.shape[0]
    count = 4 * length
    qkv_wide = weights[0].shape[1] + weights[1].shape[1] + weights[2].shape[1]
    any_space = pl.BlockSpec(memory_space=pl.ANY)
    vmem = pl.BlockSpec(memory_space=pltpu.VMEM)
    sems = pltpu.SemaphoreType.DMA

    def rows(wide, dtype=bf16):
        return jax.ShapeDtypeStruct((length, wide), dtype)

    turned = jax.ShapeDtypeStruct((dp_size, 2, 2, n // 4, length), bf16)
    return pl.pallas_call(
        functools.partial(gather_kernel, rows_y, n // 6),
        name="gather",
        out_shape=(
            jax.ShapeDtypeStruct((dp_size, n, qkv_wide), bf16),
            jax.ShapeDtypeStruct((dp_size, n, width), bf16),
            jax.ShapeDtypeStruct((ZLINE, count, width + 128), bf16),
            jax.ShapeDtypeStruct((ZLINE, count, owned * hidden), bf16),
            jax.ShapeDtypeStruct((dp_size, n, 128), bf16),
            rows(H * HD),
            rows(KV * HD),
            rows(KV * HD),
            rows(width, f32),
            rows(width),
            turned,
            turned,
            jax.ShapeDtypeStruct((8, width), f32),
            rows(128, f32),
            rows(length, f32),
        ),
        in_specs=[vmem] * (len(weights) + len(rest)) + [any_space],
        out_specs=(any_space,) * 4 + (vmem,) * 11,
        scratch_shapes=[
            pltpu.VMEM((dp_size, n, qkv_wide), bf16),
            pltpu.VMEM((dp_size, n, width), bf16),
            pltpu.VMEM((ZLINE, count, width + 128), bf16),
            pltpu.VMEM((owned, hidden, width), bf16),
            pltpu.VMEM((2, count, owned * hidden), bf16),
            pltpu.VMEM((length, qkv_wide), f32),
            pltpu.VMEM((length, width), bf16),
            pltpu.VMEM((length, H * HD), bf16),
            sems((3, 3)),
            sems((3, 3)),
            sems((3, ZLINE)),
            sems((3, ZLINE)),
            sems((3, dp_size)),
            sems((3, dp_size)),
            sems((3, dp_size)),
            sems((3, dp_size)),
            sems((3,)),
            sems((3,)),
            sems((ZLINE,)),
            sems((ZLINE,)),
            sems((ZLINE,)),
            sems((ZLINE,)),
            sems,
            sems((ZLINE,)),
            sems((2,)),
            sems((2,)),
        ],
        compiler_params=pltpu.CompilerParams(
            collective_id=2, has_side_effects=True, vmem_limit_bytes=60 * 2**20
        ),
    )(*weights, dy, *rest)


MOE_COPIES = 30


def moe_kernel(
    rows_y,
    normed_ref,
    dy_hbm,
    plain_hbm,
    gate_up_hbm,
    down_hbm,
    router_ref,
    rows_out,
    grads_out,
    down_out,
    combined_out,
    heard_out,
    total_ref,
    w_gate,
    w_up,
    w_down,
    rows,
    masks,
    plain,
    grads,
    acts,
    gate_grads,
    part_down,
    heard_down,
    stage_down,
    parts,
    heard_c,
    heard_x,
    heard_z1,
    heard_z,
    combined,
    heard_combined,
    spread_ref,
    sends,
    recvs,
    d_send,
    d_recv,
    load_sems,
    plain_sems,
    dy_sems,
    rows_sems,
    grads_sems,
    down_sems,
    combined_sems,
):
    owned, hidden = w_down.shape[:2]
    length, width = normed_ref.shape
    count = rows.shape[1]
    tokens = ZLINE * count
    half = count // 2
    span = owned * hidden
    dp = lax.axis_index("dp")
    z, y = dp // rows_y, dp % rows_y
    to = partners(rows_y)
    to["z3"] = (other(to["z1"][0], 2 * rows_y), lax.axis_index("expert"))
    links = Links(sends, recvs)

    loads = []
    mine = pl.ds(pl.multiple_of(z * hidden, hidden), hidden)
    theirs = pl.ds(pl.multiple_of(F + z * hidden, hidden), hidden)
    for e in range(owned):
        at = pl.ds(e * hidden, hidden)
        for k, (cut, kept) in enumerate(((mine, w_gate), (theirs, w_up))):
            loads.append(
                pltpu.make_async_copy(
                    gate_up_hbm.at[e, :, cut], kept.at[:, at], load_sems.at[2 * e + k]
                )
            )
    loads.append(
        pltpu.make_async_copy(dy_hbm.at[:, :, pl.ds(width, 128)], masks, load_sems.at[2 * owned])
    )
    load_down = pltpu.make_async_copy(
        down_hbm.at[:, mine, :], w_down, load_sems.at[2 * owned + 1]
    )
    for load in loads:
        load.start()

    def fetch(r):
        return pltpu.make_async_copy(plain_hbm.at[r], plain.at[r % 2], plain_sems.at[r % 2])

    fetch(0).start()
    fetch(1).start()
    load_down.start()
    rows[0, :length] = normed_ref[...]
    first = lax.axis_index("expert") * owned
    expert = first + lax.broadcasted_iota(jnp.int32, (128, span), 1) // hidden
    spread_ref[...] = (
        (lax.broadcasted_iota(jnp.int32, (128, span), 0) == expert).astype(f32).astype(bf16)
    )
    greet([to[name] for name in ("z1", "z2", "z3", "y", "x", "c")])

    own = pl.ds(0, length)
    pair = pl.ds(length, length)
    near, far = pl.ds(0, half), pl.ds(half, half)

    def row_x(r):
        return links.copy(rows.at[r, own], rows.at[r, pair], to["x"])

    def row_c(r):
        return links.copy(rows.at[r, near], rows.at[r, far], to["c"])

    z1 = links.copy(rows.at[0, own], rows.at[1, own], to["z1"])
    z2 = links.copy(rows.at[0, own], rows.at[2, own], to["z2"])
    x0 = row_x(0)
    for load in loads:
        load.wait()
    x0.wait_recv()
    z1_pair = links.copy(rows.at[0, pair], rows.at[1, pair], to["z1"])
    c0 = row_c(0)
    c0.wait_recv()

    def keep_rows(r):
        return pltpu.make_async_copy(rows.at[r], rows_out.at[r], rows_sems.at[r])

    def keep_grads(r):
        return pltpu.make_async_copy(grads.at[min(r, 1)], grads_out.at[r], grads_sems.at[r])

    def forward(r):
        slot, held = r % 2, min(r, 1)
        keep_rows(r).start()
        fetch(r).wait()
        if r >= 2:
            keep_grads(r - 1).wait()
        logits = jnp.dot(rows[r], router_ref[...], preferred_element_type=f32)
        mask = masks[r].astype(f32) > 0.5
        logits = jnp.where(mask, logits, -1e30)
        lifted = jnp.where(
            mask, jnp.exp(logits - jnp.max(logits, axis=-1, keepdims=True)), 0.0
        )
        gates = lifted / jnp.sum(lifted, axis=-1, keepdims=True)
        gates_high = gates.astype(bf16)
        gates_low = (gates - gates_high.astype(f32)).astype(bf16)
        gate_grads[...] = jnp.zeros_like(gate_grads)

        def step(p, _):
            at = pl.ds(pl.multiple_of(p * 2 * hidden, 2 * hidden), 2 * hidden)
            up_at = pl.ds(pl.multiple_of(span + p * 2 * hidden, 2 * hidden), 2 * hidden)
            spread = spread_ref[:, at]
            gate_part = jnp.dot(rows[r], w_gate[:, at], preferred_element_type=f32)
            up_part = jnp.dot(rows[r], w_up[:, at], preferred_element_type=f32)
            plain_grad = plain[slot, :, at].astype(f32)
            spread_gates = jnp.dot(gates_high, spread, preferred_element_type=f32) + jnp.dot(
                gates_low, spread, preferred_element_type=f32
            )
            sigmoid_gate = 1.0 / (1.0 + jnp.exp(-gate_part))
            swished = gate_part * sigmoid_gate
            activation = swished * up_part
            gate_grads[...] += against((plain_grad * activation).astype(bf16), spread)
            acts[r, :, at] = (spread_gates * activation).astype(bf16)
            grad_act = plain_grad * spread_gates
            grads[held, :, at] = (
                grad_act * up_part * (sigmoid_gate + swished * (1.0 - sigmoid_gate))
            ).astype(bf16)
            grads[held, :, up_at] = (grad_act * swished).astype(bf16)
            return 0

        lax.fori_loop(0, owned // 2, step, 0, unroll=True)
        parts[r, :, width:] = gate_grads[...].astype(bf16)
        if r + 2 < ZLINE:
            fetch(r + 2).start()
        keep_grads(r).start()

    def backward(r):
        held = min(r, 1)

        def step(j, _):
            at = pl.ds(pl.multiple_of(j * 768, 768), 768)
            part = against(grads[held, :, :span], w_gate[at, :]) + against(
                grads[held, :, span:], w_up[at, :]
            )
            parts[r, :, at] = part.astype(bf16)
            return 0

        lax.fori_loop(0, width // 768, step, 0)

    def add(left, right):
        return (left[...].astype(f32) + right[...].astype(f32)).astype(bf16)

    made = {}

    def sum_c(r):
        made["c", r] = links.copy(parts.at[r, far], heard_c.at[r], to["c"])

    def sum_x(r):
        made["c", r].wait_recv()
        parts[r, near] = add(parts.at[r, near], heard_c.at[r])
        if r == 1:
            made["z", 1] = links.copy(parts.at[1, near], heard_z1, to["z1"])
            return
        if r == 0:
            made["z", 1].wait_recv()
            parts[0, near] = add(parts.at[0, near], heard_z1)
        made["x", r] = links.copy(parts.at[r, pair], heard_x.at[r], to["x"])

    def sum_z(r):
        made["x", r].wait_recv()
        parts[r, own] = add(parts.at[r, own], heard_x.at[r])
        if r:
            made["z", r] = links.copy(parts.at[r, own], heard_z.at[r - 2], to[f"z{r}"])

    def keep_combined(r):
        return pltpu.make_async_copy(
            combined.at[r % 2, near], combined_out.at[r], combined_sems.at[r]
        )

    def combine(r):
        slot = r % 2
        if r >= 2:
            made["oc", r - 2].wait_send()

        def step(j, _):
            at = pl.ds(pl.multiple_of(j * 512, 512), 512)
            down = w_down[:, :, at].reshape(span, 512)
            combined[slot, :, at] = jnp.dot(
                acts[r], down, preferred_element_type=f32
            ).astype(bf16)
            return 0

        lax.fori_loop(0, width // 512, step, 0)
        made["oc", r] = links.copy(combined.at[slot, far], heard_combined.at[r], to["c"])

    def out_c(r):
        made["oc", r].wait_recv()
        combined[r % 2, near] = add(combined.at[r % 2, near], heard_combined.at[r])
        keep_combined(r).start()

    def out_x(r):
        made["ox", r] = links.copy(combined_out.at[r, pair], heard_out.at[r], to["x"])

    def fetch_dy(r):
        return pltpu.make_async_copy(
            dy_hbm.at[r, :, pl.ds(0, width)], rows.at[r], dy_sems.at[r]
        )

    def send_down(e):
        return pltpu.make_async_remote_copy(
            src_ref=part_down.at[e, 1 - y],
            dst_ref=heard_down.at[e],
            send_sem=d_send.at[e],
            recv_sem=d_recv.at[e],
            device_id=to["y"],
            device_id_type=pl.DeviceIdType.MESH,
        )

    def down(p, _):
        at = pl.ds(pl.multiple_of(p * 2 * hidden, 2 * hidden), 2 * hidden)
        left = acts[:, :, at].reshape(tokens, 2 * hidden)

        def step(j, _):
            columns = pl.ds(pl.multiple_of(j * 768, 768), 768)
            result = transposed(left, rows[:, :, columns].reshape(tokens, 768)).astype(bf16)
            for k in range(2):
                for i in range(rows_y):
                    first = k * hidden + i * (hidden // rows_y)
                    part_down[2 * p + k, i, :, columns] = result[
                        first : first + hidden // rows_y
                    ]
            return 0

        lax.fori_loop(0, width // 768, step, 0)
        for k in range(2):
            send_down(2 * p + k).start()
        return 0

    def keep_down(e):
        return pltpu.make_async_copy(
            stage_down.at[lax.rem(e, 2)], down_out.at[e], down_sems.at[lax.rem(e, 2)]
        )

    def finish_down(e, _):
        @pl.when(e >= 2)
        def _():
            keep_down(e - 2).wait()

        send_down(e).wait_recv()
        stage_down[lax.rem(e, 2)] = add(part_down.at[e, y], heard_down.at[e])
        keep_down(e).start()
        return 0

    forward(0)
    z2.wait_recv()
    z3 = links.copy(rows.at[2, own], rows.at[3, own], to["z1"])
    x2 = row_x(2)
    load_down.wait()
    combine(0)
    z1.wait_recv()
    z1_pair.wait_recv()
    c1 = row_c(1)
    c1.wait_recv()
    forward(1)
    z3.wait_recv()
    x3 = row_x(3)
    backward(1)
    sum_c(1)
    x2.wait_recv()
    c2 = row_c(2)
    out_c(0)
    sum_x(1)
    c2.wait_recv()
    forward(2)
    backward(2)
    sum_c(2)
    x3.wait_recv()
    c3 = row_c(3)
    sum_x(2)
    c3.wait_recv()
    forward(3)
    backward(3)
    sum_c(3)
    keep_combined(0).wait()
    out_x(0)
    for r in range(ZLINE):
        keep_rows(r).wait()
    gathered = (z1, z2, z3, z1_pair, x0, x2, x3, c0, c1, c2, c3)
    for copy in gathered:
        copy.wait_send()
    for r in range(ZLINE):
        fetch_dy(r).start()
    sum_x(3)
    sum_z(2)
    for r in range(ZLINE):
        fetch_dy(r).wait()
    backward(0)
    sum_c(0)
    lax.fori_loop(0, 2, down, 0)
    sum_x(0)
    combine(1)
    sum_z(3)
    lax.fori_loop(2, 3, down, 0)
    out_c(1)
    combine(2)
    keep_combined(1).wait()
    out_x(1)
    sum_z(0)
    lax.fori_loop(3, 4, down, 0)
    out_c(2)
    combine(3)
    keep_combined(2).wait()
    out_x(2)
    lax.fori_loop(4, owned // 2, down, 0)
    out_c(3)
    total = parts[0, own].astype(f32)
    for r in (2, 3):
        made["z", r].wait_recv()
        total = total + heard_z[r - 2].astype(f32)
    total_ref[...] = total
    keep_combined(3).wait()
    out_x(3)
    lax.fori_loop(0, owned, finish_down, 0)
    for r in range(ZLINE):
        made["ox", r].wait_recv()
    done = gathered + (made["oc", 0], made["oc", 1])
    links.open = [v for v in links.open if not any(v is copy for copy in done)]
    links.close()
    for e in range(owned):
        send_down(e).wait_send()
    for e in (owned - 2, owned - 1):
        keep_down(e).wait()
    for r in (0, ZLINE - 1):
        keep_grads(r).wait()


def moe(rows_y, normed, dy, plain, w_gate_up, w_down, router):
    owned, width, _ = w_gate_up.shape
    hidden = F // ZLINE
    length = normed.shape[0]
    count = dy.shape[1]
    any_space = pl.BlockSpec(memory_space=pl.ANY)
    vmem = pl.BlockSpec(memory_space=pltpu.VMEM)
    sems = pltpu.SemaphoreType.DMA
    span = owned * hidden
    wide = width + 128
    return pl.pallas_call(
        functools.partial(moe_kernel, rows_y),
        name="moe",
        out_shape=(
            jax.ShapeDtypeStruct((ZLINE, count, width), bf16),
            jax.ShapeDtypeStruct((ZLINE, count, 2 * span), bf16),
            jax.ShapeDtypeStruct((owned, hidden // rows_y, width), bf16),
            jax.ShapeDtypeStruct((ZLINE, count // 2, width), bf16),
            jax.ShapeDtypeStruct((ZLINE, length, width), bf16),
            jax.ShapeDtypeStruct((length, wide), f32),
        ),
        in_specs=[vmem, any_space, any_space, any_space, any_space, vmem],
        out_specs=(any_space,) * 5 + (vmem,),
        scratch_shapes=[
            pltpu.VMEM((width, span), bf16),
            pltpu.VMEM((width, span), bf16),
            pltpu.VMEM((owned, hidden, width), bf16),
            pltpu.VMEM((ZLINE, count, width), bf16),
            pltpu.VMEM((ZLINE, count, 128), bf16),
            pltpu.VMEM((2, count, span), bf16),
            pltpu.VMEM((2, count, 2 * span), bf16),
            pltpu.VMEM((ZLINE, count, span), bf16),
            pltpu.VMEM((count, 128), f32),
            pltpu.VMEM((owned, rows_y, hidden // rows_y, width), bf16),
            pltpu.VMEM((owned, hidden // rows_y, width), bf16),
            pltpu.VMEM((2, hidden // rows_y, width), bf16),
            pltpu.VMEM((ZLINE, count, wide), bf16),
            pltpu.VMEM((ZLINE, count // 2, wide), bf16),
            pltpu.VMEM((ZLINE, length, wide), bf16),
            pltpu.VMEM((count // 2, wide), bf16),
            pltpu.VMEM((ZLINE - 2, length, wide), bf16),
            pltpu.VMEM((2, count, width), bf16),
            pltpu.VMEM((ZLINE, count // 2, width), bf16),
            pltpu.VMEM((128, span), bf16),
            sems((MOE_COPIES,)),
            sems((MOE_COPIES,)),
            sems((owned,)),
            sems((owned,)),
            sems((2 * owned + 2,)),
            sems((2,)),
            sems((ZLINE,)),
            sems((ZLINE,)),
            sems((ZLINE,)),
            sems((2,)),
            sems((ZLINE,)),
        ],
        compiler_params=pltpu.CompilerParams(
            collective_id=1, has_side_effects=True, vmem_limit_bytes=63 * 2**20
        ),
    )(normed, dy, plain, w_gate_up, w_down, router)


def finish_kernel(
    rows_y,
    rows_hbm,
    grads_hbm,
    combined_hbm,
    heard_hbm,
    w_output_hbm,
    w_qkv_hbm,
    row_grads,
    gates,
    cotangent,
    residual,
    normed_moe,
    gains,
    router,
    tokens_ref,
    mixed,
    normed,
    queries,
    keys,
    values,
    allowed,
    cosine,
    sine,
    gate_up_out,
    output_out,
    grad_tokens_out,
    out_0,
    out_1,
    out_2,
    rows,
    turned,
    grads,
    part_gate_up,
    heard_gate_up,
    heard_z,
    stage,
    o_own,
    o_x,
    o_z1,
    o_z2,
    w_output,
    w_qkv,
    grad_qkv,
    grad_normed,
    left_output,
    left_qkv,
    right_output,
    right_qkv,
    part_small,
    grad_residual,
    grad_branch,
    base_small,
    *refs,
):
    owned, n = gate_up_out.shape[:2]
    hidden = F // ZLINE
    count, width = rows.shape
    length = tokens_ref.shape[0]
    tokens = ZLINE * count
    dp, ex = lax.axis_index("dp"), lax.axis_index("expert")
    z, y = dp // rows_y, dp % rows_y
    core, side = ex % 2, (ex // 2) % 2
    to = partners(rows_y)
    to["z3"] = (other(to["z1"][0], 2 * rows_y), ex)
    to["xc"] = (dp, other(other(ex, 1), 2))
    z_of = [z, other(z, 1), other(z, 2), other(other(z, 1), 2)]
    half, quarter = n // 2, n // 4
    of_core = pl.ds(pl.multiple_of(core * half, 16), half)
    of_sibling = pl.ds(pl.multiple_of((1 - core) * half, 16), half)
    of_side = pl.ds(pl.multiple_of(side * quarter, 16), quarter)
    of_far_side = pl.ds(pl.multiple_of((1 - side) * quarter, 16), quarter)
    mine = pl.ds(pl.multiple_of(core * half + side * quarter, 16), quarter)
    (
        load_sem,
        own_sems,
        weight_sems,
        grads_sems,
        store_sems,
        y_send,
        y_recv,
        z_send,
        z_recv,
        a_send,
        a_recv,
        f_send,
        f_recv,
        o_send,
        o_recv,
    ) = refs[18:]

    def remote(source, target, send_sem, recv_sem, device):
        return pltpu.make_async_remote_copy(
            src_ref=source,
            dst_ref=target,
            send_sem=send_sem,
            recv_sem=recv_sem,
            device_id=device,
            device_id_type=pl.DeviceIdType.MESH,
        )

    def add(left, right):
        return (left.astype(f32) + right.astype(f32)).astype(bf16)

    def load_rows(r):
        return pltpu.make_async_copy(rows_hbm.at[r], rows, load_sem)

    def load_grads(e, k):
        at = pl.ds(pl.multiple_of((k * owned + e) * hidden, hidden), hidden)
        return pltpu.make_async_copy(
            grads_hbm.at[:, :, at],
            grads.at[lax.rem(e, 2), :, :, pl.ds(k * hidden, hidden)],
            grads_sems.at[lax.rem(e, 2), k],
        )

    load_combined = [
        pltpu.make_async_copy(combined_hbm.at[:, pl.ds(0, length)], o_own, own_sems.at[0]),
        pltpu.make_async_copy(heard_hbm, o_x, own_sems.at[1]),
    ]

    def o_copy(k):
        if k < 2:
            return remote(o_own.at[1 + 2 * k], o_z1.at[k], o_send.at[k], o_recv.at[k], to["z1"])
        return remote(o_own.at[2], o_z2, o_send.at[k], o_recv.at[k], to["z2"])

    def o_start():
        for load in load_combined:
            load.wait()
        for r in (3, 1, 2, 0):
            o_own[r] = add(o_own[r], o_x[r])
            if r % 2:
                o_copy(r // 2).start()

    def o_after_z1():
        for k in (1, 0):
            o_copy(k).wait_recv()
            o_own[2 * k] = add(o_own[2 * k], o_z1[k])
            if k:
                o_copy(2).start()

    def o_end():
        o_copy(2).wait_recv()
        total = o_own[0].astype(f32) + o_z2[...].astype(f32)
        output_out[...] = (residual[...] + total).astype(bf16)

    def left_copies(k, source, target):
        made = []
        for m, name in ((1, "c"), (2, "x"), (3, "xc")):
            c = 1 - core if m % 2 else core
            s = 1 - side if m // 2 else side
            made.append(
                remote(
                    source.at[:, c, s],
                    target.at[:, :, pl.ds(m * length, length)],
                    f_send.at[k, m],
                    f_recv.at[k, m],
                    to[name],
                )
            )
        return made

    def right_copy(k, source, target, m):
        if m == 3:
            source = target.at[pl.ds(2 * length, length)]
        return remote(
            source,
            target.at[pl.ds(m * length, length)],
            f_send.at[k, m],
            f_recv.at[k, m],
            to["x" if m == 2 else "c"],
        )

    class Sum:
        def __init__(self, k, out, rows, z_first=False):
            self.k, self.out, self.rows, self.z_first = k, out, rows, z_first
            self.own, self.c, self.x, self.y, self.z1, self.z2 = refs[6 * k : 6 * k + 6]

        def copy(self, step, source, target, device):
            return remote(
                source, target, a_send.at[self.k, step], a_recv.at[self.k, step], device
            )

        def line(self, m):
            if self.z_first:
                return self.own.at[z_of[m], :, self.rows]
            return self.own.at[z_of[m], y, self.rows]

        def last_y(self):
            return self.copy(8, self.own.at[z, 1 - y, self.rows], self.y.at[0], to["y"])

        def to_y(self, b):
            return self.copy(8 + b, self.own.at[b, 1 - y, self.rows], self.y.at[b], to["y"])

        def to_z1(self, m):
            return self.copy(1 + m, self.line(1 + 2 * m), self.z1.at[m], to["z1"])

        def to_z2(self):
            return self.copy(3, self.line(2), self.z2, to["z2"])

        def back_x(self):
            return self.copy(4, self.out.at[mine], self.out.at[mine], to["x"])

        def back_c(self):
            return self.copy(5, self.out.at[of_core], self.out.at[of_core], to["c"])

        def to_c(self):
            return self.copy(6, part_small.at[:, :, of_sibling], self.c, to["c"])

        def to_x(self):
            return self.copy(7, self.own.at[:, :, of_far_side], self.x, to["x"])

        def after_c(self):
            self.to_c().wait_recv()
            for b in range(ZLINE):
                for k in range(rows_y):
                    self.own[b, k] = add(part_small[b, k, of_core], self.c[b, k])
            self.to_x().start()

        def after_x(self):
            self.to_x().wait_recv()
            for b in range(ZLINE):
                for k in range(rows_y):
                    self.own[b, k, self.rows] = add(self.own[b, k, self.rows], self.x[b, k])
            self.along_y()

        def begin(self):
            if self.z_first:
                self.along_z()
            else:
                self.along_y()

        def along_y(self):
            for b in range(ZLINE):
                self.to_y(b).start()

        def along_z(self):
            for m in (1, 0):
                self.to_z1(m).start()

        def after_y(self):
            if self.z_first:
                self.last_y().wait_recv()
                self.out[mine] = add(self.own[z, y, self.rows], self.y[0])
                self.back_x().start()
                return
            for b in range(ZLINE):
                self.to_y(b).wait_recv()
                self.own[b, y, self.rows] = add(self.own[b, y, self.rows], self.y[b])
            self.along_z()

        def after_z1(self):
            for m in (1, 0):
                self.to_z1(m).wait_recv()
                line = self.line(2 * m)
                line[...] = add(line[...], self.z1[m])
                if m:
                    self.to_z2().start()

        def after_z2(self):
            self.to_z2().wait_recv()
            if self.z_first:
                line = self.line(0)
                line[...] = add(line[...], self.z2[...])
                self.last_y().start()
                return
            self.out[mine] = add(self.own[z, y, self.rows], self.z2[...])
            self.back_x().start()

        def after_back(self):
            self.back_x().wait_recv()
            self.back_c().start()

        def close(self):
            self.back_c().wait()
            for made in (self.to_z1(0), self.to_z1(1), self.to_z2(), self.back_x()):
                made.wait_send()
            if self.z_first:
                self.last_y().wait_send()
                return
            for b in range(ZLINE):
                self.to_y(b).wait_send()

    whole = pl.ds(0, quarter)
    output = Sum(0, out_0, whole, True)
    small = Sum(1, out_1, of_side)
    qkv = Sum(2, out_2, whole)

    def products(array, left, right):
        rows_all = left[...].reshape(ZLINE * rows_y * quarter, 4 * length)

        def step(j, _):
            at = pl.ds(pl.multiple_of(j * 512, 512), 512)
            result = jnp.dot(rows_all, right[:, at], preferred_element_type=f32).astype(bf16)
            array.own[:, :, :, at] = result.reshape(ZLINE, rows_y, quarter, 512)
            return 0

        lax.fori_loop(0, right.shape[1] // 512, step, 0)
        array.begin()

    def load_output(i):
        step = w_output.shape[1]
        at = pl.ds(pl.multiple_of(i * step, step), step)
        return pltpu.make_async_copy(
            w_output_hbm.at[at], w_output.at[lax.rem(i, 2)], weight_sems.at[0, lax.rem(i, 2)]
        )

    def load_qkv(i):
        step = w_qkv.shape[1]
        at = pl.ds(pl.multiple_of(i * step, step), step)
        return pltpu.make_async_copy(
            w_qkv_hbm.at[at], w_qkv.at[lax.rem(i, 2)], weight_sems.at[1, lax.rem(i, 2)]
        )

    def unrotate(value):
        lanes = value.shape[1]
        lane = lax.broadcasted_iota(jnp.int32, value.shape, 1)
        swapped = jnp.where(
            lane % HD < HD // 2,
            pltpu.roll(value, lanes - HD // 2, 1),
            pltpu.roll(value, HD // 2, 1),
        )
        return (value * cosine[:, :lanes] + swapped * sine[:, :lanes]).astype(bf16)

    per_group = H // KV
    wide = GROUP * per_group * HD
    narrow = GROUP * HD

    def attend(i, _):
        load_output(i).wait()
        at = pl.ds(pl.multiple_of(i * wide, wide), wide)
        kv_at = pl.ds(pl.multiple_of(i * narrow, narrow), narrow)
        grad_mixed = against(grad_branch[...], w_output[lax.rem(i, 2)]).astype(bf16)
        query, key, value = queries[:, at], keys[:, kv_at], values[:, kv_at]
        is_allowed = allowed[...] > 0.5
        grad_queries, grad_keys, grad_values = [], [], []
        for k in range(GROUP):
            k_head, v_head = key[:, k * HD : (k + 1) * HD], value[:, k * HD : (k + 1) * HD]
            grad_k = grad_v = None
            for j in range(k * per_group, (k + 1) * per_group):
                q_head = query[:, j * HD : (j + 1) * HD]
                mixed_head = grad_mixed[:, j * HD : (j + 1) * HD]
                scores = jnp.where(is_allowed, against(q_head, k_head) * 0.125, -1e30)
                lifted = jnp.exp(scores - jnp.max(scores, axis=-1, keepdims=True))
                weights = lifted / jnp.sum(lifted, axis=-1, keepdims=True)
                grad_weights = against(mixed_head, v_head)
                inner = jnp.sum(weights * grad_weights, axis=-1, keepdims=True)
                grad_scores = (weights * (grad_weights - inner)).astype(bf16)
                part_v = transposed(weights.astype(bf16), mixed_head)
                part_k = transposed(grad_scores, q_head)
                grad_v = part_v if grad_v is None else grad_v + part_v
                grad_k = part_k if grad_k is None else grad_k + part_k
                grad_queries.append(
                    jnp.dot(grad_scores, k_head, preferred_element_type=f32) * 0.125
                )
            grad_keys.append(grad_k * 0.125)
            grad_values.append(grad_v)
        grad_qkv[:, at] = unrotate(jnp.concatenate(grad_queries, axis=1))
        k_at = pl.ds(pl.multiple_of(H * HD + i * narrow, narrow), narrow)
        v_at = pl.ds(pl.multiple_of((H + KV) * HD + i * narrow, narrow), narrow)
        grad_qkv[:, k_at] = unrotate(jnp.concatenate(grad_keys, axis=1))
        grad_qkv[:, v_at] = jnp.concatenate(grad_values, axis=1).astype(bf16)

        @pl.when(i + 2 < KV // GROUP)
        def _():
            load_output(i + 2).start()

        return 0

    def column(value, lane):
        at_lane = lax.broadcasted_iota(jnp.int32, (length, 128), 1) == lane
        at_lane = at_lane.astype(f32).astype(bf16)
        high = value.astype(bf16)
        low = (value - high.astype(f32)).astype(bf16)
        return transposed(high, at_lane) + transposed(low, at_lane)

    def norm_grads():
        grad_gates = row_grads[:, width:]
        inner = jnp.sum(gates[...] * grad_gates, axis=-1, keepdims=True)
        grad_logits = (gates[...] * (grad_gates - inner)).astype(bf16)
        grad_normed_moe = row_grads[:, :width] + against(grad_logits, router[...])
        inv = lax.rsqrt(jnp.mean(residual[...] * residual[...], axis=-1, keepdims=True) + epsilon)
        unit = residual[...] * inv
        scaled = grad_normed_moe * gains[1:2]
        total = cotangent[...].astype(f32) + inv * (
            scaled - unit * jnp.mean(scaled * unit, axis=-1, keepdims=True)
        )
        grad_residual[...] = total
        grad_branch[...] = total.astype(bf16)
        base_small[...] = transposed(normed_moe[...], grad_logits) + column(
            grad_normed_moe * unit, EXPERTS + 1
        )

    def input_grads():
        tile = w_qkv.shape[1]

        def step(i, _):
            load_qkv(i).wait()
            at = pl.ds(pl.multiple_of(i * tile, tile), tile)
            grad_normed[:, at] = against(grad_qkv[...], w_qkv[lax.rem(i, 2)])

            @pl.when(i + 2 < width // tile)
            def _():
                load_qkv(i + 2).start()

            return 0

        lax.fori_loop(0, width // tile, step, 0)
        inputs = tokens_ref[...].astype(f32)
        inv = lax.rsqrt(jnp.mean(inputs * inputs, axis=-1, keepdims=True) + epsilon)
        unit = inputs * inv
        onto = grad_normed[...] * unit
        scaled = grad_normed[...] * gains[:1]
        grad_tokens_out[...] = (
            grad_residual[...]
            + inv * (scaled - unit * jnp.mean(scaled * unit, axis=-1, keepdims=True))
        ).astype(bf16)
        part = base_small[...] + column(onto, EXPERTS)
        part_small[...] = part.astype(bf16).reshape(part_small.shape)
        small.to_c().start()

    load_rows(0).start()
    for load in load_combined:
        load.start()
    for e in range(2):
        for k in range(2):
            load_grads(e, k).start()
    for i in range(2):
        load_output(i).start()
        load_qkv(i).start()
    norm_grads()
    greet([to[name] for name in ("z1", "z2", "z3", "y", "x", "c", "xc")])
    own_tokens = pl.ds(0, length)
    lefts = left_copies(0, mixed, left_output) + left_copies(1, normed, left_qkv)
    rights = {m: right_copy(2, grad_branch, right_output, m) for m in (1, 2, 3)}
    qkv_rights = {m: right_copy(3, grad_qkv, right_qkv, m) for m in (1, 2, 3)}
    rights[2].start()
    rights[1].start()
    for made in lefts:
        made.start()
    left_output[:, :, own_tokens] = mixed[:, core, side]
    left_qkv[:, :, own_tokens] = normed[:, core, side]
    right_output[own_tokens] = grad_branch[...]
    o_start()

    for r in range(ZLINE):
        load_rows(r).wait()

        def turn(j, _, r=r):
            at = pl.ds(pl.multiple_of(j * 256, 256), 256)
            turned[at, pl.ds(r * count, count)] = rows[:, at].T
            return 0

        lax.fori_loop(0, width // 256, turn, 0)
        if r + 1 < ZLINE:
            load_rows(r + 1).start()

    def send_y(e):
        return remote(
            part_gate_up.at[e, 1 - y], heard_gate_up.at[e], y_send.at[e], y_recv.at[e], to["y"]
        )

    def send_z(e, m):
        return remote(
            part_gate_up.at[e, y, z_of[m]],
            heard_z.at[m - 1, e],
            z_send.at[m - 1, e],
            z_recv.at[m - 1, e],
            to[f"z{m}"],
        )

    def reduce(e):
        send_y(e).wait_recv()
        for b in range(ZLINE):
            part_gate_up[e, y, b] = add(part_gate_up[e, y, b], heard_gate_up[e, b])
        for m in range(1, ZLINE):
            send_z(e, m).start()

    def gate_up(e, _):
        for k in range(2):
            load_grads(e, k).wait()
        right = grads[lax.rem(e, 2)].reshape(tokens, 2 * hidden)

        def step(b, _):
            at = pl.ds(pl.multiple_of(b * rows_y * n, 128), rows_y * n)
            result = jnp.dot(turned[at, :], right, preferred_element_type=f32).astype(bf16)
            for k in range(rows_y):
                part_gate_up[e, k, b] = result[k * n : (k + 1) * n]
            return 0

        lax.fori_loop(0, ZLINE, step, 0)

        @pl.when(e + 2 < owned)
        def _():
            for k in range(2):
                load_grads(e + 2, k).start()

        return 0

    rights[2].wait_recv()
    rights[3].start()
    lax.fori_loop(0, 1, gate_up, 0)
    send_y(0).start()
    lax.fori_loop(0, KV // GROUP // 2, attend, 0)
    lax.fori_loop(1, 2, gate_up, 0)
    send_y(1).start()
    lax.fori_loop(KV // GROUP // 2, KV // GROUP, attend, 0)
    qkv_rights[2].start()
    qkv_rights[1].start()
    right_qkv[own_tokens] = grad_qkv[...]
    o_after_z1()
    for made in lefts:
        made.wait_recv()
    rights[1].wait_recv()
    rights[3].wait_recv()
    products(output, left_output, right_output)
    reduce(0)
    lax.fori_loop(2, 3, gate_up, 0)
    send_y(2).start()
    o_end()
    qkv_rights[2].wait_recv()
    qkv_rights[3].start()
    reduce(1)
    lax.fori_loop(3, 4, gate_up, 0)
    send_y(3).start()
    qkv_rights[1].wait_recv()
    qkv_rights[3].wait_recv()
    products(qkv, left_qkv, right_qkv)
    input_grads()
    reduce(2)
    lax.fori_loop(4, 5, gate_up, 0)
    send_y(4).start()
    small.after_c()
    output.after_z1()
    reduce(3)
    lax.fori_loop(5, 6, gate_up, 0)
    send_y(5).start()
    lax.fori_loop(6, 7, gate_up, 0)
    small.after_x()
    output.after_z2()
    reduce(4)
    send_y(6).start()
    lax.fori_loop(7, 8, gate_up, 0)
    qkv.after_y()
    reduce(5)
    send_y(7).start()
    lax.fori_loop(8, 9, gate_up, 0)
    lax.fori_loop(9, 10, gate_up, 0)
    output.after_y()
    qkv.after_z1()
    reduce(6)
    send_y(8).start()
    small.after_y()
    reduce(7)
    send_y(9).start()
    qkv.after_z2()
    output.after_back()
    small.after_z1()
    reduce(8)
    small.after_z2()
    qkv.after_back()
    small.after_back()
    reduce(9)

    def keep(e):
        return pltpu.make_async_copy(
            stage.at[lax.rem(e, 2)], gate_up_out.at[e], store_sems.at[lax.rem(e, 2)]
        )

    def collect(e, _):
        slot = lax.rem(e, 2)

        @pl.when(e >= 2)
        def _():
            keep(e - 2).wait()

        for m in range(ZLINE):
            if m:
                send_z(e, m).wait_recv()
                block = heard_z[m - 1, e]
            else:
                block = part_gate_up[e, y, z]
            for k in range(2):
                at = pl.ds(pl.multiple_of(k * F + z_of[m] * hidden, hidden), hidden)
                stage[slot, :, at] = block[:, k * hidden : (k + 1) * hidden]
        keep(e).start()
        return 0

    lax.fori_loop(0, owned, collect, 0)

    for e in (owned - 2, owned - 1):
        keep(e).wait()

    def close(e, _):
        send_y(e).wait_send()
        for m in range(1, ZLINE):
            send_z(e, m).wait_send()
        return 0

    lax.fori_loop(0, owned, close, 0)
    for array in (output, small, qkv):
        array.close()
    small.to_c().wait_send()
    small.to_x().wait_send()
    for k in range(3):
        o_copy(k).wait_send()
    for made in lefts + list(rights.values()) + list(qkv_rights.values()):
        made.wait_send()


def finish(rows_y, rows, grads, combined, heard, w_output, w_qkv, *small):
    _, count, width = rows.shape
    hidden = F // ZLINE
    owned = grads.shape[2] // (2 * hidden)
    length = small[0].shape[0]
    blocks = ZLINE * rows_y
    n = width // blocks
    columns = (w_output.shape[1], 128, w_qkv.shape[1])
    any_space = pl.BlockSpec(memory_space=pl.ANY)
    vmem = pl.BlockSpec(memory_space=pltpu.VMEM)
    sems = pltpu.SemaphoreType.DMA

    def summed(wide, own_rows, z_first=False):
        heard = own_rows != n // 4
        ends = (rows_y, n // 4, wide) if z_first else (n // 4, wide)
        return [
            pltpu.VMEM((ZLINE, rows_y, own_rows, wide), bf16),
            pltpu.VMEM((ZLINE, rows_y, n // 2, wide) if heard else (16, 128), bf16),
            pltpu.VMEM((ZLINE, rows_y, n // 4, wide) if heard else (16, 128), bf16),
            pltpu.VMEM((1 if z_first else ZLINE, n // 4, wide), bf16),
            pltpu.VMEM((2,) + ends, bf16),
            pltpu.VMEM(ends, bf16),
        ]

    return pl.pallas_call(
        functools.partial(finish_kernel, rows_y),
        name="finish",
        out_shape=(
            jax.ShapeDtypeStruct((owned, n, 2 * F), bf16),
            jax.ShapeDtypeStruct((length, width), bf16),
            jax.ShapeDtypeStruct((length, width), bf16),
        )
        + tuple(jax.ShapeDtypeStruct((n, v), bf16) for v in columns),
        in_specs=[any_space] * 6 + [vmem] * len(small),
        out_specs=(any_space,) + (vmem,) * 5,
        scratch_shapes=[
            pltpu.VMEM((count, width), bf16),
            pltpu.VMEM((width, ZLINE * count), bf16),
            pltpu.VMEM((2, ZLINE, count, 2 * hidden), bf16),
            pltpu.VMEM((owned, rows_y, ZLINE, n, 2 * hidden), bf16),
            pltpu.VMEM((owned, ZLINE, n, 2 * hidden), bf16),
            pltpu.VMEM((ZLINE - 1, owned, n, 2 * hidden), bf16),
            pltpu.VMEM((2, n, 2 * F), bf16),
            pltpu.VMEM((ZLINE, length, width), bf16),
            pltpu.VMEM((ZLINE, length, width), bf16),
            pltpu.VMEM((2, length, width), bf16),
            pltpu.VMEM((length, width), bf16),
            pltpu.VMEM((2, GROUP * (H // KV) * HD, width), bf16),
            pltpu.VMEM((2, 256, columns[2]), bf16),
            pltpu.VMEM((length, columns[2]), bf16),
            pltpu.VMEM((length, width), f32),
            pltpu.VMEM((blocks, n // 4, 4 * length), bf16),
            pltpu.VMEM((blocks, n // 4, 4 * length), bf16),
            pltpu.VMEM((4 * length, columns[0]), bf16),
            pltpu.VMEM((4 * length, columns[2]), bf16),
            pltpu.VMEM((ZLINE, rows_y, n, 128), bf16),
            pltpu.VMEM((length, width), f32),
            pltpu.VMEM((length, width), bf16),
            pltpu.VMEM((width, 128), f32),
            *summed(columns[0], n // 4, True),
            *summed(columns[1], n // 2),
            *summed(columns[2], n // 4),
            sems,
            sems((2,)),
            sems((2, 2)),
            sems((2, 2)),
            sems((2,)),
            sems((owned,)),
            sems((owned,)),
            sems((ZLINE - 1, owned)),
            sems((ZLINE - 1, owned)),
            sems((3, 8 + ZLINE)),
            sems((3, 8 + ZLINE)),
            sems((4, 4)),
            sems((4, 4)),
            sems((3,)),
            sems((3,)),
        ],
        compiler_params=pltpu.CompilerParams(
            collective_id=3, has_side_effects=True, vmem_limit_bytes=63 * 2**20
        ),
    )(rows, grads, combined, heard, w_output, w_qkv, *small)


def widen_kernel(
    gate_up,
    down,
    qkv,
    output,
    small,
    tokens,
    grad_tokens,
    gate_up_out,
    down_out,
    query_out,
    key_out,
    value_out,
    output_out,
    router_out,
    gains_out,
    tokens_out,
    grad_tokens_out,
):
    gate_up_out[...] = gate_up[...].astype(f32)
    down_out[...] = down[...].astype(f32)

    @pl.when(pl.program_id(0) == 0)
    def _():
        query_out[...] = qkv[:, : H * HD].astype(f32)
        key_out[...] = qkv[:, H * HD : (H + KV) * HD].astype(f32)
        value_out[...] = qkv[:, (H + KV) * HD :].astype(f32)
        output_out[...] = output[...].astype(f32)
        router_out[...] = small[:, :EXPERTS].astype(f32)
        lane, row = (lax.broadcasted_iota(jnp.int32, (8, 128), k) for k in (1, 0))
        gains_out[...] = against((lane == row + EXPERTS).astype(f32).astype(bf16), small[...])
        tokens_out[...] = tokens[...]
        grad_tokens_out[...] = grad_tokens[...]


def widen(*sums):
    gate_up, down, qkv, output, small, tokens, grad_tokens = sums
    n = qkv.shape[0]

    def whole(shape):
        return pl.BlockSpec(shape, lambda e: (0,) * len(shape))

    def one(shape):
        return pl.BlockSpec((1,) + shape[1:], lambda e: (e, 0, 0))

    shapes = [(n, H * HD), (n, KV * HD), (n, KV * HD), output.shape, (n, EXPERTS), (8, n)]
    return pl.pallas_call(
        widen_kernel,
        name="widen",
        grid=(gate_up.shape[0],),
        out_shape=[jax.ShapeDtypeStruct(v, f32) for v in [gate_up.shape, down.shape] + shapes]
        + [jax.ShapeDtypeStruct(tokens.shape, bf16)] * 2,
        in_specs=[one(gate_up.shape), one(down.shape)] + [whole(v.shape) for v in sums[2:]],
        out_specs=[one(gate_up.shape), one(down.shape)]
        + [whole(v) for v in shapes + [tokens.shape] * 2],
        compiler_params=pltpu.CompilerParams(vmem_limit_bytes=63 * 2**20),
    )(*sums)


def permuted(
    tokens,
    segments,
    routes,
    w_query,
    w_key,
    w_value,
    w_output,
    w_router,
    gain_attn,
    gain_moe,
    w_gate_up,
    w_down,
    cotangent,
):
    place = Place()
    length, width = tokens.shape
    owned = w_gate_up.shape[0]
    rows = w_query.shape[0]
    hidden = F // ZLINE
    per_group = H // KV
    q_end, k_end, v_end = H * HD, (H + KV) * HD, (H + 2 * KV) * HD
    o_end = v_end + width

    small = jnp.concatenate(
        [w_router, gain_attn[:, None], gain_moe[:, None], jnp.zeros((rows, 128 - EXPERTS - 2), bf16)],
        axis=1,
    )
    shard = jnp.concatenate([w_query, w_key, w_value, w_output, small], axis=1)
    full, order = gather_weights(place, shard)
    full_qkv, full_output = full[:, :v_end], full[:, v_end:o_end]
    full_small = transposed(order, full[:, o_end:]).astype(bf16)
    full_router = full_small[:, :EXPERTS]
    attn_gain = full_small[:, EXPERTS].astype(f32)
    moe_gain = full_small[:, EXPERTS + 1].astype(f32)

    chosen_mask = jnp.any(
        routes[:, :, None] == jnp.arange(EXPERTS, dtype=jnp.int32), axis=1
    )
    dy_block = jnp.concatenate(
        [cotangent, chosen_mask.astype(bf16), jnp.zeros((length, 128 - EXPERTS), bf16)], axis=1
    )
    dy_groups = gather_tokens(place, dy_block)

    cosine_table, sine_table = tables(length, HD)
    inputs = tokens.astype(f32)
    inv_attn = lax.rsqrt(jnp.mean(inputs * inputs, axis=-1, keepdims=True) + epsilon)
    unit_attn = inputs * inv_attn
    normed = (unit_attn * attn_gain).astype(bf16)
    normed = against(normed, order).astype(bf16)
    qkv = dot(normed, full_qkv)
    queries = rotate(qkv[:, :q_end].reshape(length, H, HD), cosine_table, sine_table)
    queries = queries.astype(bf16).reshape(length, KV, per_group, HD)
    key_rows = rotate(
        qkv[:, q_end:k_end].reshape(length, KV, HD), cosine_table, sine_table
    ).astype(bf16)
    values = qkv[:, k_end:].astype(bf16).reshape(length, KV, HD)
    segment = segments[0]
    position = jnp.arange(length, dtype=jnp.int32)
    allowed = (segment[:, None] == segment[None, :]) & (position[:, None] >= position[None, :])
    scores = (
        jnp.einsum("qkgd,skd->kgqs", queries, key_rows, preferred_element_type=f32) * 0.125
    )
    scores = jnp.where(allowed, scores, -1e30)
    maximum = jnp.max(scores, axis=-1, keepdims=True)
    lifted_scores = jnp.exp(scores - maximum)
    full_weights = lifted_scores / jnp.sum(lifted_scores, axis=-1, keepdims=True)
    attn_weights = full_weights.astype(bf16)
    mixed = jnp.einsum("kgqs,skd->qkgd", attn_weights, values, preferred_element_type=f32)
    mixed = mixed.reshape(length, H * HD).astype(bf16)
    mixed = against(mixed, order).astype(bf16)
    residual = inputs + dot(mixed, full_output)
    inv_moe = lax.rsqrt(jnp.mean(residual * residual, axis=-1, keepdims=True) + epsilon)
    unit_moe = residual * inv_moe
    normed_moe = (unit_moe * moe_gain).astype(bf16)

    def gates_of(rows_in, mask):
        logits = jnp.where(mask, dot(rows_in, full_router), -1e30)
        lifted = jnp.where(mask, jnp.exp(logits - jnp.max(logits, axis=-1, keepdims=True)), 0.0)
        return lifted / jnp.sum(lifted, axis=-1, keepdims=True)

    gates = gates_of(normed_moe, chosen_mask)

    def columns(start):
        cut = lax.dynamic_slice_in_dim(w_gate_up, start + place.z * hidden, hidden, 2)
        return cut.swapaxes(0, 1).reshape(width, owned * hidden)

    slice_gate_up = jnp.concatenate([columns(0), columns(F)], axis=1)
    slice_down = lax.dynamic_slice_in_dim(w_down, place.z * hidden, hidden, 1)
    slice_down = slice_down.reshape(owned * hidden, width)
    moe_groups = gather_tokens(place, normed_moe)
    span = owned * hidden
    acts, grads_gate_up, gate_parts = [], [], []
    for normed_rows, dy_rows in zip(moe_groups, dy_groups):
        count = normed_rows.shape[0]
        group_gates = gates_of(normed_rows, dy_rows[:, width : width + EXPERTS] > 0.5)
        group_gates = lax.dynamic_slice_in_dim(group_gates, place.ex * owned, owned, 1)
        spread_gates = jnp.broadcast_to(group_gates[:, :, None], (count, owned, hidden))
        spread_gates = spread_gates.reshape(count, span)
        gate_up = dot(normed_rows, slice_gate_up)
        gate_part, up_part = gate_up[:, :span], gate_up[:, span:]
        plain_grad = against(dy_rows[:, :width], slice_down)
        sigmoid_gate = jax.nn.sigmoid(gate_part)
        swished = gate_part * sigmoid_gate
        activation = swished * up_part
        grad_act = plain_grad * spread_gates
        gate_parts.append(jnp.sum((plain_grad * activation).reshape(count, owned, hidden), axis=-1))
        acts.append((spread_gates * activation).astype(bf16))
        grads_gate_up.append(
            jnp.concatenate(
                [
                    grad_act * up_part * sigmoid_gate * (1.0 + gate_part * (1.0 - sigmoid_gate)),
                    grad_act * swished,
                ],
                axis=-1,
            ).astype(bf16)
        )
    row_parts = [against(g, slice_gate_up).astype(bf16) for g in grads_gate_up]
    row_grads = scatter_tokens(place, row_parts, length)
    out_parts = [dot(a, slice_down).astype(bf16) for a in acts]
    output = (residual + scatter_tokens(place, out_parts, length)).astype(bf16)

    gate_parts = [g.T for g in gate_parts]
    two = [gate_parts[i] + swap(gate_parts[i + 2], "dp", place.z_bits[1]) for i in range(2)]
    mine = two[0] + swap(two[1], "dp", place.z_bits[0])
    mine = mine.reshape(owned, 2, place.ex_size // 2, length)
    heard = [
        swap(mine[:, m % 2, m // 2], "expert", m) if m else mine[:, 0, 0]
        for m in range(place.ex_size)
    ]
    heard = jnp.stack(heard)
    grad_gates = jnp.concatenate(
        [pick(heard, place.ex ^ j) for j in range(place.ex_size)], axis=0
    ).T
    grad_logits = (
        gates * (grad_gates - jnp.sum(gates * grad_gates, axis=-1, keepdims=True))
    ).astype(bf16)

    all_rows = jnp.concatenate([v for v in moe_groups], axis=0)
    all_dy = jnp.concatenate([v[:, :width] for v in dy_groups], axis=0)
    all_grads = jnp.concatenate(grads_gate_up, axis=0)
    all_acts = jnp.concatenate(acts, axis=0)

    def reduce_y(part, axis):
        part = jnp.moveaxis(part, axis, 0)
        for mask in place.y_bits[::-1]:
            at = (place.y // mask) % 2
            half = part.reshape((2, part.shape[0] // 2) + part.shape[1:])
            away = swap(pick(half, 1 - at), "dp", mask)
            part = (pick(half, at).astype(f32) + away.astype(f32)).astype(bf16)
        return part[0]

    shard_down = transposed(all_acts, all_dy).astype(bf16)
    shard_down = shard_down.reshape(owned, place.rows_y, hidden // place.rows_y, width)
    shard_down = reduce_y(shard_down, 1).astype(f32)
    part_gate_up = transposed(all_rows, all_grads).astype(bf16)
    part_gate_up = part_gate_up.reshape(ZLINE, place.rows_y, rows, 2 * span)
    part_gate_up = reduce_y(part_gate_up, 1)
    heard = [pick(part_gate_up, place.z)] + [
        swap(pick(part_gate_up, place.z ^ m), "dp", m * place.rows_y) for m in range(1, ZLINE)
    ]
    heard = jnp.stack(heard)
    shard_gate_up = jnp.stack([pick(heard, place.z ^ j) for j in range(ZLINE)], axis=0)
    shard_gate_up = shard_gate_up.reshape(ZLINE, rows, 2, owned, hidden)
    shard_gate_up = shard_gate_up.transpose(3, 1, 2, 0, 4).reshape(owned, rows, 2 * F).astype(f32)

    grad_out = cotangent.astype(f32)
    part_router = transposed(normed_moe, grad_logits)
    grad_normed_moe = row_grads + against(grad_logits, full_router)
    part_gain_moe = jnp.sum(grad_normed_moe * unit_moe, axis=0)
    scaled_moe = grad_normed_moe * moe_gain
    grad_residual = grad_out + inv_moe * (
        scaled_moe - unit_moe * jnp.mean(scaled_moe * unit_moe, axis=-1, keepdims=True)
    )
    grad_branch = grad_residual.astype(bf16)
    part_output = transposed(mixed, grad_branch)
    grad_mixed = dot(against(grad_branch, full_output).astype(bf16), order).astype(bf16)
    grad_mixed = grad_mixed.reshape(length, KV, per_group, HD)
    grad_weights = jnp.einsum(
        "qkgd,skd->kgqs", grad_mixed, values, preferred_element_type=f32
    )
    grad_values = jnp.einsum(
        "kgqs,qkgd->skd", attn_weights, grad_mixed, preferred_element_type=f32
    )
    grad_values = grad_values.astype(bf16).reshape(length, KV * HD)
    grad_scores = (
        full_weights * (grad_weights - jnp.sum(full_weights * grad_weights, axis=-1, keepdims=True))
    ).astype(bf16)
    grad_queries = (
        jnp.einsum("kgqs,skd->qkgd", grad_scores, key_rows, preferred_element_type=f32) * 0.125
    )
    grad_queries = rotate(grad_queries.reshape(length, H, HD), cosine_table, -sine_table)
    grad_queries = grad_queries.astype(bf16).reshape(length, H * HD)
    grad_keys = (
        jnp.einsum("kgqs,qkgd->skd", grad_scores, queries, preferred_element_type=f32) * 0.125
    )
    grad_keys = rotate(grad_keys, cosine_table, -sine_table)
    grad_keys = grad_keys.astype(bf16).reshape(length, KV * HD)
    grad_qkv = jnp.concatenate([grad_queries, grad_keys, grad_values], axis=1)
    part_qkv = transposed(normed, grad_qkv)
    grad_normed = against(grad_qkv, full_qkv)
    grad_normed = lax.dot_general(
        grad_normed,
        order.astype(f32),
        (((1,), (0,)), ((), ())),
        precision=lax.Precision.HIGHEST,
        preferred_element_type=f32,
    )
    part_gain_attn = jnp.sum(grad_normed * unit_attn, axis=0)
    scaled_attn = grad_normed * attn_gain
    grad_tokens = (
        grad_residual
        + inv_attn
        * (scaled_attn - unit_attn * jnp.mean(scaled_attn * unit_attn, axis=-1, keepdims=True))
    ).astype(bf16)
    part_small = jnp.concatenate(
        [
            part_router.astype(bf16),
            part_gain_attn[:, None].astype(bf16),
            part_gain_moe[:, None].astype(bf16),
            jnp.zeros((width, 128 - EXPERTS - 2), bf16),
        ],
        axis=1,
    )
    part_small = dot(order, part_small).astype(bf16)
    summed = scatter_weights(
        place,
        jnp.concatenate([part_qkv.astype(bf16), part_output.astype(bf16), part_small], axis=1),
    )
    return (
        output,
        grad_tokens,
        summed[:, :q_end],
        summed[:, q_end:k_end],
        summed[:, k_end:v_end],
        summed[:, v_end:o_end],
        summed[:, o_end : o_end + EXPERTS],
        summed[:, o_end + EXPERTS],
        summed[:, o_end + EXPERTS + 1],
        shard_gate_up,
        shard_down,
    )


def local(
    tokens,
    segments,
    routes,
    w_query,
    w_key,
    w_value,
    w_output,
    w_router,
    gain_attn,
    gain_moe,
    w_gate_up,
    w_down,
    cotangent,
):
    place = Place()
    if place.ex_size != 4 or place.rows_y != 2:
        return permuted(
            tokens,
            segments,
            routes,
            w_query,
            w_key,
            w_value,
            w_output,
            w_router,
            gain_attn,
            gain_moe,
            w_gate_up,
            w_down,
            cotangent,
        )
    length, width = tokens.shape
    per_group = H // KV
    v_end = (H + 2 * KV) * HD

    angles = np.arange(length)[:, None] * 10000.0 ** (-2.0 * np.arange(HD // 2) / HD)[None, :]
    repeats = (1, GROUP * per_group)
    cosine = jnp.asarray(np.tile(np.tile(np.cos(angles), (1, 2)), repeats), f32)
    sine = np.concatenate([np.sin(angles), -np.sin(angles)], axis=1)
    sine = jnp.asarray(np.tile(sine, repeats), f32)
    (
        full_qkv,
        full_output,
        all_dy,
        plain_grads,
        full_small,
        queries,
        key_rows,
        values,
        residual,
        normed_moe,
        normed,
        mixed,
        gains,
        gates,
        allowed,
    ) = gather(
        place.rows_y,
        (w_query, w_key, w_value, w_output, w_router.T, gain_attn, gain_moe),
        cotangent,
        tokens,
        segments,
        routes.T,
        cosine,
        sine,
        w_down,
    )
    full_small = full_small.reshape(width, 128)
    all_rows, all_grads, shard_down, combined, heard, row_grads = moe(
        place.rows_y, normed_moe, all_dy, plain_grads, w_gate_up, w_down, full_small
    )
    shard_gate_up, output, grad_tokens, sum_output, sum_small, sum_qkv = finish(
        place.rows_y,
        all_rows,
        all_grads,
        combined,
        heard,
        full_output.reshape(width, width),
        full_qkv.reshape(width, v_end),
        row_grads,
        gates,
        cotangent,
        residual,
        normed_moe,
        gains,
        full_small,
        tokens,
        mixed,
        normed,
        queries,
        key_rows,
        values,
        allowed,
        cosine,
        sine,
    )
    (
        shard_gate_up,
        shard_down,
        shard_query,
        shard_key,
        shard_value,
        shard_output,
        shard_router,
        shard_gains,
        output,
        grad_tokens,
    ) = widen(shard_gate_up, shard_down, sum_qkv, sum_output, sum_small, output, grad_tokens)
    return (
        output,
        grad_tokens,
        shard_query,
        shard_key,
        shard_value,
        shard_output,
        shard_router,
        shard_gains[0],
        shard_gains[1],
        shard_gate_up,
        shard_down,
    )


def solution(mesh):
    return jax.shard_map(
        local,
        mesh=mesh,
        in_specs=(
            P(("dp", "expert"), None),
            P(("dp", "expert"), None),
            P(("dp", "expert"), None),
            P("dp", None),
            P("dp", None),
            P("dp", None),
            P("dp", None),
            P("dp", None),
            P("dp"),
            P("dp"),
            P("expert", None, None),
            P("expert", None, None),
            P(("dp", "expert"), None),
        ),
        out_specs=(
            P(("dp", "expert"), None),
            P(("dp", "expert"), None),
            P("dp", None),
            P("dp", None),
            P("dp", None),
            P("dp", None),
            P("dp", None),
            P("dp"),
            P("dp"),
            P("expert", "dp", None),
            P("expert", "dp", None),
        ),
        check_vma=False,
    )
```
